32 devices in a mesh: grp: 2 (over y), gx: 8 (over z, x), gy: 2 (over core).
Axes of the slice: x: 2, y: 2, z: 4, core: 2. Of those that a mesh axis runs over, the one named last changes fastest.
Arguments:
- density: float32 [32, 128, 256], P('gx', ('grp', 'gy')), may hold values from 1 to 2
- momentum: float32 [3, 32, 128, 256], P(None, 'gx', ('grp', 'gy')), may hold values from -0.5 to 0.5
- energy: float32 [32, 128, 256], P('gx', ('grp', 'gy')), may hold values from 3 to 6
- displacement: float32 [3, 72, 68, 512], P(None, 'gx', ('grp', 'gy')), as said below
- velocity_field: float32 [3, 72, 68, 512], P(None, 'gx', ('grp', 'gy')), as said below
- acceleration: float32 [3, 72, 68, 512], P(None, 'gx', ('grp', 'gy')), as said below
- material: float32 [3, 8], replicated, may hold values from 1 to 4
- element_region_index: int32 [16, 16, 128], P('gx', ('grp', 'gy')), may hold values from 0 to 7
- face_dest: int32 [32, 128, 1], P(('grp', 'gx', 'gy')), may hold values from 0 to 31; in each aligned block of 128 rows (0 to 127, 128 to 255, ..., all dimensions but the last counted through in order) at most 8 rows name the same one
- face_slot: int32 [32, 128], P(('grp', 'gx', 'gy')), may hold values from 0 to 152
Outputs:
- hydro_final: float32 [5, 32, 128, 256], P(None, 'gx', ('grp', 'gy'))
- displacement_out: float32 [3, 72, 68, 512], P(None, 'gx', ('grp', 'gy'))
- velocity_out: float32 [3, 72, 68, 512], P(None, 'gx', ('grp', 'gy'))
- acceleration_out: float32 [3, 72, 68, 512], P(None, 'gx', ('grp', 'gy'))
The draws below stay inside these ranges and needn't reach their ends.
Inputs may be any that keep to these rules, and one draw needn't show every extreme that they name: `face_dest`: among the 128 rows of one device no owner is named more than 8 times; some owner is named exactly 8 times by some device. `displacement`: copies of one node held by neighbouring blocks are equal. `velocity_field`: copies of one node held by neighbouring blocks are equal. `acceleration`: copies of one node held by neighbouring blocks are equal.
All inputs are finite; a program needn't handle non-finite values.
Results may differ from the reference program's by a relative error of at most 0.0003.
Values sent between devices are 32-bit elements; how exact they have to be, the bound alone decides.
No kernel may reach another device: no remote copies, remote signals or barrier semaphores. Data moves between devices by JAX's collectives and lax.ppermute only.
A program may use at most 128 MiB of HBM per device.

```python
import math
import jax
import jax.numpy as jnp
import numpy as np
from jax import lax

CX = 4
CY = 32
NZH = 256
EX = 2
EY = 4
ELEMENTS_DEPTH = 128
MATERIAL_REGIONS = 8
NXH = 32
NYH = 128
SURF_DEV = 128
CAP = 8
NX1 = 9
NY1 = 17
ELEMENTS_ALONG_X = 16
ELEMENTS_ALONG_Y = 16
NNX = 65
NNY = 65
NZN = 512
SX = 72
SY = 68
N_GRP = 2
N_GX = 8
N_GY = 2
DEVICES = 32


def copy_to_blocks(unique):
    parts_x = SX // NX1
    parts_y = SY // NY1
    index_x = (jnp.arange(parts_x, dtype=jnp.int32)[:, None] * (NX1 - 1) + jnp.arange(NX1, dtype=jnp.int32)[None, :]).reshape(-1)
    index_y = (jnp.arange(parts_y, dtype=jnp.int32)[:, None] * (NY1 - 1) + jnp.arange(NY1, dtype=jnp.int32)[None, :]).reshape(-1)
    return jnp.take(jnp.take(unique, index_x, axis=1), index_y, axis=2)


def draw_displacement(key, part):
    key = jax.random.fold_in(key, 11)
    unique = 0.1 * jax.random.normal(key, (3, NNX, NNY, NZN), jnp.float32)
    return copy_to_blocks(unique)


def draw_velocity_field(key, part):
    key = jax.random.fold_in(key, 12)
    unique = jax.random.normal(key, (3, NNX, NNY, NZN), jnp.float32)
    return copy_to_blocks(unique)


def draw_acceleration(key, part):
    key = jax.random.fold_in(key, 13)
    unique = 2.0 * jax.random.normal(key, (3, NNX, NNY, NZN), jnp.float32)
    return copy_to_blocks(unique)


def plant(values, key, least, largest):
    spot = [jax.random.randint(jax.random.fold_in(key, axis), (), 0, length) for axis, length in enumerate(values.shape)]
    longest = values.shape.index(max(values.shape))
    beside = spot[:longest] + [(spot[longest] + 1) % values.shape[longest]] + spot[longest + 1:]
    return values.at[tuple(spot)].set(least).at[tuple(beside)].set(largest)


def level_of(rng, dims, split, least, top_value):
    factor_of, own = 1.0, jax.random.fold_in(rng, 6)
    for dim, parts in split:
        steps = jnp.exp(jax.random.uniform(jax.random.fold_in(own, dim), (parts,), jnp.float32, least / len(split), top_value / len(split)))
        factor_of = factor_of * jnp.repeat(steps, dims[dim] // parts).reshape([-1 if axis == dim else 1 for axis in range(len(dims))])
    return factor_of


def deal_out(key, own, number, rows, count, top, most, lean):
    sequence = jax.random.permutation(key, count)
    packed, usual = shares(count, rows * top, most, lean, True), shares(count, rows * top, most, lean, False)
    places = jnp.arange(count)

    def named(tallies, rotation):
        used = int((tallies > 0).sum())
        fixed = max(1, used // 4)
        shifted = fixed + (places - fixed + rotation * (used - fixed)) % max(1, count - fixed)
        return jnp.zeros((count,), jnp.int32).at[sequence[jnp.where(places < fixed, places, shifted)]].set(jnp.asarray(tallies, jnp.int32))

    tallies = jnp.where(number % 4 == 0, named(packed, number // 4), named(usual, number - number // 4 - 1))
    mixed = jax.random.permutation(jax.random.fold_in(own, 3), count)
    donor, receiver = mixed[0:count // 2 * 2:2], mixed[1:count // 2 * 2:2]
    room = jnp.minimum(tallies[donor] - 1, most - tallies[receiver]) // 2
    room = jnp.where((donor == sequence[0]) | (receiver == sequence[0]) | (tallies[receiver] == 0), 0, jnp.maximum(room, 0))
    shifted = jax.random.randint(jax.random.fold_in(own, 4), (count // 2,), 0, 1 << 20) % (room + 1)
    tallies = tallies.at[donor].add(-shifted).at[receiver].add(shifted)
    members = jnp.searchsorted(jnp.cumsum(tallies), jnp.arange(rows * top), side="right").astype(jnp.int32)
    grid = members.reshape(top, rows).T
    grid = grid[jax.random.permutation(jax.random.fold_in(own, 1), rows)]
    rotation = jax.random.randint(jax.random.fold_in(own, 2), (rows, 1), 0, top)
    return jnp.take_along_axis(grid, (jnp.arange(top)[None, :] + rotation) % top, axis=1)


def shares(count, total, most, lean, full):
    loads = [(1 << 20) // math.isqrt(rank ** lean) + 1 for rank in range(1, count + 1)]
    largest = most if full else min(most, max(-(-total // count), total * loads[0] // sum(loads)))
    least = 1 if total - largest >= count - 1 else 0
    counts, surplus = [largest] + [least] * (count - 1), total - largest - least * (count - 1)
    while surplus > 0:
        movable = [i for i in range(1, count) if counts[i] < largest] or [i for i in range(1, count) if counts[i] < most]
        mass, budget = sum([loads[i] for i in movable]), surplus
        for i in movable:
            extra = min(most - counts[i], max(1, budget * loads[i] // mass), surplus)
            counts[i] = counts[i] + extra
            surplus = surplus - extra
    return np.array(counts)


def setup_inputs(seed: int = 0) -> dict:
    streams_of = jax.random.split(jax.random.key(seed), 11)
    density = jnp.clip(1.0 + 1.0 * jax.random.uniform(streams_of[0], (NXH, NYH, NZH), jnp.float32) ** level_of(streams_of[0], (NXH, NYH, NZH), ((0, 8), (1, 4)), -0.2, 0.2), 1.0, 2.0)
    momentum = jnp.clip(jax.random.uniform(streams_of[1], (3, NXH, NYH, NZH), jnp.float32, -0.5, 0.5) * level_of(streams_of[1], (3, NXH, NYH, NZH), ((1, 8), (2, 4)), -0.4, 0.0), -0.5, 0.5)
    energy = jnp.clip(3.0 + 3.0 * jax.random.uniform(streams_of[2], (NXH, NYH, NZH), jnp.float32) ** level_of(streams_of[2], (NXH, NYH, NZH), ((0, 8), (1, 4)), -0.2, 0.2), 3.0, 6.0)
    displacement = draw_displacement(jax.random.fold_in(streams_of[10], 71), 0)
    velocity_field = draw_velocity_field(jax.random.fold_in(streams_of[10], 71), 0)
    acceleration = draw_acceleration(jax.random.fold_in(streams_of[10], 71), 0)
    material = jnp.clip(jnp.exp(jax.random.uniform(streams_of[6], (3, MATERIAL_REGIONS), jnp.float32, math.log(1.0), math.log(4.0))), 1.0, 4.0)
    element_region_index = plant(jax.random.randint(streams_of[7], (ELEMENTS_ALONG_X, ELEMENTS_ALONG_Y, ELEMENTS_DEPTH), 0, MATERIAL_REGIONS), jax.random.fold_in(streams_of[7], 1), 0, MATERIAL_REGIONS - 1).astype(jnp.int32)
    face_dest_keys = jax.random.split(jax.random.fold_in(streams_of[8], 1), DEVICES * SURF_DEV // SURF_DEV)
    face_dest_turns = jax.random.permutation(jax.random.fold_in(streams_of[8], 3), DEVICES * SURF_DEV // SURF_DEV)
    face_dest = jax.vmap(lambda own, number: deal_out(jax.random.fold_in(streams_of[8], 2), own, number, SURF_DEV, DEVICES, 1, CAP, 2))(face_dest_keys, face_dest_turns).reshape((DEVICES, SURF_DEV, 1))
    face_slot = plant(jax.random.randint(streams_of[9], (DEVICES, SURF_DEV), 0, NX1 * NY1), jax.random.fold_in(streams_of[9], 1), 0, (NX1 * NY1) - 1).astype(jnp.int32)
    return dict(density=density, momentum=momentum, energy=energy, displacement=displacement, velocity_field=velocity_field, acceleration=acceleration, material=material, element_region_index=element_region_index, face_dest=face_dest, face_slot=face_slot)


gamma_gas = 1.4
cell_ratio = 0.05
half_size = 2.0
time_step = 0.1
face_area = 2.0

def gll_tables():
    gll_root = np.sqrt(3.0 / 7.0)
    points = np.array([-1.0, -gll_root, 0.0, gll_root, 1.0])
    weights = np.array([0.1, 49.0 / 90.0, 32.0 / 45.0, 49.0 / 90.0, 0.1])
    products = np.array([np.prod([points[row_num] - points[col_num] for col_num in range(5) if col_num != row_num]) for row_num in range(5)])
    derivative = np.zeros((5, 5))
    for row_num in range(5):
        for col_num in range(5):
            if row_num != col_num:
                derivative[row_num, col_num] = products[row_num] / products[col_num] / (points[row_num] - points[col_num])
        derivative[row_num, row_num] = sum((1.0 / (points[row_num] - points[col_num]) for col_num in range(5) if col_num != row_num))
    return (jnp.asarray(derivative, dtype=jnp.float32), jnp.asarray(weights, dtype=jnp.float32))

def pressure_of(hydro_state):
    velocity = hydro_state[1:4] / hydro_state[0]
    pressure = (gamma_gas - 1.0) * (hydro_state[4] - 0.5 * lax.optimization_barrier(jnp.sum(hydro_state[1:4] * velocity, axis=0)))
    return (velocity, pressure)

def euler_flux(hydro_state, axis_num):
    velocity, pressure = pressure_of(hydro_state)
    sound_speed = jnp.sqrt(gamma_gas * pressure / hydro_state[0])
    normal_vel = velocity[axis_num]
    unit_row = jnp.eye(3, dtype=jnp.float32)[axis_num].reshape(3, 1, 1, 1)
    momentum_flux = hydro_state[1:4] * normal_vel + pressure * unit_row
    energy_flux = (hydro_state[4] + pressure) * normal_vel
    flux_all = jnp.concatenate([hydro_state[1 + axis_num][None], momentum_flux, energy_flux[None]], axis=0)
    return (flux_all, jnp.abs(normal_vel) + sound_speed)

def advance(padded):
    interior = padded[:, 1:-1, 1:-1, 1:-1]
    change = jnp.zeros_like(interior)
    for axis_num in range(3):
        pencil = padded
        for other_axis in range(3):
            if other_axis != axis_num:
                pencil = lax.slice_in_dim(pencil, 1, pencil.shape[other_axis + 1] - 1, axis=other_axis + 1)
        flux_all, wave_speed = euler_flux(pencil, axis_num)
        length = pencil.shape[axis_num + 1]
        low_state = lax.slice_in_dim(pencil, 0, length - 1, axis=axis_num + 1)
        high_state = lax.slice_in_dim(pencil, 1, length, axis=axis_num + 1)
        low_flux = lax.slice_in_dim(flux_all, 0, length - 1, axis=axis_num + 1)
        high_flux = lax.slice_in_dim(flux_all, 1, length, axis=axis_num + 1)
        fastest = jnp.maximum(lax.slice_in_dim(wave_speed, 0, length - 1, axis=axis_num), lax.slice_in_dim(wave_speed, 1, length, axis=axis_num))
        face_flux = 0.5 * (low_flux + high_flux) - 0.5 * fastest * (high_state - low_state)
        change = change + lax.slice_in_dim(face_flux, 1, length - 1, axis=axis_num + 1) - lax.slice_in_dim(face_flux, 0, length - 2, axis=axis_num + 1)
    return interior - cell_ratio * change

def surface_traction(hydro_state):
    bottom = hydro_state[:, :, :, -1]
    velocity, pressure = pressure_of(bottom[:, :, :, None])
    vertical = velocity[2, :, :, 0]
    return jnp.stack([bottom[1] * vertical, bottom[2] * vertical, bottom[3] * vertical + pressure[:, :, 0]]) * face_area

def split_points(field, axis_num, elements):
    return jnp.stack([lax.slice_in_dim(field, offset, offset + 4 * elements - 3, stride=4, axis=axis_num) for offset in range(5)], axis=1)

def scatter_to_elements(nodes, count_x, count_y, count_z):
    deeper = jnp.concatenate([nodes, jnp.zeros(nodes.shape[:3] + (1,), nodes.dtype)], axis=3)
    along_z = split_points(deeper, 3, count_z)
    along_y = split_points(along_z, 3, count_y)
    return split_points(along_y, 3, count_x)

def fold_points(values, elem_axis):
    pieces = [values[:, offset] for offset in range(5)]
    axis_num = elem_axis - 1
    widths = [(0, 0)] * pieces[0].ndim
    pad_after = list(widths)
    pad_after[axis_num] = (0, 1)
    pad_before = list(widths)
    pad_before[axis_num] = (1, 0)
    head_part = jnp.pad(pieces[0], pad_after) + jnp.pad(pieces[4], pad_before)
    stacked = jnp.stack([head_part] + [jnp.pad(portion, pad_after) for portion in pieces[1:4]], axis=axis_num + 1)
    new_shape = stacked.shape[:axis_num] + (stacked.shape[axis_num] * 4,) + stacked.shape[axis_num + 2:]
    merged = stacked.reshape(new_shape)
    return lax.slice_in_dim(merged, 0, merged.shape[axis_num] - 3, axis=axis_num)

def gather_to_nodes(values):
    folded = fold_points(fold_points(fold_points(values, 4), 4), 4)
    return folded[..., :-1]

def cell_weight(weights):
    cube = weights[:, None, None] * weights[None, :, None] * weights[None, None, :] * half_size ** 3
    return cube[:, :, :, None, None, None]

def material_fields(material, element_region_index):
    regions = jnp.arange(material.shape[1], dtype=jnp.int32)
    onehot = (element_region_index[None] == regions[:, None, None, None]).astype(jnp.float32)
    return [lax.optimization_barrier(jnp.sum(onehot * material[material_row][:, None, None, None], axis=0)) for material_row in range(3)]

def forces_per_element(elem_disp, first_lame_modulus, shear_lame_modulus):
    derivative, weights = gll_tables()
    inv_half = 1.0 / half_size
    highest = lax.Precision.HIGHEST
    gradients = [inv_half * jnp.einsum('ap,cpjkxyz->cajkxyz', derivative, elem_disp, precision=highest), inv_half * jnp.einsum('ap,cipkxyz->ciakxyz', derivative, elem_disp, precision=highest), inv_half * jnp.einsum('ap,cijpxyz->cijaxyz', derivative, elem_disp, precision=highest)]
    dilation = gradients[0][0] + gradients[1][1] + gradients[2][2]
    weighting = cell_weight(weights)
    forces = []
    for component in range(3):
        stress_row = [shear_lame_modulus * (gradients[direction][component] + gradients[component][direction]) for direction in range(3)]
        stress_row[component] = stress_row[component] + first_lame_modulus * dilation
        total = jnp.einsum('pa,pjkxyz->ajkxyz', derivative, weighting * stress_row[0], precision=highest)
        total = total + jnp.einsum('pa,ipkxyz->iakxyz', derivative, weighting * stress_row[1], precision=highest)
        total = total + jnp.einsum('pa,ijpxyz->ijaxyz', derivative, weighting * stress_row[2], precision=highest)
        forces.append(inv_half * total)
    return jnp.stack(forces)

def unique_nodes(field):
    parts_y = field.shape[2] // NY1
    blocks = field.reshape(3, N_GX, NX1, field.shape[2], NZN)[:, :, :NX1 - 1].reshape(3, N_GX * (NX1 - 1), field.shape[2], NZN)
    field_x = jnp.concatenate([blocks, field[:, -1:]], axis=1)
    blocks = field_x.reshape(3, field_x.shape[1], parts_y, NY1, NZN)[:, :, :, :NY1 - 1].reshape(3, field_x.shape[1], parts_y * (NY1 - 1), NZN)
    return jnp.concatenate([blocks, field_x[:, :, -1:]], axis=2)

def copy_nodes(unique):
    parts_y = SY // NY1
    index_x = (jnp.arange(N_GX, dtype=jnp.int32)[:, None] * (NX1 - 1) + jnp.arange(NX1, dtype=jnp.int32)[None, :]).reshape(-1)
    index_y = (jnp.arange(parts_y, dtype=jnp.int32)[:, None] * (NY1 - 1) + jnp.arange(NY1, dtype=jnp.int32)[None, :]).reshape(-1)
    return jnp.take(jnp.take(unique, index_x, axis=1), index_y, axis=2)

def reference(density, momentum, energy, displacement, velocity_field, acceleration, material, element_region_index, face_dest, face_slot):
    hydro_state = jnp.concatenate([density[None], momentum, energy[None]], axis=0)
    for repeat in range(2):
        hydro_state = advance(jnp.pad(hydro_state, ((0, 0), (1, 1), (1, 1), (1, 1)), mode='edge'))
    traction = surface_traction(hydro_state)
    by_device = traction.reshape(3, N_GX, CX, N_GRP, N_GY, CY).transpose(0, 3, 1, 4, 2, 5).reshape(3, DEVICES * CX * CY)
    targets = face_dest[:, :, 0].reshape(-1)
    slot_ids = face_slot.reshape(-1)
    target_grp = targets // (N_GX * N_GY)
    target_gx = targets // N_GY % N_GX
    target_gy = targets % N_GY
    node_x = target_gx * (4 * EX) + slot_ids // NY1
    node_y = (target_grp * N_GY + target_gy) * (4 * EY) + slot_ids % NY1
    flat_node = (node_x * NNY + node_y).astype(jnp.int32)
    deposited = jax.ops.segment_sum(by_device.T, flat_node, num_segments=NNX * NNY).T.reshape(3, NNX, NNY)
    surface_force = jnp.concatenate([deposited[..., None], jnp.zeros((3, NNX, NNY, NZN - 1), jnp.float32)], axis=3)
    rock_density, first_lame_modulus, shear_lame_modulus = material_fields(material, element_region_index)
    _, weights = gll_tables()
    mass_nodes = gather_to_nodes((rock_density * cell_weight(weights))[None])[0]
    current_displacement = unique_nodes(displacement)
    veloc_now = unique_nodes(velocity_field)
    accel_now = unique_nodes(acceleration)
    for repeat in range(2):
        current_displacement = current_displacement + time_step * veloc_now + 0.5 * time_step ** 2 * accel_now
        internal_forces = gather_to_nodes(forces_per_element(scatter_to_elements(current_displacement, ELEMENTS_ALONG_X, ELEMENTS_ALONG_Y, ELEMENTS_DEPTH), first_lame_modulus, shear_lame_modulus))
        accel_new = (surface_force - internal_forces) / mass_nodes
        veloc_now = veloc_now + 0.5 * time_step * (accel_now + accel_new)
        accel_now = accel_new
    return (hydro_state, copy_nodes(current_displacement), copy_nodes(veloc_now), copy_nodes(accel_now))
```

```python
import functools

import jax
import jax.numpy as jnp
import numpy as np
from jax import lax
from jax.experimental import pallas as pl
from jax.experimental.pallas import tpu as pltpu
from jax.sharding import PartitionSpec as P

gamma_gas = 1.4
cell_ratio = 0.05
half_size = 2.0
time_step = 0.1
face_area = 2.0
vmem_bytes = 40 * 1024 * 1024


def gll_tables():
    root = np.sqrt(3.0 / 7.0)
    points = np.array([-1.0, -root, 0.0, root, 1.0])
    weights = np.array([0.1, 49.0 / 90.0, 32.0 / 45.0, 49.0 / 90.0, 0.1])
    products = [np.prod([points[r] - points[c] for c in range(5) if c != r]) for r in range(5)]
    derivative = np.zeros((5, 5))
    for r in range(5):
        for c in range(5):
            if r != c:
                derivative[r, c] = products[r] / products[c] / (points[r] - points[c])
        derivative[r, r] = sum(1.0 / (points[r] - points[c]) for c in range(5) if c != r)
    derivative[2, 2] = 0.0
    return derivative, weights


deriv, quad = gll_tables()
deriv_t = deriv.T
kind = [0, 1, 2, 1, 0]
f32 = jnp.float32


def line(matrix, v):
    even, odd = (matrix + matrix[:, ::-1]) / 2, (matrix - matrix[:, ::-1]) / 2
    e0, e1, o0, o1 = v[0] + v[4], v[1] + v[3], v[0] - v[4], v[1] - v[3]
    top = [float(even[i, 0]) * e0 + float(even[i, 1]) * e1 + float(matrix[i, 2]) * v[2] for i in range(2)]
    low = [float(odd[i, 0]) * o0 + float(odd[i, 1]) * o1 for i in range(2)]
    centre = float(matrix[2, 0]) * o0 + float(matrix[2, 1]) * o1
    return [top[0] + low[0], top[1] + low[1], centre, low[1] - top[1], low[0] - top[0]]


def rows_of(shape=(8, 128)):
    return lax.broadcasted_iota(jnp.int32, shape, 0)


def lanes_of(shape=(8, 128)):
    return lax.broadcasted_iota(jnp.int32, shape, 1)


def deeper(x):
    return jnp.where(lanes_of() == 127, 0.0, pltpu.roll(x, 127, 1))


def shallower(x):
    return jnp.where(lanes_of() == 0, 0.0, pltpu.roll(x, 1, 1))


def split_three(x):
    high = x.astype(jnp.bfloat16)
    rest = x - high.astype(f32)
    middle = rest.astype(jnp.bfloat16)
    return high, middle, (rest - middle.astype(f32)).astype(jnp.bfloat16)


def one_hot_dot(x, table, dims=(((1,), (0,)), ((), ()))):
    return sum(lax.dot_general(part, table, dims, preferred_element_type=f32) for part in split_three(x))


def depth_table(back=False):
    a = lax.broadcasted_iota(jnp.int32, (512, 512), 1 if back else 0)
    b = lax.broadcasted_iota(jnp.int32, (512, 512), 0 if back else 1)
    return jnp.where(a == 4 * (b & 127) + (b >> 7), 1.0, 0.0).astype(jnp.bfloat16)


def to_elements(nodes, table, tall, put):
    for i in range(5):
        for j in range(5):
            for ex in range(2):
                for t in range(4):
                    tall[i, j, 4 * ex : 4 * ex + 4, 128 * t : 128 * t + 128] = nodes[t, 4 * ex + i, pl.ds(j, 4, stride=4), :]
    out = one_hot_dot(tall[...].reshape(200, 512), table)
    for k in range(4):
        put(k, out[:, 128 * k : 128 * k + 128].reshape(5, 5, 8, 128))


def to_nodes(get, table, tall, nodes):
    wide = jnp.concatenate([get(k).reshape(200, 128) for k in range(4)], axis=1)
    tall[...] = one_hot_dot(wide, table).reshape(5, 5, 8, 512)
    for i in range(5):
        for j in range(5):
            for ex in range(2):
                if i == 4 and ex == 0:
                    continue
                for t in range(4):
                    lanes = slice(128 * t, 128 * t + 128)
                    if j < 4:
                        nodes[t, 4 * ex + i, pl.ds(j, 4, stride=4), :] = tall[i, j, 4 * ex : 4 * ex + 4, lanes]
                    else:
                        nodes[t, 4 * ex + i, 16:17, :] = tall[i, j, 4 * ex + 3 : 4 * ex + 4, lanes]


def lookup(material, row, region):
    total = jnp.zeros_like(region)
    for m in range(material.shape[1]):
        total = jnp.where(region == float(m + 1), material[row, m], total)
    return total


def internal(u, out, lame, shear, gx, gz, cross, planes, side):
    def depth_lines(i, carry):
        for j in range(5):
            for c in range(3):
                v = [u[c, i, j, k] for k in range(4)]
                v.append(deeper(v[0]))
                u[c, i, j, 4] = v[4]
                for k, g in enumerate(line(deriv, v)):
                    gz[c, i, j, k] = g
        return carry

    lax.fori_loop(0, 5, depth_lines, 0)

    def plane(k, carry):
        weight = jnp.where((k == 0) | (k == 4), float(quad[0]), jnp.where(k == 2, float(quad[2]), float(quad[1])))
        lame_k, shear_k = lame * (2.0 * weight), shear * (2.0 * weight)
        pairs = {}
        for a in range(3):
            for b in range(a, 3):
                w = float(quad[a] * quad[b])
                pairs[a, b] = pairs[b, a] = (lame_k * w, shear_k * w, shear_k * (2.0 * w))
        for c in range(3):
            for j in range(5):
                for i, g in enumerate(line(deriv, [u[c, i, j, k] for i in range(5)])):
                    gx[c, i, j] = g
        for i in range(5):
            gy = [line(deriv, [u[c, i, j, k] for j in range(5)]) for c in range(3)]
            ys = [[], [], []]
            for j in range(5):
                lw, mw, mw2 = pairs[kind[i], kind[j]]
                g0, g1, g2 = [[gx[c, i, j], gy[c][j], gz[c, i, j, k]] for c in range(3)]
                dilated = lw * (g0[0] + g1[1] + g2[2])
                s01 = mw * (g0[1] + g1[0])
                s02 = mw * (g0[2] + g2[0])
                s12 = mw * (g1[2] + g2[1])
                side[0, i, j] = dilated + mw2 * g0[0]
                side[1, i, j] = s01
                cross[0, i, j, k] = s02
                cross[1, i, j, k] = s12
                cross[2, i, j, k] = dilated + mw2 * g2[2]
                ys[0].append(s01)
                ys[1].append(dilated + mw2 * g1[1])
                ys[2].append(s12)
            for c in range(3):
                for j, value in enumerate(line(deriv_t, ys[c])):
                    planes[c, i, j, k] = value
        for j in range(5):
            for c in range(3):
                v = [side[c, i, j] if c < 2 else cross[0, i, j, k] for i in range(5)]
                for i, value in enumerate(line(deriv_t, v)):
                    planes[c, i, j, k] += value
        return carry

    lax.fori_loop(0, 5, plane, 0)

    def depth_sums(i, carry):
        for j in range(5):
            for c in range(3):
                v = line(deriv_t, [cross[c, i, j, k] for k in range(5)])
                v = [v[k] + planes[c, i, j, k] for k in range(5)]
                out[c, i, j, 0] = v[0] + shallower(v[4])
                for k in range(1, 4):
                    out[c, i, j, k] = v[k]
        return carry

    lax.fori_loop(0, 5, depth_sums, 0)
    sub = rows_of()

    def fold(k, carry):
        for c in range(3):
            for i in range(5):
                low, high = out[c, i, 0, k], out[c, i, 4, k]
                out[c, i, 0, k] = low + jnp.where(sub % 4 == 0, 0.0, pltpu.roll(high, 1, 0))
                out[c, i, 4, k] = high + jnp.where(sub % 4 == 3, 0.0, pltpu.roll(low, 7, 0))
            for j in range(5):
                low, high = out[c, 0, j, k], out[c, 4, j, k]
                out[c, 0, j, k] = low + jnp.where(sub < 4, 0.0, pltpu.roll(high, 4, 0))
                out[c, 4, j, k] = high + jnp.where(sub < 4, pltpu.roll(low, 4, 0), 0.0)
        return carry

    lax.fori_loop(0, 4, fold, 0)


def rolled(x, amount, axis=0):
    amount = amount % x.shape[axis]
    return pltpu.roll(x, amount, axis) if amount else x


def pack_x(force, low, high):
    sub = rows_of()
    for c in range(3):
        for j in range(5):
            for half in range(2):
                at = (c * 5 + j) * 2 + half
                a, b = force[c, 0, j, 2 * half], force[c, 0, j, 2 * half + 1]
                low[at] = jnp.where(sub < 4, a, rolled(b, 4))
                a, b = force[c, 4, j, 2 * half], force[c, 4, j, 2 * half + 1]
                high[at] = jnp.where(sub < 4, rolled(a, 4), b)


def pack_y(force, low, high):
    sub = rows_of()
    for c in range(3):
        for i in range(5):
            a, b = force[c, i, 0, 0], rolled(force[c, i, 4, 0], -3)
            for k in range(1, 4):
                a = jnp.where(sub % 4 == k, rolled(force[c, i, 0, k], k), a)
                b = jnp.where(sub % 4 == k, rolled(force[c, i, 4, k], k - 3), b)
            low[c * 5 + i] = a
            high[c * 5 + i] = b


def add_x(force, from_low, from_high):
    sub = rows_of()
    for c in range(3):
        for j in range(5):
            for half in range(2):
                at = (c * 5 + j) * 2 + half
                r, s = from_low[at], from_high[at]
                force[c, 0, j, 2 * half] += jnp.where(sub < 4, r, 0.0)
                force[c, 0, j, 2 * half + 1] += jnp.where(sub < 4, rolled(r, 4), 0.0)
                force[c, 4, j, 2 * half] += jnp.where(sub < 4, 0.0, rolled(s, 4))
                force[c, 4, j, 2 * half + 1] += jnp.where(sub < 4, 0.0, s)


def add_y(force, from_low, from_high):
    sub = rows_of()
    for c in range(3):
        for i in range(5):
            r, s = from_low[c * 5 + i], from_high[c * 5 + i]
            for k in range(4):
                force[c, i, 0, k] += jnp.where(sub % 4 == 0, rolled(r, -k), 0.0)
                force[c, i, 4, k] += jnp.where(sub % 4 == 3, rolled(s, 3 - k), 0.0)


def edge_kernel(extra, low, high, from_low, from_high, *outs):
    out_low, out_high = outs
    sub = rows_of()
    for c in range(3):
        for i in range(5):
            out_low[c * 5 + i] = low[c * 5 + i]
            out_high[c * 5 + i] = high[c * 5 + i]
        for i, came, first in ((0, from_low, 0), (4, from_high, 4)):
            for j, out, row in ((0, out_low, 0), (4, out_high, 3)):
                total = out[c * 5 + i]
                for k in range(4):
                    r = rolled(came[(c * 5 + j) * 2 + k // 2], first + k - (4 * (k % 2) + row))
                    total = total + jnp.where(sub == first + k, r, 0.0)
                out[c * 5 + i] = total
    if extra:
        for out, mine in ((out_low, low), (out_high, high)):
            out[15] = mine[15]
            out[16] = from_low[30]
            out[17] = from_high[30]


def region_grid(own, xl, xh, yl, yh):
    return [[yl[16], xl[30], yh[16]], [yl[15], own, yh[15]], [yl[17], xh[30], yh[17]]]


def shared_density(grid):
    sub = rows_of()
    across = []
    for y in range(3):
        low, mid, high = grid[0][y], grid[1][y], grid[2][y]
        turned = rolled(mid, 4)
        across.append([jnp.where(sub < 4, rolled(low, 4), turned), mid, jnp.where(sub < 4, turned, rolled(high, 4))])
    found = [[None] * 3 for _ in range(3)]
    for x in range(3):
        low, mid, high = across[0][x], across[1][x], across[2][x]
        found[x][0] = jnp.where(sub % 4 == 0, rolled(low, -3), rolled(mid, 1))
        found[x][1] = mid
        found[x][2] = jnp.where(sub % 4 == 3, rolled(high, 3), rolled(mid, -1))
    sums = []
    for x in ((1,), (0, 1), (1, 2)):
        row = []
        for y in ((1,), (0, 1), (1, 2)):
            total = sum(found[a][b] for a in x for b in y)
            row.append((total + shallower(total), total))
        sums.append(row)
    return sums


def mass_scales(sums):
    return [[[1.0 / s for s in pair] for pair in row] for row in sums]


def edge_kind(i):
    return 1 if i == 0 else 2 if i == 4 else 0


def accel_scale(i, j, k):
    return float(-1.0 / (half_size**3 * quad[i] * quad[j] * quad[k]))


def first_kernel(u, v, a, region, material, b_out, f_out, x_low, x_high, y_low, y_high,
                 elem, gx, gz, cross, planes, side, tall, nodes):
    table = depth_table()
    region_now = jnp.concatenate([region[0], region[1]], axis=0).astype(f32) + 1.0

    def one(c, carry):
        for t in range(4):
            lanes = slice(128 * t, 128 * t + 128)
            nodes[t] = u[c, :, :, lanes] + time_step * v[c, :, :, lanes] + 0.5 * time_step**2 * a[c, :, :, lanes]

        def put_u(k, value):
            elem[c, :, :, k] = value

        to_elements(nodes, table, tall, put_u)
        for t in range(4):
            lanes = slice(128 * t, 128 * t + 128)
            nodes[t] = u[c, :, :, lanes] + 2.0 * time_step * v[c, :, :, lanes] + time_step**2 * a[c, :, :, lanes]

        def put_b(k, value):
            b_out[c, :, :, k] = value

        to_elements(nodes, table, tall, put_b)
        return carry

    lax.fori_loop(0, 3, one, 0)
    internal(elem, f_out, lookup(material, 1, region_now), lookup(material, 2, region_now), gx, gz, cross, planes, side)
    pack_x(f_out, x_low, x_high)
    pack_y(f_out, y_low, y_high)
    x_low[30] = region_now
    x_high[30] = region_now
    y_low[15] = region_now
    y_high[15] = region_now


def second_kernel(b, f, xl, xh, yl, yh, region, material, a_out, f_out, x_low, x_high, y_low, y_high, scales,
                  elem, gx, gz, cross, planes, side):
    region_now = jnp.concatenate([region[0], region[1]], axis=0).astype(f32) + 1.0
    a_out[...] = f[...]
    add_x(a_out, xl, xh)
    add_y(a_out, yl, yh)
    grid = region_grid(region_now, xl, xh, yl, yh)
    inverse = mass_scales(shared_density([[lookup(material, 0, r) for r in row] for row in grid]))
    for x in range(3):
        for y in range(3):
            for z in range(2):
                scales[x, y, z] = inverse[x][y][z]
    for i in range(5):
        for j in range(5):
            for k in range(4):
                scale = scales[edge_kind(i), edge_kind(j), min(k, 1)] * accel_scale(i, j, k)
                for c in range(3):
                    value = a_out[c, i, j, k] * scale
                    a_out[c, i, j, k] = value
                    elem[c, i, j, k] = b[c, i, j, k] + time_step**2 * value
    internal(elem, f_out, lookup(material, 1, region_now), lookup(material, 2, region_now), gx, gz, cross, planes, side)
    pack_x(f_out, x_low, x_high)
    pack_y(f_out, y_low, y_high)


def last_kernel(a1, f, xl, xh, yl, yh, scales, surf1, surf2, u, v, a, u_out, v_out, a_out, tall, nodes, nodes2, force):
    table = depth_table(back=True)
    force[...] = f[...]
    add_x(force, xl, xh)
    add_y(force, yl, yh)
    for i in range(5):
        for j in range(5):
            for k in range(4):
                scale = scales[edge_kind(i), edge_kind(j), min(k, 1)] * accel_scale(i, j, k)
                for c in range(3):
                    force[c, i, j, k] = force[c, i, j, k] * scale
    lane = lanes_of((17, 128))
    for c in range(3):
        to_nodes(lambda k: a1[c, :, :, k], table, tall, nodes)
        to_nodes(lambda k: force[c, :, :, k], table, tall, nodes2)
        for x in range(9):
            at = 8 * (c * 9 + x)
            tile, shift = at // 128, (128 - at % 128) % 128
            moved = [rolled(s[0:17, 128 * tile : 128 * tile + 128], shift, 1) for s in (surf1, surf2)]
            direct = jnp.where(lane < 1, moved[0], 0.0)
            nodes[0, x] += direct
            nodes2[0, x] += direct + jnp.where(lane < 5, moved[1], 0.0)
        for t in range(4):
            at = (c, slice(None), slice(None), slice(128 * t, 128 * t + 128))
            first, second = nodes[t], nodes2[t]
            a_out[at] = second
            u_out[at] = u[at] + 2.0 * time_step * v[at] + time_step**2 * (a[at] + first)
            v_out[at] = v[at] + 0.5 * time_step * (a[at] + 2.0 * first + second)


def whole():
    return pl.BlockSpec(memory_space=pltpu.VMEM)


def scalars():
    return pl.BlockSpec(memory_space=pltpu.SMEM)


def call(kernel, ins, outs, scratch, smem=()):
    return pl.pallas_call(
        kernel,
        out_shape=[jax.ShapeDtypeStruct(s, f32) for s in outs],
        in_specs=[scalars() if n in smem else whole() for n in range(len(ins))],
        out_specs=[whole() for _ in outs],
        scratch_shapes=[pltpu.VMEM(s, f32) for s in scratch],
        compiler_params=pltpu.CompilerParams(vmem_limit_bytes=vmem_bytes),
    )(*ins)


element_shape = (3, 5, 5, 4, 8, 128)
lines_shape = (3, 5, 5, 5, 8, 128)
internal_scratch = [lines_shape, (3, 5, 5, 8, 128), lines_shape, lines_shape, lines_shape, (2, 5, 5, 8, 128)]


def exchange(axis, to_low, to_high):
    count = lax.axis_size(axis)
    up = [(i, i + 1) for i in range(count - 1)]
    down = [(j, i) for i, j in up]
    return lax.ppermute(to_high, axis, up), lax.ppermute(to_low, axis, down)


def extended_2(array, sides, width):
    for axis, dim in sides:
        count, length = (lax.axis_size(axis), array.shape[dim])
        up = [(i, (i + 1) % count) for i in range(count - 1)]
        down = [(j, i) for i, j in up]
        last = lax.slice_in_dim(array, length - width, length, axis=dim)
        first = lax.slice_in_dim(array, 0, width, axis=dim)
        before = lax.ppermute(last, axis, up)
        after = lax.ppermute(first, axis, down)
        array = jnp.concatenate([before, array, after], axis=dim)
    return array


def pressure_of(hydro_state):
    velocity = hydro_state[1:4] / hydro_state[0]
    pressure = (gamma_gas - 1.0) * (
        hydro_state[4] - 0.5 * jnp.sum(hydro_state[1:4] * velocity, axis=0)
    )
    return (velocity, pressure)


def euler_flux(hydro_state, axis_num):
    velocity, pressure = pressure_of(hydro_state)
    sound_speed = jnp.sqrt(gamma_gas * pressure / hydro_state[0])
    normal_vel = velocity[axis_num]
    unit_row = jnp.eye(3, dtype=jnp.float32)[axis_num].reshape(3, 1, 1, 1)
    momentum_flux = hydro_state[1:4] * normal_vel + pressure * unit_row
    energy_flux = (hydro_state[4] + pressure) * normal_vel
    flux_all = jnp.concatenate(
        [hydro_state[1 + axis_num][None], momentum_flux, energy_flux[None]], axis=0
    )
    return (flux_all, jnp.abs(normal_vel) + sound_speed)


def advance(padded):
    interior = padded[:, 1:-1, 1:-1, 1:-1]
    change = jnp.zeros_like(interior)
    for axis_num in range(3):
        pencil = padded
        for other_axis in range(3):
            if other_axis != axis_num:
                pencil = lax.slice_in_dim(
                    pencil, 1, pencil.shape[other_axis + 1] - 1, axis=other_axis + 1
                )
        flux_all, wave_speed = euler_flux(pencil, axis_num)
        length = pencil.shape[axis_num + 1]
        low_state = lax.slice_in_dim(pencil, 0, length - 1, axis=axis_num + 1)
        high_state = lax.slice_in_dim(pencil, 1, length, axis=axis_num + 1)
        low_flux = lax.slice_in_dim(flux_all, 0, length - 1, axis=axis_num + 1)
        high_flux = lax.slice_in_dim(flux_all, 1, length, axis=axis_num + 1)
        fastest = jnp.maximum(
            lax.slice_in_dim(wave_speed, 0, length - 1, axis=axis_num),
            lax.slice_in_dim(wave_speed, 1, length, axis=axis_num),
        )
        face_flux = 0.5 * (low_flux + high_flux) - 0.5 * fastest * (high_state - low_state)
        change = (
            change
            + lax.slice_in_dim(face_flux, 1, length - 1, axis=axis_num + 1)
            - lax.slice_in_dim(face_flux, 0, length - 2, axis=axis_num + 1)
        )
    return interior - cell_ratio * change


def surface_traction(hydro_state):
    bottom = hydro_state[:, :, :, -1]
    velocity, pressure = pressure_of(bottom[:, :, :, None])
    vertical = velocity[2, :, :, 0]
    return (
        jnp.stack(
            [bottom[1] * vertical, bottom[2] * vertical, bottom[3] * vertical + pressure[:, :, 0]]
        )
        * face_area
    )


def fix_edges(padded, depth):
    placings = (
        (lax.axis_index("gx"), lax.axis_size("gx"), 1),
        (lax.axis_index(("grp", "gy")), lax.axis_size(("grp", "gy")), 2),
    )
    for position, extent, axis_num in placings:
        length = padded.shape[axis_num]
        inner_low = lax.slice_in_dim(padded, depth, depth + 1, axis=axis_num)
        inner_high = lax.slice_in_dim(padded, length - depth - 1, length - depth, axis=axis_num)
        place = lax.broadcasted_iota(jnp.int32, padded.shape, axis_num)
        padded = jnp.where((position == 0) & (place < depth), inner_low, padded)
        padded = jnp.where((position == extent - 1) & (place >= length - depth), inner_high, padded)
    return padded


def pad_depth(padded):
    return jnp.pad(padded, ((0, 0), (0, 0), (0, 0), (1, 1)), mode="edge")


def surface_tables():
    lane = np.arange(128)
    j, ey = lane // 8, lane % 8
    used = (j < 5) & (ey < 6)
    place = np.where(used, ey + 1, -9)
    source = lane[:, None]
    centre = source == place
    meet = centre | ((j == 0) & (source == place - 1)) | ((j == 4) & (source == place + 1))
    along = np.zeros((128, 128))
    for a in range(40):
        for b in range(40):
            if a % 8 == b % 8 and a % 8 < 6:
                along[a, b] = deriv[b // 8, a // 8]
    node = np.where(used, 4 * (ey - 1) + j, -9)
    fold = (lane[:, None] == node) & (lane[:, None] < 17)
    keep = fold & ((j < 4) & (ey < 5) | (j == 4) & (ey == 4))
    return np.stack([centre, meet, along, along.T, fold, keep]).astype(np.float32)


def full_dot(x, y, back=False):
    dims = (((1,), (1 if back else 0,)), ((), ()))
    return lax.dot_general(x, y, dims, precision=lax.Precision.HIGHEST, preferred_element_type=f32)


def deposit(faces, nodes_y, base_x, base_y, total):
    rows = faces.shape[1]
    sub = rows_of((8, 512)).astype(f32)
    total[...] = jnp.zeros_like(total)

    def one(step, carry):
        def wide(q):
            block = faces[q, pl.ds(4 * step, 4), :]
            return jnp.concatenate([block[n : n + 1] for n in range(4)], axis=1)

        ids = wide(3)
        node_x = jnp.floor((ids + 0.5) * (1.0 / nodes_y))
        rel_y = jnp.broadcast_to(ids - node_x * nodes_y - base_y, (8, 512))
        rel_x = jnp.broadcast_to(node_x - base_x, (8, 512))
        left = []
        hits = [(rel_x - i == 4.0 * sub) & (sub < 4.0) for i in range(5)]
        parts = [split_three(wide(c)) for c in range(3)]
        for part in range(3):
            for c in range(3):
                value = jnp.broadcast_to(parts[c][part].astype(f32), (8, 512))
                left += [jnp.where(hit, value, 0.0) for hit in hits]
        right = [jnp.where((rel_y - j == 4.0 * sub) & (sub < 6.0), 1.0, 0.0) for j in range(5)]
        right.append(jnp.zeros((88, 512), f32))
        left, right = jnp.concatenate(left, axis=0), jnp.concatenate(right, axis=0)
        total[...] += lax.dot_general(
            left.astype(jnp.bfloat16), right.astype(jnp.bfloat16), (((1,), (1,)), ((), ())), preferred_element_type=f32
        )
        return carry

    lax.fori_loop(0, rows // 4, one, 0)


def top_grid(grid, z):
    sub, lane = rows_of(), lanes_of()
    out = jnp.zeros((8, 128), f32)
    for x in range(3):
        total = jnp.zeros((8, 128), f32)
        for y in range(3):
            column = jnp.broadcast_to(grid[x][y][:, z : z + 1], (8, 128))
            total = total + jnp.where((lane == 4 * y + (sub & 3) - 2), column, 0.0)
        total = total + rolled(total, -1)
        total = total + rolled(total, -2)
        for ex in range(2):
            out = jnp.where(sub == 2 * x + ex, rolled(total, 2 * x + ex - 4 * ex), out)
    return out


def respond(total, grid, material, tables, out1, out2):
    sub, lane = rows_of(), lanes_of()
    top, below = top_grid(grid, 0), top_grid(grid, 1)
    centre, meet, along, along_t, fold, keep = [tables[n] for n in range(6)]
    sums0 = full_dot(lookup(material, 0, top), meet)
    sums1 = full_dot(lookup(material, 0, below), meet)
    lame = rolled(full_dot(lookup(material, 1, top), centre), -1)
    shear = rolled(full_dot(lookup(material, 2, top), centre), -1)
    weight_y = jnp.ones((8, 128), f32)
    for j in range(5):
        weight_y = jnp.where(lane // 8 == j, float(quad[j]), weight_y)

    def inverse(sums):
        mid = rolled(sums, -1)
        found = {0: mid + sums, 1: mid, 4: mid + rolled(sums, -2)}
        found = {i: jnp.where(s > 0.0, 1.0 / (s * weight_y), 0.0) for i, s in found.items()}
        found[2] = found[3] = found[1]
        return found

    light, heavy = inverse(sums0), inverse(sums0 + sums1)
    first = [[None] * 5 for _ in range(3)]
    moved = [[None] * 5 for _ in range(3)]
    for c in range(3):
        for i in range(5):
            at = (c * 5 + i) * 8
            force = total[at : at + 8] + total[at + 120 : at + 128] + total[at + 240 : at + 248]
            first[c][i] = force * light[i] * -accel_scale(i, 2, 0) * float(quad[2])
            moved[c][i] = first[c][i] * time_step**2
    gx = [line(deriv, moved[c]) for c in range(3)]
    gy = full_dot(jnp.concatenate([moved[c][i] for c in range(3) for i in range(5)], axis=0), along)
    gy = [[gy[(c * 5 + i) * 8 : (c * 5 + i) * 8 + 8] for i in range(5)] for c in range(3)]
    lame_w, shear_w = lame * weight_y * 2.0, shear * weight_y * 2.0
    d00 = float(deriv[0, 0])
    sx = [[], [], []]
    sy = [[], [], []]
    sz = [[], [], []]
    qs = [[], [], []]
    pressed = []
    for i in range(5):
        lw, mw = lame_w * float(quad[i]), shear_w * float(quad[i])
        d = [moved[c][i] for c in range(3)]
        gz = [d00 * x for x in d]
        dilated = lw * (gx[0][i] + gy[1][i] + gz[2])
        s01 = mw * (gx[1][i] + gy[0][i])
        s02 = mw * (gx[2][i] + gz[0])
        s12 = mw * (gy[2][i] + gz[1])
        for c, value in enumerate((dilated + 2.0 * mw * gx[0][i], s01, s02)):
            sx[c].append(value)
        for c, value in enumerate((s01, dilated + 2.0 * mw * gy[1][i], s12)):
            sy[c].append(value)
        for c, value in enumerate((s02, s12, dilated + 2.0 * mw * gz[2])):
            sz[c].append(value)
        for c, value in enumerate((mw * d[0], mw * d[1], (lw + 2.0 * mw) * d[2])):
            qs[c].append(value)
        pressed.append(lw * d[2])
    ydiv = full_dot(jnp.concatenate(sy[0] + sy[1] + sy[2] + pressed + qs[1], axis=0), along_t)
    ydiv = [[ydiv[(n * 5 + i) * 8 : (n * 5 + i) * 8 + 8] for i in range(5)] for n in range(5)]
    xdiv = [line(deriv_t, v) for v in sx + [pressed, qs[0]]]
    base = [xdiv[3], ydiv[3], [p + q for p, q in zip(xdiv[4], ydiv[4])]]
    second = {}
    for c in range(3):
        for i in range(5):
            for l in range(5):
                stiff = float(sum(deriv[k, l] * quad[k] * deriv[k, 0] for k in range(1, 5)))
                value = float(deriv[0, l] * quad[0]) * sz[c][i] + stiff * qs[c][i]
                if l:
                    value = value + float(deriv[l, 0] * quad[l]) * base[c][i]
                else:
                    value = value + float(quad[0]) * (xdiv[c][i] + ydiv[c][i])
                scale = (heavy if l == 4 else light)[i]
                second[c, i, l] = value * scale * (accel_scale(i, 2, l) * float(quad[2]))
    rows1, rows2 = [], []
    for c in range(3):
        for x in range(9):
            own = 1 if x < 4 else 2
            rows1.append(jnp.where(sub == 0, rolled(first[c][x - 4 * (own - 1)], -own), 0.0))
            block = jnp.zeros((8, 128), f32)
            for l in range(5):
                for ex in range(4):
                    i = x - 4 * (ex - 1)
                    if 0 <= i <= 4:
                        block = block + jnp.where(sub == l, rolled(second[c, i, l], l - ex), 0.0)
            rows2.append(block)
    blank = [jnp.zeros((40, 128), f32)]
    out1[...] = full_dot(keep[0:24], jnp.concatenate(rows1 + blank, axis=0), back=True)
    out2[...] = full_dot(fold[0:24], jnp.concatenate(rows2 + blank, axis=0), back=True)


def surface_kernel(nodes_y, faces, here, region, xl, xh, yl, yh, material, tables, out1, out2, total):
    base_x = (8 * here[0] - 4).astype(f32)
    base_y = (16 * here[1] - 4).astype(f32)
    deposit(faces, nodes_y, base_x, base_y, total)
    region_now = jnp.concatenate([region[0], region[1]], axis=0).astype(f32) + 1.0
    respond(total, region_grid(region_now, xl, xh, yl, yh), material, tables, out1, out2)


def shards(density, momentum, energy, displacement, velocity_field, acceleration, material, element_region_index,
           face_dest, face_slot):
    along_y = ("grp", "gy")
    place_x, place_y = lax.axis_index("gx"), lax.axis_index(along_y)
    nodes_y = 16 * lax.axis_size(along_y) + 1
    region = element_region_index
    b, f, x_low, x_high, y_low, y_high = call(
        first_kernel,
        (displacement, velocity_field, acceleration, region, material),
        [element_shape, element_shape, (31, 8, 128), (31, 8, 128), (16, 8, 128), (16, 8, 128)],
        internal_scratch + [(5, 5, 8, 512), (4, 9, 17, 128)],
        smem=(4,),
    )
    xl, xh = exchange("gx", x_low, x_high)
    y_low, y_high = call(
        functools.partial(edge_kernel, True), (y_low, y_high, xl, xh), [(18, 8, 128), (18, 8, 128)], []
    )
    yl, yh = exchange(along_y, y_low, y_high)
    hydro_state = jnp.concatenate([density[None], momentum, energy[None]], axis=0)
    for repeat in range(2):
        padded = extended_2(hydro_state, (("gx", 1), (("grp", "gy"), 2)), 1)
        hydro_state = advance(pad_depth(fix_edges(padded, 1)))
    traction = surface_traction(hydro_state).reshape(3, -1)
    targets, slots = face_dest[0, :, 0], face_slot[0]
    count_x, count_gy = lax.axis_size("gx"), lax.axis_size("gy")
    node_x = targets // count_gy % count_x * 8 + slots // 17
    node_y = (targets // (count_gy * count_x) * count_gy + targets % count_gy) * 16 + slots % 17
    ids = (node_x * nodes_y + node_y).astype(f32)
    faces = lax.all_gather(
        jnp.concatenate([traction, ids[None]], axis=0)[:, None, :], ("grp", "gx", "gy"), axis=1, tiled=True
    )
    here = jnp.stack([place_x, place_y]).astype(jnp.int32)
    surf1, surf2 = call(
        functools.partial(surface_kernel, float(nodes_y)),
        (faces, here, region, xl, xh, yl, yh, material, jnp.asarray(surface_tables())),
        [(24, 256), (24, 256)],
        [(360, 128)],
        smem=(1, 7),
    )
    a1, f2, x_low, x_high, y_low, y_high, scales = call(
        second_kernel,
        (b, f, xl, xh, yl, yh, region, material),
        [element_shape, element_shape, (30, 8, 128), (30, 8, 128), (15, 8, 128), (15, 8, 128), (3, 3, 2, 8, 128)],
        internal_scratch,
        smem=(7,),
    )
    xl2, xh2 = exchange("gx", x_low, x_high)
    y_low, y_high = call(
        functools.partial(edge_kernel, False), (y_low, y_high, xl2, xh2), [(15, 8, 128), (15, 8, 128)], []
    )
    yl2, yh2 = exchange(along_y, y_low, y_high)
    u_out, v_out, a_out = call(
        last_kernel,
        (a1, f2, xl2, xh2, yl2, yh2, scales, surf1, surf2, displacement, velocity_field, acceleration),
        [displacement.shape] * 3,
        [(5, 5, 8, 512), (4, 9, 17, 128), (4, 9, 17, 128), element_shape],
    )
    return hydro_state, u_out, v_out, a_out


def solution(mesh):
    field = P(None, "gx", ("grp", "gy"), None)
    cells = P("gx", ("grp", "gy"), None)
    rank = ("grp", "gx", "gy")
    return jax.shard_map(
        shards,
        mesh=mesh,
        in_specs=(cells, field, cells, field, field, field, P(), cells, P(rank, None, None), P(rank, None)),
        out_specs=(field, field, field, field),
        check_vma=False,
    )
```

```python
import functools

import jax
import jax.numpy as jnp
import numpy as np
from jax import lax
from jax.experimental import pallas as pl
from jax.experimental.pallas import tpu as pltpu
from jax.sharding import PartitionSpec as P

gamma_gas = 1.4
cell_ratio = 0.05
half_size = 2.0
time_step = 0.1
face_area = 2.0
vmem_bytes = 40 * 1024 * 1024


def gll_tables():
    root = np.sqrt(3.0 / 7.0)
    points = np.array([-1.0, -root, 0.0, root, 1.0])
    weights = np.array([0.1, 49.0 / 90.0, 32.0 / 45.0, 49.0 / 90.0, 0.1])
    products = [np.prod([points[r] - points[c] for c in range(5) if c != r]) for r in range(5)]
    derivative = np.zeros((5, 5))
    for r in range(5):
        for c in range(5):
            if r != c:
                derivative[r, c] = products[r] / products[c] / (points[r] - points[c])
        derivative[r, r] = sum(1.0 / (points[r] - points[c]) for c in range(5) if c != r)
    derivative[2, 2] = 0.0
    return derivative, weights


deriv, quad = gll_tables()
deriv_t = deriv.T
kind = [0, 1, 2, 1, 0]
f32 = jnp.float32


def line(matrix, v):
    even, odd = (matrix + matrix[:, ::-1]) / 2, (matrix - matrix[:, ::-1]) / 2
    e0, e1, o0, o1 = v[0] + v[4], v[1] + v[3], v[0] - v[4], v[1] - v[3]
    top = [float(even[i, 0]) * e0 + float(even[i, 1]) * e1 + float(matrix[i, 2]) * v[2] for i in range(2)]
    low = [float(odd[i, 0]) * o0 + float(odd[i, 1]) * o1 for i in range(2)]
    centre = float(matrix[2, 0]) * o0 + float(matrix[2, 1]) * o1
    return [top[0] + low[0], top[1] + low[1], centre, low[1] - top[1], low[0] - top[0]]


def rows_of(shape=(8, 128)):
    return lax.broadcasted_iota(jnp.int32, shape, 0)


def lanes_of(shape=(8, 128)):
    return lax.broadcasted_iota(jnp.int32, shape, 1)


def deeper(x):
    return jnp.where(lanes_of() == 127, 0.0, pltpu.roll(x, 127, 1))


def shallower(x):
    return jnp.where(lanes_of() == 0, 0.0, pltpu.roll(x, 1, 1))


def split_three(x):
    high = x.astype(jnp.bfloat16)
    rest = x - high.astype(f32)
    middle = rest.astype(jnp.bfloat16)
    return high, middle, (rest - middle.astype(f32)).astype(jnp.bfloat16)


def one_hot_dot(x, table, dims=(((1,), (0,)), ((), ()))):
    return sum(lax.dot_general(part, table, dims, preferred_element_type=f32) for part in split_three(x))


def depth_table(back=False):
    a = lax.broadcasted_iota(jnp.int32, (512, 512), 1 if back else 0)
    b = lax.broadcasted_iota(jnp.int32, (512, 512), 0 if back else 1)
    return jnp.where(a == 4 * (b & 127) + (b >> 7), 1.0, 0.0).astype(jnp.bfloat16)


def to_elements(nodes, table, tall, put):
    for i in range(5):
        for j in range(5):
            for ex in range(2):
                for t in range(4):
                    tall[i, j, 4 * ex : 4 * ex + 4, 128 * t : 128 * t + 128] = nodes[t, 4 * ex + i, pl.ds(j, 4, stride=4), :]
    out = one_hot_dot(tall[...].reshape(200, 512), table)
    for k in range(4):
        put(k, out[:, 128 * k : 128 * k + 128].reshape(5, 5, 8, 128))


def to_nodes(get, table, tall, nodes):
    wide = jnp.concatenate([get(k).reshape(200, 128) for k in range(4)], axis=1)
    tall[...] = one_hot_dot(wide, table).reshape(5, 5, 8, 512)
    for i in range(5):
        for j in range(5):
            for ex in range(2):
                if i == 4 and ex == 0:
                    continue
                for t in range(4):
                    lanes = slice(128 * t, 128 * t + 128)
                    if j < 4:
                        nodes[t, 4 * ex + i, pl.ds(j, 4, stride=4), :] = tall[i, j, 4 * ex : 4 * ex + 4, lanes]
                    else:
                        nodes[t, 4 * ex + i, 16:17, :] = tall[i, j, 4 * ex + 3 : 4 * ex + 4, lanes]


def lookup(material, row, region):
    total = jnp.zeros_like(region)
    for m in range(material.shape[1]):
        total = jnp.where(region == float(m + 1), material[row, m], total)
    return total


def internal(u, out, lame, shear, gx, gz, cross, planes, side):
    def depth_lines(i, carry):
        for j in range(5):
            for c in range(3):
                v = [u[c, i, j, k] for k in range(4)]
                v.append(deeper(v[0]))
                u[c, i, j, 4] = v[4]
                for k, g in enumerate(line(deriv, v)):
                    gz[c, i, j, k] = g
        return carry

    lax.fori_loop(0, 5, depth_lines, 0)

    def plane(k, carry):
        weight = jnp.where((k == 0) | (k == 4), float(quad[0]), jnp.where(k == 2, float(quad[2]), float(quad[1])))
        lame_k, shear_k = lame * (2.0 * weight), shear * (2.0 * weight)
        pairs = {}
        for a in range(3):
            for b in range(a, 3):
                w = float(quad[a] * quad[b])
                pairs[a, b] = pairs[b, a] = (lame_k * w, shear_k * w, shear_k * (2.0 * w))
        for c in range(3):
            for j in range(5):
                for i, g in enumerate(line(deriv, [u[c, i, j, k] for i in range(5)])):
                    gx[c, i, j] = g
        for i in range(5):
            gy = [line(deriv, [u[c, i, j, k] for j in range(5)]) for c in range(3)]
            ys = [[], [], []]
            for j in range(5):
                lw, mw, mw2 = pairs[kind[i], kind[j]]
                g0, g1, g2 = [[gx[c, i, j], gy[c][j], gz[c, i, j, k]] for c in range(3)]
                dilated = lw * (g0[0] + g1[1] + g2[2])
                s01 = mw * (g0[1] + g1[0])
                s02 = mw * (g0[2] + g2[0])
                s12 = mw * (g1[2] + g2[1])
                side[0, i, j] = dilated + mw2 * g0[0]
                side[1, i, j] = s01
                cross[0, i, j, k] = s02
                cross[1, i, j, k] = s12
                cross[2, i, j, k] = dilated + mw2 * g2[2]
                ys[0].append(s01)
                ys[1].append(dilated + mw2 * g1[1])
                ys[2].append(s12)
            for c in range(3):
                for j, value in enumerate(line(deriv_t, ys[c])):
                    planes[c, i, j, k] = value
        for j in range(5):
            for c in range(3):
                v = [side[c, i, j] if c < 2 else cross[0, i, j, k] for i in range(5)]
                for i, value in enumerate(line(deriv_t, v)):
                    planes[c, i, j, k] += value
        return carry

    lax.fori_loop(0, 5, plane, 0)

    def depth_sums(i, carry):
        for j in range(5):
            for c in range(3):
                v = line(deriv_t, [cross[c, i, j, k] for k in range(5)])
                v = [v[k] + planes[c, i, j, k] for k in range(5)]
                out[c, i, j, 0] = v[0] + shallower(v[4])
                for k in range(1, 4):
                    out[c, i, j, k] = v[k]
        return carry

    lax.fori_loop(0, 5, depth_sums, 0)
    sub = rows_of()

    def fold(k, carry):
        for c in range(3):
            for i in range(5):
                low, high = out[c, i, 0, k], out[c, i, 4, k]
                out[c, i, 0, k] = low + jnp.where(sub % 4 == 0, 0.0, pltpu.roll(high, 1, 0))
                out[c, i, 4, k] = high + jnp.where(sub % 4 == 3, 0.0, pltpu.roll(low, 7, 0))
            for j in range(5):
                low, high = out[c, 0, j, k], out[c, 4, j, k]
                out[c, 0, j, k] = low + jnp.where(sub < 4, 0.0, pltpu.roll(high, 4, 0))
                out[c, 4, j, k] = high + jnp.where(sub < 4, pltpu.roll(low, 4, 0), 0.0)
        return carry

    lax.fori_loop(0, 4, fold, 0)


def rolled(x, amount, axis=0):
    amount = amount % x.shape[axis]
    return pltpu.roll(x, amount, axis) if amount else x


def pack_x(force, low, high):
    sub = rows_of()
    for c in range(3):
        for j in range(5):
            for half in range(2):
                at = (c * 5 + j) * 2 + half
                a, b = force[c, 0, j, 2 * half], force[c, 0, j, 2 * half + 1]
                low[at] = jnp.where(sub < 4, a, rolled(b, 4))
                a, b = force[c, 4, j, 2 * half], force[c, 4, j, 2 * half + 1]
                high[at] = jnp.where(sub < 4, rolled(a, 4), b)


def pack_y(force, low, high):
    sub = rows_of()
    for c in range(3):
        for i in range(5):
            a, b = force[c, i, 0, 0], rolled(force[c, i, 4, 0], -3)
            for k in range(1, 4):
                a = jnp.where(sub % 4 == k, rolled(force[c, i, 0, k], k), a)
                b = jnp.where(sub % 4 == k, rolled(force[c, i, 4, k], k - 3), b)
            low[c * 5 + i] = a
            high[c * 5 + i] = b


def add_x(force, from_low, from_high):
    sub = rows_of()
    for c in range(3):
        for j in range(5):
            for half in range(2):
                at = (c * 5 + j) * 2 + half
                r, s = from_low[at], from_high[at]
                force[c, 0, j, 2 * half] += jnp.where(sub < 4, r, 0.0)
                force[c, 0, j, 2 * half + 1] += jnp.where(sub < 4, rolled(r, 4), 0.0)
                force[c, 4, j, 2 * half] += jnp.where(sub < 4, 0.0, rolled(s, 4))
                force[c, 4, j, 2 * half + 1] += jnp.where(sub < 4, 0.0, s)


def add_y(force, from_low, from_high):
    sub = rows_of()
    for c in range(3):
        for i in range(5):
            r, s = from_low[c * 5 + i], from_high[c * 5 + i]
            for k in range(4):
                force[c, i, 0, k] += jnp.where(sub % 4 == 0, rolled(r, -k), 0.0)
                force[c, i, 4, k] += jnp.where(sub % 4 == 3, rolled(s, 3 - k), 0.0)


def edge_kernel(extra, low, high, from_low, from_high, *outs):
    out_low, out_high = outs
    sub = rows_of()
    for c in range(3):
        for i in range(5):
            out_low[c * 5 + i] = low[c * 5 + i]
            out_high[c * 5 + i] = high[c * 5 + i]
        for i, came, first in ((0, from_low, 0), (4, from_high, 4)):
            for j, out, row in ((0, out_low, 0), (4, out_high, 3)):
                total = out[c * 5 + i]
                for k in range(4):
                    r = rolled(came[(c * 5 + j) * 2 + k // 2], first + k - (4 * (k % 2) + row))
                    total = total + jnp.where(sub == first + k, r, 0.0)
                out[c * 5 + i] = total
    if extra:
        for out, mine in ((out_low, low), (out_high, high)):
            out[15] = mine[15]
            out[16] = from_low[30]
            out[17] = from_high[30]


def region_grid(own, xl, xh, yl, yh):
    return [[yl[16], xl[30], yh[16]], [yl[15], own, yh[15]], [yl[17], xh[30], yh[17]]]


def shared_density(grid):
    sub = rows_of()
    across = []
    for y in range(3):
        low, mid, high = grid[0][y], grid[1][y], grid[2][y]
        turned = rolled(mid, 4)
        across.append([jnp.where(sub < 4, rolled(low, 4), turned), mid, jnp.where(sub < 4, turned, rolled(high, 4))])
    found = [[None] * 3 for _ in range(3)]
    for x in range(3):
        low, mid, high = across[0][x], across[1][x], across[2][x]
        found[x][0] = jnp.where(sub % 4 == 0, rolled(low, -3), rolled(mid, 1))
        found[x][1] = mid
        found[x][2] = jnp.where(sub % 4 == 3, rolled(high, 3), rolled(mid, -1))
    sums = []
    for x in ((1,), (0, 1), (1, 2)):
        row = []
        for y in ((1,), (0, 1), (1, 2)):
            total = sum(found[a][b] for a in x for b in y)
            row.append((total + shallower(total), total))
        sums.append(row)
    return sums


def mass_scales(sums):
    return [[[1.0 / s for s in pair] for pair in row] for row in sums]


def edge_kind(i):
    return 1 if i == 0 else 2 if i == 4 else 0


def accel_scale(i, j, k):
    return float(-1.0 / (half_size**3 * quad[i] * quad[j] * quad[k]))


def first_kernel(u, v, a, region, material, b_out, f_out, x_low, x_high, y_low, y_high,
                 elem, gx, gz, cross, planes, side, tall, nodes):
    table = depth_table()
    region_now = jnp.concatenate([region[0], region[1]], axis=0).astype(f32) + 1.0

    def one(c, carry):
        for t in range(4):
            lanes = slice(128 * t, 128 * t + 128)
            nodes[t] = u[c, :, :, lanes] + time_step * v[c, :, :, lanes] + 0.5 * time_step**2 * a[c, :, :, lanes]

        def put_u(k, value):
            elem[c, :, :, k] = value

        to_elements(nodes, table, tall, put_u)
        for t in range(4):
            lanes = slice(128 * t, 128 * t + 128)
            nodes[t] = u[c, :, :, lanes] + 2.0 * time_step * v[c, :, :, lanes] + time_step**2 * a[c, :, :, lanes]

        def put_b(k, value):
            b_out[c, :, :, k] = value

        to_elements(nodes, table, tall, put_b)
        return carry

    lax.fori_loop(0, 3, one, 0)
    internal(elem, f_out, lookup(material, 1, region_now), lookup(material, 2, region_now), gx, gz, cross, planes, side)
    pack_x(f_out, x_low, x_high)
    pack_y(f_out, y_low, y_high)
    x_low[30] = region_now
    x_high[30] = region_now
    y_low[15] = region_now
    y_high[15] = region_now


def second_kernel(b, f, xl, xh, yl, yh, region, material, a_out, f_out, x_low, x_high, y_low, y_high, scales,
                  elem, gx, gz, cross, planes, side):
    region_now = jnp.concatenate([region[0], region[1]], axis=0).astype(f32) + 1.0
    a_out[...] = f[...]
    add_x(a_out, xl, xh)
    add_y(a_out, yl, yh)
    grid = region_grid(region_now, xl, xh, yl, yh)
    inverse = mass_scales(shared_density([[lookup(material, 0, r) for r in row] for row in grid]))
    for x in range(3):
        for y in range(3):
            for z in range(2):
                scales[x, y, z] = inverse[x][y][z]
    for i in range(5):
        for j in range(5):
            for k in range(4):
                scale = scales[edge_kind(i), edge_kind(j), min(k, 1)] * accel_scale(i, j, k)
                for c in range(3):
                    value = a_out[c, i, j, k] * scale
                    a_out[c, i, j, k] = value
                    elem[c, i, j, k] = b[c, i, j, k] + time_step**2 * value
    internal(elem, f_out, lookup(material, 1, region_now), lookup(material, 2, region_now), gx, gz, cross, planes, side)
    pack_x(f_out, x_low, x_high)
    pack_y(f_out, y_low, y_high)


def last_kernel(a1, f, xl, xh, yl, yh, scales, surf1, surf2, u, v, a, u_out, v_out, a_out, tall, nodes, nodes2, force):
    table = depth_table(back=True)
    force[...] = f[...]
    add_x(force, xl, xh)
    add_y(force, yl, yh)
    for i in range(5):
        for j in range(5):
            for k in range(4):
                scale = scales[edge_kind(i), edge_kind(j), min(k, 1)] * accel_scale(i, j, k)
                for c in range(3):
                    force[c, i, j, k] = force[c, i, j, k] * scale
    lane = lanes_of((17, 128))
    for c in range(3):
        to_nodes(lambda k: a1[c, :, :, k], table, tall, nodes)
        to_nodes(lambda k: force[c, :, :, k], table, tall, nodes2)
        for x in range(9):
            at = 8 * (c * 9 + x)
            tile, shift = at // 128, (128 - at % 128) % 128
            moved = [rolled(s[0:17, 128 * tile : 128 * tile + 128], shift, 1) for s in (surf1, surf2)]
            direct = jnp.where(lane < 1, moved[0], 0.0)
            nodes[0, x] += direct
            nodes2[0, x] += direct + jnp.where(lane < 5, moved[1], 0.0)
        for t in range(4):
            at = (c, slice(None), slice(None), slice(128 * t, 128 * t + 128))
            first, second = nodes[t], nodes2[t]
            a_out[at] = second
            u_out[at] = u[at] + 2.0 * time_step * v[at] + time_step**2 * (a[at] + first)
            v_out[at] = v[at] + 0.5 * time_step * (a[at] + 2.0 * first + second)


def whole():
    return pl.BlockSpec(memory_space=pltpu.VMEM)


def scalars():
    return pl.BlockSpec(memory_space=pltpu.SMEM)


def call(kernel, ins, outs, scratch, smem=()):
    return pl.pallas_call(
        kernel,
        out_shape=[jax.ShapeDtypeStruct(s, f32) for s in outs],
        in_specs=[scalars() if n in smem else whole() for n in range(len(ins))],
        out_specs=[whole() for _ in outs],
        scratch_shapes=[pltpu.VMEM(s, f32) for s in scratch],
        compiler_params=pltpu.CompilerParams(vmem_limit_bytes=vmem_bytes),
    )(*ins)


element_shape = (3, 5, 5, 4, 8, 128)
lines_shape = (3, 5, 5, 5, 8, 128)
internal_scratch = [lines_shape, (3, 5, 5, 8, 128), lines_shape, lines_shape, lines_shape, (2, 5, 5, 8, 128)]


def exchange(axis, to_low, to_high):
    count = lax.axis_size(axis)
    up = [(i, i + 1) for i in range(count - 1)]
    down = [(j, i) for i, j in up]
    return lax.ppermute(to_high, axis, up), lax.ppermute(to_low, axis, down)


def extended_2(array, sides, width):
    for axis, dim in sides:
        count, length = (lax.axis_size(axis), array.shape[dim])
        up = [(i, (i + 1) % count) for i in range(count - 1)]
        down = [(j, i) for i, j in up]
        last = lax.slice_in_dim(array, length - width, length, axis=dim)
        first = lax.slice_in_dim(array, 0, width, axis=dim)
        before = lax.ppermute(last, axis, up)
        after = lax.ppermute(first, axis, down)
        array = jnp.concatenate([before, array, after], axis=dim)
    return array


def pressure_of(hydro_state):
    velocity = hydro_state[1:4] / hydro_state[0]
    pressure = (gamma_gas - 1.0) * (
        hydro_state[4] - 0.5 * jnp.sum(hydro_state[1:4] * velocity, axis=0)
    )
    return (velocity, pressure)


def euler_flux(hydro_state, axis_num):
    velocity, pressure = pressure_of(hydro_state)
    sound_speed = jnp.sqrt(gamma_gas * pressure / hydro_state[0])
    normal_vel = velocity[axis_num]
    unit_row = jnp.eye(3, dtype=jnp.float32)[axis_num].reshape(3, 1, 1, 1)
    momentum_flux = hydro_state[1:4] * normal_vel + pressure * unit_row
    energy_flux = (hydro_state[4] + pressure) * normal_vel
    flux_all = jnp.concatenate(
        [hydro_state[1 + axis_num][None], momentum_flux, energy_flux[None]], axis=0
    )
    return (flux_all, jnp.abs(normal_vel) + sound_speed)


def advance(padded):
    interior = padded[:, 1:-1, 1:-1, 1:-1]
    change = jnp.zeros_like(interior)
    for axis_num in range(3):
        pencil = padded
        for other_axis in range(3):
            if other_axis != axis_num:
                pencil = lax.slice_in_dim(
                    pencil, 1, pencil.shape[other_axis + 1] - 1, axis=other_axis + 1
                )
        flux_all, wave_speed = euler_flux(pencil, axis_num)
        length = pencil.shape[axis_num + 1]
        low_state = lax.slice_in_dim(pencil, 0, length - 1, axis=axis_num + 1)
        high_state = lax.slice_in_dim(pencil, 1, length, axis=axis_num + 1)
        low_flux = lax.slice_in_dim(flux_all, 0, length - 1, axis=axis_num + 1)
        high_flux = lax.slice_in_dim(flux_all, 1, length, axis=axis_num + 1)
        fastest = jnp.maximum(
            lax.slice_in_dim(wave_speed, 0, length - 1, axis=axis_num),
            lax.slice_in_dim(wave_speed, 1, length, axis=axis_num),
        )
        face_flux = 0.5 * (low_flux + high_flux) - 0.5 * fastest * (high_state - low_state)
        change = (
            change
            + lax.slice_in_dim(face_flux, 1, length - 1, axis=axis_num + 1)
            - lax.slice_in_dim(face_flux, 0, length - 2, axis=axis_num + 1)
        )
    return interior - cell_ratio * change


def surface_traction(hydro_state):
    bottom = hydro_state[:, :, :, -1]
    velocity, pressure = pressure_of(bottom[:, :, :, None])
    vertical = velocity[2, :, :, 0]
    return (
        jnp.stack(
            [bottom[1] * vertical, bottom[2] * vertical, bottom[3] * vertical + pressure[:, :, 0]]
        )
        * face_area
    )


def fix_edges(padded, depth):
    placings = (
        (lax.axis_index("gx"), lax.axis_size("gx"), 1),
        (lax.axis_index(("grp", "gy")), lax.axis_size(("grp", "gy")), 2),
    )
    for position, extent, axis_num in placings:
        length = padded.shape[axis_num]
        inner_low = lax.slice_in_dim(padded, depth, depth + 1, axis=axis_num)
        inner_high = lax.slice_in_dim(padded, length - depth - 1, length - depth, axis=axis_num)
        place = lax.broadcasted_iota(jnp.int32, padded.shape, axis_num)
        padded = jnp.where((position == 0) & (place < depth), inner_low, padded)
        padded = jnp.where((position == extent - 1) & (place >= length - depth), inner_high, padded)
    return padded


def pad_depth(padded):
    return jnp.pad(padded, ((0, 0), (0, 0), (0, 0), (1, 1)), mode="edge")


def surface_tables():
    lane = np.arange(128)
    j, ey = lane // 8, lane % 8
    used = (j < 5) & (ey < 6)
    place = np.where(used, ey + 1, -9)
    source = lane[:, None]
    centre = source == place
    meet = centre | ((j == 0) & (source == place - 1)) | ((j == 4) & (source == place + 1))
    along = np.zeros((128, 128))
    for a in range(40):
        for b in range(40):
            if a % 8 == b % 8 and a % 8 < 6:
                along[a, b] = deriv[b // 8, a // 8]
    node = np.where(used, 4 * (ey - 1) + j, -9)
    fold = (lane[:, None] == node) & (lane[:, None] < 17)
    keep = fold & ((j < 4) & (ey < 5) | (j == 4) & (ey == 4))
    return np.stack([centre, meet, along, along.T, fold, keep]).astype(np.float32)


def full_dot(x, y, back=False):
    dims = (((1,), (1 if back else 0,)), ((), ()))
    return lax.dot_general(x, y, dims, precision=lax.Precision.HIGHEST, preferred_element_type=f32)


def deposit(faces, nodes_y, base_x, base_y, total):
    rows = faces.shape[1]
    sub = rows_of((8, 512)).astype(f32)
    total[...] = jnp.zeros_like(total)

    def one(step, carry):
        def wide(q):
            block = faces[q, pl.ds(4 * step, 4), :]
            return jnp.concatenate([block[n : n + 1] for n in range(4)], axis=1)

        ids = wide(3)
        node_x = jnp.floor((ids + 0.5) * (1.0 / nodes_y))
        rel_y = jnp.broadcast_to(ids - node_x * nodes_y - base_y, (8, 512))
        rel_x = jnp.broadcast_to(node_x - base_x, (8, 512))
        left = []
        hits = [(rel_x - i == 4.0 * sub) & (sub < 4.0) for i in range(5)]
        parts = [split_three(wide(c)) for c in range(3)]
        for part in range(3):
            for c in range(3):
                value = jnp.broadcast_to(parts[c][part].astype(f32), (8, 512))
                left += [jnp.where(hit, value, 0.0) for hit in hits]
        right = [jnp.where((rel_y - j == 4.0 * sub) & (sub < 6.0), 1.0, 0.0) for j in range(5)]
        right.append(jnp.zeros((88, 512), f32))
        left, right = jnp.concatenate(left, axis=0), jnp.concatenate(right, axis=0)
        total[...] += lax.dot_general(
            left.astype(jnp.bfloat16), right.astype(jnp.bfloat16), (((1,), (1,)), ((), ())), preferred_element_type=f32
        )
        return carry

    lax.fori_loop(0, rows // 4, one, 0)


def top_grid(grid, z):
    sub, lane = rows_of(), lanes_of()
    out = jnp.zeros((8, 128), f32)
    for x in range(3):
        total = jnp.zeros((8, 128), f32)
        for y in range(3):
            column = jnp.broadcast_to(grid[x][y][:, z : z + 1], (8, 128))
            total = total + jnp.where((lane == 4 * y + (sub & 3) - 2), column, 0.0)
        total = total + rolled(total, -1)
        total = total + rolled(total, -2)
        for ex in range(2):
            out = jnp.where(sub == 2 * x + ex, rolled(total, 2 * x + ex - 4 * ex), out)
    return out


def respond(total, grid, material, tables, out1, out2):
    sub, lane = rows_of(), lanes_of()
    top, below = top_grid(grid, 0), top_grid(grid, 1)
    centre, meet, along, along_t, fold, keep = [tables[n] for n in range(6)]
    sums0 = full_dot(lookup(material, 0, top), meet)
    sums1 = full_dot(lookup(material, 0, below), meet)
    lame = rolled(full_dot(lookup(material, 1, top), centre), -1)
    shear = rolled(full_dot(lookup(material, 2, top), centre), -1)
    weight_y = jnp.ones((8, 128), f32)
    for j in range(5):
        weight_y = jnp.where(lane // 8 == j, float(quad[j]), weight_y)

    def inverse(sums):
        mid = rolled(sums, -1)
        found = {0: mid + sums, 1: mid, 4: mid + rolled(sums, -2)}
        found = {i: jnp.where(s > 0.0, 1.0 / (s * weight_y), 0.0) for i, s in found.items()}
        found[2] = found[3] = found[1]
        return found

    light, heavy = inverse(sums0), inverse(sums0 + sums1)
    first = [[None] * 5 for _ in range(3)]
    moved = [[None] * 5 for _ in range(3)]
    for c in range(3):
        for i in range(5):
            at = (c * 5 + i) * 8
            force = total[at : at + 8] + total[at + 120 : at + 128] + total[at + 240 : at + 248]
            first[c][i] = force * light[i] * -accel_scale(i, 2, 0) * float(quad[2])
            moved[c][i] = first[c][i] * time_step**2
    gx = [line(deriv, moved[c]) for c in range(3)]
    gy = full_dot(jnp.concatenate([moved[c][i] for c in range(3) for i in range(5)], axis=0), along)
    gy = [[gy[(c * 5 + i) * 8 : (c * 5 + i) * 8 + 8] for i in range(5)] for c in range(3)]
    lame_w, shear_w = lame * weight_y * 2.0, shear * weight_y * 2.0
    d00 = float(deriv[0, 0])
    sx = [[], [], []]
    sy = [[], [], []]
    sz = [[], [], []]
    qs = [[], [], []]
    pressed = []
    for i in range(5):
        lw, mw = lame_w * float(quad[i]), shear_w * float(quad[i])
        d = [moved[c][i] for c in range(3)]
        gz = [d00 * x for x in d]
        dilated = lw * (gx[0][i] + gy[1][i] + gz[2])
        s01 = mw * (gx[1][i] + gy[0][i])
        s02 = mw * (gx[2][i] + gz[0])
        s12 = mw * (gy[2][i] + gz[1])
        for c, value in enumerate((dilated + 2.0 * mw * gx[0][i], s01, s02)):
            sx[c].append(value)
        for c, value in enumerate((s01, dilated + 2.0 * mw * gy[1][i], s12)):
            sy[c].append(value)
        for c, value in enumerate((s02, s12, dilated + 2.0 * mw * gz[2])):
            sz[c].append(value)
        for c, value in enumerate((mw * d[0], mw * d[1], (lw + 2.0 * mw) * d[2])):
            qs[c].append(value)
        pressed.append(lw * d[2])
    ydiv = full_dot(jnp.concatenate(sy[0] + sy[1] + sy[2] + pressed + qs[1], axis=0), along_t)
    ydiv = [[ydiv[(n * 5 + i) * 8 : (n * 5 + i) * 8 + 8] for i in range(5)] for n in range(5)]
    xdiv = [line(deriv_t, v) for v in sx + [pressed, qs[0]]]
    base = [xdiv[3], ydiv[3], [p + q for p, q in zip(xdiv[4], ydiv[4])]]
    second = {}
    for c in range(3):
        for i in range(5):
            for l in range(5):
                stiff = float(sum(deriv[k, l] * quad[k] * deriv[k, 0] for k in range(1, 5)))
                value = float(deriv[0, l] * quad[0]) * sz[c][i] + stiff * qs[c][i]
                if l:
                    value = value + float(deriv[l, 0] * quad[l]) * base[c][i]
                else:
                    value = value + float(quad[0]) * (xdiv[c][i] + ydiv[c][i])
                scale = (heavy if l == 4 else light)[i]
                second[c, i, l] = value * scale * (accel_scale(i, 2, l) * float(quad[2]))
    rows1, rows2 = [], []
    for c in range(3):
        for x in range(9):
            own = 1 if x < 4 else 2
            rows1.append(jnp.where(sub == 0, rolled(first[c][x - 4 * (own - 1)], -own), 0.0))
            block = jnp.zeros((8, 128), f32)
            for l in range(5):
                for ex in range(4):
                    i = x - 4 * (ex - 1)
                    if 0 <= i <= 4:
                        block = block + jnp.where(sub == l, rolled(second[c, i, l], l - ex), 0.0)
            rows2.append(block)
    blank = [jnp.zeros((40, 128), f32)]
    out1[...] = full_dot(keep[0:24], jnp.concatenate(rows1 + blank, axis=0), back=True)
    out2[...] = full_dot(fold[0:24], jnp.concatenate(rows2 + blank, axis=0), back=True)


def surface_kernel(nodes_y, faces, here, region, xl, xh, yl, yh, material, tables, out1, out2, total):
    base_x = (8 * here[0] - 4).astype(f32)
    base_y = (16 * here[1] - 4).astype(f32)
    deposit(faces, nodes_y, base_x, base_y, total)
    region_now = jnp.concatenate([region[0], region[1]], axis=0).astype(f32) + 1.0
    respond(total, region_grid(region_now, xl, xh, yl, yh), material, tables, out1, out2)


def shards(density, momentum, energy, displacement, velocity_field, acceleration, material, element_region_index,
           face_dest, face_slot):
    along_y = ("grp", "gy")
    place_x, place_y = lax.axis_index("gx"), lax.axis_index(along_y)
    nodes_y = 16 * lax.axis_size(along_y) + 1
    region = element_region_index
    b, f, x_low, x_high, y_low, y_high = call(
        first_kernel,
        (displacement, velocity_field, acceleration, region, material),
        [element_shape, element_shape, (31, 8, 128), (31, 8, 128), (16, 8, 128), (16, 8, 128)],
        internal_scratch + [(5, 5, 8, 512), (4, 9, 17, 128)],
        smem=(4,),
    )
    xl, xh = exchange("gx", x_low, x_high)
    y_low, y_high = call(
        functools.partial(edge_kernel, True), (y_low, y_high, xl, xh), [(18, 8, 128), (18, 8, 128)], []
    )
    yl, yh = exchange(along_y, y_low, y_high)
    hydro_state = jnp.concatenate([density[None], momentum, energy[None]], axis=0)
    for repeat in range(2):
        padded = extended_2(hydro_state, (("gx", 1), (("grp", "gy"), 2)), 1)
        hydro_state = advance(pad_depth(fix_edges(padded, 1)))
    traction = surface_traction(hydro_state).reshape(3, -1)
    targets, slots = face_dest[0, :, 0], face_slot[0]
    count_x, count_gy = lax.axis_size("gx"), lax.axis_size("gy")
    node_x = targets // count_gy % count_x * 8 + slots // 17
    node_y = (targets // (count_gy * count_x) * count_gy + targets % count_gy) * 16 + slots % 17
    ids = (node_x * nodes_y + node_y).astype(f32)
    rank = ("grp", "gx", "gy")
    mine = jnp.concatenate([traction, ids[None]], axis=0)
    copies = jnp.broadcast_to(mine, (lax.axis_size(rank),) + mine.shape)
    faces = jnp.swapaxes(lax.all_to_all(copies, rank, 0, 0, tiled=True), 0, 1)
    here = jnp.stack([place_x, place_y]).astype(jnp.int32)
    surf1, surf2 = call(
        functools.partial(surface_kernel, float(nodes_y)),
        (faces, here, region, xl, xh, yl, yh, material, jnp.asarray(surface_tables())),
        [(24, 256), (24, 256)],
        [(360, 128)],
        smem=(1, 7),
    )
    a1, f2, x_low, x_high, y_low, y_high, scales = call(
        second_kernel,
        (b, f, xl, xh, yl, yh, region, material),
        [element_shape, element_shape, (30, 8, 128), (30, 8, 128), (15, 8, 128), (15, 8, 128), (3, 3, 2, 8, 128)],
        internal_scratch,
        smem=(7,),
    )
    xl2, xh2 = exchange("gx", x_low, x_high)
    y_low, y_high = call(
        functools.partial(edge_kernel, False), (y_low, y_high, xl2, xh2), [(15, 8, 128), (15, 8, 128)], []
    )
    yl2, yh2 = exchange(along_y, y_low, y_high)
    u_out, v_out, a_out = call(
        last_kernel,
        (a1, f2, xl2, xh2, yl2, yh2, scales, surf1, surf2, displacement, velocity_field, acceleration),
        [displacement.shape] * 3,
        [(5, 5, 8, 512), (4, 9, 17, 128), (4, 9, 17, 128), element_shape],
    )
    return hydro_state, u_out, v_out, a_out


def solution(mesh):
    field = P(None, "gx", ("grp", "gy"), None)
    cells = P("gx", ("grp", "gy"), None)
    rank = ("grp", "gx", "gy")
    return jax.shard_map(
        shards,
        mesh=mesh,
        in_specs=(cells, field, cells, field, field, field, P(), cells, P(rank, None, None), P(rank, None)),
        out_specs=(field, field, field, field),
        check_vma=False,
    )
```

```python
import functools

import jax
import jax.numpy as jnp
import numpy as np
from jax import lax
from jax.experimental import pallas as pl
from jax.experimental.pallas import tpu as pltpu
from jax.sharding import PartitionSpec as P

gamma_gas = 1.4
cell_ratio = 0.05
half_size = 2.0
time_step = 0.1
face_area = 2.0
vmem_bytes = 40 * 1024 * 1024


def gll_tables():
    root = np.sqrt(3.0 / 7.0)
    points = np.array([-1.0, -root, 0.0, root, 1.0])
    weights = np.array([0.1, 49.0 / 90.0, 32.0 / 45.0, 49.0 / 90.0, 0.1])
    products = [np.prod([points[r] - points[c] for c in range(5) if c != r]) for r in range(5)]
    derivative = np.zeros((5, 5))
    for r in range(5):
        for c in range(5):
            if r != c:
                derivative[r, c] = products[r] / products[c] / (points[r] - points[c])
        derivative[r, r] = sum(1.0 / (points[r] - points[c]) for c in range(5) if c != r)
    derivative[2, 2] = 0.0
    return derivative, weights


deriv, quad = gll_tables()
deriv_t = deriv.T
kind = [0, 1, 2, 1, 0]
f32 = jnp.float32


def line(matrix, v):
    even, odd = (matrix + matrix[:, ::-1]) / 2, (matrix - matrix[:, ::-1]) / 2
    e0, e1, o0, o1 = v[0] + v[4], v[1] + v[3], v[0] - v[4], v[1] - v[3]
    top = [float(even[i, 0]) * e0 + float(even[i, 1]) * e1 + float(matrix[i, 2]) * v[2] for i in range(2)]
    low = [float(odd[i, 0]) * o0 + float(odd[i, 1]) * o1 for i in range(2)]
    centre = float(matrix[2, 0]) * o0 + float(matrix[2, 1]) * o1
    return [top[0] + low[0], top[1] + low[1], centre, low[1] - top[1], low[0] - top[0]]


def rows_of(shape=(8, 128)):
    return lax.broadcasted_iota(jnp.int32, shape, 0)


def lanes_of(shape=(8, 128)):
    return lax.broadcasted_iota(jnp.int32, shape, 1)


def deeper(x):
    return jnp.where(lanes_of() == 127, 0.0, pltpu.roll(x, 127, 1))


def shallower(x):
    return jnp.where(lanes_of() == 0, 0.0, pltpu.roll(x, 1, 1))


def split_three(x):
    high = x.astype(jnp.bfloat16)
    rest = x - high.astype(f32)
    middle = rest.astype(jnp.bfloat16)
    return high, middle, (rest - middle.astype(f32)).astype(jnp.bfloat16)


def one_hot_dot(x, table, dims=(((1,), (0,)), ((), ()))):
    return sum(lax.dot_general(part, table, dims, preferred_element_type=f32) for part in split_three(x))


def depth_table(back=False):
    a = lax.broadcasted_iota(jnp.int32, (512, 512), 1 if back else 0)
    b = lax.broadcasted_iota(jnp.int32, (512, 512), 0 if back else 1)
    return jnp.where(a == 4 * (b & 127) + (b >> 7), 1.0, 0.0).astype(jnp.bfloat16)


def to_elements(nodes, table, tall, put):
    for i in range(5):
        for j in range(5):
            for ex in range(2):
                for t in range(4):
                    tall[i, j, 4 * ex : 4 * ex + 4, 128 * t : 128 * t + 128] = nodes[t, 4 * ex + i, pl.ds(j, 4, stride=4), :]
    out = one_hot_dot(tall[...].reshape(200, 512), table)
    for k in range(4):
        put(k, out[:, 128 * k : 128 * k + 128].reshape(5, 5, 8, 128))


def to_nodes(get, table, tall, nodes):
    wide = jnp.concatenate([get(k).reshape(200, 128) for k in range(4)], axis=1)
    tall[...] = one_hot_dot(wide, table).reshape(5, 5, 8, 512)
    for i in range(5):
        for j in range(5):
            for ex in range(2):
                if i == 4 and ex == 0:
                    continue
                for t in range(4):
                    lanes = slice(128 * t, 128 * t + 128)
                    if j < 4:
                        nodes[t, 4 * ex + i, pl.ds(j, 4, stride=4), :] = tall[i, j, 4 * ex : 4 * ex + 4, lanes]
                    else:
                        nodes[t, 4 * ex + i, 16:17, :] = tall[i, j, 4 * ex + 3 : 4 * ex + 4, lanes]


def lookup(material, row, region):
    total = jnp.zeros_like(region)
    for m in range(material.shape[1]):
        total = jnp.where(region == float(m + 1), material[row, m], total)
    return total


def internal(u, out, lame, shear, gx, gz, cross, planes, side):
    def depth_lines(i, carry):
        for j in range(5):
            for c in range(3):
                v = [u[c, i, j, k] for k in range(4)]
                v.append(deeper(v[0]))
                u[c, i, j, 4] = v[4]
                for k, g in enumerate(line(deriv, v)):
                    gz[c, i, j, k] = g
        return carry

    lax.fori_loop(0, 5, depth_lines, 0)

    def plane(k, carry):
        weight = jnp.where((k == 0) | (k == 4), float(quad[0]), jnp.where(k == 2, float(quad[2]), float(quad[1])))
        lame_k, shear_k = lame * (2.0 * weight), shear * (2.0 * weight)
        pairs = {}
        for a in range(3):
            for b in range(a, 3):
                w = float(quad[a] * quad[b])
                pairs[a, b] = pairs[b, a] = (lame_k * w, shear_k * w, shear_k * (2.0 * w))
        for c in range(3):
            for j in range(5):
                for i, g in enumerate(line(deriv, [u[c, i, j, k] for i in range(5)])):
                    gx[c, i, j] = g
        for i in range(5):
            gy = [line(deriv, [u[c, i, j, k] for j in range(5)]) for c in range(3)]
            ys = [[], [], []]
            for j in range(5):
                lw, mw, mw2 = pairs[kind[i], kind[j]]
                g0, g1, g2 = [[gx[c, i, j], gy[c][j], gz[c, i, j, k]] for c in range(3)]
                dilated = lw * (g0[0] + g1[1] + g2[2])
                s01 = mw * (g0[1] + g1[0])
                s02 = mw * (g0[2] + g2[0])
                s12 = mw * (g1[2] + g2[1])
                side[0, i, j] = dilated + mw2 * g0[0]
                side[1, i, j] = s01
                cross[0, i, j, k] = s02
                cross[1, i, j, k] = s12
                cross[2, i, j, k] = dilated + mw2 * g2[2]
                ys[0].append(s01)
                ys[1].append(dilated + mw2 * g1[1])
                ys[2].append(s12)
            for c in range(3):
                for j, value in enumerate(line(deriv_t, ys[c])):
                    planes[c, i, j, k] = value
        for j in range(5):
            for c in range(3):
                v = [side[c, i, j] if c < 2 else cross[0, i, j, k] for i in range(5)]
                for i, value in enumerate(line(deriv_t, v)):
                    planes[c, i, j, k] += value
        return carry

    lax.fori_loop(0, 5, plane, 0)

    def depth_sums(i, carry):
        for j in range(5):
            for c in range(3):
                v = line(deriv_t, [cross[c, i, j, k] for k in range(5)])
                v = [v[k] + planes[c, i, j, k] for k in range(5)]
                out[c, i, j, 0] = v[0] + shallower(v[4])
                for k in range(1, 4):
                    out[c, i, j, k] = v[k]
        return carry

    lax.fori_loop(0, 5, depth_sums, 0)
    sub = rows_of()

    def fold(k, carry):
        for c in range(3):
            for i in range(5):
                low, high = out[c, i, 0, k], out[c, i, 4, k]
                out[c, i, 0, k] = low + jnp.where(sub % 4 == 0, 0.0, pltpu.roll(high, 1, 0))
                out[c, i, 4, k] = high + jnp.where(sub % 4 == 3, 0.0, pltpu.roll(low, 7, 0))
            for j in range(5):
                low, high = out[c, 0, j, k], out[c, 4, j, k]
                out[c, 0, j, k] = low + jnp.where(sub < 4, 0.0, pltpu.roll(high, 4, 0))
                out[c, 4, j, k] = high + jnp.where(sub < 4, pltpu.roll(low, 4, 0), 0.0)
        return carry

    lax.fori_loop(0, 4, fold, 0)


def rolled(x, amount, axis=0):
    amount = amount % x.shape[axis]
    return pltpu.roll(x, amount, axis) if amount else x


def pack_x(force, low, high):
    sub = rows_of()
    for c in range(3):
        for j in range(5):
            for half in range(2):
                at = (c * 5 + j) * 2 + half
                a, b = force[c, 0, j, 2 * half], force[c, 0, j, 2 * half + 1]
                low[at] = jnp.where(sub < 4, a, rolled(b, 4))
                a, b = force[c, 4, j, 2 * half], force[c, 4, j, 2 * half + 1]
                high[at] = jnp.where(sub < 4, rolled(a, 4), b)


def pack_y(force, low, high):
    sub = rows_of()
    for c in range(3):
        for i in range(5):
            a, b = force[c, i, 0, 0], rolled(force[c, i, 4, 0], -3)
            for k in range(1, 4):
                a = jnp.where(sub % 4 == k, rolled(force[c, i, 0, k], k), a)
                b = jnp.where(sub % 4 == k, rolled(force[c, i, 4, k], k - 3), b)
            low[c * 5 + i] = a
            high[c * 5 + i] = b


def add_x(force, from_low, from_high):
    sub = rows_of()
    for c in range(3):
        for j in range(5):
            for half in range(2):
                at = (c * 5 + j) * 2 + half
                r, s = from_low[at], from_high[at]
                force[c, 0, j, 2 * half] += jnp.where(sub < 4, r, 0.0)
                force[c, 0, j, 2 * half + 1] += jnp.where(sub < 4, rolled(r, 4), 0.0)
                force[c, 4, j, 2 * half] += jnp.where(sub < 4, 0.0, rolled(s, 4))
                force[c, 4, j, 2 * half + 1] += jnp.where(sub < 4, 0.0, s)


def add_y(force, from_low, from_high):
    sub = rows_of()
    for c in range(3):
        for i in range(5):
            r, s = from_low[c * 5 + i], from_high[c * 5 + i]
            for k in range(4):
                force[c, i, 0, k] += jnp.where(sub % 4 == 0, rolled(r, -k), 0.0)
                force[c, i, 4, k] += jnp.where(sub % 4 == 3, rolled(s, 3 - k), 0.0)


def edge_kernel(extra, low, high, from_low, from_high, *outs):
    out_low, out_high = outs
    sub = rows_of()
    for c in range(3):
        for i in range(5):
            out_low[c * 5 + i] = low[c * 5 + i]
            out_high[c * 5 + i] = high[c * 5 + i]
        for i, came, first in ((0, from_low, 0), (4, from_high, 4)):
            for j, out, row in ((0, out_low, 0), (4, out_high, 3)):
                total = out[c * 5 + i]
                for k in range(4):
                    r = rolled(came[(c * 5 + j) * 2 + k // 2], first + k - (4 * (k % 2) + row))
                    total = total + jnp.where(sub == first + k, r, 0.0)
                out[c * 5 + i] = total
    if extra:
        for out, mine in ((out_low, low), (out_high, high)):
            out[15] = mine[15]
            out[16] = from_low[30]
            out[17] = from_high[30]


def region_grid(own, xl, xh, yl, yh):
    return [[yl[16], xl[30], yh[16]], [yl[15], own, yh[15]], [yl[17], xh[30], yh[17]]]


def shared_density(grid):
    sub = rows_of()
    across = []
    for y in range(3):
        low, mid, high = grid[0][y], grid[1][y], grid[2][y]
        turned = rolled(mid, 4)
        across.append([jnp.where(sub < 4, rolled(low, 4), turned), mid, jnp.where(sub < 4, turned, rolled(high, 4))])
    found = [[None] * 3 for _ in range(3)]
    for x in range(3):
        low, mid, high = across[0][x], across[1][x], across[2][x]
        found[x][0] = jnp.where(sub % 4 == 0, rolled(low, -3), rolled(mid, 1))
        found[x][1] = mid
        found[x][2] = jnp.where(sub % 4 == 3, rolled(high, 3), rolled(mid, -1))
    sums = []
    for x in ((1,), (0, 1), (1, 2)):
        row = []
        for y in ((1,), (0, 1), (1, 2)):
            total = sum(found[a][b] for a in x for b in y)
            row.append((total + shallower(total), total))
        sums.append(row)
    return sums


def mass_scales(sums):
    return [[[1.0 / s for s in pair] for pair in row] for row in sums]


def edge_kind(i):
    return 1 if i == 0 else 2 if i == 4 else 0


def accel_scale(i, j, k):
    return float(-1.0 / (half_size**3 * quad[i] * quad[j] * quad[k]))


def first_kernel(u, v, a, region, material, b_out, f_out, x_low, x_high, y_low, y_high,
                 elem, gx, gz, cross, planes, side, tall, nodes):
    table = depth_table()
    region_now = jnp.concatenate([region[0], region[1]], axis=0).astype(f32) + 1.0

    def one(c, carry):
        for t in range(4):
            lanes = slice(128 * t, 128 * t + 128)
            nodes[t] = u[c, :, :, lanes] + time_step * v[c, :, :, lanes] + 0.5 * time_step**2 * a[c, :, :, lanes]

        def put_u(k, value):
            elem[c, :, :, k] = value

        to_elements(nodes, table, tall, put_u)
        for t in range(4):
            lanes = slice(128 * t, 128 * t + 128)
            nodes[t] = u[c, :, :, lanes] + 2.0 * time_step * v[c, :, :, lanes] + time_step**2 * a[c, :, :, lanes]

        def put_b(k, value):
            b_out[c, :, :, k] = value

        to_elements(nodes, table, tall, put_b)
        return carry

    lax.fori_loop(0, 3, one, 0)
    internal(elem, f_out, lookup(material, 1, region_now), lookup(material, 2, region_now), gx, gz, cross, planes, side)
    pack_x(f_out, x_low, x_high)
    pack_y(f_out, y_low, y_high)
    x_low[30] = region_now
    x_high[30] = region_now
    y_low[15] = region_now
    y_high[15] = region_now


def second_kernel(b, f, xl, xh, yl, yh, region, material, a_out, f_out, x_low, x_high, y_low, y_high, scales,
                  elem, gx, gz, cross, planes, side):
    region_now = jnp.concatenate([region[0], region[1]], axis=0).astype(f32) + 1.0
    a_out[...] = f[...]
    add_x(a_out, xl, xh)
    add_y(a_out, yl, yh)
    grid = region_grid(region_now, xl, xh, yl, yh)
    inverse = mass_scales(shared_density([[lookup(material, 0, r) for r in row] for row in grid]))
    for x in range(3):
        for y in range(3):
            for z in range(2):
                scales[x, y, z] = inverse[x][y][z]
    for i in range(5):
        for j in range(5):
            for k in range(4):
                scale = scales[edge_kind(i), edge_kind(j), min(k, 1)] * accel_scale(i, j, k)
                for c in range(3):
                    value = a_out[c, i, j, k] * scale
                    a_out[c, i, j, k] = value
                    elem[c, i, j, k] = b[c, i, j, k] + time_step**2 * value
    internal(elem, f_out, lookup(material, 1, region_now), lookup(material, 2, region_now), gx, gz, cross, planes, side)
    pack_x(f_out, x_low, x_high)
    pack_y(f_out, y_low, y_high)


def last_kernel(a1, f, xl, xh, yl, yh, scales, surf1, surf2, u, v, a, u_out, v_out, a_out, tall, nodes, nodes2, force):
    table = depth_table(back=True)
    force[...] = f[...]
    add_x(force, xl, xh)
    add_y(force, yl, yh)
    for i in range(5):
        for j in range(5):
            for k in range(4):
                scale = scales[edge_kind(i), edge_kind(j), min(k, 1)] * accel_scale(i, j, k)
                for c in range(3):
                    force[c, i, j, k] = force[c, i, j, k] * scale
    lane = lanes_of((17, 128))
    for c in range(3):
        to_nodes(lambda k: a1[c, :, :, k], table, tall, nodes)
        to_nodes(lambda k: force[c, :, :, k], table, tall, nodes2)
        for x in range(9):
            at = 8 * (c * 9 + x)
            tile, shift = at // 128, (128 - at % 128) % 128
            moved = [rolled(s[0:17, 128 * tile : 128 * tile + 128], shift, 1) for s in (surf1, surf2)]
            direct = jnp.where(lane < 1, moved[0], 0.0)
            nodes[0, x] += direct
            nodes2[0, x] += direct + jnp.where(lane < 5, moved[1], 0.0)
        for t in range(4):
            at = (c, slice(None), slice(None), slice(128 * t, 128 * t + 128))
            first, second = nodes[t], nodes2[t]
            a_out[at] = second
            u_out[at] = u[at] + 2.0 * time_step * v[at] + time_step**2 * (a[at] + first)
            v_out[at] = v[at] + 0.5 * time_step * (a[at] + 2.0 * first + second)


def whole():
    return pl.BlockSpec(memory_space=pltpu.VMEM)


def scalars():
    return pl.BlockSpec(memory_space=pltpu.SMEM)


def call(kernel, ins, outs, scratch, smem=()):
    return pl.pallas_call(
        kernel,
        out_shape=[jax.ShapeDtypeStruct(s, f32) for s in outs],
        in_specs=[scalars() if n in smem else whole() for n in range(len(ins))],
        out_specs=[whole() for _ in outs],
        scratch_shapes=[pltpu.VMEM(s, f32) for s in scratch],
        compiler_params=pltpu.CompilerParams(vmem_limit_bytes=vmem_bytes),
    )(*ins)


element_shape = (3, 5, 5, 4, 8, 128)
lines_shape = (3, 5, 5, 5, 8, 128)
internal_scratch = [lines_shape, (3, 5, 5, 8, 128), lines_shape, lines_shape, lines_shape, (2, 5, 5, 8, 128)]


def exchange(axis, to_low, to_high):
    count = lax.axis_size(axis)
    up = [(i, i + 1) for i in range(count - 1)]
    down = [(j, i) for i, j in up]
    return lax.ppermute(to_high, axis, up), lax.ppermute(to_low, axis, down)


def surface_tables():
    lane = np.arange(128)
    j, ey = lane // 8, lane % 8
    used = (j < 5) & (ey < 6)
    place = np.where(used, ey + 1, -9)
    source = lane[:, None]
    centre = source == place
    meet = centre | ((j == 0) & (source == place - 1)) | ((j == 4) & (source == place + 1))
    along = np.zeros((128, 128))
    for a in range(40):
        for b in range(40):
            if a % 8 == b % 8 and a % 8 < 6:
                along[a, b] = deriv[b // 8, a // 8]
    node = np.where(used, 4 * (ey - 1) + j, -9)
    fold = (lane[:, None] == node) & (lane[:, None] < 17)
    keep = fold & ((j < 4) & (ey < 5) | (j == 4) & (ey == 4))
    return np.stack([centre, meet, along, along.T, fold, keep]).astype(np.float32)


def full_dot(x, y, back=False):
    dims = (((1,), (1 if back else 0,)), ((), ()))
    return lax.dot_general(x, y, dims, precision=lax.Precision.HIGHEST, preferred_element_type=f32)


def deposit(faces, nodes_y, base_x, base_y, total):
    rows = faces.shape[1]
    sub = rows_of((8, 512)).astype(f32)
    total[...] = jnp.zeros_like(total)

    def one(step, carry):
        def wide(q):
            block = faces[q, pl.ds(4 * step, 4), :]
            return jnp.concatenate([block[n : n + 1] for n in range(4)], axis=1)

        ids = wide(3)
        node_x = jnp.floor((ids + 0.5) * (1.0 / nodes_y))
        rel_y = jnp.broadcast_to(ids - node_x * nodes_y - base_y, (8, 512))
        rel_x = jnp.broadcast_to(node_x - base_x, (8, 512))
        left = []
        hits = [(rel_x - i == 4.0 * sub) & (sub < 4.0) for i in range(5)]
        parts = [split_three(wide(c)) for c in range(3)]
        for part in range(3):
            for c in range(3):
                value = jnp.broadcast_to(parts[c][part].astype(f32), (8, 512))
                left += [jnp.where(hit, value, 0.0) for hit in hits]
        right = [jnp.where((rel_y - j == 4.0 * sub) & (sub < 6.0), 1.0, 0.0) for j in range(5)]
        right.append(jnp.zeros((88, 512), f32))
        left, right = jnp.concatenate(left, axis=0), jnp.concatenate(right, axis=0)
        total[...] += lax.dot_general(
            left.astype(jnp.bfloat16), right.astype(jnp.bfloat16), (((1,), (1,)), ((), ())), preferred_element_type=f32
        )
        return carry

    lax.fori_loop(0, rows // 4, one, 0)


def top_grid(grid, z):
    sub, lane = rows_of(), lanes_of()
    out = jnp.zeros((8, 128), f32)
    for x in range(3):
        total = jnp.zeros((8, 128), f32)
        for y in range(3):
            column = jnp.broadcast_to(grid[x][y][:, z : z + 1], (8, 128))
            total = total + jnp.where((lane == 4 * y + (sub & 3) - 2), column, 0.0)
        total = total + rolled(total, -1)
        total = total + rolled(total, -2)
        for ex in range(2):
            out = jnp.where(sub == 2 * x + ex, rolled(total, 2 * x + ex - 4 * ex), out)
    return out


def respond(total, grid, material, tables, out1, out2):
    sub, lane = rows_of(), lanes_of()
    top, below = top_grid(grid, 0), top_grid(grid, 1)
    centre, meet, along, along_t, fold, keep = [tables[n] for n in range(6)]
    sums0 = full_dot(lookup(material, 0, top), meet)
    sums1 = full_dot(lookup(material, 0, below), meet)
    lame = rolled(full_dot(lookup(material, 1, top), centre), -1)
    shear = rolled(full_dot(lookup(material, 2, top), centre), -1)
    weight_y = jnp.ones((8, 128), f32)
    for j in range(5):
        weight_y = jnp.where(lane // 8 == j, float(quad[j]), weight_y)

    def inverse(sums):
        mid = rolled(sums, -1)
        found = {0: mid + sums, 1: mid, 4: mid + rolled(sums, -2)}
        found = {i: jnp.where(s > 0.0, 1.0 / (s * weight_y), 0.0) for i, s in found.items()}
        found[2] = found[3] = found[1]
        return found

    light, heavy = inverse(sums0), inverse(sums0 + sums1)
    first = [[None] * 5 for _ in range(3)]
    moved = [[None] * 5 for _ in range(3)]
    for c in range(3):
        for i in range(5):
            at = (c * 5 + i) * 8
            force = total[at : at + 8] + total[at + 120 : at + 128] + total[at + 240 : at + 248]
            first[c][i] = force * light[i] * -accel_scale(i, 2, 0) * float(quad[2])
            moved[c][i] = first[c][i] * time_step**2
    gx = [line(deriv, moved[c]) for c in range(3)]
    gy = full_dot(jnp.concatenate([moved[c][i] for c in range(3) for i in range(5)], axis=0), along)
    gy = [[gy[(c * 5 + i) * 8 : (c * 5 + i) * 8 + 8] for i in range(5)] for c in range(3)]
    lame_w, shear_w = lame * weight_y * 2.0, shear * weight_y * 2.0
    d00 = float(deriv[0, 0])
    sx = [[], [], []]
    sy = [[], [], []]
    sz = [[], [], []]
    qs = [[], [], []]
    pressed = []
    for i in range(5):
        lw, mw = lame_w * float(quad[i]), shear_w * float(quad[i])
        d = [moved[c][i] for c in range(3)]
        gz = [d00 * x for x in d]
        dilated = lw * (gx[0][i] + gy[1][i] + gz[2])
        s01 = mw * (gx[1][i] + gy[0][i])
        s02 = mw * (gx[2][i] + gz[0])
        s12 = mw * (gy[2][i] + gz[1])
        for c, value in enumerate((dilated + 2.0 * mw * gx[0][i], s01, s02)):
            sx[c].append(value)
        for c, value in enumerate((s01, dilated + 2.0 * mw * gy[1][i], s12)):
            sy[c].append(value)
        for c, value in enumerate((s02, s12, dilated + 2.0 * mw * gz[2])):
            sz[c].append(value)
        for c, value in enumerate((mw * d[0], mw * d[1], (lw + 2.0 * mw) * d[2])):
            qs[c].append(value)
        pressed.append(lw * d[2])
    ydiv = full_dot(jnp.concatenate(sy[0] + sy[1] + sy[2] + pressed + qs[1], axis=0), along_t)
    ydiv = [[ydiv[(n * 5 + i) * 8 : (n * 5 + i) * 8 + 8] for i in range(5)] for n in range(5)]
    xdiv = [line(deriv_t, v) for v in sx + [pressed, qs[0]]]
    base = [xdiv[3], ydiv[3], [p + q for p, q in zip(xdiv[4], ydiv[4])]]
    second = {}
    for c in range(3):
        for i in range(5):
            for l in range(5):
                stiff = float(sum(deriv[k, l] * quad[k] * deriv[k, 0] for k in range(1, 5)))
                value = float(deriv[0, l] * quad[0]) * sz[c][i] + stiff * qs[c][i]
                if l:
                    value = value + float(deriv[l, 0] * quad[l]) * base[c][i]
                else:
                    value = value + float(quad[0]) * (xdiv[c][i] + ydiv[c][i])
                scale = (heavy if l == 4 else light)[i]
                second[c, i, l] = value * scale * (accel_scale(i, 2, l) * float(quad[2]))
    rows1, rows2 = [], []
    for c in range(3):
        for x in range(9):
            own = 1 if x < 4 else 2
            rows1.append(jnp.where(sub == 0, rolled(first[c][x - 4 * (own - 1)], -own), 0.0))
            block = jnp.zeros((8, 128), f32)
            for l in range(5):
                for ex in range(4):
                    i = x - 4 * (ex - 1)
                    if 0 <= i <= 4:
                        block = block + jnp.where(sub == l, rolled(second[c, i, l], l - ex), 0.0)
            rows2.append(block)
    blank = [jnp.zeros((40, 128), f32)]
    out1[...] = full_dot(keep[0:24], jnp.concatenate(rows1 + blank, axis=0), back=True)
    out2[...] = full_dot(fold[0:24], jnp.concatenate(rows2 + blank, axis=0), back=True)


def position(axis):
    return lax.axis_index(axis)


def along_y():
    return lax.axis_index("grp") * lax.axis_size("gy") + lax.axis_index("gy")


def primitives(state):
    inverse = 1.0 / state[0]
    v = [state[1 + c] * inverse for c in range(3)]
    p = (gamma_gas - 1.0) * (state[4] - 0.5 * (state[1] * v[0] + state[2] * v[1] + state[3] * v[2]))
    return v + [p, jnp.sqrt(gamma_gas * p * inverse), state[4] + p]


def flux(state, prim, d):
    out = [state[1 + d]] + [state[1 + c] * prim[d] for c in range(3)] + [prim[5] * prim[d]]
    out[1 + d] = out[1 + d] + prim[3]
    return out, jnp.abs(prim[d]) + prim[4]


def twice_face(low, high):
    fastest = jnp.maximum(low[2], high[2])
    return [fl + fh - fastest * (uh - ul) for ul, uh, fl, fh in zip(low[0], high[0], low[1], high[1])]


def turned_change(state, prim, d, axis, ends):
    size = state[0].shape[axis]
    fluxes, speed = flux(state, prim, d)
    up = lambda x: pltpu.roll(x, size - 1, axis)
    high = ([up(x) for x in state], [up(x) for x in fluxes], up(speed))
    upper = twice_face((state, fluxes, speed), high)
    if ends is None:
        return [g - pltpu.roll(g, 1, axis) for g in upper]
    upper = [jnp.where(ends[1], 2.0 * f, g) for f, g in zip(fluxes, upper)]
    return [g - jnp.where(ends[0], 2.0 * f, pltpu.roll(g, 1, axis)) for f, g in zip(fluxes, upper)]


def field_of(f, density, momentum, energy):
    return density if f == 0 else energy if f == 4 else momentum.at[f - 1]


def start_kernel(nodes_y, density, momentum, energy, dest, slot, bottoms, rows):
    lane = lanes_of()
    pick = jnp.where(lane == 125 + rows_of(), 1.0, 0.0)
    pieces = []
    place = along_y()
    for f in range(5):
        field = field_of(f, density, momentum, energy)
        columns = jnp.concatenate([field[x, :, 128:256] for x in range(4)], axis=0)
        pieces.append(full_dot(pick, columns, back=True)[0:3])
        low = jnp.concatenate([field[x, r : r + 1, :] for r in (0, 1) for x in range(4)], axis=0)
        high = jnp.concatenate([field[x, r : r + 1, :] for r in (31, 30) for x in range(4)], axis=0)
        for p in range(4):
            rows[p, f] = jnp.where(p < place, low, high)
    count_gy, count_x = lax.axis_size("gy"), lax.axis_size("gx")
    target, node = dest[...].astype(f32), slot[...].astype(f32)
    grp = jnp.floor((target + 0.5) * (1.0 / (count_gy * count_x)))
    rest = target - grp * (count_gy * count_x)
    gx = jnp.floor((rest + 0.5) * (1.0 / count_gy))
    gy = rest - gx * count_gy
    i = jnp.floor((node + 0.5) * (1.0 / 17.0))
    j = node - 17.0 * i
    pieces.append((8.0 * gx + i) * nodes_y + 16.0 * (grp * count_gy + gy) + j)
    block = jnp.concatenate(pieces, axis=0)
    for n in range(bottoms.shape[0]):
        bottoms[n] = block


def widen_kernel(density, momentum, energy, came, own, first, second):
    place, last = along_y(), lax.axis_size("grp") * lax.axis_size("gy") - 1
    odd = position("gx") % 2
    low_slot, high_slot = jnp.maximum(place - 1, 0), jnp.minimum(place + 1, last)
    for f in range(5):
        field = field_of(f, density, momentum, energy)
        low, high = came[low_slot, f], came[high_slot, f]
        for x in range(4):
            own[f, x, 0:32, :] = field[x]
            bottom, top = field[x, 0:1, :], field[x, 31:32, :]
            own[f, x, 39:40, :] = jnp.where(place == 0, bottom, low[x : x + 1])
            own[f, x, 38:39, :] = jnp.where(place == 0, bottom, low[4 + x : 5 + x])
            own[f, x, 32:33, :] = jnp.where(place == last, top, high[x : x + 1])
            own[f, x, 33:34, :] = jnp.where(place == last, top, high[4 + x : 5 + x])
            own[f, x, 34:38, :] = jnp.broadcast_to(top, (4, 256))
        for out, low_way in ((first, odd), (second, 1 - odd)):
            near = jnp.where(low_way == 1, 0, 3)
            far = jnp.where(low_way == 1, 1, 2)
            out[f, 0:40, :] = own[f, near]
            out[f, 40:72, :] = own[f, far, 0:32, :]


def crater_kernel(own, came1, came2, out, wide, mid, prims, face, fluxes):
    place, last_y = along_y(), lax.axis_size("grp") * lax.axis_size("gy") - 1
    gx, last_x = position("gx"), lax.axis_size("gx") - 1
    odd = gx % 2
    for f in range(5):
        for x in range(4):
            wide[f, 2 + x] = own[f, x]

    def spread(came, near, far):
        for f in range(5):
            wide[f, near] = came[f, 0:40, :]
            wide[f, far, 0:32, :] = came[f, 40:72, :]
            wide[f, far, 32:40, :] = came[f, 32:40, :]

    @pl.when(odd == 1)
    def _():
        spread(came1, 1, 0)
        spread(came2, 6, 7)

    @pl.when(odd == 0)
    def _():
        spread(came2, 1, 0)
        spread(came1, 6, 7)

    @pl.when(gx == 0)
    def _():
        for f in range(5):
            wide[f, 0] = own[f, 0]
            wide[f, 1] = own[f, 0]

    @pl.when(gx == last_x)
    def _():
        for f in range(5):
            wide[f, 6] = own[f, 3]
            wide[f, 7] = own[f, 3]

    lane = lanes_of((40, 256))
    ends = (lane == 0, lane == 255)

    def step(source, low, high, put):
        def along_x(p):
            state = [source[f, p] for f in range(5)]
            prim = primitives(state)
            return state, prim, flux(state, prim, 0)

        state, prim, (fx, speed) = along_x(low - 1)
        next_state, next_prim, (next_fx, next_speed) = along_x(low)
        g = twice_face((state, fx, speed), (next_state, next_fx, next_speed))
        for f in range(5):
            face[f] = g[f]
            fluxes[f] = next_fx[f]
        for n in range(6):
            prims[n] = next_prim[n]
        fluxes[5] = next_speed

        def plane(p, carry):
            state = [source[f, p] for f in range(5)]
            prim = [prims[n] for n in range(6)]
            next_state, next_prim, (next_fx, next_speed) = along_x(p + 1)
            g = twice_face((state, [fluxes[f] for f in range(5)], fluxes[5]), (next_state, next_fx, next_speed))
            change = [g[f] - face[f] for f in range(5)]
            for f in range(5):
                face[f] = g[f]
                fluxes[f] = next_fx[f]
            for n in range(6):
                prims[n] = next_prim[n]
            fluxes[5] = next_speed
            change = [a + b for a, b in zip(change, turned_change(state, prim, 1, 0, None))]
            change = [a + b for a, b in zip(change, turned_change(state, prim, 2, 1, ends))]
            for f in range(5):
                put(f, p, state[f] - (0.5 * cell_ratio) * change[f])
            return carry

        lax.fori_loop(low, high, plane, 0)

    def put_mid(f, p, value):
        mid[f, p] = value

    def put_out(f, p, value):
        out[f, p - 2] = value[0:32]

    step(wide, 1, 7, put_mid)

    @pl.when(gx == 0)
    def _():
        for f in range(5):
            mid[f, 1] = mid[f, 2]

    @pl.when(gx == last_x)
    def _():
        for f in range(5):
            mid[f, 6] = mid[f, 5]

    for f in range(5):
        for p in range(2, 6):
            edge = mid[f, p, 39:40, :]
            mid[f, p, 39:40, :] = jnp.where(place == 0, mid[f, p, 0:1, :], edge)
            edge = mid[f, p, 32:33, :]
            mid[f, p, 32:33, :] = jnp.where(place == last_y, mid[f, p, 31:32, :], edge)
    step(mid, 2, 6, put_out)


def bottom_tractions(bottoms, count_x, faces):
    shape = (count_x, 128)
    sub, lane = rows_of(shape), lanes_of(shape)
    count_gy = lax.axis_size("gy")

    def columns(q):
        parts = []
        for y in range(4):
            start = (y // count_gy * count_x * count_gy + y % count_gy) * 16 + q
            parts.append(bottoms[pl.ds(start, count_x, stride=16 * count_gy), :])
        found = []
        for x in range(4):
            total = rolled(parts[0], -32 * x, 1)
            for y in range(1, 4):
                total = jnp.where(lane // 32 == y, rolled(parts[y], 32 * (y - x), 1), total)
            found.append(total)
        return found

    cells = [[columns(f * 3 + z) for f in range(5)] for z in range(3)]
    state = [[[cells[z][f][x] for f in range(5)] for x in range(4)] for z in range(3)]
    ends_y = (lane == 0, lane == 127)

    def across_x(states, prims):
        fluxes = [flux(s, p, 0) for s, p in zip(states, prims)]
        data = [(s, f, a) for s, (f, a) in zip(states, fluxes)]
        up = lambda x: rolled(x, -1)
        wrap = ([up(v) for v in data[0][0]], [up(v) for v in data[0][1]], up(data[0][2]))
        upper = [twice_face(data[x], data[x + 1] if x < 3 else wrap) for x in range(4)]
        upper[3] = [jnp.where(sub == count_x - 1, 2.0 * f, g) for f, g in zip(data[3][1], upper[3])]
        below = [jnp.where(sub == 0, 2.0 * f, rolled(g, 1)) for f, g in zip(data[0][1], upper[3])]
        lower = [below] + upper[:3]
        return [[a - b for a, b in zip(u, l)] for u, l in zip(upper, lower)]

    def advanced(above, here, under, prim_above, prim_here, prim_under):
        changes = across_x(here, prim_here)
        out = []
        for x in range(4):
            change = [a + b for a, b in zip(changes[x], turned_change(here[x], prim_here[x], 1, 1, ends_y))]
            fz, az = flux(here[x], prim_here[x], 2)
            fa, aa = flux(above[x], prim_above[x], 2)
            lower = twice_face((above[x], fa, aa), (here[x], fz, az))
            if under is None:
                upper = [2.0 * f for f in fz]
            else:
                fu, au = flux(under[x], prim_under[x], 2)
                upper = twice_face((here[x], fz, az), (under[x], fu, au))
            out.append([s - (0.5 * cell_ratio) * (c + u - l) for s, c, u, l in zip(here[x], change, upper, lower)])
        return out

    prims = [[primitives(state[z][x]) for x in range(4)] for z in range(3)]
    middle = advanced(state[0], state[1], state[2], prims[0], prims[1], prims[2])
    deepest = advanced(state[1], state[2], None, prims[1], prims[2], None)
    prim_mid, prim_deep = [primitives(s) for s in middle], [primitives(s) for s in deepest]
    final = advanced(middle, deepest, None, prim_mid, prim_deep, None)
    ids = columns(15)
    for x in range(4):
        s, prim = final[x], primitives(final[x])
        at = pl.ds(x * count_x, count_x)
        faces[0, at, :] = face_area * s[1] * prim[2]
        faces[1, at, :] = face_area * s[2] * prim[2]
        faces[2, at, :] = face_area * (s[3] * prim[2] + prim[3])
        faces[3, at, :] = ids[x]


def surface_kernel(nodes_y, count_x, bottoms, region, xl, xh, yl, yh, material, tables, out1, out2, total, faces):
    base_x = (8 * position("gx") - 4).astype(f32)
    base_y = (16 * along_y() - 4).astype(f32)
    bottom_tractions(bottoms, count_x, faces)
    deposit(faces, nodes_y, base_x, base_y, total)
    region_now = jnp.concatenate([region[0], region[1]], axis=0).astype(f32) + 1.0
    respond(total, region_grid(region_now, xl, xh, yl, yh), material, tables, out1, out2)


def shards(density, momentum, energy, displacement, velocity_field, acceleration, material, element_region_index,
           face_dest, face_slot):
    along = ("grp", "gy")
    nodes_y = 16 * lax.axis_size(along) + 1
    count_x, rank = lax.axis_size("gx"), ("grp", "gx", "gy")
    devices = lax.axis_size(rank)
    crater = (density, momentum, energy)
    bottoms, rows = call(
        functools.partial(start_kernel, float(nodes_y)),
        crater + (face_dest.reshape(1, -1), face_slot),
        [(devices, 16, 128), (4, 5, 8, 256)],
        [],
    )
    bottoms = lax.all_to_all(bottoms, rank, 0, 0, tiled=True)
    rows = lax.all_to_all(rows, along, 0, 0, tiled=True)
    own, first, second = call(widen_kernel, crater + (rows,), [(5, 4, 40, 256), (5, 72, 256), (5, 72, 256)], [])
    first = lax.ppermute(first, "gx", [(i, i ^ 1) for i in range(count_x)])
    pairs = [(i, i + 1) for i in range(1, count_x - 1, 2)]
    second = lax.ppermute(second, "gx", pairs + [(j, i) for i, j in pairs])
    region = element_region_index
    b, f, x_low, x_high, y_low, y_high = call(
        first_kernel,
        (displacement, velocity_field, acceleration, region, material),
        [element_shape, element_shape, (31, 8, 128), (31, 8, 128), (16, 8, 128), (16, 8, 128)],
        internal_scratch + [(5, 5, 8, 512), (4, 9, 17, 128)],
        smem=(4,),
    )
    xl, xh = exchange("gx", x_low, x_high)
    y_low, y_high = call(
        functools.partial(edge_kernel, True), (y_low, y_high, xl, xh), [(18, 8, 128), (18, 8, 128)], []
    )
    yl, yh = exchange(along, y_low, y_high)
    (hydro_state,) = call(
        crater_kernel,
        (own, first, second),
        [(5, 4, 32, 256)],
        [(5, 8, 40, 256), (5, 8, 40, 256), (6, 40, 256), (5, 40, 256), (6, 40, 256)],
    )
    surf1, surf2 = call(
        functools.partial(surface_kernel, float(nodes_y), count_x),
        (bottoms.reshape(devices * 16, 128), region, xl, xh, yl, yh, material, jnp.asarray(surface_tables())),
        [(24, 256), (24, 256)],
        [(360, 128), (4, 4 * count_x, 128)],
        smem=(6,),
    )
    a1, f2, x_low, x_high, y_low, y_high, scales = call(
        second_kernel,
        (b, f, xl, xh, yl, yh, region, material),
        [element_shape, element_shape, (30, 8, 128), (30, 8, 128), (15, 8, 128), (15, 8, 128), (3, 3, 2, 8, 128)],
        internal_scratch,
        smem=(7,),
    )
    xl2, xh2 = exchange("gx", x_low, x_high)
    y_low, y_high = call(
        functools.partial(edge_kernel, False), (y_low, y_high, xl2, xh2), [(15, 8, 128), (15, 8, 128)], []
    )
    yl2, yh2 = exchange(along, y_low, y_high)
    u_out, v_out, a_out = call(
        last_kernel,
        (a1, f2, xl2, xh2, yl2, yh2, scales, surf1, surf2, displacement, velocity_field, acceleration),
        [displacement.shape] * 3,
        [(5, 5, 8, 512), (4, 9, 17, 128), (4, 9, 17, 128), element_shape],
    )
    return hydro_state, u_out, v_out, a_out


def solution(mesh):
    field = P(None, "gx", ("grp", "gy"), None)
    cells = P("gx", ("grp", "gy"), None)
    rank = ("grp", "gx", "gy")
    return jax.shard_map(
        shards,
        mesh=mesh,
        in_specs=(cells, field, cells, field, field, field, P(), cells, P(rank, None, None), P(rank, None)),
        out_specs=(field, field, field, field),
        check_vma=False,
    )
```

```python
import functools

import jax
import jax.numpy as jnp
import numpy as np
from jax import lax
from jax.experimental import pallas as pl
from jax.experimental.pallas import tpu as pltpu
from jax.sharding import PartitionSpec as P

gamma_gas = 1.4
cell_ratio = 0.05
half_size = 2.0
time_step = 0.1
face_area = 2.0


def gll_tables():
    root = np.sqrt(3.0 / 7.0)
    points = np.array([-1.0, -root, 0.0, root, 1.0])
    weights = np.array([0.1, 49.0 / 90.0, 32.0 / 45.0, 49.0 / 90.0, 0.1])
    products = [np.prod([points[r] - points[c] for c in range(5) if c != r]) for r in range(5)]
    derivative = np.zeros((5, 5))
    for r in range(5):
        for c in range(5):
            if r != c:
                derivative[r, c] = products[r] / products[c] / (points[r] - points[c])
        derivative[r, r] = sum(1.0 / (points[r] - points[c]) for c in range(5) if c != r)
    derivative[2, 2] = 0.0
    return derivative, weights


deriv, quad = gll_tables()
deriv_t = deriv.T
kind = [0, 1, 2, 1, 0]
f32 = jnp.float32


def line(matrix, v):
    even, odd = (matrix + matrix[:, ::-1]) / 2, (matrix - matrix[:, ::-1]) / 2
    e0, e1, o0, o1 = v[0] + v[4], v[1] + v[3], v[0] - v[4], v[1] - v[3]
    top = [float(even[i, 0]) * e0 + float(even[i, 1]) * e1 + float(matrix[i, 2]) * v[2] for i in range(2)]
    low = [float(odd[i, 0]) * o0 + float(odd[i, 1]) * o1 for i in range(2)]
    centre = float(matrix[2, 0]) * o0 + float(matrix[2, 1]) * o1
    return [top[0] + low[0], top[1] + low[1], centre, low[1] - top[1], low[0] - top[0]]


def rows_of(shape=(8, 128)):
    return lax.broadcasted_iota(jnp.int32, shape, 0)


def lanes_of(shape=(8, 128)):
    return lax.broadcasted_iota(jnp.int32, shape, 1)


def deeper(x):
    return jnp.where(lanes_of() == 127, 0.0, pltpu.roll(x, 127, 1))


def shallower(x):
    return jnp.where(lanes_of() == 0, 0.0, pltpu.roll(x, 1, 1))


def split_three(x):
    high = x.astype(jnp.bfloat16)
    rest = x - high.astype(f32)
    middle = rest.astype(jnp.bfloat16)
    return high, middle, (rest - middle.astype(f32)).astype(jnp.bfloat16)


def one_hot_dot(x, table, dims=(((1,), (0,)), ((), ()))):
    return sum(lax.dot_general(part, table, dims, preferred_element_type=f32) for part in split_three(x))


def depth_table(back=False):
    a = lax.broadcasted_iota(jnp.int32, (512, 512), 1 if back else 0)
    b = lax.broadcasted_iota(jnp.int32, (512, 512), 0 if back else 1)
    return jnp.where(a == 4 * (b & 127) + (b >> 7), 1.0, 0.0).astype(jnp.bfloat16)


def to_elements(nodes, table, tall, put):
    for i in range(5):
        for j in range(5):
            for ex in range(2):
                for t in range(4):
                    tall[i, j, 4 * ex : 4 * ex + 4, 128 * t : 128 * t + 128] = nodes[t, 4 * ex + i, pl.ds(j, 4, stride=4), :]
    out = one_hot_dot(tall[...].reshape(200, 512), table)
    for k in range(4):
        put(k, out[:, 128 * k : 128 * k + 128].reshape(5, 5, 8, 128))


def to_nodes(get, table, tall, nodes):
    wide = jnp.concatenate([get(k).reshape(200, 128) for k in range(4)], axis=1)
    tall[...] = one_hot_dot(wide, table).reshape(5, 5, 8, 512)
    for i in range(5):
        for j in range(5):
            for ex in range(2):
                if i == 4 and ex == 0:
                    continue
                for t in range(4):
                    lanes = slice(128 * t, 128 * t + 128)
                    if j < 4:
                        nodes[t, 4 * ex + i, pl.ds(j, 4, stride=4), :] = tall[i, j, 4 * ex : 4 * ex + 4, lanes]
                    else:
                        nodes[t, 4 * ex + i, 16:17, :] = tall[i, j, 4 * ex + 3 : 4 * ex + 4, lanes]


def lookup(material, row, region):
    total = jnp.zeros_like(region)
    for m in range(material.shape[1]):
        total = jnp.where(region == float(m + 1), material[row, m], total)
    return total


def internal(u, out, lame, shear, gx, gz, cross, planes, side):
    def depth_lines(i, carry):
        for j in range(5):
            for c in range(3):
                v = [u[c, i, j, k] for k in range(4)]
                v.append(deeper(v[0]))
                u[c, i, j, 4] = v[4]
                for k, g in enumerate(line(deriv, v)):
                    gz[c, i, j, k] = g
        return carry

    lax.fori_loop(0, 5, depth_lines, 0)

    def plane(k, carry):
        weight = jnp.where((k == 0) | (k == 4), float(quad[0]), jnp.where(k == 2, float(quad[2]), float(quad[1])))
        lame_k, shear_k = lame * (2.0 * weight), shear * (2.0 * weight)
        pairs = {}
        for a in range(3):
            for b in range(a, 3):
                w = float(quad[a] * quad[b])
                pairs[a, b] = pairs[b, a] = (lame_k * w, shear_k * w, shear_k * (2.0 * w))
        for c in range(3):
            for j in range(5):
                for i, g in enumerate(line(deriv, [u[c, i, j, k] for i in range(5)])):
                    gx[c, i, j] = g
        for i in range(5):
            gy = [line(deriv, [u[c, i, j, k] for j in range(5)]) for c in range(3)]
            ys = [[], [], []]
            for j in range(5):
                lw, mw, mw2 = pairs[kind[i], kind[j]]
                g0, g1, g2 = [[gx[c, i, j], gy[c][j], gz[c, i, j, k]] for c in range(3)]
                dilated = lw * (g0[0] + g1[1] + g2[2])
                s01 = mw * (g0[1] + g1[0])
                s02 = mw * (g0[2] + g2[0])
                s12 = mw * (g1[2] + g2[1])
                side[0, i, j] = dilated + mw2 * g0[0]
                side[1, i, j] = s01
                cross[0, i, j, k] = s02
                cross[1, i, j, k] = s12
                cross[2, i, j, k] = dilated + mw2 * g2[2]
                ys[0].append(s01)
                ys[1].append(dilated + mw2 * g1[1])
                ys[2].append(s12)
            for c in range(3):
                for j, value in enumerate(line(deriv_t, ys[c])):
                    planes[c, i, j, k] = value
        for j in range(5):
            for c in range(3):
                v = [side[c, i, j] if c < 2 else cross[0, i, j, k] for i in range(5)]
                for i, value in enumerate(line(deriv_t, v)):
                    planes[c, i, j, k] += value
        return carry

    lax.fori_loop(0, 5, plane, 0)

    def depth_sums(i, carry):
        for j in range(5):
            for c in range(3):
                v = line(deriv_t, [cross[c, i, j, k] for k in range(5)])
                v = [v[k] + planes[c, i, j, k] for k in range(5)]
                out[c, i, j, 0] = v[0] + shallower(v[4])
                for k in range(1, 4):
                    out[c, i, j, k] = v[k]
        return carry

    lax.fori_loop(0, 5, depth_sums, 0)
    sub = rows_of()

    def fold(k, carry):
        for c in range(3):
            for i in range(5):
                low, high = out[c, i, 0, k], out[c, i, 4, k]
                out[c, i, 0, k] = low + jnp.where(sub % 4 == 0, 0.0, pltpu.roll(high, 1, 0))
                out[c, i, 4, k] = high + jnp.where(sub % 4 == 3, 0.0, pltpu.roll(low, 7, 0))
            for j in range(5):
                low, high = out[c, 0, j, k], out[c, 4, j, k]
                out[c, 0, j, k] = low + jnp.where(sub < 4, 0.0, pltpu.roll(high, 4, 0))
                out[c, 4, j, k] = high + jnp.where(sub < 4, pltpu.roll(low, 4, 0), 0.0)
        return carry

    lax.fori_loop(0, 4, fold, 0)


def rolled(x, amount, axis=0):
    amount = amount % x.shape[axis]
    return pltpu.roll(x, amount, axis) if amount else x


def parity_x():
    return position("gx") % 2


def parity_y():
    return along_y() % 2


def sort_out(odd, low, high):
    return jnp.where(odd == 1, low, high), jnp.where(odd == 1, high, low)


def pack_x(force, first, second):
    sub, odd = rows_of(), parity_x()
    for c in range(3):
        for j in range(5):
            for half in range(2):
                at = (c * 5 + j) * 2 + half
                a, b = force[c, 0, j, 2 * half], force[c, 0, j, 2 * half + 1]
                low = jnp.where(sub < 4, a, rolled(b, 4))
                a, b = force[c, 4, j, 2 * half], force[c, 4, j, 2 * half + 1]
                high = jnp.where(sub < 4, rolled(a, 4), b)
                first[at], second[at] = sort_out(odd, low, high)


def pack_y(force, low, high):
    sub = rows_of()
    for c in range(3):
        for i in range(5):
            a, b = force[c, i, 0, 0], rolled(force[c, i, 4, 0], -3)
            for k in range(1, 4):
                a = jnp.where(sub % 4 == k, rolled(force[c, i, 0, k], k), a)
                b = jnp.where(sub % 4 == k, rolled(force[c, i, 4, k], k - 3), b)
            low[c * 5 + i] = a
            high[c * 5 + i] = b


def add_x(force, first, second):
    sub, odd = rows_of(), parity_x()
    for c in range(3):
        for j in range(5):
            for half in range(2):
                at = (c * 5 + j) * 2 + half
                r, s = sort_out(odd, first[at], second[at])
                force[c, 0, j, 2 * half] += jnp.where(sub < 4, r, 0.0)
                force[c, 0, j, 2 * half + 1] += jnp.where(sub < 4, rolled(r, 4), 0.0)
                force[c, 4, j, 2 * half] += jnp.where(sub < 4, 0.0, rolled(s, 4))
                force[c, 4, j, 2 * half + 1] += jnp.where(sub < 4, 0.0, s)


def add_y(force, first, second):
    sub, odd = rows_of(), parity_y()
    for c in range(3):
        for i in range(5):
            r, s = sort_out(odd, first[c * 5 + i], second[c * 5 + i])
            for k in range(4):
                force[c, i, 0, k] += jnp.where(sub % 4 == 0, rolled(r, -k), 0.0)
                force[c, i, 4, k] += jnp.where(sub % 4 == 3, rolled(s, 3 - k), 0.0)


def edge_rows(low, high, came1, came2, first, second):
    sub, odd, odd_y = rows_of(), parity_x(), parity_y()
    for c in range(3):
        came = [[sort_out(odd, came1[at], came2[at]) for at in range((c * 5 + j) * 2, (c * 5 + j) * 2 + 2)] for j in (0, 4)]
        for i in range(5):
            rows = [low[c * 5 + i], high[c * 5 + i]]
            if i in (0, 4):
                start, side = i, i // 4
                for end, row in ((0, 0), (1, 3)):
                    for k in range(4):
                        r = rolled(came[end][k // 2][side], start + k - (4 * (k % 2) + row))
                        rows[end] = rows[end] + jnp.where(sub == start + k, r, 0.0)
            first[c * 5 + i], second[c * 5 + i] = sort_out(odd_y, *rows)


def first_edge_kernel(low, high, came1, came2, density, momentum, energy, crater1, crater2, after, first, second):
    edge_rows(low, high, came1, came2, first, second)
    odd, odd_y = parity_x(), parity_y()
    regions = sort_out(odd, came1[30], came2[30])
    for n, value in enumerate((low[15], regions[0], regions[1])):
        first[15 + n] = value
        second[15 + n] = value
    for f in range(5):
        field = field_of(f, density, momentum, energy)
        for t in range(2):
            lanes = slice(128 * t, 128 * t + 128)
            ends = []
            for near, far in ((0, 1), (31, 30)):
                own = [field[x, r : r + 1, lanes] for r in (near, far) for x in range(4)]
                sides = sort_out(odd, crater1[f, near : near + 1, lanes], crater2[f, near : near + 1, lanes])
                ends.append((jnp.concatenate(own, axis=0), jnp.concatenate(list(sides) * 4, axis=0)))
            for h in range(2):
                at = 18 + f * 4 + t * 2 + h
                first[at], second[at] = sort_out(odd_y, ends[0][h], ends[1][h])


def second_edge_kernel(low, high, came1, came2, after, first, second):
    edge_rows(low, high, came1, came2, first, second)


def region_grid(own, x1, x2, y1, y2):
    xl, xh = sort_out(parity_x(), x1[30], x2[30])
    yl, yh = [list(v) for v in zip(*[sort_out(parity_y(), y1[n], y2[n]) for n in (15, 16, 17)])]
    return [[yl[1], xl, yh[1]], [yl[0], own, yh[0]], [yl[2], xh, yh[2]]]


def shared_density(grid):
    sub = rows_of()
    across = []
    for y in range(3):
        low, mid, high = grid[0][y], grid[1][y], grid[2][y]
        turned = rolled(mid, 4)
        across.append([jnp.where(sub < 4, rolled(low, 4), turned), mid, jnp.where(sub < 4, turned, rolled(high, 4))])
    found = [[None] * 3 for _ in range(3)]
    for x in range(3):
        low, mid, high = across[0][x], across[1][x], across[2][x]
        found[x][0] = jnp.where(sub % 4 == 0, rolled(low, -3), rolled(mid, 1))
        found[x][1] = mid
        found[x][2] = jnp.where(sub % 4 == 3, rolled(high, 3), rolled(mid, -1))
    sums = []
    for x in ((1,), (0, 1), (1, 2)):
        row = []
        for y in ((1,), (0, 1), (1, 2)):
            total = sum(found[a][b] for a in x for b in y)
            row.append((total + shallower(total), total))
        sums.append(row)
    return sums


def mass_scales(sums):
    return [[[1.0 / s for s in pair] for pair in row] for row in sums]


def edge_kind(i):
    return 1 if i == 0 else 2 if i == 4 else 0


def accel_scale(i, j, k):
    return float(-1.0 / (half_size**3 * quad[i] * quad[j] * quad[k]))


def first_kernel(u, v, a, region, material, b_out, f_out, x1, x2, y_low, y_high,
                 elem, gx, gz, cross, planes, side, tall, nodes):
    table = depth_table()
    region_now = jnp.concatenate([region[0], region[1]], axis=0).astype(f32) + 1.0

    def one(c, carry):
        for t in range(4):
            lanes = slice(128 * t, 128 * t + 128)
            nodes[t] = u[c, :, :, lanes] + time_step * v[c, :, :, lanes] + 0.5 * time_step**2 * a[c, :, :, lanes]

        def put_u(k, value):
            elem[c, :, :, k] = value

        to_elements(nodes, table, tall, put_u)
        for t in range(4):
            lanes = slice(128 * t, 128 * t + 128)
            nodes[t] = u[c, :, :, lanes] + 2.0 * time_step * v[c, :, :, lanes] + time_step**2 * a[c, :, :, lanes]

        def put_b(k, value):
            b_out[c, :, :, k] = value

        to_elements(nodes, table, tall, put_b)
        return carry

    lax.fori_loop(0, 3, one, 0)
    internal(elem, f_out, lookup(material, 1, region_now), lookup(material, 2, region_now), gx, gz, cross, planes, side)
    pack_x(f_out, x1, x2)
    pack_y(f_out, y_low, y_high)
    x1[30] = region_now
    x2[30] = region_now
    y_low[15] = region_now


def second_kernel(b, f, came_x1, came_x2, came_y1, came_y2, region, material, a_out, f_out, x1, x2, y_low, y_high, scales,
                  elem, gx, gz, cross, planes, side):
    region_now = jnp.concatenate([region[0], region[1]], axis=0).astype(f32) + 1.0
    a_out[...] = f[...]
    add_x(a_out, came_x1, came_x2)
    add_y(a_out, came_y1, came_y2)
    grid = region_grid(region_now, came_x1, came_x2, came_y1, came_y2)
    inverse = mass_scales(shared_density([[lookup(material, 0, r) for r in row] for row in grid]))
    for x in range(3):
        for y in range(3):
            for z in range(2):
                scales[x, y, z] = inverse[x][y][z]
    for i in range(5):
        for j in range(5):
            for k in range(4):
                scale = scales[edge_kind(i), edge_kind(j), min(k, 1)] * accel_scale(i, j, k)
                for c in range(3):
                    value = a_out[c, i, j, k] * scale
                    a_out[c, i, j, k] = value
                    elem[c, i, j, k] = b[c, i, j, k] + time_step**2 * value
    internal(elem, f_out, lookup(material, 1, region_now), lookup(material, 2, region_now), gx, gz, cross, planes, side)
    pack_x(f_out, x1, x2)
    pack_y(f_out, y_low, y_high)


def add_surface(source, x, c, count):
    at = 8 * (c * 9 + x)
    tile, shift = at // 128, (128 - at % 128) % 128
    moved = rolled(source[0:17, 128 * tile : 128 * tile + 128], shift, 1)
    return jnp.where(lanes_of((17, 128)) < count, moved, 0.0)


def place_kernel(a1, surf1, u, v, a, after, u_out, first, tall, nodes):
    table = depth_table(back=True)
    for c in range(3):
        to_nodes(lambda k: a1[c, :, :, k], table, tall, nodes)
        for x in range(9):
            nodes[0, x] += add_surface(surf1, x, c, 1)
        for t in range(4):
            at = (c, slice(None), slice(None), slice(128 * t, 128 * t + 128))
            first[c, t] = nodes[t]
            u_out[at] = u[at] + 2.0 * time_step * v[at] + time_step**2 * (a[at] + nodes[t])


def last_kernel(first, f, x1, x2, y1, y2, scales, surf1, surf2, v, a, v_out, a_out, tall, nodes, force):
    table = depth_table(back=True)
    force[...] = f[...]
    add_x(force, x1, x2)
    add_y(force, y1, y2)
    for i in range(5):
        for j in range(5):
            for k in range(4):
                scale = scales[edge_kind(i), edge_kind(j), min(k, 1)] * accel_scale(i, j, k)
                for c in range(3):
                    force[c, i, j, k] = force[c, i, j, k] * scale
    for c in range(3):
        to_nodes(lambda k: force[c, :, :, k], table, tall, nodes)
        for x in range(9):
            nodes[0, x] += add_surface(surf1, x, c, 1) + add_surface(surf2, x, c, 5)
        for t in range(4):
            at = (c, slice(None), slice(None), slice(128 * t, 128 * t + 128))
            a_out[at] = nodes[t]
            v_out[at] = v[at] + 0.5 * time_step * (a[at] + 2.0 * first[c, t] + nodes[t])


def whole():
    return pl.BlockSpec(memory_space=pltpu.VMEM)


def scalars():
    return pl.BlockSpec(memory_space=pltpu.SMEM)


def call(kernel, ins, outs, scratch, smem=(), away=(), mib=20):
    def spec(n):
        return scalars() if n in smem else pl.BlockSpec(memory_space=pl.ANY) if n in away else whole()

    return pl.pallas_call(
        kernel,
        out_shape=[jax.ShapeDtypeStruct(s, f32) for s in outs],
        in_specs=[spec(n) for n in range(len(ins))],
        out_specs=[whole() for _ in outs],
        scratch_shapes=[pltpu.VMEM(s, f32) for s in scratch],
        compiler_params=pltpu.CompilerParams(vmem_limit_bytes=mib * 1024 * 1024),
    )(*ins)


element_shape = (3, 5, 5, 4, 8, 128)
lines_shape = (3, 5, 5, 5, 8, 128)
internal_scratch = [lines_shape, (3, 5, 5, 8, 128), lines_shape, lines_shape, lines_shape, (2, 5, 5, 8, 128)]


def exchange(axis, first, second):
    count = lax.axis_size(axis)
    pairs = [(i, i + 1) for i in range(1, count - 1, 2)]
    first = lax.ppermute(first, axis, [(i, i ^ 1) for i in range(count)])
    return first, lax.ppermute(second, axis, pairs + [(j, i) for i, j in pairs])


def surface_tables():
    lane = np.arange(128)
    j, ey = lane // 8, lane % 8
    used = (j < 5) & (ey < 6)
    place = np.where(used, ey + 1, -9)
    source = lane[:, None]
    centre = source == place
    meet = centre | ((j == 0) & (source == place - 1)) | ((j == 4) & (source == place + 1))
    along = np.zeros((128, 128))
    for a in range(40):
        for b in range(40):
            if a % 8 == b % 8 and a % 8 < 6:
                along[a, b] = deriv[b // 8, a // 8]
    node = np.where(used, 4 * (ey - 1) + j, -9)
    fold = (lane[:, None] == node) & (lane[:, None] < 17)
    keep = fold & ((j < 4) & (ey < 5) | (j == 4) & (ey == 4))
    return np.stack([centre, meet, along, along.T, fold, keep]).astype(np.float32)


def full_dot(x, y, back=False):
    dims = (((1,), (1 if back else 0,)), ((), ()))
    return lax.dot_general(x, y, dims, precision=lax.Precision.HIGHEST, preferred_element_type=f32)


def deposit(faces, nodes_y, base_x, base_y, total):
    rows = faces.shape[1]
    sub = rows_of((8, 512)).astype(f32)
    total[...] = jnp.zeros_like(total)

    def one(step, carry):
        def wide(q):
            block = faces[q, pl.ds(4 * step, 4), :]
            return jnp.concatenate([block[n : n + 1] for n in range(4)], axis=1)

        ids = wide(3)
        node_x = jnp.floor((ids + 0.5) * (1.0 / nodes_y))
        rel_y = jnp.broadcast_to(ids - node_x * nodes_y - base_y, (8, 512))
        rel_x = jnp.broadcast_to(node_x - base_x, (8, 512))
        left = []
        hits = [(rel_x - i == 4.0 * sub) & (sub < 4.0) for i in range(5)]
        parts = [split_three(wide(c)) for c in range(3)]
        for part in range(3):
            for c in range(3):
                value = jnp.broadcast_to(parts[c][part].astype(f32), (8, 512))
                left += [jnp.where(hit, value, 0.0) for hit in hits]
        right = [jnp.where((rel_y - j == 4.0 * sub) & (sub < 6.0), 1.0, 0.0) for j in range(5)]
        right.append(jnp.zeros((88, 512), f32))
        left, right = jnp.concatenate(left, axis=0), jnp.concatenate(right, axis=0)
        total[...] += lax.dot_general(
            left.astype(jnp.bfloat16), right.astype(jnp.bfloat16), (((1,), (1,)), ((), ())), preferred_element_type=f32
        )
        return carry

    lax.fori_loop(0, rows // 4, one, 0)


def top_grid(rows, z):
    sub, lane = rows_of(), lanes_of()
    out = jnp.zeros((8, 128), f32)
    for x in range(3):
        for y in range(3):
            row = jnp.broadcast_to(rows[x][y], (8, 128))
            for ex in range(2):
                here = (sub == 2 * x + ex) & (lane >= 4 * y - 2) & (lane < 4 * y + 2) & (lane < 8)
                out = jnp.where(here, rolled(row, 4 * y - 2 - 8 * z - 4 * ex, 1), out)
    return out


def region_rows(bottoms, count_x):
    gx, place, count_gy = position("gx"), along_y(), lax.axis_size("gy")
    last_y = lax.axis_size("grp") * count_gy - 1
    found = []
    for x in range(3):
        found.append([])
        for y in range(3):
            px, py = gx + x - 1, place + y - 1
            inside = (px >= 0) & (px < count_x) & (py >= 0) & (py <= last_y)
            cx, cy = jnp.clip(px, 0, count_x - 1), jnp.clip(py, 0, last_y)
            rank = (cy // count_gy) * (count_x * count_gy) + cx * count_gy + cy % count_gy
            row = bottoms[pl.ds(pl.multiple_of(rank * 24 + 16, 8), 1), :]
            found[x].append(jnp.where(inside, row, 0.0))
    return found


def respond(total, grid, material, tables, out1, out2):
    sub, lane = rows_of(), lanes_of()
    top, below = top_grid(grid, 0), top_grid(grid, 1)
    centre, meet, along, along_t, fold, keep = [tables[n] for n in range(6)]
    sums0 = full_dot(lookup(material, 0, top), meet)
    sums1 = full_dot(lookup(material, 0, below), meet)
    lame = rolled(full_dot(lookup(material, 1, top), centre), -1)
    shear = rolled(full_dot(lookup(material, 2, top), centre), -1)
    weight_y = jnp.ones((8, 128), f32)
    for j in range(5):
        weight_y = jnp.where(lane // 8 == j, float(quad[j]), weight_y)

    def inverse(sums):
        mid = rolled(sums, -1)
        found = {0: mid + sums, 1: mid, 4: mid + rolled(sums, -2)}
        found = {i: jnp.where(s > 0.0, 1.0 / (s * weight_y), 0.0) for i, s in found.items()}
        found[2] = found[3] = found[1]
        return found

    light, heavy = inverse(sums0), inverse(sums0 + sums1)
    first = [[None] * 5 for _ in range(3)]
    moved = [[None] * 5 for _ in range(3)]
    for c in range(3):
        for i in range(5):
            at = (c * 5 + i) * 8
            force = total[at : at + 8] + total[at + 120 : at + 128] + total[at + 240 : at + 248]
            first[c][i] = force * light[i] * -accel_scale(i, 2, 0) * float(quad[2])
            moved[c][i] = first[c][i] * time_step**2
    gx = [line(deriv, moved[c]) for c in range(3)]
    gy = full_dot(jnp.concatenate([moved[c][i] for c in range(3) for i in range(5)], axis=0), along)
    gy = [[gy[(c * 5 + i) * 8 : (c * 5 + i) * 8 + 8] for i in range(5)] for c in range(3)]
    lame_w, shear_w = lame * weight_y * 2.0, shear * weight_y * 2.0
    d00 = float(deriv[0, 0])
    sx = [[], [], []]
    sy = [[], [], []]
    sz = [[], [], []]
    qs = [[], [], []]
    pressed = []
    for i in range(5):
        lw, mw = lame_w * float(quad[i]), shear_w * float(quad[i])
        d = [moved[c][i] for c in range(3)]
        gz = [d00 * x for x in d]
        dilated = lw * (gx[0][i] + gy[1][i] + gz[2])
        s01 = mw * (gx[1][i] + gy[0][i])
        s02 = mw * (gx[2][i] + gz[0])
        s12 = mw * (gy[2][i] + gz[1])
        for c, value in enumerate((dilated + 2.0 * mw * gx[0][i], s01, s02)):
            sx[c].append(value)
        for c, value in enumerate((s01, dilated + 2.0 * mw * gy[1][i], s12)):
            sy[c].append(value)
        for c, value in enumerate((s02, s12, dilated + 2.0 * mw * gz[2])):
            sz[c].append(value)
        for c, value in enumerate((mw * d[0], mw * d[1], (lw + 2.0 * mw) * d[2])):
            qs[c].append(value)
        pressed.append(lw * d[2])
    ydiv = full_dot(jnp.concatenate(sy[0] + sy[1] + sy[2] + pressed + qs[1], axis=0), along_t)
    ydiv = [[ydiv[(n * 5 + i) * 8 : (n * 5 + i) * 8 + 8] for i in range(5)] for n in range(5)]
    xdiv = [line(deriv_t, v) for v in sx + [pressed, qs[0]]]
    base = [xdiv[3], ydiv[3], [p + q for p, q in zip(xdiv[4], ydiv[4])]]
    second = {}
    for c in range(3):
        for i in range(5):
            for l in range(5):
                stiff = float(sum(deriv[k, l] * quad[k] * deriv[k, 0] for k in range(1, 5)))
                value = float(deriv[0, l] * quad[0]) * sz[c][i] + stiff * qs[c][i]
                if l:
                    value = value + float(deriv[l, 0] * quad[l]) * base[c][i]
                else:
                    value = value + float(quad[0]) * (xdiv[c][i] + ydiv[c][i])
                scale = (heavy if l == 4 else light)[i]
                second[c, i, l] = value * scale * (accel_scale(i, 2, l) * float(quad[2]))
    rows1, rows2 = [], []
    for c in range(3):
        for x in range(9):
            own = 1 if x < 4 else 2
            rows1.append(jnp.where(sub == 0, rolled(first[c][x - 4 * (own - 1)], -own), 0.0))
            block = jnp.zeros((8, 128), f32)
            for l in range(5):
                for ex in range(4):
                    i = x - 4 * (ex - 1)
                    if 0 <= i <= 4:
                        block = block + jnp.where(sub == l, rolled(second[c, i, l], l - ex), 0.0)
            rows2.append(block)
    blank = [jnp.zeros((40, 128), f32)]
    out1[...] = full_dot(keep[0:24], jnp.concatenate(rows1 + blank, axis=0), back=True)
    out2[...] = full_dot(fold[0:24], jnp.concatenate(rows2 + blank, axis=0), back=True)


def position(axis):
    return lax.axis_index(axis)


def along_y():
    return lax.axis_index("grp") * lax.axis_size("gy") + lax.axis_index("gy")


def primitives(state):
    inverse = 1.0 / state[0]
    v = [state[1 + c] * inverse for c in range(3)]
    p = (gamma_gas - 1.0) * (state[4] - 0.5 * (state[1] * v[0] + state[2] * v[1] + state[3] * v[2]))
    return v + [p, jnp.sqrt(gamma_gas * p * inverse), state[4] + p]


def flux(state, prim, d):
    out = [state[1 + d]] + [state[1 + c] * prim[d] for c in range(3)] + [prim[5] * prim[d]]
    out[1 + d] = out[1 + d] + prim[3]
    return out, jnp.abs(prim[d]) + prim[4]


def twice_face(low, high):
    fastest = jnp.maximum(low[2], high[2])
    return [fl + fh - fastest * (uh - ul) for ul, uh, fl, fh in zip(low[0], high[0], low[1], high[1])]


def turned_change(state, prim, d, axis, ends):
    size = state[0].shape[axis]
    fluxes, speed = flux(state, prim, d)
    up = lambda x: pltpu.roll(x, size - 1, axis)
    high = ([up(x) for x in state], [up(x) for x in fluxes], up(speed))
    upper = twice_face((state, fluxes, speed), high)
    if ends is None:
        return [g - pltpu.roll(g, 1, axis) for g in upper]
    upper = [jnp.where(ends[1], 2.0 * f, g) for f, g in zip(fluxes, upper)]
    return [g - jnp.where(ends[0], 2.0 * f, pltpu.roll(g, 1, axis)) for f, g in zip(fluxes, upper)]


def field_of(f, density, momentum, energy):
    return density if f == 0 else energy if f == 4 else momentum.at[f - 1]


def start_kernel(nodes_y, density, momentum, energy, dest, slot, region, bottoms, first, second):
    sub, lane = rows_of(), lanes_of()
    pick = jnp.where(lane == 125 + sub, 1.0, 0.0)
    pieces = []
    odd = parity_x()
    for f in range(5):
        field = field_of(f, density, momentum, energy)
        columns = jnp.concatenate([field[x, :, 128:256] for x in range(4)], axis=0)
        pieces.append(full_dot(pick, columns, back=True)[0:3])
        for out, down in ((first, odd), (second, 1 - odd)):
            out[f, 0:32, :] = field[3 - 3 * down]
            out[f, 32:64, :] = field[2 - down]
    count_gy, count_x = lax.axis_size("gy"), lax.axis_size("gx")
    target, node = dest[...].astype(f32), slot[...].astype(f32)
    grp = jnp.floor((target + 0.5) * (1.0 / (count_gy * count_x)))
    rest = target - grp * (count_gy * count_x)
    gx = jnp.floor((rest + 0.5) * (1.0 / count_gy))
    gy = rest - gx * count_gy
    i = jnp.floor((node + 0.5) * (1.0 / 17.0))
    j = node - 17.0 * i
    pieces.append((8.0 * gx + i) * nodes_y + 16.0 * (grp * count_gy + gy) + j)
    region_now = jnp.concatenate([region[0], region[1]], axis=0).astype(f32) + 1.0
    found = jnp.zeros((8, 128), f32)
    for z in range(2):
        found = jnp.where(lane == 8 * z + sub, jnp.broadcast_to(region_now[:, z : z + 1], (8, 128)), found)
    pieces.append(jnp.broadcast_to(jnp.sum(found, axis=0, keepdims=True), (8, 128)))
    block = jnp.concatenate(pieces, axis=0)
    for n in range(bottoms.shape[0]):
        bottoms[n] = block


def crater_kernel(density, momentum, energy, came1, came2, rows1, rows2, after, out, wide, mid, prims, face, fluxes):
    place, last_y = along_y(), lax.axis_size("grp") * lax.axis_size("gy") - 1
    gx, last_x = position("gx"), lax.axis_size("gx") - 1
    odd, odd_y = parity_x(), parity_y()
    for f in range(5):
        field = field_of(f, density, momentum, energy)
        low, high = sort_out(odd, came1[f], came2[f])
        for p, value in ((0, low[32:64]), (1, low[0:32]), (6, high[0:32]), (7, high[32:64])):
            wide[f, p, 0:32, :] = value
            wide[f, p, 32:40, :] = value[0:8]
        for x in range(4):
            wide[f, 2 + x, 0:32, :] = field[x]
            wide[f, 2 + x, 32:40, :] = field[x, 24:32, :]
        for t in range(2):
            lanes = slice(128 * t, 128 * t + 128)
            at = 18 + f * 4 + t * 2
            below, above = sort_out(odd_y, rows1[at], rows2[at])
            sides_below, sides_above = sort_out(odd_y, rows1[at + 1], rows2[at + 1])

            def put(p, row, edge, value):
                clamped = jnp.where(edge == 0, place == 0, place == last_y)
                at_edge = wide[f, p, 31 * edge : 31 * edge + 1, lanes]
                wide[f, p, row : row + 1, lanes] = jnp.where(clamped, at_edge, value)

            for x in range(4):
                put(2 + x, 39, 0, below[x : x + 1])
                put(2 + x, 38, 0, below[4 + x : 5 + x])
                put(2 + x, 32, 1, above[x : x + 1])
                put(2 + x, 33, 1, above[4 + x : 5 + x])
            for p, n in ((1, 0), (6, 1)):
                put(p, 39, 0, sides_below[n : n + 1])
                put(p, 32, 1, sides_above[n : n + 1])

    @pl.when(gx == 0)
    def _():
        for f in range(5):
            wide[f, 0] = wide[f, 2]
            wide[f, 1] = wide[f, 2]

    @pl.when(gx == last_x)
    def _():
        for f in range(5):
            wide[f, 6] = wide[f, 5]
            wide[f, 7] = wide[f, 5]

    lane = lanes_of((40, 256))
    ends = (lane == 0, lane == 255)

    def step(source, low, high, put):
        def along_x(p):
            state = [source[f, p] for f in range(5)]
            prim = primitives(state)
            return state, prim, flux(state, prim, 0)

        state, prim, (fx, speed) = along_x(low - 1)
        next_state, next_prim, (next_fx, next_speed) = along_x(low)
        g = twice_face((state, fx, speed), (next_state, next_fx, next_speed))
        for f in range(5):
            face[f] = g[f]
            fluxes[f] = next_fx[f]
        for n in range(6):
            prims[n] = next_prim[n]
        fluxes[5] = next_speed

        def plane(p, carry):
            state = [source[f, p] for f in range(5)]
            prim = [prims[n] for n in range(6)]
            next_state, next_prim, (next_fx, next_speed) = along_x(p + 1)
            g = twice_face((state, [fluxes[f] for f in range(5)], fluxes[5]), (next_state, next_fx, next_speed))
            change = [g[f] - face[f] for f in range(5)]
            for f in range(5):
                face[f] = g[f]
                fluxes[f] = next_fx[f]
            for n in range(6):
                prims[n] = next_prim[n]
            fluxes[5] = next_speed
            change = [a + b for a, b in zip(change, turned_change(state, prim, 1, 0, None))]
            change = [a + b for a, b in zip(change, turned_change(state, prim, 2, 1, ends))]
            for f in range(5):
                put(f, p, state[f] - (0.5 * cell_ratio) * change[f])
            return carry

        lax.fori_loop(low, high, plane, 0)

    def put_mid(f, p, value):
        mid[f, p] = value

    def put_out(f, p, value):
        out[f, p - 2] = value[0:32]

    step(wide, 1, 7, put_mid)

    @pl.when(gx == 0)
    def _():
        for f in range(5):
            mid[f, 1] = mid[f, 2]

    @pl.when(gx == last_x)
    def _():
        for f in range(5):
            mid[f, 6] = mid[f, 5]

    for f in range(5):
        for p in range(2, 6):
            edge = mid[f, p, 39:40, :]
            mid[f, p, 39:40, :] = jnp.where(place == 0, mid[f, p, 0:1, :], edge)
            edge = mid[f, p, 32:33, :]
            mid[f, p, 32:33, :] = jnp.where(place == last_y, mid[f, p, 31:32, :], edge)
    step(mid, 2, 6, put_out)


def bottom_tractions(bottoms, count_x, faces):
    shape = (count_x, 128)
    sub, lane = rows_of(shape), lanes_of(shape)
    count_gy = lax.axis_size("gy")

    def columns(q):
        parts = []
        for y in range(4):
            start = (y // count_gy * count_x * count_gy + y % count_gy) * 24 + q
            parts.append(bottoms[pl.ds(start, count_x, stride=24 * count_gy), :])
        found = []
        for x in range(4):
            total = rolled(parts[0], -32 * x, 1)
            for y in range(1, 4):
                total = jnp.where(lane // 32 == y, rolled(parts[y], 32 * (y - x), 1), total)
            found.append(total)
        return found

    cells = [[columns(f * 3 + z) for f in range(5)] for z in range(3)]
    state = [[[cells[z][f][x] for f in range(5)] for x in range(4)] for z in range(3)]
    ends_y = (lane == 0, lane == 127)

    def across_x(states, prims):
        fluxes = [flux(s, p, 0) for s, p in zip(states, prims)]
        data = [(s, f, a) for s, (f, a) in zip(states, fluxes)]
        up = lambda x: rolled(x, -1)
        wrap = ([up(v) for v in data[0][0]], [up(v) for v in data[0][1]], up(data[0][2]))
        upper = [twice_face(data[x], data[x + 1] if x < 3 else wrap) for x in range(4)]
        upper[3] = [jnp.where(sub == count_x - 1, 2.0 * f, g) for f, g in zip(data[3][1], upper[3])]
        below = [jnp.where(sub == 0, 2.0 * f, rolled(g, 1)) for f, g in zip(data[0][1], upper[3])]
        lower = [below] + upper[:3]
        return [[a - b for a, b in zip(u, l)] for u, l in zip(upper, lower)]

    def advanced(above, here, under, prim_above, prim_here, prim_under):
        changes = across_x(here, prim_here)
        out = []
        for x in range(4):
            change = [a + b for a, b in zip(changes[x], turned_change(here[x], prim_here[x], 1, 1, ends_y))]
            fz, az = flux(here[x], prim_here[x], 2)
            fa, aa = flux(above[x], prim_above[x], 2)
            lower = twice_face((above[x], fa, aa), (here[x], fz, az))
            if under is None:
                upper = [2.0 * f for f in fz]
            else:
                fu, au = flux(under[x], prim_under[x], 2)
                upper = twice_face((here[x], fz, az), (under[x], fu, au))
            out.append([s - (0.5 * cell_ratio) * (c + u - l) for s, c, u, l in zip(here[x], change, upper, lower)])
        return out

    prims = [[primitives(state[z][x]) for x in range(4)] for z in range(3)]
    middle = advanced(state[0], state[1], state[2], prims[0], prims[1], prims[2])
    deepest = advanced(state[1], state[2], None, prims[1], prims[2], None)
    prim_mid, prim_deep = [primitives(s) for s in middle], [primitives(s) for s in deepest]
    final = advanced(middle, deepest, None, prim_mid, prim_deep, None)
    ids = columns(15)
    for x in range(4):
        s, prim = final[x], primitives(final[x])
        at = pl.ds(x * count_x, count_x)
        faces[0, at, :] = face_area * s[1] * prim[2]
        faces[1, at, :] = face_area * s[2] * prim[2]
        faces[2, at, :] = face_area * (s[3] * prim[2] + prim[3])
        faces[3, at, :] = ids[x]


def surface_kernel(nodes_y, count_x, bottoms, material, tables, after, out1, out2, total, faces):
    base_x = (8 * position("gx") - 4).astype(f32)
    base_y = (16 * along_y() - 4).astype(f32)
    bottom_tractions(bottoms, count_x, faces)
    deposit(faces, nodes_y, base_x, base_y, total)
    respond(total, region_rows(bottoms, count_x), material, tables, out1, out2)


def shards(density, momentum, energy, displacement, velocity_field, acceleration, material, element_region_index,
           face_dest, face_slot):
    along, rank = ("grp", "gy"), ("grp", "gx", "gy")
    nodes_y = 16 * lax.axis_size(along) + 1
    count_x, devices = lax.axis_size("gx"), lax.axis_size(rank)
    crater, region = (density, momentum, energy), element_region_index
    bottoms, crater1, crater2 = call(
        functools.partial(start_kernel, float(nodes_y)),
        crater + (face_dest.reshape(1, -1), face_slot, region),
        [(devices, 24, 128), (5, 64, 256), (5, 64, 256)],
        [],
        mib=12,
    )
    bottoms = lax.all_to_all(bottoms, rank, 0, 0, tiled=True)
    crater1, crater2 = exchange("gx", crater1, crater2)
    b, f, x1, x2, y_low, y_high = call(
        first_kernel,
        (displacement, velocity_field, acceleration, region, material),
        [element_shape, element_shape, (31, 8, 128), (31, 8, 128), (16, 8, 128), (15, 8, 128)],
        internal_scratch + [(5, 5, 8, 512), (4, 9, 17, 128)],
        smem=(4,),
        mib=24,
    )
    surf1, surf2 = call(
        functools.partial(surface_kernel, float(nodes_y), count_x),
        (bottoms.reshape(devices * 24, 128), material, jnp.asarray(surface_tables()), x1),
        [(24, 256), (24, 256)],
        [(360, 128), (4, 4 * count_x, 128)],
        smem=(1,),
        away=(3,),
        mib=12,
    )
    x1, x2 = exchange("gx", x1, x2)
    y1, y2 = call(
        first_edge_kernel,
        (y_low, y_high, x1, x2) + crater + (crater1, crater2, surf1),
        [(38, 8, 128), (38, 8, 128)],
        [],
        away=(9,),
        mib=12,
    )
    y1, y2 = exchange(along, y1, y2)
    a1, f2, p1, p2, y_low, y_high, scales = call(
        second_kernel,
        (b, f, x1, x2, y1, y2, region, material),
        [element_shape, element_shape, (30, 8, 128), (30, 8, 128), (15, 8, 128), (15, 8, 128), (3, 3, 2, 8, 128)],
        internal_scratch,
        smem=(7,),
        mib=24,
    )
    (hydro_state,) = call(
        crater_kernel,
        crater + (crater1, crater2, y1, y2, p1),
        [(5, 4, 32, 256)],
        [(5, 8, 40, 256), (5, 8, 40, 256), (6, 40, 256), (5, 40, 256), (6, 40, 256)],
        away=(7,),
        mib=16,
    )
    p1, p2 = exchange("gx", p1, p2)
    r1, r2 = call(
        second_edge_kernel,
        (y_low, y_high, p1, p2, hydro_state),
        [(15, 8, 128), (15, 8, 128)],
        [],
        away=(4,),
        mib=8,
    )
    u_out, first = call(
        place_kernel,
        (a1, surf1, displacement, velocity_field, acceleration, r1),
        [displacement.shape, (3, 4, 9, 17, 128)],
        [(5, 5, 8, 512), (4, 9, 17, 128)],
        away=(5,),
        mib=20,
    )
    r1, r2 = exchange(along, r1, r2)
    v_out, a_out = call(
        last_kernel,
        (first, f2, p1, p2, r1, r2, scales, surf1, surf2, velocity_field, acceleration),
        [displacement.shape] * 2,
        [(5, 5, 8, 512), (4, 9, 17, 128), element_shape],
        mib=22,
    )
    return hydro_state, u_out, v_out, a_out


def solution(mesh):
    field = P(None, "gx", ("grp", "gy"), None)
    cells = P("gx", ("grp", "gy"), None)
    rank = ("grp", "gx", "gy")
    return jax.shard_map(
        shards,
        mesh=mesh,
        in_specs=(cells, field, cells, field, field, field, P(), cells, P(rank, None, None), P(rank, None)),
        out_specs=(field, field, field, field),
        check_vma=False,
    )
```

```python
import functools

import jax
import jax.numpy as jnp
import numpy as np
from jax import lax
from jax.experimental import pallas as pl
from jax.experimental.pallas import tpu as pltpu
from jax.sharding import PartitionSpec as P

gamma_gas = 1.4
cell_ratio = 0.05
half_size = 2.0
time_step = 0.1
face_area = 2.0


def gll_tables():
    root = np.sqrt(3.0 / 7.0)
    points = np.array([-1.0, -root, 0.0, root, 1.0])
    weights = np.array([0.1, 49.0 / 90.0, 32.0 / 45.0, 49.0 / 90.0, 0.1])
    products = [np.prod([points[r] - points[c] for c in range(5) if c != r]) for r in range(5)]
    derivative = np.zeros((5, 5))
    for r in range(5):
        for c in range(5):
            if r != c:
                derivative[r, c] = products[r] / products[c] / (points[r] - points[c])
        derivative[r, r] = sum(1.0 / (points[r] - points[c]) for c in range(5) if c != r)
    derivative[2, 2] = 0.0
    return derivative, weights


deriv, quad = gll_tables()
deriv_t = deriv.T
kind = [0, 1, 2, 1, 0]
f32 = jnp.float32


def line(matrix, v):
    even, odd = (matrix + matrix[:, ::-1]) / 2, (matrix - matrix[:, ::-1]) / 2
    e0, e1, o0, o1 = v[0] + v[4], v[1] + v[3], v[0] - v[4], v[1] - v[3]
    top = [float(even[i, 0]) * e0 + float(even[i, 1]) * e1 + float(matrix[i, 2]) * v[2] for i in range(2)]
    low = [float(odd[i, 0]) * o0 + float(odd[i, 1]) * o1 for i in range(2)]
    centre = float(matrix[2, 0]) * o0 + float(matrix[2, 1]) * o1
    return [top[0] + low[0], top[1] + low[1], centre, low[1] - top[1], low[0] - top[0]]


def rows_of(shape=(8, 128)):
    return lax.broadcasted_iota(jnp.int32, shape, 0)


def lanes_of(shape=(8, 128)):
    return lax.broadcasted_iota(jnp.int32, shape, 1)


def deeper(x):
    return jnp.where(lanes_of() == 127, 0.0, pltpu.roll(x, 127, 1))


def shallower(x):
    return jnp.where(lanes_of() == 0, 0.0, pltpu.roll(x, 1, 1))


def split_three(x):
    high = x.astype(jnp.bfloat16)
    rest = x - high.astype(f32)
    middle = rest.astype(jnp.bfloat16)
    return high, middle, (rest - middle.astype(f32)).astype(jnp.bfloat16)


def one_hot_dot(x, table, dims=(((1,), (0,)), ((), ()))):
    return sum(lax.dot_general(part, table, dims, preferred_element_type=f32) for part in split_three(x))


def depth_table(back=False):
    a = lax.broadcasted_iota(jnp.int32, (512, 512), 1 if back else 0)
    b = lax.broadcasted_iota(jnp.int32, (512, 512), 0 if back else 1)
    return jnp.where(a == 4 * (b & 127) + (b >> 7), 1.0, 0.0).astype(jnp.bfloat16)


def rows_at(i, j, ex, c, count=4):
    return pl.ds(((4 * ex + i) * 17 + j) * 8 + c, count, stride=32)


def to_elements(nodes, c, table, tall, put):
    for i in range(5):
        for j in range(5):
            for ex in range(2):
                for t in range(4):
                    tall[i, j, 4 * ex : 4 * ex + 4, 128 * t : 128 * t + 128] = nodes[t, rows_at(i, j, ex, c), :]
    out = one_hot_dot(tall[...].reshape(200, 512), table)
    for k in range(4):
        put(k, out[:, 128 * k : 128 * k + 128].reshape(5, 5, 8, 128))


def to_nodes(get, c, table, tall, nodes):
    wide = jnp.concatenate([get(k).reshape(200, 128) for k in range(4)], axis=1)
    tall[...] = one_hot_dot(wide, table).reshape(5, 5, 8, 512)
    for i in range(5):
        for j in range(5):
            for ex in range(2):
                if i == 4 and ex == 0:
                    continue
                for t in range(4):
                    lanes = slice(128 * t, 128 * t + 128)
                    if j < 4:
                        nodes[t, rows_at(i, j, ex, c), :] = tall[i, j, 4 * ex : 4 * ex + 4, lanes]
                    else:
                        at = ((4 * ex + i) * 17 + 16) * 8 + c
                        nodes[t, at : at + 1, :] = tall[i, j, 4 * ex + 3 : 4 * ex + 4, lanes]


def node_lanes(x, y, t):
    return x, y, slice(None), slice(128 * t, 128 * t + 128)


def node_rows(x, y, t):
    return t, pl.ds(pl.multiple_of((x * 17 + y) * 8, 8), 3), slice(None)


def lookup(material, row, region):
    total = jnp.zeros_like(region)
    for m in range(material.shape[1]):
        total = jnp.where(region == float(m + 1), material[row, m], total)
    return total


def internal(u, out, lame, shear, gx, gz, cross, planes, side):
    def depth_lines(i, carry):
        for j in range(5):
            for c in range(3):
                v = [u[c, i, j, k] for k in range(4)]
                v.append(deeper(v[0]))
                u[c, i, j, 4] = v[4]
                for k, g in enumerate(line(deriv, v)):
                    gz[c, i, j, k] = g
        return carry

    lax.fori_loop(0, 5, depth_lines, 0)

    def plane(k, carry):
        weight = jnp.where((k == 0) | (k == 4), float(quad[0]), jnp.where(k == 2, float(quad[2]), float(quad[1])))
        lame_k, shear_k = lame * (2.0 * weight), shear * (2.0 * weight)
        pairs = {}
        for a in range(3):
            for b in range(a, 3):
                w = float(quad[a] * quad[b])
                pairs[a, b] = pairs[b, a] = (lame_k * w, shear_k * w, shear_k * (2.0 * w))
        for c in range(3):
            for j in range(5):
                for i, g in enumerate(line(deriv, [u[c, i, j, k] for i in range(5)])):
                    gx[c, i, j] = g
        for i in range(5):
            gy = [line(deriv, [u[c, i, j, k] for j in range(5)]) for c in range(3)]
            ys = [[], [], []]
            for j in range(5):
                lw, mw, mw2 = pairs[kind[i], kind[j]]
                g0, g1, g2 = [[gx[c, i, j], gy[c][j], gz[c, i, j, k]] for c in range(3)]
                dilated = lw * (g0[0] + g1[1] + g2[2])
                s01 = mw * (g0[1] + g1[0])
                s02 = mw * (g0[2] + g2[0])
                s12 = mw * (g1[2] + g2[1])
                side[0, i, j] = dilated + mw2 * g0[0]
                side[1, i, j] = s01
                cross[0, i, j, k] = s02
                cross[1, i, j, k] = s12
                cross[2, i, j, k] = dilated + mw2 * g2[2]
                ys[0].append(s01)
                ys[1].append(dilated + mw2 * g1[1])
                ys[2].append(s12)
            for c in range(3):
                for j, value in enumerate(line(deriv_t, ys[c])):
                    planes[c, i, j, k] = value
        for j in range(5):
            for c in range(3):
                v = [side[c, i, j] if c < 2 else cross[0, i, j, k] for i in range(5)]
                for i, value in enumerate(line(deriv_t, v)):
                    planes[c, i, j, k] += value
        return carry

    lax.fori_loop(0, 5, plane, 0)

    def depth_sums(i, carry):
        for j in range(5):
            for c in range(3):
                v = line(deriv_t, [cross[c, i, j, k] for k in range(5)])
                v = [v[k] + planes[c, i, j, k] for k in range(5)]
                out[c, i, j, 0] = v[0] + shallower(v[4])
                for k in range(1, 4):
                    out[c, i, j, k] = v[k]
        return carry

    lax.fori_loop(0, 5, depth_sums, 0)
    sub = rows_of()

    def fold(k, carry):
        for c in range(3):
            for i in range(5):
                low, high = out[c, i, 0, k], out[c, i, 4, k]
                out[c, i, 0, k] = low + jnp.where(sub % 4 == 0, 0.0, pltpu.roll(high, 1, 0))
                out[c, i, 4, k] = high + jnp.where(sub % 4 == 3, 0.0, pltpu.roll(low, 7, 0))
            for j in range(5):
                low, high = out[c, 0, j, k], out[c, 4, j, k]
                out[c, 0, j, k] = low + jnp.where(sub < 4, 0.0, pltpu.roll(high, 4, 0))
                out[c, 4, j, k] = high + jnp.where(sub < 4, pltpu.roll(low, 4, 0), 0.0)
        return carry

    lax.fori_loop(0, 4, fold, 0)


def rolled(x, amount, axis=0):
    amount = amount % x.shape[axis]
    return pltpu.roll(x, amount, axis) if amount else x


def parity_x():
    return position("gx") % 2


def parity_y():
    return along_y() % 2


def sort_out(odd, low, high):
    return jnp.where(odd == 1, low, high), jnp.where(odd == 1, high, low)


def pack_x(force, first, second):
    sub, odd = rows_of(), parity_x()
    for c in range(3):
        for j in range(5):
            for half in range(2):
                at = (c * 5 + j) * 2 + half
                a, b = force[c, 0, j, 2 * half], force[c, 0, j, 2 * half + 1]
                low = jnp.where(sub < 4, a, rolled(b, 4))
                a, b = force[c, 4, j, 2 * half], force[c, 4, j, 2 * half + 1]
                high = jnp.where(sub < 4, rolled(a, 4), b)
                first[at], second[at] = sort_out(odd, low, high)


def pack_y(force, low, high):
    sub = rows_of()
    for c in range(3):
        for i in range(5):
            a, b = force[c, i, 0, 0], rolled(force[c, i, 4, 0], -3)
            for k in range(1, 4):
                a = jnp.where(sub % 4 == k, rolled(force[c, i, 0, k], k), a)
                b = jnp.where(sub % 4 == k, rolled(force[c, i, 4, k], k - 3), b)
            low[c * 5 + i] = a
            high[c * 5 + i] = b


def add_x(force, first, second):
    sub, odd = rows_of(), parity_x()
    for c in range(3):
        for j in range(5):
            for half in range(2):
                at = (c * 5 + j) * 2 + half
                r, s = sort_out(odd, first[at], second[at])
                force[c, 0, j, 2 * half] += jnp.where(sub < 4, r, 0.0)
                force[c, 0, j, 2 * half + 1] += jnp.where(sub < 4, rolled(r, 4), 0.0)
                force[c, 4, j, 2 * half] += jnp.where(sub < 4, 0.0, rolled(s, 4))
                force[c, 4, j, 2 * half + 1] += jnp.where(sub < 4, 0.0, s)


def add_y(force, first, second):
    sub, odd = rows_of(), parity_y()
    for c in range(3):
        for i in range(5):
            r, s = sort_out(odd, first[c * 5 + i], second[c * 5 + i])
            for k in range(4):
                force[c, i, 0, k] += jnp.where(sub % 4 == 0, rolled(r, -k), 0.0)
                force[c, i, 4, k] += jnp.where(sub % 4 == 3, rolled(s, 3 - k), 0.0)


def edge_rows(low, high, came1, came2, first, second):
    sub, odd, odd_y = rows_of(), parity_x(), parity_y()
    for c in range(3):
        came = [[sort_out(odd, came1[at], came2[at]) for at in range((c * 5 + j) * 2, (c * 5 + j) * 2 + 2)] for j in (0, 4)]
        for i in range(5):
            rows = [low[c * 5 + i], high[c * 5 + i]]
            if i in (0, 4):
                start, side = i, i // 4
                for end, row in ((0, 0), (1, 3)):
                    for k in range(4):
                        r = rolled(came[end][k // 2][side], start + k - (4 * (k % 2) + row))
                        rows[end] = rows[end] + jnp.where(sub == start + k, r, 0.0)
            first[c * 5 + i], second[c * 5 + i] = sort_out(odd_y, *rows)


def first_edge_kernel(low, high, came1, came2, rows_low, rows_high, crater1, crater2, after, first, second):
    edge_rows(low, high, came1, came2, first, second)
    odd, odd_y = parity_x(), parity_y()
    regions = sort_out(odd, came1[30], came2[30])
    for n, value in enumerate((low[15], regions[0], regions[1])):
        first[15 + n] = value
        second[15 + n] = value
    for f in range(5):
        for t in range(2):
            lanes = slice(128 * t, 128 * t + 128)
            at = 18 + f * 4 + t * 2
            first[at], second[at] = sort_out(odd_y, rows_low[f * 2 + t], rows_high[f * 2 + t])
            ends = []
            for near in (0, 31):
                sides = sort_out(odd, crater1[f, near : near + 1, lanes], crater2[f, near : near + 1, lanes])
                ends.append(jnp.concatenate(list(sides) * 4, axis=0))
            first[at + 1], second[at + 1] = sort_out(odd_y, *ends)


def second_edge_kernel(low, high, came1, came2, after, first, second, token):
    edge_rows(low, high, came1, came2, first, second)
    token[...] = after[...]


def region_grid(own, x1, x2, y1, y2):
    xl, xh = sort_out(parity_x(), x1[30], x2[30])
    yl, yh = [list(v) for v in zip(*[sort_out(parity_y(), y1[n], y2[n]) for n in (15, 16, 17)])]
    return [[yl[1], xl, yh[1]], [yl[0], own, yh[0]], [yl[2], xh, yh[2]]]


def shared_density(grid):
    sub = rows_of()
    across = []
    for y in range(3):
        low, mid, high = grid[0][y], grid[1][y], grid[2][y]
        turned = rolled(mid, 4)
        across.append([jnp.where(sub < 4, rolled(low, 4), turned), mid, jnp.where(sub < 4, turned, rolled(high, 4))])
    found = [[None] * 3 for _ in range(3)]
    for x in range(3):
        low, mid, high = across[0][x], across[1][x], across[2][x]
        found[x][0] = jnp.where(sub % 4 == 0, rolled(low, -3), rolled(mid, 1))
        found[x][1] = mid
        found[x][2] = jnp.where(sub % 4 == 3, rolled(high, 3), rolled(mid, -1))
    sums = []
    for x in ((1,), (0, 1), (1, 2)):
        row = []
        for y in ((1,), (0, 1), (1, 2)):
            total = sum(found[a][b] for a in x for b in y)
            row.append((total + shallower(total), total))
        sums.append(row)
    return sums


def mass_scales(sums):
    return [[[1.0 / s for s in pair] for pair in row] for row in sums]


def edge_kind(i):
    return 1 if i == 0 else 2 if i == 4 else 0


def accel_scale(i, j, k):
    return float(-1.0 / (half_size**3 * quad[i] * quad[j] * quad[k]))


def first_kernel(u, v, a, region, material, b_out, f_out, x1, x2, y_low, y_high, token,
                 elem, gx, gz, cross, planes, side, tall, nodes, later):
    table = depth_table()
    region_now = region[...]

    def column(x, carry):
        for y in range(17):
            for t in range(4):
                at = node_lanes(x, y, t)
                uu, vv, aa = u[at], v[at], a[at]
                nodes[node_rows(x, y, t)] = uu + time_step * vv + 0.5 * time_step**2 * aa
                later[node_rows(x, y, t)] = uu + 2.0 * time_step * vv + time_step**2 * aa
        return carry

    lax.fori_loop(0, 9, column, 0)
    for c in range(3):

        def put_u(k, value):
            elem[c, :, :, k] = value

        to_elements(nodes, c, table, tall, put_u)

        def put_b(k, value):
            b_out[c, :, :, k] = value

        to_elements(later, c, table, tall, put_b)
    internal(elem, f_out, lookup(material, 1, region_now), lookup(material, 2, region_now), gx, gz, cross, planes, side)
    pack_x(f_out, x1, x2)
    pack_y(f_out, y_low, y_high)
    x1[30] = region_now
    x2[30] = region_now
    y_low[15] = region_now
    token[...] = region_now


def second_kernel(b, f, came_x1, came_x2, came_y1, came_y2, region, material, a_out, f_out, x1, x2, y_low, y_high, scales, token,
                  elem, gx, gz, cross, planes, side):
    region_now = region[...]
    token[...] = region_now
    a_out[...] = f[...]
    add_x(a_out, came_x1, came_x2)
    add_y(a_out, came_y1, came_y2)
    grid = region_grid(region_now, came_x1, came_x2, came_y1, came_y2)
    inverse = mass_scales(shared_density([[lookup(material, 0, r) for r in row] for row in grid]))
    for x in range(3):
        for y in range(3):
            for z in range(2):
                scales[x, y, z] = inverse[x][y][z]
    for i in range(5):
        for j in range(5):
            for k in range(4):
                scale = scales[edge_kind(i), edge_kind(j), min(k, 1)] * accel_scale(i, j, k)
                for c in range(3):
                    value = a_out[c, i, j, k] * scale
                    a_out[c, i, j, k] = value
                    elem[c, i, j, k] = b[c, i, j, k] + time_step**2 * value
    internal(elem, f_out, lookup(material, 1, region_now), lookup(material, 2, region_now), gx, gz, cross, planes, side)
    pack_x(f_out, x1, x2)
    pack_y(f_out, y_low, y_high)


def add_surface(source, x, c, count):
    at = 8 * (c * 9 + x)
    tile, shift = at // 128, (128 - at % 128) % 128
    moved = rolled(source[0:17, 128 * tile : 128 * tile + 128], shift, 1)
    return jnp.where(lanes_of((17, 128)) < count, moved, 0.0)


def surface_rows(x, c):
    return 0, pl.ds(x * 136 + c, 17, stride=8), slice(None)


def place_kernel(a1, surf1, u, v, a, after, u_out, first, tall, nodes):
    table = depth_table(back=True)
    for c in range(3):
        to_nodes(lambda k: a1[c, :, :, k], c, table, tall, nodes)
        for x in range(9):
            nodes[surface_rows(x, c)] += add_surface(surf1, x, c, 1)

    def column(x, carry):
        for y in range(17):
            for t in range(4):
                at, accel = node_lanes(x, y, t), nodes[node_rows(x, y, t)]
                first[at] = accel
                u_out[at] = u[at] + 2.0 * time_step * v[at] + time_step**2 * (a[at] + accel)
        return carry

    lax.fori_loop(0, 9, column, 0)


def last_kernel(first, f, x1, x2, y1, y2, scales, surf1, surf2, v, a, v_out, a_out, tall, nodes, force):
    table = depth_table(back=True)
    force[...] = f[...]
    add_x(force, x1, x2)
    add_y(force, y1, y2)
    for i in range(5):
        for j in range(5):
            for k in range(4):
                scale = scales[edge_kind(i), edge_kind(j), min(k, 1)] * accel_scale(i, j, k)
                for c in range(3):
                    force[c, i, j, k] = force[c, i, j, k] * scale
    for c in range(3):
        to_nodes(lambda k: force[c, :, :, k], c, table, tall, nodes)
        for x in range(9):
            nodes[surface_rows(x, c)] += add_surface(surf1, x, c, 1) + add_surface(surf2, x, c, 5)

    def column(x, carry):
        for y in range(17):
            for t in range(4):
                at, accel = node_lanes(x, y, t), nodes[node_rows(x, y, t)]
                a_out[at] = accel
                v_out[at] = v[at] + 0.5 * time_step * (a[at] + 2.0 * first[at] + accel)
        return carry

    lax.fori_loop(0, 9, column, 0)


def whole():
    return pl.BlockSpec(memory_space=pltpu.VMEM)


def scalars():
    return pl.BlockSpec(memory_space=pltpu.SMEM)


def call(kernel, ins, outs, scratch, smem=(), away=(), mib=10, copies=0):
    def spec(n):
        return scalars() if n in smem else pl.BlockSpec(memory_space=pltpu.HBM) if n in away else whole()

    scratch = [pltpu.VMEM(s, f32) if isinstance(s, tuple) else s for s in scratch]
    return pl.pallas_call(
        kernel,
        out_shape=[jax.ShapeDtypeStruct(s, f32) for s in outs],
        in_specs=[spec(n) for n in range(len(ins))],
        out_specs=[whole() for _ in outs],
        scratch_shapes=scratch + ([pltpu.SemaphoreType.DMA((copies,))] if copies else []),
        compiler_params=pltpu.CompilerParams(vmem_limit_bytes=mib * 1024 * 1024),
    )(*ins)


def fetch(pairs, semaphores):
    copies = [pltpu.make_async_copy(source, target, semaphores.at[n]) for n, (source, target) in enumerate(pairs)]
    for copy in copies:
        copy.start()
    return copies


element_shape = (3, 5, 5, 4, 8, 128)
lines_shape = (3, 5, 5, 5, 8, 128)
internal_scratch = [lines_shape, (3, 5, 5, 8, 128), lines_shape, lines_shape, lines_shape, (2, 5, 5, 8, 128)]


def exchange(axis, first, second):
    count = lax.axis_size(axis)
    pairs = [(i, i + 1) for i in range(1, count - 1, 2)]
    first = lax.ppermute(first, axis, [(i, i ^ 1) for i in range(count)])
    return first, lax.ppermute(second, axis, pairs + [(j, i) for i, j in pairs])


def surface_tables():
    lane = np.arange(128)
    j, ey = lane // 8, lane % 8
    used = (j < 5) & (ey < 6)
    place = np.where(used, ey + 1, -9)
    source = lane[:, None]
    centre = source == place
    meet = centre | ((j == 0) & (source == place - 1)) | ((j == 4) & (source == place + 1))
    along = np.zeros((128, 128))
    for a in range(40):
        for b in range(40):
            if a % 8 == b % 8 and a % 8 < 6:
                along[a, b] = deriv[b // 8, a // 8]
    node = np.where(used, 4 * (ey - 1) + j, -9)
    fold = (lane[:, None] == node) & (lane[:, None] < 17)
    keep = fold & ((j < 4) & (ey < 5) | (j == 4) & (ey == 4))
    return np.stack([centre, meet, along, along.T, fold, keep]).astype(np.float32)


def full_dot(x, y, back=False):
    dims = (((1,), (1 if back else 0,)), ((), ()))
    return lax.dot_general(x, y, dims, precision=lax.Precision.HIGHEST, preferred_element_type=f32)


def deposit(faces, nodes_y, base_x, base_y, total):
    rows = faces.shape[1]
    sub = rows_of((8, 512)).astype(f32)
    total[...] = jnp.zeros_like(total)

    def one(step, carry):
        def wide(q):
            block = faces[q, pl.ds(4 * step, 4), :]
            return jnp.concatenate([block[n : n + 1] for n in range(4)], axis=1)

        ids = wide(3)
        node_x = jnp.floor((ids + 0.5) * (1.0 / nodes_y))
        rel_y = jnp.broadcast_to(ids - node_x * nodes_y - base_y, (8, 512))
        rel_x = jnp.broadcast_to(node_x - base_x, (8, 512))
        left = []
        hits = [(rel_x - i == 4.0 * sub) & (sub < 4.0) for i in range(5)]
        parts = [split_three(wide(c)) for c in range(3)]
        for part in range(3):
            for c in range(3):
                value = jnp.broadcast_to(parts[c][part].astype(f32), (8, 512))
                left += [jnp.where(hit, value, 0.0) for hit in hits]
        right = [jnp.where((rel_y - j == 4.0 * sub) & (sub < 6.0), 1.0, 0.0) for j in range(5)]
        right.append(jnp.zeros((88, 512), f32))
        left, right = jnp.concatenate(left, axis=0), jnp.concatenate(right, axis=0)
        total[...] += lax.dot_general(
            left.astype(jnp.bfloat16), right.astype(jnp.bfloat16), (((1,), (1,)), ((), ())), preferred_element_type=f32
        )
        return carry

    lax.fori_loop(0, rows // 4, one, 0)


def top_grid(rows, z):
    sub, lane = rows_of(), lanes_of()
    out = jnp.zeros((8, 128), f32)
    for x in range(3):
        for y in range(3):
            row = jnp.broadcast_to(rows[x][y], (8, 128))
            for ex in range(2):
                here = (sub == 2 * x + ex) & (lane >= 4 * y - 2) & (lane < 4 * y + 2) & (lane < 8)
                out = jnp.where(here, rolled(row, 4 * y - 2 - 8 * z - 4 * ex, 1), out)
    return out


def region_rows(bottoms, count_x):
    gx, place, count_gy = position("gx"), along_y(), lax.axis_size("gy")
    last_y = lax.axis_size("grp") * count_gy - 1
    found = []
    for x in range(3):
        found.append([])
        for y in range(3):
            px, py = gx + x - 1, place + y - 1
            inside = (px >= 0) & (px < count_x) & (py >= 0) & (py <= last_y)
            cx, cy = jnp.clip(px, 0, count_x - 1), jnp.clip(py, 0, last_y)
            rank = (cy // count_gy) * (count_x * count_gy) + cx * count_gy + cy % count_gy
            row = bottoms[pl.ds(pl.multiple_of(rank * 24 + 16, 8), 1), :]
            found[x].append(jnp.where(inside, row, 0.0))
    return found


def respond(total, grid, material, tables, out1, out2):
    sub, lane = rows_of(), lanes_of()
    top, below = top_grid(grid, 0), top_grid(grid, 1)
    centre, meet, along, along_t, fold, keep = [tables[n] for n in range(6)]
    sums0 = full_dot(lookup(material, 0, top), meet)
    sums1 = full_dot(lookup(material, 0, below), meet)
    lame = rolled(full_dot(lookup(material, 1, top), centre), -1)
    shear = rolled(full_dot(lookup(material, 2, top), centre), -1)
    weight_y = jnp.ones((8, 128), f32)
    for j in range(5):
        weight_y = jnp.where(lane // 8 == j, float(quad[j]), weight_y)

    def inverse(sums):
        mid = rolled(sums, -1)
        found = {0: mid + sums, 1: mid, 4: mid + rolled(sums, -2)}
        found = {i: jnp.where(s > 0.0, 1.0 / (s * weight_y), 0.0) for i, s in found.items()}
        found[2] = found[3] = found[1]
        return found

    light, heavy = inverse(sums0), inverse(sums0 + sums1)
    first = [[None] * 5 for _ in range(3)]
    moved = [[None] * 5 for _ in range(3)]
    for c in range(3):
        for i in range(5):
            at = (c * 5 + i) * 8
            force = total[at : at + 8] + total[at + 120 : at + 128] + total[at + 240 : at + 248]
            first[c][i] = force * light[i] * -accel_scale(i, 2, 0) * float(quad[2])
            moved[c][i] = first[c][i] * time_step**2
    gx = [line(deriv, moved[c]) for c in range(3)]
    gy = full_dot(jnp.concatenate([moved[c][i] for c in range(3) for i in range(5)], axis=0), along)
    gy = [[gy[(c * 5 + i) * 8 : (c * 5 + i) * 8 + 8] for i in range(5)] for c in range(3)]
    lame_w, shear_w = lame * weight_y * 2.0, shear * weight_y * 2.0
    d00 = float(deriv[0, 0])
    sx = [[], [], []]
    sy = [[], [], []]
    sz = [[], [], []]
    qs = [[], [], []]
    pressed = []
    for i in range(5):
        lw, mw = lame_w * float(quad[i]), shear_w * float(quad[i])
        d = [moved[c][i] for c in range(3)]
        gz = [d00 * x for x in d]
        dilated = lw * (gx[0][i] + gy[1][i] + gz[2])
        s01 = mw * (gx[1][i] + gy[0][i])
        s02 = mw * (gx[2][i] + gz[0])
        s12 = mw * (gy[2][i] + gz[1])
        for c, value in enumerate((dilated + 2.0 * mw * gx[0][i], s01, s02)):
            sx[c].append(value)
        for c, value in enumerate((s01, dilated + 2.0 * mw * gy[1][i], s12)):
            sy[c].append(value)
        for c, value in enumerate((s02, s12, dilated + 2.0 * mw * gz[2])):
            sz[c].append(value)
        for c, value in enumerate((mw * d[0], mw * d[1], (lw + 2.0 * mw) * d[2])):
            qs[c].append(value)
        pressed.append(lw * d[2])
    ydiv = full_dot(jnp.concatenate(sy[0] + sy[1] + sy[2] + pressed + qs[1], axis=0), along_t)
    ydiv = [[ydiv[(n * 5 + i) * 8 : (n * 5 + i) * 8 + 8] for i in range(5)] for n in range(5)]
    xdiv = [line(deriv_t, v) for v in sx + [pressed, qs[0]]]
    base = [xdiv[3], ydiv[3], [p + q for p, q in zip(xdiv[4], ydiv[4])]]
    second = {}
    for c in range(3):
        for i in range(5):
            for l in range(5):
                stiff = float(sum(deriv[k, l] * quad[k] * deriv[k, 0] for k in range(1, 5)))
                value = float(deriv[0, l] * quad[0]) * sz[c][i] + stiff * qs[c][i]
                if l:
                    value = value + float(deriv[l, 0] * quad[l]) * base[c][i]
                else:
                    value = value + float(quad[0]) * (xdiv[c][i] + ydiv[c][i])
                scale = (heavy if l == 4 else light)[i]
                second[c, i, l] = value * scale * (accel_scale(i, 2, l) * float(quad[2]))
    rows1, rows2 = [], []
    for c in range(3):
        for x in range(9):
            own = 1 if x < 4 else 2
            rows1.append(jnp.where(sub == 0, rolled(first[c][x - 4 * (own - 1)], -own), 0.0))
            block = jnp.zeros((8, 128), f32)
            for l in range(5):
                for ex in range(4):
                    i = x - 4 * (ex - 1)
                    if 0 <= i <= 4:
                        block = block + jnp.where(sub == l, rolled(second[c, i, l], l - ex), 0.0)
            rows2.append(block)
    blank = [jnp.zeros((40, 128), f32)]
    out1[...] = full_dot(keep[0:24], jnp.concatenate(rows1 + blank, axis=0), back=True)
    out2[...] = full_dot(fold[0:24], jnp.concatenate(rows2 + blank, axis=0), back=True)


def position(axis):
    return lax.axis_index(axis)


def along_y():
    return lax.axis_index("grp") * lax.axis_size("gy") + lax.axis_index("gy")


def primitives(state):
    inverse = 1.0 / state[0]
    v = [state[1 + c] * inverse for c in range(3)]
    p = (gamma_gas - 1.0) * (state[4] - 0.5 * (state[1] * v[0] + state[2] * v[1] + state[3] * v[2]))
    return v + [p, jnp.sqrt(gamma_gas * p * inverse), state[4] + p]


def flux(state, prim, d):
    out = [state[1 + d]] + [state[1 + c] * prim[d] for c in range(3)] + [prim[5] * prim[d]]
    out[1 + d] = out[1 + d] + prim[3]
    return out, jnp.abs(prim[d]) + prim[4]


def twice_face(low, high):
    fastest = jnp.maximum(low[2], high[2])
    return [fl + fh - fastest * (uh - ul) for ul, uh, fl, fh in zip(low[0], high[0], low[1], high[1])]


def turned_change(state, prim, d, axis, ends):
    size = state[0].shape[axis]
    fluxes, speed = flux(state, prim, d)
    up = lambda x: pltpu.roll(x, size - 1, axis)
    high = ([up(x) for x in state], [up(x) for x in fluxes], up(speed))
    upper = twice_face((state, fluxes, speed), high)
    if ends is None:
        return [g - pltpu.roll(g, 1, axis) for g in upper]
    upper = [jnp.where(ends[1], 2.0 * f, g) for f, g in zip(fluxes, upper)]
    return [g - jnp.where(ends[0], 2.0 * f, pltpu.roll(g, 1, axis)) for f, g in zip(fluxes, upper)]


def start_kernel(nodes_y, density, momentum, energy, dest, slot, region, bottoms, first, second, rows_low, rows_high,
                 region_out, cells, dest_in, slot_in, region_in, semaphores):
    copies = fetch(
        [(dest, dest_in), (slot, slot_in), (region, region_in), (density, cells.at[0]),
         (momentum, cells.at[pl.ds(1, 3)]), (energy, cells.at[4])],
        semaphores,
    )
    for copy in copies:
        copy.wait()
    sub, lane = rows_of(), lanes_of()
    pick = jnp.where(lane == 125 + sub, 1.0, 0.0)
    pieces = []
    odd = parity_x()
    for f in range(5):
        columns = jnp.concatenate([cells[f, x, :, 128:256] for x in range(4)], axis=0)
        pieces.append(full_dot(pick, columns, back=True)[0:3])
        for out, down in ((first, odd), (second, 1 - odd)):
            out[f, 0:32, :] = cells[f, 3 - 3 * down]
            out[f, 32:64, :] = cells[f, 2 - down]
        for t in range(2):
            lanes = slice(128 * t, 128 * t + 128)
            for out, pair in ((rows_low, (0, 1)), (rows_high, (31, 30))):
                out[f * 2 + t] = jnp.concatenate([cells[f, x, r : r + 1, lanes] for r in pair for x in range(4)], axis=0)
    count_gy, count_x = lax.axis_size("gy"), lax.axis_size("gx")
    target, node = dest_in[...].astype(f32), slot_in[...].astype(f32)
    grp = jnp.floor((target + 0.5) * (1.0 / (count_gy * count_x)))
    rest = target - grp * (count_gy * count_x)
    gx = jnp.floor((rest + 0.5) * (1.0 / count_gy))
    gy = rest - gx * count_gy
    i = jnp.floor((node + 0.5) * (1.0 / 17.0))
    j = node - 17.0 * i
    pieces.append((8.0 * gx + i) * nodes_y + 16.0 * (grp * count_gy + gy) + j)
    region_now = jnp.concatenate([region_in[0], region_in[1]], axis=0).astype(f32) + 1.0
    region_out[...] = region_now
    found = jnp.zeros((8, 128), f32)
    for z in range(2):
        found = jnp.where(lane == 8 * z + sub, jnp.broadcast_to(region_now[:, z : z + 1], (8, 128)), found)
    pieces.append(jnp.broadcast_to(jnp.sum(found, axis=0, keepdims=True), (8, 128)))
    block = jnp.concatenate(pieces, axis=0)
    for n in range(bottoms.shape[0]):
        bottoms[n] = block


def crater_kernel(density, momentum, energy, came1, came2, rows1, rows2, after, out, token,
                  wide, mid, prims, face, fluxes, semaphores):
    planes, inner = pl.ds(2, 4), pl.ds(0, 32)
    copies = fetch(
        [(density, wide.at[0, planes, inner]), (momentum, wide.at[pl.ds(1, 3), planes, inner]),
         (energy, wide.at[4, planes, inner])],
        semaphores,
    )
    place, last_y = along_y(), lax.axis_size("grp") * lax.axis_size("gy") - 1
    gx, last_x = position("gx"), lax.axis_size("gx") - 1
    odd, odd_y = parity_x(), parity_y()
    for f in range(5):
        low, high = sort_out(odd, came1[f], came2[f])
        for p, value in ((0, low[32:64]), (1, low[0:32]), (6, high[0:32]), (7, high[32:64])):
            wide[f, p, 0:32, :] = value
            wide[f, p, 32:40, :] = value[0:8]
    token[...] = after[...]
    for copy in copies:
        copy.wait()
    for f in range(5):
        for x in range(4):
            wide[f, 2 + x, 32:40, :] = wide[f, 2 + x, 24:32, :]
        for t in range(2):
            lanes = slice(128 * t, 128 * t + 128)
            at = 18 + f * 4 + t * 2
            below, above = sort_out(odd_y, rows1[at], rows2[at])
            sides_below, sides_above = sort_out(odd_y, rows1[at + 1], rows2[at + 1])

            def put(p, row, edge, value):
                clamped = jnp.where(edge == 0, place == 0, place == last_y)
                at_edge = wide[f, p, 31 * edge : 31 * edge + 1, lanes]
                wide[f, p, row : row + 1, lanes] = jnp.where(clamped, at_edge, value)

            for x in range(4):
                put(2 + x, 39, 0, below[x : x + 1])
                put(2 + x, 38, 0, below[4 + x : 5 + x])
                put(2 + x, 32, 1, above[x : x + 1])
                put(2 + x, 33, 1, above[4 + x : 5 + x])
            for p, n in ((1, 0), (6, 1)):
                put(p, 39, 0, sides_below[n : n + 1])
                put(p, 32, 1, sides_above[n : n + 1])

    @pl.when(gx == 0)
    def _():
        for f in range(5):
            wide[f, 0] = wide[f, 2]
            wide[f, 1] = wide[f, 2]

    @pl.when(gx == last_x)
    def _():
        for f in range(5):
            wide[f, 6] = wide[f, 5]
            wide[f, 7] = wide[f, 5]

    lane = lanes_of((40, 256))
    ends = (lane == 0, lane == 255)

    def step(source, low, high, put):
        def along_x(p):
            state = [source[f, p] for f in range(5)]
            prim = primitives(state)
            return state, prim, flux(state, prim, 0)

        state, prim, (fx, speed) = along_x(low - 1)
        next_state, next_prim, (next_fx, next_speed) = along_x(low)
        g = twice_face((state, fx, speed), (next_state, next_fx, next_speed))
        for f in range(5):
            face[f] = g[f]
            fluxes[f] = next_fx[f]
        for n in range(6):
            prims[n] = next_prim[n]
        fluxes[5] = next_speed

        def plane(p, carry):
            state = [source[f, p] for f in range(5)]
            prim = [prims[n] for n in range(6)]
            next_state, next_prim, (next_fx, next_speed) = along_x(p + 1)
            g = twice_face((state, [fluxes[f] for f in range(5)], fluxes[5]), (next_state, next_fx, next_speed))
            change = [g[f] - face[f] for f in range(5)]
            for f in range(5):
                face[f] = g[f]
                fluxes[f] = next_fx[f]
            for n in range(6):
                prims[n] = next_prim[n]
            fluxes[5] = next_speed
            change = [a + b for a, b in zip(change, turned_change(state, prim, 1, 0, None))]
            change = [a + b for a, b in zip(change, turned_change(state, prim, 2, 1, ends))]
            for f in range(5):
                put(f, p, state[f] - (0.5 * cell_ratio) * change[f])
            return carry

        lax.fori_loop(low, high, plane, 0)

    def put_mid(f, p, value):
        mid[f, p] = value

    def put_out(f, p, value):
        out[f, p - 2] = value[0:32]

    step(wide, 1, 7, put_mid)

    @pl.when(gx == 0)
    def _():
        for f in range(5):
            mid[f, 1] = mid[f, 2]

    @pl.when(gx == last_x)
    def _():
        for f in range(5):
            mid[f, 6] = mid[f, 5]

    for f in range(5):
        for p in range(2, 6):
            edge = mid[f, p, 39:40, :]
            mid[f, p, 39:40, :] = jnp.where(place == 0, mid[f, p, 0:1, :], edge)
            edge = mid[f, p, 32:33, :]
            mid[f, p, 32:33, :] = jnp.where(place == last_y, mid[f, p, 31:32, :], edge)
    step(mid, 2, 6, put_out)


def bottom_tractions(bottoms, count_x, faces):
    shape = (count_x, 128)
    sub, lane = rows_of(shape), lanes_of(shape)
    count_gy = lax.axis_size("gy")

    def columns(q):
        parts = []
        for y in range(4):
            start = (y // count_gy * count_x * count_gy + y % count_gy) * 24 + q
            parts.append(bottoms[pl.ds(start, count_x, stride=24 * count_gy), :])
        found = []
        for x in range(4):
            total = rolled(parts[0], -32 * x, 1)
            for y in range(1, 4):
                total = jnp.where(lane // 32 == y, rolled(parts[y], 32 * (y - x), 1), total)
            found.append(total)
        return found

    cells = [[columns(f * 3 + z) for f in range(5)] for z in range(3)]
    state = [[[cells[z][f][x] for f in range(5)] for x in range(4)] for z in range(3)]
    ends_y = (lane == 0, lane == 127)

    def across_x(states, prims):
        fluxes = [flux(s, p, 0) for s, p in zip(states, prims)]
        data = [(s, f, a) for s, (f, a) in zip(states, fluxes)]
        up = lambda x: rolled(x, -1)
        wrap = ([up(v) for v in data[0][0]], [up(v) for v in data[0][1]], up(data[0][2]))
        upper = [twice_face(data[x], data[x + 1] if x < 3 else wrap) for x in range(4)]
        upper[3] = [jnp.where(sub == count_x - 1, 2.0 * f, g) for f, g in zip(data[3][1], upper[3])]
        below = [jnp.where(sub == 0, 2.0 * f, rolled(g, 1)) for f, g in zip(data[0][1], upper[3])]
        lower = [below] + upper[:3]
        return [[a - b for a, b in zip(u, l)] for u, l in zip(upper, lower)]

    def advanced(above, here, under, prim_above, prim_here, prim_under):
        changes = across_x(here, prim_here)
        out = []
        for x in range(4):
            change = [a + b for a, b in zip(changes[x], turned_change(here[x], prim_here[x], 1, 1, ends_y))]
            fz, az = flux(here[x], prim_here[x], 2)
            fa, aa = flux(above[x], prim_above[x], 2)
            lower = twice_face((above[x], fa, aa), (here[x], fz, az))
            if under is None:
                upper = [2.0 * f for f in fz]
            else:
                fu, au = flux(under[x], prim_under[x], 2)
                upper = twice_face((here[x], fz, az), (under[x], fu, au))
            out.append([s - (0.5 * cell_ratio) * (c + u - l) for s, c, u, l in zip(here[x], change, upper, lower)])
        return out

    prims = [[primitives(state[z][x]) for x in range(4)] for z in range(3)]
    middle = advanced(state[0], state[1], state[2], prims[0], prims[1], prims[2])
    deepest = advanced(state[1], state[2], None, prims[1], prims[2], None)
    prim_mid, prim_deep = [primitives(s) for s in middle], [primitives(s) for s in deepest]
    final = advanced(middle, deepest, None, prim_mid, prim_deep, None)
    ids = columns(15)
    for x in range(4):
        s, prim = final[x], primitives(final[x])
        at = pl.ds(x * count_x, count_x)
        faces[0, at, :] = face_area * s[1] * prim[2]
        faces[1, at, :] = face_area * s[2] * prim[2]
        faces[2, at, :] = face_area * (s[3] * prim[2] + prim[3])
        faces[3, at, :] = ids[x]


def surface_kernel(nodes_y, count_x, bottoms, material, tables, after, out1, out2, total, faces, held, semaphores):
    copies = fetch([(tables, held)], semaphores)
    base_x = (8 * position("gx") - 4).astype(f32)
    base_y = (16 * along_y() - 4).astype(f32)
    bottom_tractions(bottoms, count_x, faces)
    deposit(faces, nodes_y, base_x, base_y, total)
    copies[0].wait()
    respond(total, region_rows(bottoms, count_x), material, held, out1, out2)


def shards(density, momentum, energy, displacement, velocity_field, acceleration, material, element_region_index,
           face_dest, face_slot):
    along, rank = ("grp", "gy"), ("grp", "gx", "gy")
    nodes_y = 16 * lax.axis_size(along) + 1
    count_x, devices = lax.axis_size("gx"), lax.axis_size(rank)
    crater = (density, momentum, energy)
    u, v, a = [jnp.transpose(x, (1, 2, 0, 3)) for x in (displacement, velocity_field, acceleration)]
    register = (8, 128)
    bottoms, crater1, crater2, rows_low, rows_high, region = call(
        functools.partial(start_kernel, float(nodes_y)),
        crater + (face_dest.reshape(1, -1), face_slot, element_region_index),
        [(devices, 24, 128), (5, 64, 256), (5, 64, 256), (10, 8, 128), (10, 8, 128), register],
        [(5, 4, 32, 256), pltpu.VMEM((1, 128), jnp.int32), pltpu.VMEM((1, 128), jnp.int32),
         pltpu.VMEM((2, 4, 128), jnp.int32)],
        away=(0, 1, 2, 3, 4, 5),
        copies=6,
    )
    bottoms = lax.all_to_all(bottoms, rank, 0, 0, tiled=True)
    crater1, crater2 = exchange("gx", crater1, crater2)
    b, f, x1, x2, y_low, y_high, token = call(
        first_kernel,
        (u, v, a, region, material),
        [element_shape, element_shape, (31, 8, 128), (31, 8, 128), (16, 8, 128), (15, 8, 128), register],
        internal_scratch + [(5, 5, 8, 512), (4, 1224, 128), (4, 1224, 128)],
        smem=(4,),
        mib=14,
    )
    surf1, surf2 = call(
        functools.partial(surface_kernel, float(nodes_y), count_x),
        (bottoms.reshape(devices * 24, 128), material, jnp.asarray(surface_tables()), token),
        [(24, 256), (24, 256)],
        [(360, 128), (4, 4 * count_x, 128), (6, 128, 128)],
        smem=(1,),
        away=(2,),
        copies=1,
    )
    x1, x2 = exchange("gx", x1, x2)
    y1, y2 = call(
        first_edge_kernel,
        (y_low, y_high, x1, x2, rows_low, rows_high, crater1, crater2, surf1),
        [(38, 8, 128), (38, 8, 128)],
        [],
    )
    y1, y2 = exchange(along, y1, y2)
    a1, f2, p1, p2, y_low, y_high, scales, token = call(
        second_kernel,
        (b, f, x1, x2, y1, y2, region, material),
        [element_shape, element_shape, (30, 8, 128), (30, 8, 128), (15, 8, 128), (15, 8, 128), (3, 3, 2, 8, 128), register],
        internal_scratch,
        smem=(7,),
    )
    hydro_state, token = call(
        crater_kernel,
        crater + (crater1, crater2, y1, y2, token),
        [(5, 4, 32, 256), register],
        [(5, 8, 40, 256), (5, 8, 40, 256), (6, 40, 256), (5, 40, 256), (6, 40, 256)],
        away=(0, 1, 2),
        copies=3,
    )
    p1, p2 = exchange("gx", p1, p2)
    r1, r2, token = call(
        second_edge_kernel, (y_low, y_high, p1, p2, token), [(15, 8, 128), (15, 8, 128), register], []
    )
    u_out, first = call(
        place_kernel,
        (a1, surf1, u, v, a, token),
        [u.shape, u.shape],
        [(5, 5, 8, 512), (4, 1224, 128)],
    )
    r1, r2 = exchange(along, r1, r2)
    v_out, a_out = call(
        last_kernel,
        (first, f2, p1, p2, r1, r2, scales, surf1, surf2, v, a),
        [u.shape] * 2,
        [(5, 5, 8, 512), (4, 1224, 128), element_shape],
    )
    u_out, v_out, a_out = [jnp.transpose(x, (2, 0, 1, 3)) for x in (u_out, v_out, a_out)]
    return hydro_state, u_out, v_out, a_out


def solution(mesh):
    field = P(None, "gx", ("grp", "gy"), None)
    cells = P("gx", ("grp", "gy"), None)
    rank = ("grp", "gx", "gy")
    return jax.shard_map(
        shards,
        mesh=mesh,
        in_specs=(cells, field, cells, field, field, field, P(), cells, P(rank, None, None), P(rank, None)),
        out_specs=(field, field, field, field),
        check_vma=False,
    )
```

```python
import functools

import jax
import jax.numpy as jnp
import numpy as np
from jax import lax
from jax.experimental import pallas as pl
from jax.experimental.pallas import tpu as pltpu
from jax.sharding import PartitionSpec as P

gamma_gas = 1.4
cell_ratio = 0.05
half_size = 2.0
time_step = 0.1
face_area = 2.0


def gll_tables():
    root = np.sqrt(3.0 / 7.0)
    points = np.array([-1.0, -root, 0.0, root, 1.0])
    weights = np.array([0.1, 49.0 / 90.0, 32.0 / 45.0, 49.0 / 90.0, 0.1])
    products = [np.prod([points[r] - points[c] for c in range(5) if c != r]) for r in range(5)]
    derivative = np.zeros((5, 5))
    for r in range(5):
        for c in range(5):
            if r != c:
                derivative[r, c] = products[r] / products[c] / (points[r] - points[c])
        derivative[r, r] = sum(1.0 / (points[r] - points[c]) for c in range(5) if c != r)
    derivative[2, 2] = 0.0
    return derivative, weights


deriv, quad = gll_tables()
deriv_t = deriv.T
kind = [0, 1, 2, 1, 0]
f32 = jnp.float32


def line(matrix, v):
    even, odd = (matrix + matrix[:, ::-1]) / 2, (matrix - matrix[:, ::-1]) / 2
    e0, e1, o0, o1 = v[0] + v[4], v[1] + v[3], v[0] - v[4], v[1] - v[3]
    top = [float(even[i, 0]) * e0 + float(even[i, 1]) * e1 + float(matrix[i, 2]) * v[2] for i in range(2)]
    low = [float(odd[i, 0]) * o0 + float(odd[i, 1]) * o1 for i in range(2)]
    centre = float(matrix[2, 0]) * o0 + float(matrix[2, 1]) * o1
    return [top[0] + low[0], top[1] + low[1], centre, low[1] - top[1], low[0] - top[0]]


def rows_of(shape=(8, 128)):
    return lax.broadcasted_iota(jnp.int32, shape, 0)


def lanes_of(shape=(8, 128)):
    return lax.broadcasted_iota(jnp.int32, shape, 1)


def deeper(x):
    return jnp.where(lanes_of() == 127, 0.0, pltpu.roll(x, 127, 1))


def shallower(x):
    return jnp.where(lanes_of() == 0, 0.0, pltpu.roll(x, 1, 1))


def split_three(x):
    high = x.astype(jnp.bfloat16)
    rest = x - high.astype(f32)
    middle = rest.astype(jnp.bfloat16)
    return high, middle, (rest - middle.astype(f32)).astype(jnp.bfloat16)


def depth_table(back=False):
    a = lax.broadcasted_iota(jnp.int32, (256, 256), 1 if back else 0)
    b = lax.broadcasted_iota(jnp.int32, (256, 256), 0 if back else 1)
    table = jnp.where(a == 4 * (b & 63) + (b >> 6), 1.0, 0.0).astype(jnp.bfloat16)
    return jnp.concatenate([table] * 3, axis=0)


def moved_lanes(x, table):
    return jnp.dot(jnp.concatenate(split_three(x), axis=1), table, preferred_element_type=f32)


def interleave(x, y):
    front = lanes_of(x.shape) < 64
    return jnp.where(front, x, pltpu.roll(y, 64, 1)), jnp.where(front, pltpu.roll(x, 64, 1), y)


def rows_at(i, j, ex, c, count=4):
    return pl.ds(((4 * ex + i) * 17 + j) * 8 + c, count, stride=32)


def tile_copies(field, held, semaphores, first, out=False):
    copies = []
    for t in range(4):
        outside = field.at[:, :, :, pl.ds(128 * t, 128)]
        inside = held.reshape(4, 9, 17, 8, 128).at[t, :, :, pl.ds(0, 3), :]
        ends = (inside, outside) if out else (outside, inside)
        copies.append(pltpu.make_async_copy(*ends, semaphores.at[first + t]))
    return copies


def to_elements(half, wide, table, kept, puts):
    moved = moved_lanes(wide[...].reshape(600, 256), table)
    if half == 0:
        kept[...] = moved
        return
    for pair in range(2):
        lanes = slice(128 * pair, 128 * pair + 128)
        for l, value in enumerate(interleave(kept[:, lanes], moved[:, lanes])):
            puts(2 * pair + l, value.reshape(3, 5, 5, 8, 128))


def to_nodes(get, table, tall):
    pairs = [interleave(get(2 * p).reshape(600, 128), get(2 * p + 1).reshape(600, 128)) for p in range(2)]
    for half in range(2):
        wide = jnp.concatenate([pairs[0][half], pairs[1][half]], axis=1)
        tall[half] = moved_lanes(wide, table).reshape(3, 5, 5, 8, 256)


def node_pieces(tall, t):
    lanes = slice(128 * (t % 2), 128 * (t % 2) + 128)
    for c in range(3):
        for i in range(5):
            for ex in range(2):
                if i == 4 and ex == 0:
                    continue
                for j in range(4):
                    yield rows_at(i, j, ex, c), j, 4 * ex + i, c, tall[t // 2, c, i, j, 4 * ex : 4 * ex + 4, lanes]
                at = ((4 * ex + i) * 17 + 16) * 8 + c
                yield pl.ds(at, 1), 16, 4 * ex + i, c, tall[t // 2, c, i, 4, 4 * ex + 3 : 4 * ex + 4, lanes]


def lookup(material, row, region):
    total = jnp.zeros_like(region)
    for m in range(material.shape[1]):
        total = jnp.where(region == float(m + 1), material[row, m], total)
    return total


def internal(u, out, lame, shear, gx, gz, cross, planes, side):
    def depth_lines(i, carry):
        for j in range(5):
            for c in range(3):
                v = [u[c, i, j, k] for k in range(4)]
                v.append(deeper(v[0]))
                u[c, i, j, 4] = v[4]
                for k, g in enumerate(line(deriv, v)):
                    gz[c, i, j, k] = g
        return carry

    lax.fori_loop(0, 5, depth_lines, 0)

    def plane(k, carry):
        weight = jnp.where((k == 0) | (k == 4), float(quad[0]), jnp.where(k == 2, float(quad[2]), float(quad[1])))
        lame_k, shear_k = lame * (2.0 * weight), shear * (2.0 * weight)
        pairs = {}
        for a in range(3):
            for b in range(a, 3):
                w = float(quad[a] * quad[b])
                pairs[a, b] = pairs[b, a] = (lame_k * w, shear_k * w, shear_k * (2.0 * w))
        for c in range(3):
            for j in range(5):
                for i, g in enumerate(line(deriv, [u[c, i, j, k] for i in range(5)])):
                    gx[c, i, j] = g
        for i in range(5):
            gy = [line(deriv, [u[c, i, j, k] for j in range(5)]) for c in range(3)]
            ys = [[], [], []]
            for j in range(5):
                lw, mw, mw2 = pairs[kind[i], kind[j]]
                g0, g1, g2 = [[gx[c, i, j], gy[c][j], gz[c, i, j, k]] for c in range(3)]
                dilated = lw * (g0[0] + g1[1] + g2[2])
                s01 = mw * (g0[1] + g1[0])
                s02 = mw * (g0[2] + g2[0])
                s12 = mw * (g1[2] + g2[1])
                side[0, i, j] = dilated + mw2 * g0[0]
                side[1, i, j] = s01
                cross[0, i, j, k] = s02
                cross[1, i, j, k] = s12
                cross[2, i, j, k] = dilated + mw2 * g2[2]
                ys[0].append(s01)
                ys[1].append(dilated + mw2 * g1[1])
                ys[2].append(s12)
            for c in range(3):
                for j, value in enumerate(line(deriv_t, ys[c])):
                    planes[c, i, j, k] = value
        for j in range(5):
            for c in range(3):
                v = [side[c, i, j] if c < 2 else cross[0, i, j, k] for i in range(5)]
                for i, value in enumerate(line(deriv_t, v)):
                    planes[c, i, j, k] += value
        return carry

    lax.fori_loop(0, 5, plane, 0)

    def depth_sums(i, carry):
        for j in range(5):
            for c in range(3):
                v = line(deriv_t, [cross[c, i, j, k] for k in range(5)])
                v = [v[k] + planes[c, i, j, k] for k in range(5)]
                out[c, i, j, 0] = v[0] + shallower(v[4])
                for k in range(1, 4):
                    out[c, i, j, k] = v[k]
        return carry

    lax.fori_loop(0, 5, depth_sums, 0)
    sub = rows_of()

    def fold(k, carry):
        for c in range(3):
            for i in range(5):
                low, high = out[c, i, 0, k], out[c, i, 4, k]
                out[c, i, 0, k] = low + jnp.where(sub % 4 == 0, 0.0, pltpu.roll(high, 1, 0))
                out[c, i, 4, k] = high + jnp.where(sub % 4 == 3, 0.0, pltpu.roll(low, 7, 0))
            for j in range(5):
                low, high = out[c, 0, j, k], out[c, 4, j, k]
                out[c, 0, j, k] = low + jnp.where(sub < 4, 0.0, pltpu.roll(high, 4, 0))
                out[c, 4, j, k] = high + jnp.where(sub < 4, pltpu.roll(low, 4, 0), 0.0)
        return carry

    lax.fori_loop(0, 4, fold, 0)


def rolled(x, amount, axis=0):
    amount = amount % x.shape[axis]
    return pltpu.roll(x, amount, axis) if amount else x


def parity_x():
    return position("gx") % 2


def parity_y():
    return along_y() % 2


def sort_out(odd, low, high):
    return jnp.where(odd == 1, low, high), jnp.where(odd == 1, high, low)


def pack_x(force, first, second):
    sub, odd = rows_of(), parity_x()
    for c in range(3):
        for j in range(5):
            for half in range(2):
                at = (c * 5 + j) * 2 + half
                a, b = force[c, 0, j, 2 * half], force[c, 0, j, 2 * half + 1]
                low = jnp.where(sub < 4, a, rolled(b, 4))
                a, b = force[c, 4, j, 2 * half], force[c, 4, j, 2 * half + 1]
                high = jnp.where(sub < 4, rolled(a, 4), b)
                first[at], second[at] = sort_out(odd, low, high)


def pack_y(force, low, high):
    sub = rows_of()
    for c in range(3):
        for i in range(5):
            a, b = force[c, i, 0, 0], rolled(force[c, i, 4, 0], -3)
            for k in range(1, 4):
                a = jnp.where(sub % 4 == k, rolled(force[c, i, 0, k], k), a)
                b = jnp.where(sub % 4 == k, rolled(force[c, i, 4, k], k - 3), b)
            low[c * 5 + i] = a
            high[c * 5 + i] = b


def add_x(force, first, second):
    sub, odd = rows_of(), parity_x()
    for c in range(3):
        for j in range(5):
            for half in range(2):
                at = (c * 5 + j) * 2 + half
                r, s = sort_out(odd, first[at], second[at])
                force[c, 0, j, 2 * half] += jnp.where(sub < 4, r, 0.0)
                force[c, 0, j, 2 * half + 1] += jnp.where(sub < 4, rolled(r, 4), 0.0)
                force[c, 4, j, 2 * half] += jnp.where(sub < 4, 0.0, rolled(s, 4))
                force[c, 4, j, 2 * half + 1] += jnp.where(sub < 4, 0.0, s)


def add_y(force, first, second):
    sub, odd = rows_of(), parity_y()
    for c in range(3):
        for i in range(5):
            r, s = sort_out(odd, first[c * 5 + i], second[c * 5 + i])
            for k in range(4):
                force[c, i, 0, k] += jnp.where(sub % 4 == 0, rolled(r, -k), 0.0)
                force[c, i, 4, k] += jnp.where(sub % 4 == 3, rolled(s, 3 - k), 0.0)


def edge_rows(low, high, came1, came2, first, second):
    sub, odd, odd_y = rows_of(), parity_x(), parity_y()
    for c in range(3):
        came = [[sort_out(odd, came1[at], came2[at]) for at in range((c * 5 + j) * 2, (c * 5 + j) * 2 + 2)] for j in (0, 4)]
        for i in range(5):
            rows = [low[c * 5 + i], high[c * 5 + i]]
            if i in (0, 4):
                start, side = i, i // 4
                for end, row in ((0, 0), (1, 3)):
                    for k in range(4):
                        r = rolled(came[end][k // 2][side], start + k - (4 * (k % 2) + row))
                        rows[end] = rows[end] + jnp.where(sub == start + k, r, 0.0)
            first[c * 5 + i], second[c * 5 + i] = sort_out(odd_y, *rows)


def first_edge_kernel(low, high, came1, came2, rows_low, rows_high, crater1, crater2, after, first, second, ends, semaphores):
    copies = fetch(
        [(c.at[:, pl.ds(24 * h, 8), :], ends.at[n, :, pl.ds(8 * h, 8), :]) for n, c in enumerate((crater1, crater2)) for h in range(2)],
        semaphores,
    )
    edge_rows(low, high, came1, came2, first, second)
    odd, odd_y = parity_x(), parity_y()
    regions = sort_out(odd, came1[30], came2[30])
    for n, value in enumerate((low[15], regions[0], regions[1])):
        first[15 + n] = value
        second[15 + n] = value
    for copy in copies:
        copy.wait()
    for f in range(5):
        for t in range(2):
            lanes = slice(128 * t, 128 * t + 128)
            at = 18 + f * 4 + t * 2
            first[at], second[at] = sort_out(odd_y, rows_low[f * 2 + t], rows_high[f * 2 + t])
            found = []
            for row in (0, 15):
                sides = sort_out(odd, ends[0, f, row : row + 1, lanes], ends[1, f, row : row + 1, lanes])
                found.append(jnp.concatenate(list(sides) * 4, axis=0))
            first[at + 1], second[at + 1] = sort_out(odd_y, *found)


def second_edge_kernel(low, high, came1, came2, after, first, second, token):
    edge_rows(low, high, came1, came2, first, second)
    token[...] = after[...]


def region_grid(own, x1, x2, y1, y2):
    xl, xh = sort_out(parity_x(), x1[30], x2[30])
    yl, yh = [list(v) for v in zip(*[sort_out(parity_y(), y1[n], y2[n]) for n in (15, 16, 17)])]
    return [[yl[1], xl, yh[1]], [yl[0], own, yh[0]], [yl[2], xh, yh[2]]]


def shared_density(grid):
    sub = rows_of()
    across = []
    for y in range(3):
        low, mid, high = grid[0][y], grid[1][y], grid[2][y]
        turned = rolled(mid, 4)
        across.append([jnp.where(sub < 4, rolled(low, 4), turned), mid, jnp.where(sub < 4, turned, rolled(high, 4))])
    found = [[None] * 3 for _ in range(3)]
    for x in range(3):
        low, mid, high = across[0][x], across[1][x], across[2][x]
        found[x][0] = jnp.where(sub % 4 == 0, rolled(low, -3), rolled(mid, 1))
        found[x][1] = mid
        found[x][2] = jnp.where(sub % 4 == 3, rolled(high, 3), rolled(mid, -1))
    sums = []
    for x in ((1,), (0, 1), (1, 2)):
        row = []
        for y in ((1,), (0, 1), (1, 2)):
            total = sum(found[a][b] for a in x for b in y)
            row.append((total + shallower(total), total))
        sums.append(row)
    return sums


def mass_scales(sums):
    return [[[1.0 / s for s in pair] for pair in row] for row in sums]


def edge_kind(i):
    return 1 if i == 0 else 2 if i == 4 else 0


def accel_scale(i, j, k):
    return float(-1.0 / (half_size**3 * quad[i] * quad[j] * quad[k]))


def first_kernel(u, v, a, region, material, b_out, f_out, x1, x2, y_low, y_high, token,
                 elem, gx, gz, cross, planes, side, u_in, v_in, a_in, wide_u, wide_b, kept_u, kept_b, b_held, semaphores):
    copies = [tile_copies(f, h, semaphores, 4 * n) for n, (f, h) in enumerate(((u, u_in), (v, v_in), (a, a_in)))]
    for t in range(4):
        for copy in copies:
            copy[t].start()
    table = depth_table()
    region_now = region[...]

    def put_u(l, value):
        elem[:, :, :, l] = value

    def put_b(l, value):
        b_held[:, :, :, l] = value

    for half in range(2):
        for t in (2 * half, 2 * half + 1):
            for copy in copies:
                copy[t].wait()
        for t in (2 * half, 2 * half + 1):
            lanes = slice(128 * (t % 2), 128 * (t % 2) + 128)
            for c in range(3):
                for i in range(5):
                    for j in range(5):
                        for ex in range(2):
                            at = (t, rows_at(i, j, ex, c), slice(None))
                            to = (c, i, j, slice(4 * ex, 4 * ex + 4), lanes)
                            step = time_step * v_in[at] + (0.5 * time_step**2) * a_in[at]
                            uu = u_in[at] + step
                            wide_u[to] = uu
                            wide_b[to] = uu + step
        to_elements(half, wide_u, table, kept_u, put_u)
        to_elements(half, wide_b, table, kept_b, put_b)
    save_b = pltpu.make_async_copy(b_held, b_out, semaphores.at[12])
    save_b.start()
    internal(elem, f_out, lookup(material, 1, region_now), lookup(material, 2, region_now), gx, gz, cross, planes, side)
    pack_x(f_out, x1, x2)
    pack_y(f_out, y_low, y_high)
    x1[30] = region_now
    x2[30] = region_now
    y_low[15] = region_now
    token[...] = region_now
    save_b.wait()


def second_kernel(b, f, came_x1, came_x2, came_y1, came_y2, region, material, a_out, f_out, x1, x2, y_low, y_high, scales, token,
                  elem, gx, gz, cross, planes, side):
    region_now = region[...]
    token[...] = region_now
    a_out[...] = f[...]
    add_x(a_out, came_x1, came_x2)
    add_y(a_out, came_y1, came_y2)
    grid = region_grid(region_now, came_x1, came_x2, came_y1, came_y2)
    inverse = mass_scales(shared_density([[lookup(material, 0, r) for r in row] for row in grid]))
    for x in range(3):
        for y in range(3):
            for z in range(2):
                scales[x, y, z] = inverse[x][y][z]
    for i in range(5):
        for j in range(5):
            for k in range(4):
                scale = scales[edge_kind(i), edge_kind(j), min(k, 1)] * accel_scale(i, j, k)
                for c in range(3):
                    value = a_out[c, i, j, k] * scale
                    a_out[c, i, j, k] = value
                    elem[c, i, j, k] = b[c, i, j, k] + time_step**2 * value
    internal(elem, f_out, lookup(material, 1, region_now), lookup(material, 2, region_now), gx, gz, cross, planes, side)
    pack_x(f_out, x1, x2)
    pack_y(f_out, y_low, y_high)


def spread_surface(source, held, count):
    lane = lanes_of((24, 128))
    for n in range(27):
        at = 8 * n
        tile, shift = at // 128, (128 - at % 128) % 128
        moved = rolled(source[:, 128 * tile : 128 * tile + 128], shift, 1)
        held[n] = jnp.where(lane < count, moved, 0.0)


def surface_piece(held, y, x, c):
    return held[c * 9 + x, pl.ds(y, 4, stride=4), :] if y < 16 else held[c * 9 + x, 16:17, :]


def place_kernel(a1, surf1, u, v, a, after, u_out, v_part, u_in, v_in, a_in, tall, surface, semaphores):
    copies = [tile_copies(f, h, semaphores, 4 * n) for n, (f, h) in enumerate(((u, u_in), (v, v_in), (a, a_in)))]
    for t in range(4):
        for copy in copies:
            copy[t].start()
    spread_surface(surf1, surface, 1)
    to_nodes(lambda l: a1[:, :, :, l], depth_table(back=True), tall)
    saves = tile_copies(u_out, u_in, semaphores, 12, out=True)
    for t in range(4):
        for copy in copies:
            copy[t].wait()
        for rows, y, x, c, accel in node_pieces(tall, t):
            at = (t, rows, slice(None))
            if t == 0:
                accel = accel + surface_piece(surface, y, x, c)
            vv, aa = v_in[at], a_in[at]
            u_in[at] = u_in[at] + 2.0 * time_step * vv + time_step**2 * (aa + accel)
            v_part[at] = vv + (0.5 * time_step) * (aa + 2.0 * accel)
        saves[t].start()
    for save in saves:
        save.wait()


def last_kernel(v_part, f, x1, x2, y1, y2, scales, surf1, surf2, v_out, a_out, v_held, a_held, tall, surface, force, semaphores):
    force[...] = f[...]
    add_x(force, x1, x2)
    add_y(force, y1, y2)
    for i in range(5):
        for j in range(5):
            for k in range(4):
                scale = scales[edge_kind(i), edge_kind(j), min(k, 1)] * accel_scale(i, j, k)
                for c in range(3):
                    force[c, i, j, k] = force[c, i, j, k] * scale
    spread_surface(surf1, surface.at[0], 1)
    spread_surface(surf2, surface.at[1], 5)
    to_nodes(lambda l: force[:, :, :, l], depth_table(back=True), tall)
    saves = tile_copies(v_out, v_held, semaphores, 0, out=True) + tile_copies(a_out, a_held, semaphores, 4, out=True)
    for t in range(4):
        for rows, y, x, c, accel in node_pieces(tall, t):
            at = (t, rows, slice(None))
            if t == 0:
                accel = accel + surface_piece(surface.at[0], y, x, c) + surface_piece(surface.at[1], y, x, c)
            a_held[at] = accel
            v_held[at] = v_part[at] + (0.5 * time_step) * accel
        saves[t].start()
        saves[4 + t].start()
    for save in saves:
        save.wait()


def whole():
    return pl.BlockSpec(memory_space=pltpu.VMEM)


def scalars():
    return pl.BlockSpec(memory_space=pltpu.SMEM)


def call(kernel, ins, outs, scratch, smem=(), away=(), out_away=(), mib=10, copies=0):
    def spec(n):
        return scalars() if n in smem else pl.BlockSpec(memory_space=pltpu.HBM) if n in away else whole()

    scratch = [pltpu.VMEM(s, f32) if isinstance(s, tuple) else s for s in scratch]
    return pl.pallas_call(
        kernel,
        out_shape=[jax.ShapeDtypeStruct(s, f32) for s in outs],
        in_specs=[spec(n) for n in range(len(ins))],
        out_specs=[pl.BlockSpec(memory_space=pltpu.HBM) if n in out_away else whole() for n in range(len(outs))],
        scratch_shapes=scratch + ([pltpu.SemaphoreType.DMA((copies,))] if copies else []),
        compiler_params=pltpu.CompilerParams(vmem_limit_bytes=mib * 1024 * 1024),
    )(*ins)


def fetch(pairs, semaphores):
    copies = [pltpu.make_async_copy(source, target, semaphores.at[n]) for n, (source, target) in enumerate(pairs)]
    for copy in copies:
        copy.start()
    return copies


element_shape = (3, 5, 5, 4, 8, 128)
lines_shape = (3, 5, 5, 5, 8, 128)
internal_scratch = [lines_shape, (3, 5, 5, 8, 128), lines_shape, lines_shape, lines_shape, (2, 5, 5, 8, 128)]


def exchange(axis, first, second):
    count = lax.axis_size(axis)
    pairs = [(i, i + 1) for i in range(1, count - 1, 2)]
    first = lax.ppermute(first, axis, [(i, i ^ 1) for i in range(count)])
    return first, lax.ppermute(second, axis, pairs + [(j, i) for i, j in pairs])


def surface_tables():
    lane = np.arange(128)
    j, ey = lane // 8, lane % 8
    used = (j < 5) & (ey < 6)
    place = np.where(used, ey + 1, -9)
    source = lane[:, None]
    centre = source == place
    meet = centre | ((j == 0) & (source == place - 1)) | ((j == 4) & (source == place + 1))
    along = np.zeros((128, 128))
    for a in range(40):
        for b in range(40):
            if a % 8 == b % 8 and a % 8 < 6:
                along[a, b] = deriv[b // 8, a // 8]
    node = np.where(used, 4 * (ey - 1) + j, -9)
    fold = (lane[:, None] == node) & (lane[:, None] < 17)
    keep = fold & ((j < 4) & (ey < 5) | (j == 4) & (ey == 4))
    return np.stack([centre, meet, along, along.T, fold, keep]).astype(np.float32)


def full_dot(x, y, back=False):
    dims = (((1,), (1 if back else 0,)), ((), ()))
    return lax.dot_general(x, y, dims, precision=lax.Precision.HIGHEST, preferred_element_type=f32)


def deposit(faces, nodes_y, base_x, base_y, total):
    rows = faces.shape[1]
    sub = rows_of((8, 512)).astype(f32)
    total[...] = jnp.zeros_like(total)

    def one(step, carry):
        def wide(q):
            block = faces[q, pl.ds(4 * step, 4), :]
            return jnp.concatenate([block[n : n + 1] for n in range(4)], axis=1)

        ids = wide(3)
        node_x = jnp.floor((ids + 0.5) * (1.0 / nodes_y))
        rel_y = jnp.broadcast_to(ids - node_x * nodes_y - base_y, (8, 512))
        rel_x = jnp.broadcast_to(node_x - base_x, (8, 512))
        left = []
        hits = [(rel_x - i == 4.0 * sub) & (sub < 4.0) for i in range(5)]
        parts = [split_three(wide(c)) for c in range(3)]
        for part in range(3):
            for c in range(3):
                value = jnp.broadcast_to(parts[c][part].astype(f32), (8, 512))
                left += [jnp.where(hit, value, 0.0) for hit in hits]
        right = [jnp.where((rel_y - j == 4.0 * sub) & (sub < 6.0), 1.0, 0.0) for j in range(5)]
        right.append(jnp.zeros((88, 512), f32))
        left, right = jnp.concatenate(left, axis=0), jnp.concatenate(right, axis=0)
        total[...] += lax.dot_general(
            left.astype(jnp.bfloat16), right.astype(jnp.bfloat16), (((1,), (1,)), ((), ())), preferred_element_type=f32
        )
        return carry

    lax.fori_loop(0, rows // 4, one, 0)


def top_grid(rows, z):
    sub, lane = rows_of(), lanes_of()
    out = jnp.zeros((8, 128), f32)
    for x in range(3):
        for y in range(3):
            row = jnp.broadcast_to(rows[x][y], (8, 128))
            for ex in range(2):
                here = (sub == 2 * x + ex) & (lane >= 4 * y - 2) & (lane < 4 * y + 2) & (lane < 8)
                out = jnp.where(here, rolled(row, 4 * y - 2 - 8 * z - 4 * ex, 1), out)
    return out


def region_rows(bottoms, count_x):
    gx, place, count_gy = position("gx"), along_y(), lax.axis_size("gy")
    last_y = lax.axis_size("grp") * count_gy - 1
    found = []
    for x in range(3):
        found.append([])
        for y in range(3):
            px, py = gx + x - 1, place + y - 1
            inside = (px >= 0) & (px < count_x) & (py >= 0) & (py <= last_y)
            cx, cy = jnp.clip(px, 0, count_x - 1), jnp.clip(py, 0, last_y)
            rank = (cy // count_gy) * (count_x * count_gy) + cx * count_gy + cy % count_gy
            row = bottoms[pl.ds(pl.multiple_of(rank * 24 + 16, 8), 1), :]
            found[x].append(jnp.where(inside, row, 0.0))
    return found


def respond(total, grid, material, tables, out1, out2):
    sub, lane = rows_of(), lanes_of()
    top, below = top_grid(grid, 0), top_grid(grid, 1)
    centre, meet, along, along_t, fold, keep = [tables[n] for n in range(6)]
    sums0 = full_dot(lookup(material, 0, top), meet)
    sums1 = full_dot(lookup(material, 0, below), meet)
    lame = rolled(full_dot(lookup(material, 1, top), centre), -1)
    shear = rolled(full_dot(lookup(material, 2, top), centre), -1)
    weight_y = jnp.ones((8, 128), f32)
    for j in range(5):
        weight_y = jnp.where(lane // 8 == j, float(quad[j]), weight_y)

    def inverse(sums):
        mid = rolled(sums, -1)
        found = {0: mid + sums, 1: mid, 4: mid + rolled(sums, -2)}
        found = {i: jnp.where(s > 0.0, 1.0 / (s * weight_y), 0.0) for i, s in found.items()}
        found[2] = found[3] = found[1]
        return found

    light, heavy = inverse(sums0), inverse(sums0 + sums1)
    first = [[None] * 5 for _ in range(3)]
    moved = [[None] * 5 for _ in range(3)]
    for c in range(3):
        for i in range(5):
            at = (c * 5 + i) * 8
            force = total[at : at + 8] + total[at + 120 : at + 128] + total[at + 240 : at + 248]
            first[c][i] = force * light[i] * -accel_scale(i, 2, 0) * float(quad[2])
            moved[c][i] = first[c][i] * time_step**2
    gx = [line(deriv, moved[c]) for c in range(3)]
    gy = full_dot(jnp.concatenate([moved[c][i] for c in range(3) for i in range(5)], axis=0), along)
    gy = [[gy[(c * 5 + i) * 8 : (c * 5 + i) * 8 + 8] for i in range(5)] for c in range(3)]
    lame_w, shear_w = lame * weight_y * 2.0, shear * weight_y * 2.0
    d00 = float(deriv[0, 0])
    sx = [[], [], []]
    sy = [[], [], []]
    sz = [[], [], []]
    qs = [[], [], []]
    pressed = []
    for i in range(5):
        lw, mw = lame_w * float(quad[i]), shear_w * float(quad[i])
        d = [moved[c][i] for c in range(3)]
        gz = [d00 * x for x in d]
        dilated = lw * (gx[0][i] + gy[1][i] + gz[2])
        s01 = mw * (gx[1][i] + gy[0][i])
        s02 = mw * (gx[2][i] + gz[0])
        s12 = mw * (gy[2][i] + gz[1])
        for c, value in enumerate((dilated + 2.0 * mw * gx[0][i], s01, s02)):
            sx[c].append(value)
        for c, value in enumerate((s01, dilated + 2.0 * mw * gy[1][i], s12)):
            sy[c].append(value)
        for c, value in enumerate((s02, s12, dilated + 2.0 * mw * gz[2])):
            sz[c].append(value)
        for c, value in enumerate((mw * d[0], mw * d[1], (lw + 2.0 * mw) * d[2])):
            qs[c].append(value)
        pressed.append(lw * d[2])
    ydiv = full_dot(jnp.concatenate(sy[0] + sy[1] + sy[2] + pressed + qs[1], axis=0), along_t)
    ydiv = [[ydiv[(n * 5 + i) * 8 : (n * 5 + i) * 8 + 8] for i in range(5)] for n in range(5)]
    xdiv = [line(deriv_t, v) for v in sx + [pressed, qs[0]]]
    base = [xdiv[3], ydiv[3], [p + q for p, q in zip(xdiv[4], ydiv[4])]]
    second = {}
    for c in range(3):
        for i in range(5):
            for l in range(5):
                stiff = float(sum(deriv[k, l] * quad[k] * deriv[k, 0] for k in range(1, 5)))
                value = float(deriv[0, l] * quad[0]) * sz[c][i] + stiff * qs[c][i]
                if l:
                    value = value + float(deriv[l, 0] * quad[l]) * base[c][i]
                else:
                    value = value + float(quad[0]) * (xdiv[c][i] + ydiv[c][i])
                scale = (heavy if l == 4 else light)[i]
                second[c, i, l] = value * scale * (accel_scale(i, 2, l) * float(quad[2]))
    rows1, rows2 = [], []
    for c in range(3):
        for x in range(9):
            own = 1 if x < 4 else 2
            rows1.append(jnp.where(sub == 0, rolled(first[c][x - 4 * (own - 1)], -own), 0.0))
            block = jnp.zeros((8, 128), f32)
            for l in range(5):
                for ex in range(4):
                    i = x - 4 * (ex - 1)
                    if 0 <= i <= 4:
                        block = block + jnp.where(sub == l, rolled(second[c, i, l], l - ex), 0.0)
            rows2.append(block)
    blank = [jnp.zeros((40, 128), f32)]
    out1[...] = full_dot(keep[0:24], jnp.concatenate(rows1 + blank, axis=0), back=True)
    out2[...] = full_dot(fold[0:24], jnp.concatenate(rows2 + blank, axis=0), back=True)


def position(axis):
    return lax.axis_index(axis)


def along_y():
    return lax.axis_index("grp") * lax.axis_size("gy") + lax.axis_index("gy")


def primitives(state):
    inverse = 1.0 / state[0]
    v = [state[1 + c] * inverse for c in range(3)]
    p = (gamma_gas - 1.0) * (state[4] - 0.5 * (state[1] * v[0] + state[2] * v[1] + state[3] * v[2]))
    return v + [p, jnp.sqrt(gamma_gas * p * inverse), state[4] + p]


def flux(state, prim, d):
    out = [state[1 + d]] + [state[1 + c] * prim[d] for c in range(3)] + [prim[5] * prim[d]]
    out[1 + d] = out[1 + d] + prim[3]
    return out, jnp.abs(prim[d]) + prim[4]


def twice_face(low, high):
    fastest = jnp.maximum(low[2], high[2])
    return [fl + fh - fastest * (uh - ul) for ul, uh, fl, fh in zip(low[0], high[0], low[1], high[1])]


def turned_change(state, prim, d, axis, ends):
    size = state[0].shape[axis]
    fluxes, speed = flux(state, prim, d)
    up = lambda x: pltpu.roll(x, size - 1, axis)
    high = ([up(x) for x in state], [up(x) for x in fluxes], up(speed))
    upper = twice_face((state, fluxes, speed), high)
    if ends is None:
        return [g - pltpu.roll(g, 1, axis) for g in upper]
    upper = [jnp.where(ends[1], 2.0 * f, g) for f, g in zip(fluxes, upper)]
    return [g - jnp.where(ends[0], 2.0 * f, pltpu.roll(g, 1, axis)) for f, g in zip(fluxes, upper)]


def start_kernel(nodes_y, density, momentum, energy, dest, slot, region, bottoms, first, second, rows_low, rows_high,
                 region_out, cells, dest_in, slot_in, region_in, semaphores):
    copies = fetch(
        [(dest, dest_in), (slot, slot_in), (region, region_in), (density, cells.at[0]),
         (momentum, cells.at[pl.ds(1, 3)]), (energy, cells.at[4])],
        semaphores,
    )
    for copy in copies:
        copy.wait()
    sub, lane = rows_of(), lanes_of()
    pick = jnp.where(lane == 125 + sub, 1.0, 0.0)
    pieces = []
    odd = parity_x()
    for f in range(5):
        columns = jnp.concatenate([cells[f, x, :, 128:256] for x in range(4)], axis=0)
        pieces.append(full_dot(pick, columns, back=True)[0:3])
        for out, down in ((first, odd), (second, 1 - odd)):
            out[f, 0:32, :] = cells[f, 3 - 3 * down]
            out[f, 32:64, :] = cells[f, 2 - down]
        for t in range(2):
            lanes = slice(128 * t, 128 * t + 128)
            for out, pair in ((rows_low, (0, 1)), (rows_high, (31, 30))):
                out[f * 2 + t] = jnp.concatenate([cells[f, x, r : r + 1, lanes] for r in pair for x in range(4)], axis=0)
    count_gy, count_x = lax.axis_size("gy"), lax.axis_size("gx")
    target, node = dest_in[...].astype(f32), slot_in[...].astype(f32)
    grp = jnp.floor((target + 0.5) * (1.0 / (count_gy * count_x)))
    rest = target - grp * (count_gy * count_x)
    gx = jnp.floor((rest + 0.5) * (1.0 / count_gy))
    gy = rest - gx * count_gy
    i = jnp.floor((node + 0.5) * (1.0 / 17.0))
    j = node - 17.0 * i
    pieces.append((8.0 * gx + i) * nodes_y + 16.0 * (grp * count_gy + gy) + j)
    region_now = jnp.concatenate([region_in[0], region_in[1]], axis=0).astype(f32) + 1.0
    region_out[...] = region_now
    found = jnp.zeros((8, 128), f32)
    for z in range(2):
        found = jnp.where(lane == 8 * z + sub, jnp.broadcast_to(region_now[:, z : z + 1], (8, 128)), found)
    pieces.append(jnp.broadcast_to(jnp.sum(found, axis=0, keepdims=True), (8, 128)))
    block = jnp.concatenate(pieces, axis=0)
    for n in range(bottoms.shape[0]):
        bottoms[n] = block


def crater_kernel(density, momentum, energy, came1, came2, rows1, rows2, after, out, token,
                  wide, mid, prims, face, fluxes, semaphores):
    planes, inner = pl.ds(2, 4), pl.ds(0, 32)
    copies = fetch(
        [(density, wide.at[0, planes, inner]), (momentum, wide.at[pl.ds(1, 3), planes, inner]),
         (energy, wide.at[4, planes, inner])],
        semaphores,
    )
    place, last_y = along_y(), lax.axis_size("grp") * lax.axis_size("gy") - 1
    gx, last_x = position("gx"), lax.axis_size("gx") - 1
    odd, odd_y = parity_x(), parity_y()
    for f in range(5):
        low, high = sort_out(odd, came1[f], came2[f])
        for p, value in ((0, low[32:64]), (1, low[0:32]), (6, high[0:32]), (7, high[32:64])):
            wide[f, p, 0:32, :] = value
            wide[f, p, 32:40, :] = value[0:8]
    token[...] = after[...]
    for copy in copies:
        copy.wait()
    for f in range(5):
        for x in range(4):
            wide[f, 2 + x, 32:40, :] = wide[f, 2 + x, 24:32, :]
        for t in range(2):
            lanes = slice(128 * t, 128 * t + 128)
            at = 18 + f * 4 + t * 2
            below, above = sort_out(odd_y, rows1[at], rows2[at])
            sides_below, sides_above = sort_out(odd_y, rows1[at + 1], rows2[at + 1])

            def put(p, row, edge, value):
                clamped = jnp.where(edge == 0, place == 0, place == last_y)
                at_edge = wide[f, p, 31 * edge : 31 * edge + 1, lanes]
                wide[f, p, row : row + 1, lanes] = jnp.where(clamped, at_edge, value)

            for x in range(4):
                put(2 + x, 39, 0, below[x : x + 1])
                put(2 + x, 38, 0, below[4 + x : 5 + x])
                put(2 + x, 32, 1, above[x : x + 1])
                put(2 + x, 33, 1, above[4 + x : 5 + x])
            for p, n in ((1, 0), (6, 1)):
                put(p, 39, 0, sides_below[n : n + 1])
                put(p, 32, 1, sides_above[n : n + 1])

    @pl.when(gx == 0)
    def _():
        for f in range(5):
            wide[f, 0] = wide[f, 2]
            wide[f, 1] = wide[f, 2]

    @pl.when(gx == last_x)
    def _():
        for f in range(5):
            wide[f, 6] = wide[f, 5]
            wide[f, 7] = wide[f, 5]

    lane = lanes_of((40, 256))
    ends = (lane == 0, lane == 255)

    def step(source, low, high, put):
        def along_x(p):
            state = [source[f, p] for f in range(5)]
            prim = primitives(state)
            return state, prim, flux(state, prim, 0)

        state, prim, (fx, speed) = along_x(low - 1)
        next_state, next_prim, (next_fx, next_speed) = along_x(low)
        g = twice_face((state, fx, speed), (next_state, next_fx, next_speed))
        for f in range(5):
            face[f] = g[f]
            fluxes[f] = next_fx[f]
        for n in range(6):
            prims[n] = next_prim[n]
        fluxes[5] = next_speed

        def plane(p, carry):
            state = [source[f, p] for f in range(5)]
            prim = [prims[n] for n in range(6)]
            next_state, next_prim, (next_fx, next_speed) = along_x(p + 1)
            g = twice_face((state, [fluxes[f] for f in range(5)], fluxes[5]), (next_state, next_fx, next_speed))
            change = [g[f] - face[f] for f in range(5)]
            for f in range(5):
                face[f] = g[f]
                fluxes[f] = next_fx[f]
            for n in range(6):
                prims[n] = next_prim[n]
            fluxes[5] = next_speed
            change = [a + b for a, b in zip(change, turned_change(state, prim, 1, 0, None))]
            change = [a + b for a, b in zip(change, turned_change(state, prim, 2, 1, ends))]
            for f in range(5):
                put(f, p, state[f] - (0.5 * cell_ratio) * change[f])
            return carry

        lax.fori_loop(low, high, plane, 0)

    def put_mid(f, p, value):
        mid[f, p] = value

    def put_out(f, p, value):
        out[f, p - 2] = value[0:32]

    step(wide, 1, 7, put_mid)

    @pl.when(gx == 0)
    def _():
        for f in range(5):
            mid[f, 1] = mid[f, 2]

    @pl.when(gx == last_x)
    def _():
        for f in range(5):
            mid[f, 6] = mid[f, 5]

    for f in range(5):
        for p in range(2, 6):
            edge = mid[f, p, 39:40, :]
            mid[f, p, 39:40, :] = jnp.where(place == 0, mid[f, p, 0:1, :], edge)
            edge = mid[f, p, 32:33, :]
            mid[f, p, 32:33, :] = jnp.where(place == last_y, mid[f, p, 31:32, :], edge)
    step(mid, 2, 6, put_out)


def bottom_tractions(bottoms, count_x, faces):
    shape = (count_x, 128)
    sub, lane = rows_of(shape), lanes_of(shape)
    count_gy = lax.axis_size("gy")

    def columns(q):
        parts = []
        for y in range(4):
            start = (y // count_gy * count_x * count_gy + y % count_gy) * 24 + q
            parts.append(bottoms[pl.ds(start, count_x, stride=24 * count_gy), :])
        found = []
        for x in range(4):
            total = rolled(parts[0], -32 * x, 1)
            for y in range(1, 4):
                total = jnp.where(lane // 32 == y, rolled(parts[y], 32 * (y - x), 1), total)
            found.append(total)
        return found

    cells = [[columns(f * 3 + z) for f in range(5)] for z in range(3)]
    state = [[[cells[z][f][x] for f in range(5)] for x in range(4)] for z in range(3)]
    ends_y = (lane == 0, lane == 127)

    def across_x(states, prims):
        fluxes = [flux(s, p, 0) for s, p in zip(states, prims)]
        data = [(s, f, a) for s, (f, a) in zip(states, fluxes)]
        up = lambda x: rolled(x, -1)
        wrap = ([up(v) for v in data[0][0]], [up(v) for v in data[0][1]], up(data[0][2]))
        upper = [twice_face(data[x], data[x + 1] if x < 3 else wrap) for x in range(4)]
        upper[3] = [jnp.where(sub == count_x - 1, 2.0 * f, g) for f, g in zip(data[3][1], upper[3])]
        below = [jnp.where(sub == 0, 2.0 * f, rolled(g, 1)) for f, g in zip(data[0][1], upper[3])]
        lower = [below] + upper[:3]
        return [[a - b for a, b in zip(u, l)] for u, l in zip(upper, lower)]

    def advanced(above, here, under, prim_above, prim_here, prim_under):
        changes = across_x(here, prim_here)
        out = []
        for x in range(4):
            change = [a + b for a, b in zip(changes[x], turned_change(here[x], prim_here[x], 1, 1, ends_y))]
            fz, az = flux(here[x], prim_here[x], 2)
            fa, aa = flux(above[x], prim_above[x], 2)
            lower = twice_face((above[x], fa, aa), (here[x], fz, az))
            if under is None:
                upper = [2.0 * f for f in fz]
            else:
                fu, au = flux(under[x], prim_under[x], 2)
                upper = twice_face((here[x], fz, az), (under[x], fu, au))
            out.append([s - (0.5 * cell_ratio) * (c + u - l) for s, c, u, l in zip(here[x], change, upper, lower)])
        return out

    prims = [[primitives(state[z][x]) for x in range(4)] for z in range(3)]
    middle = advanced(state[0], state[1], state[2], prims[0], prims[1], prims[2])
    deepest = advanced(state[1], state[2], None, prims[1], prims[2], None)
    prim_mid, prim_deep = [primitives(s) for s in middle], [primitives(s) for s in deepest]
    final = advanced(middle, deepest, None, prim_mid, prim_deep, None)
    ids = columns(15)
    for x in range(4):
        s, prim = final[x], primitives(final[x])
        at = pl.ds(x * count_x, count_x)
        faces[0, at, :] = face_area * s[1] * prim[2]
        faces[1, at, :] = face_area * s[2] * prim[2]
        faces[2, at, :] = face_area * (s[3] * prim[2] + prim[3])
        faces[3, at, :] = ids[x]


def surface_kernel(nodes_y, count_x, bottoms, material, tables, after, out1, out2, total, faces, held, semaphores):
    copies = fetch([(tables, held)], semaphores)
    base_x = (8 * position("gx") - 4).astype(f32)
    base_y = (16 * along_y() - 4).astype(f32)
    bottom_tractions(bottoms, count_x, faces)
    deposit(faces, nodes_y, base_x, base_y, total)
    copies[0].wait()
    respond(total, region_rows(bottoms, count_x), material, held, out1, out2)


def shards(density, momentum, energy, displacement, velocity_field, acceleration, material, element_region_index,
           face_dest, face_slot):
    along, rank = ("grp", "gy"), ("grp", "gx", "gy")
    nodes_y = 16 * lax.axis_size(along) + 1
    count_x, devices = lax.axis_size("gx"), lax.axis_size(rank)
    crater = (density, momentum, energy)
    u, v, a = [jnp.transpose(x, (1, 2, 0, 3)) for x in (displacement, velocity_field, acceleration)]
    register, held_shape = (8, 128), (4, 1224, 128)
    bottoms, crater1, crater2, rows_low, rows_high, region = call(
        functools.partial(start_kernel, float(nodes_y)),
        crater + (face_dest.reshape(1, -1), face_slot, element_region_index),
        [(devices, 24, 128), (5, 64, 256), (5, 64, 256), (10, 8, 128), (10, 8, 128), register],
        [(5, 4, 32, 256), pltpu.VMEM((1, 128), jnp.int32), pltpu.VMEM((1, 128), jnp.int32),
         pltpu.VMEM((2, 4, 128), jnp.int32)],
        away=(0, 1, 2, 3, 4, 5),
        mib=56,
        copies=6,
    )
    bottoms = lax.all_to_all(bottoms, rank, 0, 0, tiled=True)
    crater1, crater2 = exchange("gx", crater1, crater2)
    b, f, x1, x2, y_low, y_high, token = call(
        first_kernel,
        (u, v, a, region, material),
        [element_shape, element_shape, (31, 8, 128), (31, 8, 128), (16, 8, 128), (15, 8, 128), register],
        internal_scratch
        + [held_shape] * 3
        + [(3, 5, 5, 8, 256), (3, 5, 5, 8, 256), (600, 256), (600, 256), element_shape],
        smem=(4,),
        away=(0, 1, 2),
        out_away=(0,),
        mib=56,
        copies=13,
    )
    surf1, surf2 = call(
        functools.partial(surface_kernel, float(nodes_y), count_x),
        (bottoms.reshape(devices * 24, 128), material, jnp.asarray(surface_tables()), token),
        [(24, 256), (24, 256)],
        [(360, 128), (4, 4 * count_x, 128), (6, 128, 128)],
        smem=(1,),
        away=(2,),
        mib=56,
        copies=1,
    )
    x1, x2 = exchange("gx", x1, x2)
    y1, y2 = call(
        first_edge_kernel,
        (y_low, y_high, x1, x2, rows_low, rows_high, crater1, crater2, surf1),
        [(38, 8, 128), (38, 8, 128)],
        [(2, 5, 16, 256)],
        away=(6, 7),
        mib=56,
        copies=4,
    )
    y1, y2 = exchange(along, y1, y2)
    a1, f2, p1, p2, y_low, y_high, scales, token = call(
        second_kernel,
        (b, f, x1, x2, y1, y2, region, material),
        [element_shape, element_shape, (30, 8, 128), (30, 8, 128), (15, 8, 128), (15, 8, 128), (3, 3, 2, 8, 128), register],
        internal_scratch,
        smem=(7,),
    )
    hydro_state, token = call(
        crater_kernel,
        crater + (crater1, crater2, y1, y2, token),
        [(5, 4, 32, 256), register],
        [(5, 8, 40, 256), (5, 8, 40, 256), (6, 40, 256), (5, 40, 256), (6, 40, 256)],
        away=(0, 1, 2),
        copies=3,
    )
    p1, p2 = exchange("gx", p1, p2)
    r1, r2, token = call(
        second_edge_kernel, (y_low, y_high, p1, p2, token), [(15, 8, 128), (15, 8, 128), register], []
    )
    u_out, v_part = call(
        place_kernel,
        (a1, surf1, u, v, a, token),
        [u.shape, held_shape],
        [held_shape] * 3 + [(2, 3, 5, 5, 8, 256), (27, 24, 128)],
        away=(2, 3, 4),
        out_away=(0,),
        mib=20,
        copies=16,
    )
    r1, r2 = exchange(along, r1, r2)
    v_out, a_out = call(
        last_kernel,
        (v_part, f2, p1, p2, r1, r2, scales, surf1, surf2),
        [u.shape] * 2,
        [held_shape] * 2 + [(2, 3, 5, 5, 8, 256), (2, 27, 24, 128), element_shape],
        out_away=(0, 1),
        mib=16,
        copies=8,
    )
    u_out, v_out, a_out = [jnp.transpose(x, (2, 0, 1, 3)) for x in (u_out, v_out, a_out)]
    return hydro_state, u_out, v_out, a_out


def solution(mesh):
    field = P(None, "gx", ("grp", "gy"), None)
    cells = P("gx", ("grp", "gy"), None)
    rank = ("grp", "gx", "gy")
    return jax.shard_map(
        shards,
        mesh=mesh,
        in_specs=(cells, field, cells, field, field, field, P(), cells, P(rank, None, None), P(rank, None)),
        out_specs=(field, field, field, field),
        check_vma=False,
    )
```

```python
import functools

import jax
import jax.numpy as jnp
import numpy as np
from jax import lax
from jax.experimental import pallas as pl
from jax.experimental.pallas import tpu as pltpu
from jax.sharding import PartitionSpec as P

gamma_gas = 1.4
cell_ratio = 0.05
half_size = 2.0
time_step = 0.1
face_area = 2.0


def gll_tables():
    root = np.sqrt(3.0 / 7.0)
    points = np.array([-1.0, -root, 0.0, root, 1.0])
    weights = np.array([0.1, 49.0 / 90.0, 32.0 / 45.0, 49.0 / 90.0, 0.1])
    products = [np.prod([points[r] - points[c] for c in range(5) if c != r]) for r in range(5)]
    derivative = np.zeros((5, 5))
    for r in range(5):
        for c in range(5):
            if r != c:
                derivative[r, c] = products[r] / products[c] / (points[r] - points[c])
        derivative[r, r] = sum(1.0 / (points[r] - points[c]) for c in range(5) if c != r)
    derivative[2, 2] = 0.0
    return derivative, weights


deriv, quad = gll_tables()
deriv_t = deriv.T
kind = [0, 1, 2, 1, 0]
f32 = jnp.float32


def line(matrix, v):
    even, odd = (matrix + matrix[:, ::-1]) / 2, (matrix - matrix[:, ::-1]) / 2
    e0, e1, o0, o1 = v[0] + v[4], v[1] + v[3], v[0] - v[4], v[1] - v[3]
    top = [float(even[i, 0]) * e0 + float(even[i, 1]) * e1 + float(matrix[i, 2]) * v[2] for i in range(2)]
    low = [float(odd[i, 0]) * o0 + float(odd[i, 1]) * o1 for i in range(2)]
    centre = float(matrix[2, 0]) * o0 + float(matrix[2, 1]) * o1
    return [top[0] + low[0], top[1] + low[1], centre, low[1] - top[1], low[0] - top[0]]


def rows_of(shape=(8, 128)):
    return lax.broadcasted_iota(jnp.int32, shape, 0)


def lanes_of(shape=(8, 128)):
    return lax.broadcasted_iota(jnp.int32, shape, 1)


def deeper(x):
    return jnp.where(lanes_of() == 127, 0.0, pltpu.roll(x, 127, 1))


def shallower(x):
    return jnp.where(lanes_of() == 0, 0.0, pltpu.roll(x, 1, 1))


def split_three(x):
    high = x.astype(jnp.bfloat16)
    rest = x - high.astype(f32)
    middle = rest.astype(jnp.bfloat16)
    return high, middle, (rest - middle.astype(f32)).astype(jnp.bfloat16)


def depth_table(back=False):
    a = lax.broadcasted_iota(jnp.int32, (256, 256), 1 if back else 0)
    b = lax.broadcasted_iota(jnp.int32, (256, 256), 0 if back else 1)
    table = jnp.where(a == 4 * (b & 63) + (b >> 6), 1.0, 0.0).astype(jnp.bfloat16)
    return jnp.concatenate([table] * 3, axis=0)


def moved_lanes(x, table):
    return jnp.dot(jnp.concatenate(split_three(x), axis=1), table, preferred_element_type=f32)


def interleave(x, y):
    front = lanes_of(x.shape) < 64
    return jnp.where(front, x, pltpu.roll(y, 64, 1)), jnp.where(front, pltpu.roll(x, 64, 1), y)


def node_at(i, j, r):
    start = ((4 * (r // 4) + i) * 17 + 4 * (r % 4) + j) * 8
    return pl.ds(start if isinstance(i, int) else pl.multiple_of(start, 8), 8)


def gather_rows(nodes):
    sub = rows_of()
    turned = [rolled(v, r) for r, v in enumerate(nodes)]
    out = []
    for c in range(3):
        total = turned[0]
        for r in range(1, 8):
            total = jnp.where(sub == (r + c) % 8, turned[r], total)
        out.append(rolled(total, -c))
    return out


def scatter_rows(parts, wanted):
    sub = rows_of()
    turned = [rolled(v, c) for c, v in enumerate(parts)]
    out = []
    for r in wanted:
        total = jnp.where(sub == r, turned[0], jnp.where(sub == (r + 1) % 8, turned[1], turned[2]))
        out.append((r, rolled(total, -r)))
    return out


def every_node(body):
    def column(i, carry):
        for j in range(5):
            body(i, j, range(8) if j < 4 else (3, 7))
        return carry

    lax.fori_loop(0, 4, column, 0)
    for j in range(5):
        body(4, j, range(4, 8) if j < 4 else (7,))


def tile_copies(field, held, semaphores, first, out=False):
    copies = []
    for t in range(4):
        outside = field.at[:, :, :, pl.ds(128 * t, 128)]
        inside = held.reshape(4, 9, 17, 8, 128).at[t, :, :, pl.ds(0, 3), :]
        ends = (inside, outside) if out else (outside, inside)
        copies.append(pltpu.make_async_copy(*ends, semaphores.at[first + t]))
    return copies


def to_elements(half, wide, table, kept, puts):
    moved = moved_lanes(wide[...].reshape(600, 256), table)
    if half == 0:
        kept[...] = moved
        return
    for pair in range(2):
        lanes = slice(128 * pair, 128 * pair + 128)
        for l, value in enumerate(interleave(kept[:, lanes], moved[:, lanes])):
            puts(2 * pair + l, value.reshape(3, 5, 5, 8, 128))


def to_nodes(get, table, tall):
    pairs = [interleave(get(2 * p).reshape(600, 128), get(2 * p + 1).reshape(600, 128)) for p in range(2)]
    for half in range(2):
        wide = jnp.concatenate([pairs[0][half], pairs[1][half]], axis=1)
        tall[half] = moved_lanes(wide, table).reshape(3, 5, 5, 8, 256)


def lookup(material, row, region):
    total = jnp.zeros_like(region)
    for m in range(material.shape[1]):
        total = jnp.where(region == float(m + 1), material[row, m], total)
    return total


def internal(u, out, lame, shear, gx, gz, cross, planes, side):
    def depth_lines(i, carry):
        for j in range(5):
            for c in range(3):
                v = [u[c, i, j, k] for k in range(4)]
                v.append(deeper(v[0]))
                u[c, i, j, 4] = v[4]
                for k, g in enumerate(line(deriv, v)):
                    gz[c, i, j, k] = g
        return carry

    lax.fori_loop(0, 5, depth_lines, 0)

    def plane(k, carry):
        weight = jnp.where((k == 0) | (k == 4), float(quad[0]), jnp.where(k == 2, float(quad[2]), float(quad[1])))
        lame_k, shear_k = lame * (2.0 * weight), shear * (2.0 * weight)
        pairs = {}
        for a in range(3):
            for b in range(a, 3):
                w = float(quad[a] * quad[b])
                pairs[a, b] = pairs[b, a] = (lame_k * w, shear_k * w, shear_k * (2.0 * w))
        for c in range(3):
            for j in range(5):
                for i, g in enumerate(line(deriv, [u[c, i, j, k] for i in range(5)])):
                    gx[c, i, j] = g
        for i in range(5):
            gy = [line(deriv, [u[c, i, j, k] for j in range(5)]) for c in range(3)]
            ys = [[], [], []]
            for j in range(5):
                lw, mw, mw2 = pairs[kind[i], kind[j]]
                g0, g1, g2 = [[gx[c, i, j], gy[c][j], gz[c, i, j, k]] for c in range(3)]
                dilated = lw * (g0[0] + g1[1] + g2[2])
                s01 = mw * (g0[1] + g1[0])
                s02 = mw * (g0[2] + g2[0])
                s12 = mw * (g1[2] + g2[1])
                side[0, i, j] = dilated + mw2 * g0[0]
                side[1, i, j] = s01
                cross[0, i, j, k] = s02
                cross[1, i, j, k] = s12
                cross[2, i, j, k] = dilated + mw2 * g2[2]
                ys[0].append(s01)
                ys[1].append(dilated + mw2 * g1[1])
                ys[2].append(s12)
            for c in range(3):
                for j, value in enumerate(line(deriv_t, ys[c])):
                    planes[c, i, j, k] = value
        for j in range(5):
            for c in range(3):
                v = [side[c, i, j] if c < 2 else cross[0, i, j, k] for i in range(5)]
                for i, value in enumerate(line(deriv_t, v)):
                    planes[c, i, j, k] += value
        return carry

    lax.fori_loop(0, 5, plane, 0)

    def depth_sums(i, carry):
        for j in range(5):
            for c in range(3):
                v = line(deriv_t, [cross[c, i, j, k] for k in range(5)])
                v = [v[k] + planes[c, i, j, k] for k in range(5)]
                out[c, i, j, 0] = v[0] + shallower(v[4])
                for k in range(1, 4):
                    out[c, i, j, k] = v[k]
        return carry

    lax.fori_loop(0, 5, depth_sums, 0)
    sub = rows_of()

    def fold(k, carry):
        for c in range(3):
            for i in range(5):
                low, high = out[c, i, 0, k], out[c, i, 4, k]
                out[c, i, 0, k] = low + jnp.where(sub % 4 == 0, 0.0, pltpu.roll(high, 1, 0))
                out[c, i, 4, k] = high + jnp.where(sub % 4 == 3, 0.0, pltpu.roll(low, 7, 0))
            for j in range(5):
                low, high = out[c, 0, j, k], out[c, 4, j, k]
                out[c, 0, j, k] = low + jnp.where(sub < 4, 0.0, pltpu.roll(high, 4, 0))
                out[c, 4, j, k] = high + jnp.where(sub < 4, pltpu.roll(low, 4, 0), 0.0)
        return carry

    lax.fori_loop(0, 4, fold, 0)


def rolled(x, amount, axis=0):
    amount = amount % x.shape[axis]
    return pltpu.roll(x, amount, axis) if amount else x


def parity_x():
    return position("gx") % 2


def parity_y():
    return along_y() % 2


def sort_out(odd, low, high):
    return jnp.where(odd == 1, low, high), jnp.where(odd == 1, high, low)


def pack_x(force, first, second):
    sub, odd = rows_of(), parity_x()
    for c in range(3):
        for j in range(5):
            for half in range(2):
                at = (c * 5 + j) * 2 + half
                a, b = force[c, 0, j, 2 * half], force[c, 0, j, 2 * half + 1]
                low = jnp.where(sub < 4, a, rolled(b, 4))
                a, b = force[c, 4, j, 2 * half], force[c, 4, j, 2 * half + 1]
                high = jnp.where(sub < 4, rolled(a, 4), b)
                first[at], second[at] = sort_out(odd, low, high)


def pack_y(force, low, high):
    sub = rows_of()
    for c in range(3):
        for i in range(5):
            a, b = force[c, i, 0, 0], rolled(force[c, i, 4, 0], -3)
            for k in range(1, 4):
                a = jnp.where(sub % 4 == k, rolled(force[c, i, 0, k], k), a)
                b = jnp.where(sub % 4 == k, rolled(force[c, i, 4, k], k - 3), b)
            low[c * 5 + i] = a
            high[c * 5 + i] = b


def add_x(force, first, second):
    sub, odd = rows_of(), parity_x()
    for c in range(3):
        for j in range(5):
            for half in range(2):
                at = (c * 5 + j) * 2 + half
                r, s = sort_out(odd, first[at], second[at])
                force[c, 0, j, 2 * half] += jnp.where(sub < 4, r, 0.0)
                force[c, 0, j, 2 * half + 1] += jnp.where(sub < 4, rolled(r, 4), 0.0)
                force[c, 4, j, 2 * half] += jnp.where(sub < 4, 0.0, rolled(s, 4))
                force[c, 4, j, 2 * half + 1] += jnp.where(sub < 4, 0.0, s)


def add_y(force, first, second):
    sub, odd = rows_of(), parity_y()
    for c in range(3):
        for i in range(5):
            r, s = sort_out(odd, first[c * 5 + i], second[c * 5 + i])
            for k in range(4):
                force[c, i, 0, k] += jnp.where(sub % 4 == 0, rolled(r, -k), 0.0)
                force[c, i, 4, k] += jnp.where(sub % 4 == 3, rolled(s, 3 - k), 0.0)


def edge_rows(low, high, came1, came2, first, second):
    sub, odd, odd_y = rows_of(), parity_x(), parity_y()
    for c in range(3):
        came = [[sort_out(odd, came1[at], came2[at]) for at in range((c * 5 + j) * 2, (c * 5 + j) * 2 + 2)] for j in (0, 4)]
        for i in range(5):
            rows = [low[c * 5 + i], high[c * 5 + i]]
            if i in (0, 4):
                start, side = i, i // 4
                for end, row in ((0, 0), (1, 3)):
                    for k in range(4):
                        r = rolled(came[end][k // 2][side], start + k - (4 * (k % 2) + row))
                        rows[end] = rows[end] + jnp.where(sub == start + k, r, 0.0)
            first[c * 5 + i], second[c * 5 + i] = sort_out(odd_y, *rows)


def first_edge_kernel(low, high, came1, came2, rows_low, rows_high, crater1, crater2, after, first, second, token, ends, semaphores):
    token[...] = after[0:8]
    copies = fetch(
        [(c.at[:, pl.ds(24 * h, 8), :], ends.at[n, :, pl.ds(8 * h, 8), :]) for n, c in enumerate((crater1, crater2)) for h in range(2)],
        semaphores,
    )
    edge_rows(low, high, came1, came2, first, second)
    odd, odd_y = parity_x(), parity_y()
    regions = sort_out(odd, came1[30], came2[30])
    for n, value in enumerate((low[15], regions[0], regions[1])):
        first[15 + n] = value
        second[15 + n] = value
    for copy in copies:
        copy.wait()
    for f in range(5):
        for t in range(2):
            lanes = slice(128 * t, 128 * t + 128)
            at = 18 + f * 4 + t * 2
            first[at], second[at] = sort_out(odd_y, rows_low[f * 2 + t], rows_high[f * 2 + t])
            found = []
            for row in (0, 15):
                sides = sort_out(odd, ends[0, f, row : row + 1, lanes], ends[1, f, row : row + 1, lanes])
                found.append(jnp.concatenate(list(sides) * 4, axis=0))
            first[at + 1], second[at + 1] = sort_out(odd_y, *found)


def second_edge_kernel(low, high, came1, came2, after, first, second, token):
    edge_rows(low, high, came1, came2, first, second)
    token[...] = after[...]


def region_grid(own, x1, x2, y1, y2):
    xl, xh = sort_out(parity_x(), x1[30], x2[30])
    yl, yh = [list(v) for v in zip(*[sort_out(parity_y(), y1[n], y2[n]) for n in (15, 16, 17)])]
    return [[yl[1], xl, yh[1]], [yl[0], own, yh[0]], [yl[2], xh, yh[2]]]


def shared_density(grid):
    sub = rows_of()
    across = []
    for y in range(3):
        low, mid, high = grid[0][y], grid[1][y], grid[2][y]
        turned = rolled(mid, 4)
        across.append([jnp.where(sub < 4, rolled(low, 4), turned), mid, jnp.where(sub < 4, turned, rolled(high, 4))])
    found = [[None] * 3 for _ in range(3)]
    for x in range(3):
        low, mid, high = across[0][x], across[1][x], across[2][x]
        found[x][0] = jnp.where(sub % 4 == 0, rolled(low, -3), rolled(mid, 1))
        found[x][1] = mid
        found[x][2] = jnp.where(sub % 4 == 3, rolled(high, 3), rolled(mid, -1))
    sums = []
    for x in ((1,), (0, 1), (1, 2)):
        row = []
        for y in ((1,), (0, 1), (1, 2)):
            total = sum(found[a][b] for a in x for b in y)
            row.append((total + shallower(total), total))
        sums.append(row)
    return sums


def mass_scales(sums):
    return [[[1.0 / s for s in pair] for pair in row] for row in sums]


def edge_kind(i):
    return 1 if i == 0 else 2 if i == 4 else 0


def accel_scale(i, j, k):
    return float(-1.0 / (half_size**3 * quad[i] * quad[j] * quad[k]))


def first_kernel(u, v, a, region, material, b_out, f_out, x1, x2, y_low, y_high, token,
                 elem, gx, gz, cross, planes, side, u_in, v_in, a_in, wide_u, wide_b, kept_u, kept_b, b_held, semaphores):
    copies = [tile_copies(f, h, semaphores, 4 * n) for n, (f, h) in enumerate(((u, u_in), (v, v_in), (a, a_in)))]
    for t in range(4):
        for copy in copies:
            copy[t].start()
    table = depth_table()
    region_now = region[...]

    def put_u(l, value):
        elem[:, :, :, l] = value

    def put_b(l, value):
        b_held[:, :, :, l] = value

    for half in range(2):
        for t in (2 * half, 2 * half + 1):
            for copy in copies:
                copy[t].wait()

        def column(i, carry):
            for t in (2 * half, 2 * half + 1):
                lanes = slice(128 * (t % 2), 128 * (t % 2) + 128)
                for j in range(5):
                    now, later = [], []
                    for r in range(8):
                        at = (t, node_at(i, j, r), slice(None))
                        step = time_step * v_in[at] + (0.5 * time_step**2) * a_in[at]
                        now.append(u_in[at] + step)
                        later.append(now[-1] + step)
                    for c, value in enumerate(gather_rows(now)):
                        wide_u[c, i, j, :, lanes] = value
                    for c, value in enumerate(gather_rows(later)):
                        wide_b[c, i, j, :, lanes] = value
            return carry

        lax.fori_loop(0, 5, column, 0)
        to_elements(half, wide_u, table, kept_u, put_u)
        to_elements(half, wide_b, table, kept_b, put_b)
    save_b = pltpu.make_async_copy(b_held, b_out, semaphores.at[12])
    save_b.start()
    internal(elem, f_out, lookup(material, 1, region_now), lookup(material, 2, region_now), gx, gz, cross, planes, side)
    pack_x(f_out, x1, x2)
    pack_y(f_out, y_low, y_high)
    x1[30] = region_now
    x2[30] = region_now
    y_low[15] = region_now
    token[...] = region_now
    save_b.wait()


def second_kernel(b, f, came_x1, came_x2, came_y1, came_y2, region, material, after, a_out, f_out, x1, x2, y_low, y_high, scales, token,
                  elem, gx, gz, cross, planes, side):
    region_now = region[...]
    token[...] = after[...]
    a_out[...] = f[...]
    add_x(a_out, came_x1, came_x2)
    add_y(a_out, came_y1, came_y2)
    grid = region_grid(region_now, came_x1, came_x2, came_y1, came_y2)
    inverse = mass_scales(shared_density([[lookup(material, 0, r) for r in row] for row in grid]))
    for x in range(3):
        for y in range(3):
            for z in range(2):
                scales[x, y, z] = inverse[x][y][z]
    for i in range(5):
        for j in range(5):
            for k in range(4):
                scale = scales[edge_kind(i), edge_kind(j), min(k, 1)] * accel_scale(i, j, k)
                for c in range(3):
                    value = a_out[c, i, j, k] * scale
                    a_out[c, i, j, k] = value
                    elem[c, i, j, k] = b[c, i, j, k] + time_step**2 * value
    internal(elem, f_out, lookup(material, 1, region_now), lookup(material, 2, region_now), gx, gz, cross, planes, side)
    pack_x(f_out, x1, x2)
    pack_y(f_out, y_low, y_high)


def spread_surface(source, held, count):
    lane = lanes_of((24, 128))
    for n in range(27):
        at = 8 * n
        tile, shift = at // 128, (128 - at % 128) % 128
        moved = rolled(source[:, 128 * tile : 128 * tile + 128], shift, 1)
        held[n] = jnp.where(lane < count, moved, 0.0)


def add_surface(held, tall):
    for c in range(3):
        for i in range(5):
            for j in range(5):
                for ex in range(2):
                    value = held[c * 9 + 4 * ex + i, pl.ds(j, 4, stride=4), :]
                    tall[0, c, i, j, 4 * ex : 4 * ex + 4, 0:128] += value


def place_kernel(a1, surf1, u, v, a, after, u_out, v_part, u_in, v_in, a_in, tall, surface, u_held, semaphores):
    copies = [tile_copies(f, h, semaphores, 4 * n) for n, (f, h) in enumerate(((u, u_in), (v, v_in), (a, a_in)))]
    for t in range(4):
        for copy in copies:
            copy[t].start()
    spread_surface(surf1, surface, 1)
    to_nodes(lambda l: a1[:, :, :, l], depth_table(back=True), tall)
    add_surface(surface, tall)
    saves = tile_copies(u_out, u_held, semaphores, 12, out=True)
    for t in range(4):
        for copy in copies:
            copy[t].wait()
        lanes = slice(128 * (t % 2), 128 * (t % 2) + 128)

        def body(i, j, wanted):
            for r, accel in scatter_rows([tall[t // 2, c, i, j, :, lanes] for c in range(3)], wanted):
                at = (t, node_at(i, j, r), slice(None))
                vv, aa = v_in[at], a_in[at]
                u_held[at] = u_in[at] + 2.0 * time_step * vv + time_step**2 * (aa + accel)
                v_part[at] = vv + (0.5 * time_step) * (aa + 2.0 * accel)

        every_node(body)
        saves[t].start()
    for save in saves:
        save.wait()


def last_kernel(v_part, f, x1, x2, y1, y2, scales, surf1, surf2, v_out, a_out, v_held, a_held, tall, surface, force, semaphores):
    force[...] = f[...]
    add_x(force, x1, x2)
    add_y(force, y1, y2)
    for i in range(5):
        for j in range(5):
            for k in range(4):
                scale = scales[edge_kind(i), edge_kind(j), min(k, 1)] * accel_scale(i, j, k)
                for c in range(3):
                    force[c, i, j, k] = force[c, i, j, k] * scale
    spread_surface(surf1, surface.at[0], 1)
    spread_surface(surf2, surface.at[1], 5)
    surface[0] = surface[0] + surface[1]
    to_nodes(lambda l: force[:, :, :, l], depth_table(back=True), tall)
    add_surface(surface.at[0], tall)
    saves = tile_copies(v_out, v_held, semaphores, 0, out=True) + tile_copies(a_out, a_held, semaphores, 4, out=True)
    for t in range(4):
        lanes = slice(128 * (t % 2), 128 * (t % 2) + 128)

        def body(i, j, wanted):
            for r, accel in scatter_rows([tall[t // 2, c, i, j, :, lanes] for c in range(3)], wanted):
                at = (t, node_at(i, j, r), slice(None))
                a_held[at] = accel
                v_held[at] = v_part[at] + (0.5 * time_step) * accel

        every_node(body)
        saves[t].start()
        saves[4 + t].start()
    for save in saves:
        save.wait()


def whole():
    return pl.BlockSpec(memory_space=pltpu.VMEM)


def scalars():
    return pl.BlockSpec(memory_space=pltpu.SMEM)


def call(kernel, ins, outs, scratch, smem=(), away=(), out_away=(), mib=10, copies=0):
    def spec(n):
        return scalars() if n in smem else pl.BlockSpec(memory_space=pltpu.HBM) if n in away else whole()

    scratch = [pltpu.VMEM(s, f32) if isinstance(s, tuple) else s for s in scratch]
    return pl.pallas_call(
        kernel,
        out_shape=[jax.ShapeDtypeStruct(s, f32) for s in outs],
        in_specs=[spec(n) for n in range(len(ins))],
        out_specs=[pl.BlockSpec(memory_space=pltpu.HBM) if n in out_away else whole() for n in range(len(outs))],
        scratch_shapes=scratch + ([pltpu.SemaphoreType.DMA((copies,))] if copies else []),
        compiler_params=pltpu.CompilerParams(vmem_limit_bytes=mib * 1024 * 1024),
    )(*ins)


def fetch(pairs, semaphores):
    copies = [pltpu.make_async_copy(source, target, semaphores.at[n]) for n, (source, target) in enumerate(pairs)]
    for copy in copies:
        copy.start()
    return copies


element_shape = (3, 5, 5, 4, 8, 128)
lines_shape = (3, 5, 5, 5, 8, 128)
internal_scratch = [lines_shape, (3, 5, 5, 8, 128), lines_shape, lines_shape, lines_shape, (2, 5, 5, 8, 128)]


def exchange(axis, first, second):
    count = lax.axis_size(axis)
    pairs = [(i, i + 1) for i in range(1, count - 1, 2)]
    first = lax.ppermute(first, axis, [(i, i ^ 1) for i in range(count)])
    return first, lax.ppermute(second, axis, pairs + [(j, i) for i, j in pairs])


def surface_tables():
    lane = np.arange(128)
    j, ey = lane // 8, lane % 8
    used = (j < 5) & (ey < 6)
    place = np.where(used, ey + 1, -9)
    source = lane[:, None]
    centre = source == place
    meet = centre | ((j == 0) & (source == place - 1)) | ((j == 4) & (source == place + 1))
    along = np.zeros((128, 128))
    for a in range(40):
        for b in range(40):
            if a % 8 == b % 8 and a % 8 < 6:
                along[a, b] = deriv[b // 8, a // 8]
    node = np.where(used, 4 * (ey - 1) + j, -9)
    fold = (lane[:, None] == node) & (lane[:, None] < 17)
    keep = fold & ((j < 4) & (ey < 5) | (j == 4) & (ey == 4))
    return np.stack([centre, meet, along, along.T, fold, keep]).astype(np.float32)


def full_dot(x, y, back=False):
    dims = (((1,), (1 if back else 0,)), ((), ()))
    return lax.dot_general(x, y, dims, precision=lax.Precision.HIGHEST, preferred_element_type=f32)


def deposit(faces, nodes_y, base_x, base_y, total):
    rows = faces.shape[1]
    sub = rows_of((8, 512)).astype(f32)
    total[...] = jnp.zeros_like(total)

    def one(step, carry):
        def wide(q):
            block = faces[q, pl.ds(4 * step, 4), :]
            return jnp.concatenate([block[n : n + 1] for n in range(4)], axis=1)

        ids = wide(3)
        node_x = jnp.floor((ids + 0.5) * (1.0 / nodes_y))
        rel_y = jnp.broadcast_to(ids - node_x * nodes_y - base_y, (8, 512))
        rel_x = jnp.broadcast_to(node_x - base_x, (8, 512))
        left = []
        hits = [(rel_x - i == 4.0 * sub) & (sub < 4.0) for i in range(5)]
        parts = [split_three(wide(c)) for c in range(3)]
        for part in range(3):
            for c in range(3):
                value = jnp.broadcast_to(parts[c][part].astype(f32), (8, 512))
                left += [jnp.where(hit, value, 0.0) for hit in hits]
        right = [jnp.where((rel_y - j == 4.0 * sub) & (sub < 6.0), 1.0, 0.0) for j in range(5)]
        right.append(jnp.zeros((88, 512), f32))
        left, right = jnp.concatenate(left, axis=0), jnp.concatenate(right, axis=0)
        total[...] += lax.dot_general(
            left.astype(jnp.bfloat16), right.astype(jnp.bfloat16), (((1,), (1,)), ((), ())), preferred_element_type=f32
        )
        return carry

    lax.fori_loop(0, rows // 4, one, 0)


def top_grid(rows, z):
    sub, lane = rows_of(), lanes_of()
    out = jnp.zeros((8, 128), f32)
    for x in range(3):
        for y in range(3):
            row = jnp.broadcast_to(rows[x][y], (8, 128))
            for ex in range(2):
                here = (sub == 2 * x + ex) & (lane >= 4 * y - 2) & (lane < 4 * y + 2) & (lane < 8)
                out = jnp.where(here, rolled(row, 4 * y - 2 - 8 * z - 4 * ex, 1), out)
    return out


def respond(total, grid, material, tables, out1, out2):
    sub, lane = rows_of(), lanes_of()
    top, below = top_grid(grid, 0), top_grid(grid, 1)
    centre, meet, along, along_t, fold, keep = [tables[n] for n in range(6)]
    sums0 = full_dot(lookup(material, 0, top), meet)
    sums1 = full_dot(lookup(material, 0, below), meet)
    lame = rolled(full_dot(lookup(material, 1, top), centre), -1)
    shear = rolled(full_dot(lookup(material, 2, top), centre), -1)
    weight_y = jnp.ones((8, 128), f32)
    for j in range(5):
        weight_y = jnp.where(lane // 8 == j, float(quad[j]), weight_y)

    def inverse(sums):
        mid = rolled(sums, -1)
        found = {0: mid + sums, 1: mid, 4: mid + rolled(sums, -2)}
        found = {i: jnp.where(s > 0.0, 1.0 / (s * weight_y), 0.0) for i, s in found.items()}
        found[2] = found[3] = found[1]
        return found

    light, heavy = inverse(sums0), inverse(sums0 + sums1)
    first = [[None] * 5 for _ in range(3)]
    moved = [[None] * 5 for _ in range(3)]
    for c in range(3):
        for i in range(5):
            at = (c * 5 + i) * 8
            force = total[at : at + 8] + total[at + 120 : at + 128] + total[at + 240 : at + 248]
            first[c][i] = force * light[i] * -accel_scale(i, 2, 0) * float(quad[2])
            moved[c][i] = first[c][i] * time_step**2
    gx = [line(deriv, moved[c]) for c in range(3)]
    gy = full_dot(jnp.concatenate([moved[c][i] for c in range(3) for i in range(5)], axis=0), along)
    gy = [[gy[(c * 5 + i) * 8 : (c * 5 + i) * 8 + 8] for i in range(5)] for c in range(3)]
    lame_w, shear_w = lame * weight_y * 2.0, shear * weight_y * 2.0
    d00 = float(deriv[0, 0])
    sx = [[], [], []]
    sy = [[], [], []]
    sz = [[], [], []]
    qs = [[], [], []]
    pressed = []
    for i in range(5):
        lw, mw = lame_w * float(quad[i]), shear_w * float(quad[i])
        d = [moved[c][i] for c in range(3)]
        gz = [d00 * x for x in d]
        dilated = lw * (gx[0][i] + gy[1][i] + gz[2])
        s01 = mw * (gx[1][i] + gy[0][i])
        s02 = mw * (gx[2][i] + gz[0])
        s12 = mw * (gy[2][i] + gz[1])
        for c, value in enumerate((dilated + 2.0 * mw * gx[0][i], s01, s02)):
            sx[c].append(value)
        for c, value in enumerate((s01, dilated + 2.0 * mw * gy[1][i], s12)):
            sy[c].append(value)
        for c, value in enumerate((s02, s12, dilated + 2.0 * mw * gz[2])):
            sz[c].append(value)
        for c, value in enumerate((mw * d[0], mw * d[1], (lw + 2.0 * mw) * d[2])):
            qs[c].append(value)
        pressed.append(lw * d[2])
    ydiv = full_dot(jnp.concatenate(sy[0] + sy[1] + sy[2] + pressed + qs[1], axis=0), along_t)
    ydiv = [[ydiv[(n * 5 + i) * 8 : (n * 5 + i) * 8 + 8] for i in range(5)] for n in range(5)]
    xdiv = [line(deriv_t, v) for v in sx + [pressed, qs[0]]]
    base = [xdiv[3], ydiv[3], [p + q for p, q in zip(xdiv[4], ydiv[4])]]
    second = {}
    for c in range(3):
        for i in range(5):
            for l in range(5):
                stiff = float(sum(deriv[k, l] * quad[k] * deriv[k, 0] for k in range(1, 5)))
                value = float(deriv[0, l] * quad[0]) * sz[c][i] + stiff * qs[c][i]
                if l:
                    value = value + float(deriv[l, 0] * quad[l]) * base[c][i]
                else:
                    value = value + float(quad[0]) * (xdiv[c][i] + ydiv[c][i])
                scale = (heavy if l == 4 else light)[i]
                second[c, i, l] = value * scale * (accel_scale(i, 2, l) * float(quad[2]))
    rows1, rows2 = [], []
    for c in range(3):
        for x in range(9):
            own = 1 if x < 4 else 2
            rows1.append(jnp.where(sub == 0, rolled(first[c][x - 4 * (own - 1)], -own), 0.0))
            block = jnp.zeros((8, 128), f32)
            for l in range(5):
                for ex in range(4):
                    i = x - 4 * (ex - 1)
                    if 0 <= i <= 4:
                        block = block + jnp.where(sub == l, rolled(second[c, i, l], l - ex), 0.0)
            rows2.append(block)
    blank = [jnp.zeros((40, 128), f32)]
    out1[...] = full_dot(keep[0:24], jnp.concatenate(rows1 + blank, axis=0), back=True)
    out2[...] = full_dot(fold[0:24], jnp.concatenate(rows2 + blank, axis=0), back=True)


def position(axis):
    return lax.axis_index(axis)


def along_y():
    return lax.axis_index("grp") * lax.axis_size("gy") + lax.axis_index("gy")


def primitives(state):
    inverse = 1.0 / state[0]
    v = [state[1 + c] * inverse for c in range(3)]
    p = (gamma_gas - 1.0) * (state[4] - 0.5 * (state[1] * v[0] + state[2] * v[1] + state[3] * v[2]))
    return v + [p, jnp.sqrt(gamma_gas * p * inverse), state[4] + p]


def flux(state, prim, d):
    out = [state[1 + d]] + [state[1 + c] * prim[d] for c in range(3)] + [prim[5] * prim[d]]
    out[1 + d] = out[1 + d] + prim[3]
    return out, jnp.abs(prim[d]) + prim[4]


def twice_face(low, high):
    fastest = jnp.maximum(low[2], high[2])
    return [fl + fh - fastest * (uh - ul) for ul, uh, fl, fh in zip(low[0], high[0], low[1], high[1])]


def turned_change(state, prim, d, axis, ends):
    size = state[0].shape[axis]
    fluxes, speed = flux(state, prim, d)
    up = lambda x: pltpu.roll(x, size - 1, axis)
    high = ([up(x) for x in state], [up(x) for x in fluxes], up(speed))
    upper = twice_face((state, fluxes, speed), high)
    if ends is None:
        return [g - pltpu.roll(g, 1, axis) for g in upper]
    upper = [jnp.where(ends[1], 2.0 * f, g) for f, g in zip(fluxes, upper)]
    return [g - jnp.where(ends[0], 2.0 * f, pltpu.roll(g, 1, axis)) for f, g in zip(fluxes, upper)]


def start_kernel(nodes_y, density, momentum, energy, dest, slot, region, bottoms, first, second, rows_low, rows_high,
                 region_out, cells, dest_in, slot_in, region_in, semaphores):
    copies = fetch(
        [(dest, dest_in), (slot, slot_in), (region, region_in), (density, cells.at[0]),
         (momentum, cells.at[pl.ds(1, 3)]), (energy, cells.at[4])],
        semaphores,
    )
    for copy in copies:
        copy.wait()
    sub, lane = rows_of(), lanes_of()
    pick = jnp.where(lane == 125 + sub, 1.0, 0.0)
    pieces = []
    odd = parity_x()
    for f in range(5):
        columns = jnp.concatenate([cells[f, x, :, 128:256] for x in range(4)], axis=0)
        pieces.append(full_dot(pick, columns, back=True)[0:3])
        for out, down in ((first, odd), (second, 1 - odd)):
            out[f, 0:32, :] = cells[f, 3 - 3 * down]
            out[f, 32:64, :] = cells[f, 2 - down]
        for t in range(2):
            lanes = slice(128 * t, 128 * t + 128)
            for out, pair in ((rows_low, (0, 1)), (rows_high, (31, 30))):
                out[f * 2 + t] = jnp.concatenate([cells[f, x, r : r + 1, lanes] for r in pair for x in range(4)], axis=0)
    count_gy, count_x = lax.axis_size("gy"), lax.axis_size("gx")
    target, node = dest_in[...].astype(f32), slot_in[...].astype(f32)
    grp = jnp.floor((target + 0.5) * (1.0 / (count_gy * count_x)))
    rest = target - grp * (count_gy * count_x)
    gx = jnp.floor((rest + 0.5) * (1.0 / count_gy))
    gy = rest - gx * count_gy
    i = jnp.floor((node + 0.5) * (1.0 / 17.0))
    j = node - 17.0 * i
    pieces.append((8.0 * gx + i) * nodes_y + 16.0 * (grp * count_gy + gy) + j)
    region_now = jnp.concatenate([region_in[0], region_in[1]], axis=0).astype(f32) + 1.0
    region_out[...] = region_now
    found = jnp.zeros((8, 128), f32)
    for z in range(2):
        found = jnp.where(lane == 8 * z + sub, jnp.broadcast_to(region_now[:, z : z + 1], (8, 128)), found)
    pieces.append(jnp.broadcast_to(jnp.sum(found, axis=0, keepdims=True), (8, 128)))
    block = jnp.concatenate(pieces, axis=0)
    for n in range(bottoms.shape[0]):
        bottoms[n] = block


def crater_kernel(density, momentum, energy, came1, came2, rows1, rows2, after, out, token,
                  wide, mid, prims, face, fluxes, semaphores):
    planes, inner = pl.ds(2, 4), pl.ds(0, 32)
    copies = fetch(
        [(density, wide.at[0, planes, inner]), (momentum, wide.at[pl.ds(1, 3), planes, inner]),
         (energy, wide.at[4, planes, inner])],
        semaphores,
    )
    place, last_y = along_y(), lax.axis_size("grp") * lax.axis_size("gy") - 1
    gx, last_x = position("gx"), lax.axis_size("gx") - 1
    odd, odd_y = parity_x(), parity_y()
    for f in range(5):
        low, high = sort_out(odd, came1[f], came2[f])
        for p, value in ((0, low[32:64]), (1, low[0:32]), (6, high[0:32]), (7, high[32:64])):
            wide[f, p, 0:32, :] = value
            wide[f, p, 32:40, :] = value[0:8]
    token[...] = after[...]
    for copy in copies:
        copy.wait()
    for f in range(5):
        for x in range(4):
            wide[f, 2 + x, 32:40, :] = wide[f, 2 + x, 24:32, :]
        for t in range(2):
            lanes = slice(128 * t, 128 * t + 128)
            at = 18 + f * 4 + t * 2
            below, above = sort_out(odd_y, rows1[at], rows2[at])
            sides_below, sides_above = sort_out(odd_y, rows1[at + 1], rows2[at + 1])

            def put(p, row, edge, value):
                clamped = jnp.where(edge == 0, place == 0, place == last_y)
                at_edge = wide[f, p, 31 * edge : 31 * edge + 1, lanes]
                wide[f, p, row : row + 1, lanes] = jnp.where(clamped, at_edge, value)

            for x in range(4):
                put(2 + x, 39, 0, below[x : x + 1])
                put(2 + x, 38, 0, below[4 + x : 5 + x])
                put(2 + x, 32, 1, above[x : x + 1])
                put(2 + x, 33, 1, above[4 + x : 5 + x])
            for p, n in ((1, 0), (6, 1)):
                put(p, 39, 0, sides_below[n : n + 1])
                put(p, 32, 1, sides_above[n : n + 1])

    @pl.when(gx == 0)
    def _():
        for f in range(5):
            wide[f, 0] = wide[f, 2]
            wide[f, 1] = wide[f, 2]

    @pl.when(gx == last_x)
    def _():
        for f in range(5):
            wide[f, 6] = wide[f, 5]
            wide[f, 7] = wide[f, 5]

    lane = lanes_of((40, 256))
    ends = (lane == 0, lane == 255)

    def step(source, low, high, put):
        def along_x(p):
            state = [source[f, p] for f in range(5)]
            prim = primitives(state)
            return state, prim, flux(state, prim, 0)

        state, prim, (fx, speed) = along_x(low - 1)
        next_state, next_prim, (next_fx, next_speed) = along_x(low)
        g = twice_face((state, fx, speed), (next_state, next_fx, next_speed))
        for f in range(5):
            face[f] = g[f]
            fluxes[f] = next_fx[f]
        for n in range(6):
            prims[n] = next_prim[n]
        fluxes[5] = next_speed

        def plane(p, carry):
            state = [source[f, p] for f in range(5)]
            prim = [prims[n] for n in range(6)]
            next_state, next_prim, (next_fx, next_speed) = along_x(p + 1)
            g = twice_face((state, [fluxes[f] for f in range(5)], fluxes[5]), (next_state, next_fx, next_speed))
            change = [g[f] - face[f] for f in range(5)]
            for f in range(5):
                face[f] = g[f]
                fluxes[f] = next_fx[f]
            for n in range(6):
                prims[n] = next_prim[n]
            fluxes[5] = next_speed
            change = [a + b for a, b in zip(change, turned_change(state, prim, 1, 0, None))]
            change = [a + b for a, b in zip(change, turned_change(state, prim, 2, 1, ends))]
            for f in range(5):
                put(f, p, state[f] - (0.5 * cell_ratio) * change[f])
            return carry

        lax.fori_loop(low, high, plane, 0)

    def put_mid(f, p, value):
        mid[f, p] = value

    def put_out(f, p, value):
        out[f, p - 2] = value[0:32]

    step(wide, 1, 7, put_mid)

    @pl.when(gx == 0)
    def _():
        for f in range(5):
            mid[f, 1] = mid[f, 2]

    @pl.when(gx == last_x)
    def _():
        for f in range(5):
            mid[f, 6] = mid[f, 5]

    for f in range(5):
        for p in range(2, 6):
            edge = mid[f, p, 39:40, :]
            mid[f, p, 39:40, :] = jnp.where(place == 0, mid[f, p, 0:1, :], edge)
            edge = mid[f, p, 32:33, :]
            mid[f, p, 32:33, :] = jnp.where(place == last_y, mid[f, p, 31:32, :], edge)
    step(mid, 2, 6, put_out)


def bottom_tractions(bottoms, count_x, faces):
    shape = (count_x, 128)
    sub, lane = rows_of(shape), lanes_of(shape)
    count_gy = lax.axis_size("gy")

    def columns(q):
        parts = []
        for y in range(4):
            start = (y // count_gy * count_x * count_gy + y % count_gy) * 24 + q
            parts.append(bottoms[pl.ds(start, count_x, stride=24 * count_gy), :])
        found = []
        for x in range(4):
            total = rolled(parts[0], -32 * x, 1)
            for y in range(1, 4):
                total = jnp.where(lane // 32 == y, rolled(parts[y], 32 * (y - x), 1), total)
            found.append(total)
        return found

    cells = [[columns(f * 3 + z) for f in range(5)] for z in range(3)]
    state = [[[cells[z][f][x] for f in range(5)] for x in range(4)] for z in range(3)]
    ends_y = (lane == 0, lane == 127)

    def across_x(states, prims):
        fluxes = [flux(s, p, 0) for s, p in zip(states, prims)]
        data = [(s, f, a) for s, (f, a) in zip(states, fluxes)]
        up = lambda x: rolled(x, -1)
        wrap = ([up(v) for v in data[0][0]], [up(v) for v in data[0][1]], up(data[0][2]))
        upper = [twice_face(data[x], data[x + 1] if x < 3 else wrap) for x in range(4)]
        upper[3] = [jnp.where(sub == count_x - 1, 2.0 * f, g) for f, g in zip(data[3][1], upper[3])]
        below = [jnp.where(sub == 0, 2.0 * f, rolled(g, 1)) for f, g in zip(data[0][1], upper[3])]
        lower = [below] + upper[:3]
        return [[a - b for a, b in zip(u, l)] for u, l in zip(upper, lower)]

    def advanced(above, here, under, prim_above, prim_here, prim_under):
        changes = across_x(here, prim_here)
        out = []
        for x in range(4):
            change = [a + b for a, b in zip(changes[x], turned_change(here[x], prim_here[x], 1, 1, ends_y))]
            fz, az = flux(here[x], prim_here[x], 2)
            fa, aa = flux(above[x], prim_above[x], 2)
            lower = twice_face((above[x], fa, aa), (here[x], fz, az))
            if under is None:
                upper = [2.0 * f for f in fz]
            else:
                fu, au = flux(under[x], prim_under[x], 2)
                upper = twice_face((here[x], fz, az), (under[x], fu, au))
            out.append([s - (0.5 * cell_ratio) * (c + u - l) for s, c, u, l in zip(here[x], change, upper, lower)])
        return out

    prims = [[primitives(state[z][x]) for x in range(4)] for z in range(3)]
    middle = advanced(state[0], state[1], state[2], prims[0], prims[1], prims[2])
    deepest = advanced(state[1], state[2], None, prims[1], prims[2], None)
    prim_mid, prim_deep = [primitives(s) for s in middle], [primitives(s) for s in deepest]
    final = advanced(middle, deepest, None, prim_mid, prim_deep, None)
    ids = columns(15)
    for x in range(4):
        s, prim = final[x], primitives(final[x])
        at = pl.ds(x * count_x, count_x)
        faces[0, at, :] = face_area * s[1] * prim[2]
        faces[1, at, :] = face_area * s[2] * prim[2]
        faces[2, at, :] = face_area * (s[3] * prim[2] + prim[3])
        faces[3, at, :] = ids[x]


def deposit_kernel(nodes_y, count_x, bottoms, after, total, faces):
    base_x = (8 * position("gx") - 4).astype(f32)
    base_y = (16 * along_y() - 4).astype(f32)
    bottom_tractions(bottoms, count_x, faces)
    deposit(faces, nodes_y, base_x, base_y, total)


def respond_kernel(count_x, total, bottoms, material, tables, after, out1, out2, token, held, rows, semaphores):
    gx, place, count_gy = position("gx"), along_y(), lax.axis_size("gy")
    last_y = lax.axis_size("grp") * count_gy - 1
    pairs = [(tables, held)]
    for x in range(3):
        for y in range(3):
            cx, cy = jnp.clip(gx + x - 1, 0, count_x - 1), jnp.clip(place + y - 1, 0, last_y)
            rank = (cy // count_gy) * (count_x * count_gy) + cx * count_gy + cy % count_gy
            pairs.append((bottoms.at[rank, pl.ds(16, 8), :], rows.at[3 * x + y]))
    copies = fetch(pairs, semaphores)
    for copy in copies:
        copy.wait()
    found = []
    for x in range(3):
        found.append([])
        for y in range(3):
            px, py = gx + x - 1, place + y - 1
            inside = (px >= 0) & (px < count_x) & (py >= 0) & (py <= last_y)
            found[x].append(jnp.where(inside, rows[3 * x + y, 0:1, :], 0.0))
    respond(total, found, material, held, out1, out2)
    token[...] = after[...]


def shards(density, momentum, energy, displacement, velocity_field, acceleration, material, element_region_index,
           face_dest, face_slot):
    along, rank = ("grp", "gy"), ("grp", "gx", "gy")
    nodes_y = 16 * lax.axis_size(along) + 1
    count_x, devices = lax.axis_size("gx"), lax.axis_size(rank)
    crater = (density, momentum, energy)
    u, v, a = [jnp.transpose(x, (1, 2, 0, 3)) for x in (displacement, velocity_field, acceleration)]
    register, held_shape = (8, 128), (4, 1224, 128)
    bottoms, crater1, crater2, rows_low, rows_high, region = call(
        functools.partial(start_kernel, float(nodes_y)),
        crater + (face_dest.reshape(1, -1), face_slot, element_region_index),
        [(devices, 24, 128), (5, 64, 256), (5, 64, 256), (10, 8, 128), (10, 8, 128), register],
        [(5, 4, 32, 256), pltpu.VMEM((1, 128), jnp.int32), pltpu.VMEM((1, 128), jnp.int32),
         pltpu.VMEM((2, 4, 128), jnp.int32)],
        away=(0, 1, 2, 3, 4, 5),
        mib=56,
        copies=6,
    )
    bottoms = lax.all_to_all(bottoms, rank, 0, 0, tiled=True)
    crater1, crater2 = exchange("gx", crater1, crater2)
    b, f, x1, x2, y_low, y_high, token = call(
        first_kernel,
        (u, v, a, region, material),
        [element_shape, element_shape, (31, 8, 128), (31, 8, 128), (16, 8, 128), (15, 8, 128), register],
        internal_scratch
        + [held_shape] * 3
        + [(3, 5, 5, 8, 256), (3, 5, 5, 8, 256), (600, 256), (600, 256), element_shape],
        smem=(4,),
        away=(0, 1, 2),
        out_away=(0,),
        mib=56,
        copies=13,
    )
    (total,) = call(
        functools.partial(deposit_kernel, float(nodes_y), count_x),
        (bottoms.reshape(devices * 24, 128), token),
        [(360, 128)],
        [(4, 4 * count_x, 128)],
    )
    x1, x2 = exchange("gx", x1, x2)
    y1, y2, token = call(
        first_edge_kernel,
        (y_low, y_high, x1, x2, rows_low, rows_high, crater1, crater2, total),
        [(38, 8, 128), (38, 8, 128), register],
        [(2, 5, 16, 256)],
        away=(6, 7),
        copies=4,
    )
    surf1, surf2, token = call(
        functools.partial(respond_kernel, count_x),
        (total, bottoms, material, jnp.asarray(surface_tables()), token),
        [(24, 256), (24, 256), register],
        [(6, 128, 128), (9, 8, 128)],
        smem=(2,),
        away=(1, 3),
        copies=10,
    )
    y1, y2 = exchange(along, y1, y2)
    a1, f2, p1, p2, y_low, y_high, scales, token = call(
        second_kernel,
        (b, f, x1, x2, y1, y2, region, material, token),
        [element_shape, element_shape, (30, 8, 128), (30, 8, 128), (15, 8, 128), (15, 8, 128), (3, 3, 2, 8, 128), register],
        internal_scratch,
        smem=(7,),
    )
    hydro_state, token = call(
        crater_kernel,
        crater + (crater1, crater2, y1, y2, token),
        [(5, 4, 32, 256), register],
        [(5, 8, 40, 256), (5, 8, 40, 256), (6, 40, 256), (5, 40, 256), (6, 40, 256)],
        away=(0, 1, 2),
        copies=3,
    )
    p1, p2 = exchange("gx", p1, p2)
    r1, r2, token = call(
        second_edge_kernel, (y_low, y_high, p1, p2, token), [(15, 8, 128), (15, 8, 128), register], []
    )
    u_out, v_part = call(
        place_kernel,
        (a1, surf1, u, v, a, token),
        [u.shape, held_shape],
        [held_shape] * 3 + [(2, 3, 5, 5, 8, 256), (27, 24, 128), held_shape],
        away=(2, 3, 4),
        out_away=(0,),
        mib=20,
        copies=16,
    )
    r1, r2 = exchange(along, r1, r2)
    v_out, a_out = call(
        last_kernel,
        (v_part, f2, p1, p2, r1, r2, scales, surf1, surf2),
        [u.shape] * 2,
        [held_shape] * 2 + [(2, 3, 5, 5, 8, 256), (2, 27, 24, 128), element_shape],
        out_away=(0, 1),
        mib=16,
        copies=8,
    )
    u_out, v_out, a_out = [jnp.transpose(x, (2, 0, 1, 3)) for x in (u_out, v_out, a_out)]
    return hydro_state, u_out, v_out, a_out


def solution(mesh):
    field = P(None, "gx", ("grp", "gy"), None)
    cells = P("gx", ("grp", "gy"), None)
    rank = ("grp", "gx", "gy")
    return jax.shard_map(
        shards,
        mesh=mesh,
        in_specs=(cells, field, cells, field, field, field, P(), cells, P(rank, None, None), P(rank, None)),
        out_specs=(field, field, field, field),
        check_vma=False,
    )
```

```python
import functools

import jax
import jax.numpy as jnp
import numpy as np
from jax import lax
from jax.experimental import pallas as pl
from jax.experimental.pallas import tpu as pltpu
from jax.sharding import PartitionSpec as P

gamma_gas = 1.4
cell_ratio = 0.05
half_size = 2.0
time_step = 0.1
face_area = 2.0


def gll_tables():
    root = np.sqrt(3.0 / 7.0)
    points = np.array([-1.0, -root, 0.0, root, 1.0])
    weights = np.array([0.1, 49.0 / 90.0, 32.0 / 45.0, 49.0 / 90.0, 0.1])
    products = [np.prod([points[r] - points[c] for c in range(5) if c != r]) for r in range(5)]
    derivative = np.zeros((5, 5))
    for r in range(5):
        for c in range(5):
            if r != c:
                derivative[r, c] = products[r] / products[c] / (points[r] - points[c])
        derivative[r, r] = sum(1.0 / (points[r] - points[c]) for c in range(5) if c != r)
    derivative[2, 2] = 0.0
    return derivative, weights


deriv, quad = gll_tables()
deriv_t = deriv.T
kind = [0, 1, 2, 1, 0]
f32 = jnp.float32


def line(matrix, v):
    even, odd = (matrix + matrix[:, ::-1]) / 2, (matrix - matrix[:, ::-1]) / 2
    e0, e1, o0, o1 = v[0] + v[4], v[1] + v[3], v[0] - v[4], v[1] - v[3]
    top = [float(even[i, 0]) * e0 + float(even[i, 1]) * e1 + float(matrix[i, 2]) * v[2] for i in range(2)]
    low = [float(odd[i, 0]) * o0 + float(odd[i, 1]) * o1 for i in range(2)]
    centre = float(matrix[2, 0]) * o0 + float(matrix[2, 1]) * o1
    return [top[0] + low[0], top[1] + low[1], centre, low[1] - top[1], low[0] - top[0]]


def rows_of(shape=(8, 128)):
    return lax.broadcasted_iota(jnp.int32, shape, 0)


def lanes_of(shape=(8, 128)):
    return lax.broadcasted_iota(jnp.int32, shape, 1)


def deeper(x):
    return jnp.where(lanes_of() == 127, 0.0, pltpu.roll(x, 127, 1))


def shallower(x):
    return jnp.where(lanes_of() == 0, 0.0, pltpu.roll(x, 1, 1))


def split_three(x):
    high = x.astype(jnp.bfloat16)
    rest = x - high.astype(f32)
    middle = rest.astype(jnp.bfloat16)
    return high, middle, (rest - middle.astype(f32)).astype(jnp.bfloat16)


def depth_table(back=False):
    a = lax.broadcasted_iota(jnp.int32, (256, 256), 1 if back else 0)
    b = lax.broadcasted_iota(jnp.int32, (256, 256), 0 if back else 1)
    table = jnp.where(a == 4 * (b & 63) + (b >> 6), 1.0, 0.0).astype(jnp.bfloat16)
    return jnp.concatenate([table] * 3, axis=0)


def moved_lanes(x, table):
    return jnp.dot(jnp.concatenate(split_three(x), axis=1), table, preferred_element_type=f32)


def interleave(x, y):
    front = lanes_of(x.shape) < 64
    return jnp.where(front, x, pltpu.roll(y, 64, 1)), jnp.where(front, pltpu.roll(x, 64, 1), y)


def node_at(i, j, r):
    start = ((4 * (r // 4) + i) * 17 + 4 * (r % 4) + j) * 8
    return pl.ds(start if isinstance(i, int) else pl.multiple_of(start, 8), 8)


def gather_rows(nodes):
    sub = rows_of()
    turned = [rolled(v, r) for r, v in enumerate(nodes)]
    out = []
    for c in range(3):
        total = turned[0]
        for r in range(1, 8):
            total = jnp.where(sub == (r + c) % 8, turned[r], total)
        out.append(rolled(total, -c))
    return out


def scatter_rows(parts, wanted):
    sub = rows_of()
    turned = [rolled(v, c) for c, v in enumerate(parts)]
    out = []
    for r in wanted:
        total = jnp.where(sub == r, turned[0], jnp.where(sub == (r + 1) % 8, turned[1], turned[2]))
        out.append((r, rolled(total, -r)))
    return out


def every_node(body):
    def column(i, carry):
        for j in range(5):
            body(i, j, range(8) if j < 4 else (3, 7))
        return carry

    lax.fori_loop(0, 4, column, 0)
    for j in range(5):
        body(4, j, range(4, 8) if j < 4 else (7,))


def tile_copies(field, held, semaphores, first, out=False):
    copies = []
    for t in range(4):
        outside = field.at[:, :, :, pl.ds(128 * t, 128)]
        inside = held.reshape(4, 9, 17, 8, 128).at[t, :, :, pl.ds(0, 3), :]
        ends = (inside, outside) if out else (outside, inside)
        copies.append(pltpu.make_async_copy(*ends, semaphores.at[first + t]))
    return copies


def to_elements(half, wide, table, kept, puts):
    moved = moved_lanes(wide[...].reshape(600, 256), table)
    if half == 0:
        kept[...] = moved
        return
    for pair in range(2):
        lanes = slice(128 * pair, 128 * pair + 128)
        for l, value in enumerate(interleave(kept[:, lanes], moved[:, lanes])):
            puts(2 * pair + l, value.reshape(3, 5, 5, 8, 128))


def to_nodes(get, table, tall):
    pairs = [interleave(get(2 * p).reshape(600, 128), get(2 * p + 1).reshape(600, 128)) for p in range(2)]
    for half in range(2):
        wide = jnp.concatenate([pairs[0][half], pairs[1][half]], axis=1)
        tall[half] = moved_lanes(wide, table).reshape(3, 5, 5, 8, 256)


def lookup(material, row, region):
    total = jnp.zeros_like(region)
    for m in range(material.shape[1]):
        total = jnp.where(region == float(m + 1), material[row, m], total)
    return total


def internal(u, out, lame, shear, gx, gz, cross, planes, side):
    def depth_lines(i, carry):
        for j in range(5):
            for c in range(3):
                v = [u[c, i, j, k] for k in range(4)]
                v.append(deeper(v[0]))
                u[c, i, j, 4] = v[4]
                for k, g in enumerate(line(deriv, v)):
                    gz[c, i, j, k] = g
        return carry

    lax.fori_loop(0, 5, depth_lines, 0)

    def plane(k, carry):
        weight = jnp.where((k == 0) | (k == 4), float(quad[0]), jnp.where(k == 2, float(quad[2]), float(quad[1])))
        lame_k, shear_k = lame * (2.0 * weight), shear * (2.0 * weight)
        pairs = {}
        for a in range(3):
            for b in range(a, 3):
                w = float(quad[a] * quad[b])
                pairs[a, b] = pairs[b, a] = (lame_k * w, shear_k * w, shear_k * (2.0 * w))
        for c in range(3):
            for j in range(5):
                for i, g in enumerate(line(deriv, [u[c, i, j, k] for i in range(5)])):
                    gx[c, i, j] = g
        for i in range(5):
            gy = [line(deriv, [u[c, i, j, k] for j in range(5)]) for c in range(3)]
            ys = [[], [], []]
            for j in range(5):
                lw, mw, mw2 = pairs[kind[i], kind[j]]
                g0, g1, g2 = [[gx[c, i, j], gy[c][j], gz[c, i, j, k]] for c in range(3)]
                dilated = lw * (g0[0] + g1[1] + g2[2])
                s01 = mw * (g0[1] + g1[0])
                s02 = mw * (g0[2] + g2[0])
                s12 = mw * (g1[2] + g2[1])
                side[0, i, j] = dilated + mw2 * g0[0]
                side[1, i, j] = s01
                cross[0, i, j, k] = s02
                cross[1, i, j, k] = s12
                cross[2, i, j, k] = dilated + mw2 * g2[2]
                ys[0].append(s01)
                ys[1].append(dilated + mw2 * g1[1])
                ys[2].append(s12)
            for c in range(3):
                for j, value in enumerate(line(deriv_t, ys[c])):
                    planes[c, i, j, k] = value
        for j in range(5):
            for c in range(3):
                v = [side[c, i, j] if c < 2 else cross[0, i, j, k] for i in range(5)]
                for i, value in enumerate(line(deriv_t, v)):
                    planes[c, i, j, k] += value
        return carry

    lax.fori_loop(0, 5, plane, 0)

    def depth_sums(i, carry):
        for j in range(5):
            for c in range(3):
                v = line(deriv_t, [cross[c, i, j, k] for k in range(5)])
                v = [v[k] + planes[c, i, j, k] for k in range(5)]
                out[c, i, j, 0] = v[0] + shallower(v[4])
                for k in range(1, 4):
                    out[c, i, j, k] = v[k]
        return carry

    lax.fori_loop(0, 5, depth_sums, 0)
    sub = rows_of()

    def fold(k, carry):
        for c in range(3):
            for i in range(5):
                low, high = out[c, i, 0, k], out[c, i, 4, k]
                out[c, i, 0, k] = low + jnp.where(sub % 4 == 0, 0.0, pltpu.roll(high, 1, 0))
                out[c, i, 4, k] = high + jnp.where(sub % 4 == 3, 0.0, pltpu.roll(low, 7, 0))
            for j in range(5):
                low, high = out[c, 0, j, k], out[c, 4, j, k]
                out[c, 0, j, k] = low + jnp.where(sub < 4, 0.0, pltpu.roll(high, 4, 0))
                out[c, 4, j, k] = high + jnp.where(sub < 4, pltpu.roll(low, 4, 0), 0.0)
        return carry

    lax.fori_loop(0, 4, fold, 0)


def rolled(x, amount, axis=0):
    amount = amount % x.shape[axis]
    return pltpu.roll(x, amount, axis) if amount else x


def parity_x():
    return position("gx") % 2


def parity_y():
    return along_y() % 2


def sort_out(odd, low, high):
    return jnp.where(odd == 1, low, high), jnp.where(odd == 1, high, low)


def pack_x(force, first, second):
    sub, odd = rows_of(), parity_x()
    for c in range(3):
        for j in range(5):
            for half in range(2):
                at = (c * 5 + j) * 2 + half
                a, b = force[c, 0, j, 2 * half], force[c, 0, j, 2 * half + 1]
                low = jnp.where(sub < 4, a, rolled(b, 4))
                a, b = force[c, 4, j, 2 * half], force[c, 4, j, 2 * half + 1]
                high = jnp.where(sub < 4, rolled(a, 4), b)
                first[at], second[at] = sort_out(odd, low, high)


def pack_y(force, low, high):
    sub = rows_of()
    for c in range(3):
        for i in range(5):
            a, b = force[c, i, 0, 0], rolled(force[c, i, 4, 0], -3)
            for k in range(1, 4):
                a = jnp.where(sub % 4 == k, rolled(force[c, i, 0, k], k), a)
                b = jnp.where(sub % 4 == k, rolled(force[c, i, 4, k], k - 3), b)
            low[c * 5 + i] = a
            high[c * 5 + i] = b


def add_x(force, first, second):
    sub, odd = rows_of(), parity_x()
    for c in range(3):
        for j in range(5):
            for half in range(2):
                at = (c * 5 + j) * 2 + half
                r, s = sort_out(odd, first[at], second[at])
                force[c, 0, j, 2 * half] += jnp.where(sub < 4, r, 0.0)
                force[c, 0, j, 2 * half + 1] += jnp.where(sub < 4, rolled(r, 4), 0.0)
                force[c, 4, j, 2 * half] += jnp.where(sub < 4, 0.0, rolled(s, 4))
                force[c, 4, j, 2 * half + 1] += jnp.where(sub < 4, 0.0, s)


def add_y(force, first, second):
    sub, odd = rows_of(), parity_y()
    for c in range(3):
        for i in range(5):
            r, s = sort_out(odd, first[c * 5 + i], second[c * 5 + i])
            for k in range(4):
                force[c, i, 0, k] += jnp.where(sub % 4 == 0, rolled(r, -k), 0.0)
                force[c, i, 4, k] += jnp.where(sub % 4 == 3, rolled(s, 3 - k), 0.0)


def edge_rows(low, high, came1, came2, first, second):
    sub, odd, odd_y = rows_of(), parity_x(), parity_y()
    for c in range(3):
        came = [[sort_out(odd, came1[at], came2[at]) for at in range((c * 5 + j) * 2, (c * 5 + j) * 2 + 2)] for j in (0, 4)]
        for i in range(5):
            rows = [low[c * 5 + i], high[c * 5 + i]]
            if i in (0, 4):
                start, side = i, i // 4
                for end, row in ((0, 0), (1, 3)):
                    for k in range(4):
                        r = rolled(came[end][k // 2][side], start + k - (4 * (k % 2) + row))
                        rows[end] = rows[end] + jnp.where(sub == start + k, r, 0.0)
            first[c * 5 + i], second[c * 5 + i] = sort_out(odd_y, *rows)


def first_edge_kernel(low, high, came1, came2, rows_low, rows_high, crater1, crater2, after, first, second, token, ends, semaphores):
    token[...] = after[0:8]
    copies = fetch(
        [(c.at[:, pl.ds(24 * h, 8), :], ends.at[n, :, pl.ds(8 * h, 8), :]) for n, c in enumerate((crater1, crater2)) for h in range(2)],
        semaphores,
    )
    edge_rows(low, high, came1, came2, first, second)
    odd, odd_y = parity_x(), parity_y()
    regions = sort_out(odd, came1[30], came2[30])
    for n, value in enumerate((low[15], regions[0], regions[1])):
        first[15 + n] = value
        second[15 + n] = value
    for copy in copies:
        copy.wait()
    for f in range(5):
        for t in range(2):
            lanes = slice(128 * t, 128 * t + 128)
            at = 18 + f * 4 + t * 2
            first[at], second[at] = sort_out(odd_y, rows_low[f * 2 + t], rows_high[f * 2 + t])
            found = []
            for row in (0, 15):
                sides = sort_out(odd, ends[0, f, row : row + 1, lanes], ends[1, f, row : row + 1, lanes])
                found.append(jnp.concatenate(list(sides) * 4, axis=0))
            first[at + 1], second[at + 1] = sort_out(odd_y, *found)


def second_edge_kernel(low, high, came1, came2, after, first, second, token):
    edge_rows(low, high, came1, came2, first, second)
    token[...] = after[...]


def region_grid(own, x1, x2, y1, y2):
    xl, xh = sort_out(parity_x(), x1[30], x2[30])
    yl, yh = [list(v) for v in zip(*[sort_out(parity_y(), y1[n], y2[n]) for n in (15, 16, 17)])]
    return [[yl[1], xl, yh[1]], [yl[0], own, yh[0]], [yl[2], xh, yh[2]]]


def shared_density(grid):
    sub = rows_of()
    across = []
    for y in range(3):
        low, mid, high = grid[0][y], grid[1][y], grid[2][y]
        turned = rolled(mid, 4)
        across.append([jnp.where(sub < 4, rolled(low, 4), turned), mid, jnp.where(sub < 4, turned, rolled(high, 4))])
    found = [[None] * 3 for _ in range(3)]
    for x in range(3):
        low, mid, high = across[0][x], across[1][x], across[2][x]
        found[x][0] = jnp.where(sub % 4 == 0, rolled(low, -3), rolled(mid, 1))
        found[x][1] = mid
        found[x][2] = jnp.where(sub % 4 == 3, rolled(high, 3), rolled(mid, -1))
    sums = []
    for x in ((1,), (0, 1), (1, 2)):
        row = []
        for y in ((1,), (0, 1), (1, 2)):
            total = sum(found[a][b] for a in x for b in y)
            row.append((total + shallower(total), total))
        sums.append(row)
    return sums


def mass_scales(sums):
    return [[[1.0 / s for s in pair] for pair in row] for row in sums]


def edge_kind(i):
    return 1 if i == 0 else 2 if i == 4 else 0


def accel_scale(i, j, k):
    return float(-1.0 / (half_size**3 * quad[i] * quad[j] * quad[k]))


def first_kernel(nodes_y, u, v, a, density, momentum, energy, dest, slot, region, material,
                 b_out, bottoms, f_out, x1, x2, y_low, y_high, rows_low, rows_high, region_out,
                 elem, gx, gz, cross, planes, side, u_in, v_in, a_in, wide_u, wide_b, kept_u, kept_b, b_held,
                 cells, copies_held, dest_in, slot_in, region_in, semaphores):
    early = fetch(
        [(region, region_in), (dest, dest_in), (slot, slot_in), (density, cells.at[0]),
         (momentum, cells.at[pl.ds(1, 3)]), (energy, cells.at[4])],
        semaphores.at[pl.ds(14, 6)],
    )
    copies = [tile_copies(f, h, semaphores, 4 * n) for n, (f, h) in enumerate(((u, u_in), (v, v_in), (a, a_in)))]
    for t in range(4):
        for copy in copies:
            copy[t].start()
    table = depth_table()
    for copy in early:
        copy.wait()
    region_now = jnp.concatenate([region_in[0], region_in[1]], axis=0).astype(f32) + 1.0
    region_out[...] = region_now
    block = deepest_block(nodes_y, cells, dest_in, slot_in, region_now, rows_low, rows_high)
    for n in range(bottoms.shape[0]):
        copies_held[n] = block
    save_bottoms = pltpu.make_async_copy(copies_held, bottoms, semaphores.at[13])
    save_bottoms.start()

    def put_u(l, value):
        elem[:, :, :, l] = value

    def put_b(l, value):
        b_held[:, :, :, l] = value

    for half in range(2):
        for t in (2 * half, 2 * half + 1):
            for copy in copies:
                copy[t].wait()

        def column(i, carry):
            for t in (2 * half, 2 * half + 1):
                lanes = slice(128 * (t % 2), 128 * (t % 2) + 128)
                for j in range(5):
                    now, later = [], []
                    for r in range(8):
                        at = (t, node_at(i, j, r), slice(None))
                        step = time_step * v_in[at] + (0.5 * time_step**2) * a_in[at]
                        now.append(u_in[at] + step)
                        later.append(now[-1] + step)
                    for c, value in enumerate(gather_rows(now)):
                        wide_u[c, i, j, :, lanes] = value
                    for c, value in enumerate(gather_rows(later)):
                        wide_b[c, i, j, :, lanes] = value
            return carry

        lax.fori_loop(0, 5, column, 0)
        to_elements(half, wide_u, table, kept_u, put_u)
        to_elements(half, wide_b, table, kept_b, put_b)
    save_b = pltpu.make_async_copy(b_held, b_out, semaphores.at[12])
    save_b.start()
    internal(elem, f_out, lookup(material, 1, region_now), lookup(material, 2, region_now), gx, gz, cross, planes, side)
    pack_x(f_out, x1, x2)
    pack_y(f_out, y_low, y_high)
    x1[30] = region_now
    x2[30] = region_now
    y_low[15] = region_now
    save_b.wait()
    save_bottoms.wait()


def second_kernel(b, f, came_x1, came_x2, came_y1, came_y2, region, material, after, a_out, f_out, x1, x2, y_low, y_high, scales, token,
                  elem, gx, gz, cross, planes, side):
    region_now = region[...]
    token[...] = after[...]
    a_out[...] = f[...]
    add_x(a_out, came_x1, came_x2)
    add_y(a_out, came_y1, came_y2)
    grid = region_grid(region_now, came_x1, came_x2, came_y1, came_y2)
    inverse = mass_scales(shared_density([[lookup(material, 0, r) for r in row] for row in grid]))
    for x in range(3):
        for y in range(3):
            for z in range(2):
                scales[x, y, z] = inverse[x][y][z]
    for i in range(5):
        for j in range(5):
            for k in range(4):
                scale = scales[edge_kind(i), edge_kind(j), min(k, 1)] * accel_scale(i, j, k)
                for c in range(3):
                    value = a_out[c, i, j, k] * scale
                    a_out[c, i, j, k] = value
                    elem[c, i, j, k] = b[c, i, j, k] + time_step**2 * value
    internal(elem, f_out, lookup(material, 1, region_now), lookup(material, 2, region_now), gx, gz, cross, planes, side)
    pack_x(f_out, x1, x2)
    pack_y(f_out, y_low, y_high)


def spread_surface(source, held, count):
    lane = lanes_of((24, 128))
    for n in range(27):
        at = 8 * n
        tile, shift = at // 128, (128 - at % 128) % 128
        moved = rolled(source[:, 128 * tile : 128 * tile + 128], shift, 1)
        held[n] = jnp.where(lane < count, moved, 0.0)


def add_surface(held, tall):
    for c in range(3):
        for i in range(5):
            for j in range(5):
                for ex in range(2):
                    value = held[c * 9 + 4 * ex + i, pl.ds(j, 4, stride=4), :]
                    tall[0, c, i, j, 4 * ex : 4 * ex + 4, 0:128] += value


def place_kernel(a1, surf1, u, v, a, after, u_out, v_part, u_in, v_in, a_in, tall, surface, u_held, semaphores):
    copies = [tile_copies(f, h, semaphores, 4 * n) for n, (f, h) in enumerate(((u, u_in), (v, v_in), (a, a_in)))]
    for t in range(4):
        for copy in copies:
            copy[t].start()
    spread_surface(surf1, surface, 1)
    to_nodes(lambda l: a1[:, :, :, l], depth_table(back=True), tall)
    add_surface(surface, tall)
    saves = tile_copies(u_out, u_held, semaphores, 12, out=True)
    for t in range(4):
        for copy in copies:
            copy[t].wait()
        lanes = slice(128 * (t % 2), 128 * (t % 2) + 128)

        def body(i, j, wanted):
            for r, accel in scatter_rows([tall[t // 2, c, i, j, :, lanes] for c in range(3)], wanted):
                at = (t, node_at(i, j, r), slice(None))
                vv, aa = v_in[at], a_in[at]
                u_held[at] = u_in[at] + 2.0 * time_step * vv + time_step**2 * (aa + accel)
                v_part[at] = vv + (0.5 * time_step) * (aa + 2.0 * accel)

        every_node(body)
        saves[t].start()
    for save in saves:
        save.wait()


def last_kernel(v_part, f, x1, x2, y1, y2, scales, surf1, surf2, v_out, a_out, v_held, a_held, tall, surface, force, semaphores):
    force[...] = f[...]
    add_x(force, x1, x2)
    add_y(force, y1, y2)
    for i in range(5):
        for j in range(5):
            for k in range(4):
                scale = scales[edge_kind(i), edge_kind(j), min(k, 1)] * accel_scale(i, j, k)
                for c in range(3):
                    force[c, i, j, k] = force[c, i, j, k] * scale
    spread_surface(surf1, surface.at[0], 1)
    spread_surface(surf2, surface.at[1], 5)
    surface[0] = surface[0] + surface[1]
    to_nodes(lambda l: force[:, :, :, l], depth_table(back=True), tall)
    add_surface(surface.at[0], tall)
    saves = tile_copies(v_out, v_held, semaphores, 0, out=True) + tile_copies(a_out, a_held, semaphores, 4, out=True)
    for t in range(4):
        lanes = slice(128 * (t % 2), 128 * (t % 2) + 128)

        def body(i, j, wanted):
            for r, accel in scatter_rows([tall[t // 2, c, i, j, :, lanes] for c in range(3)], wanted):
                at = (t, node_at(i, j, r), slice(None))
                a_held[at] = accel
                v_held[at] = v_part[at] + (0.5 * time_step) * accel

        every_node(body)
        saves[t].start()
        saves[4 + t].start()
    for save in saves:
        save.wait()


def whole():
    return pl.BlockSpec(memory_space=pltpu.VMEM)


def scalars():
    return pl.BlockSpec(memory_space=pltpu.SMEM)


def call(kernel, ins, outs, scratch, smem=(), away=(), out_away=(), mib=10, copies=0):
    def spec(n):
        return scalars() if n in smem else pl.BlockSpec(memory_space=pltpu.HBM) if n in away else whole()

    scratch = [pltpu.VMEM(s, f32) if isinstance(s, tuple) else s for s in scratch]
    return pl.pallas_call(
        kernel,
        out_shape=[jax.ShapeDtypeStruct(s, f32) for s in outs],
        in_specs=[spec(n) for n in range(len(ins))],
        out_specs=[pl.BlockSpec(memory_space=pltpu.HBM) if n in out_away else whole() for n in range(len(outs))],
        scratch_shapes=scratch + ([pltpu.SemaphoreType.DMA((copies,))] if copies else []),
        compiler_params=pltpu.CompilerParams(vmem_limit_bytes=mib * 1024 * 1024),
    )(*ins)


def fetch(pairs, semaphores):
    copies = [pltpu.make_async_copy(source, target, semaphores.at[n]) for n, (source, target) in enumerate(pairs)]
    for copy in copies:
        copy.start()
    return copies


element_shape = (3, 5, 5, 4, 8, 128)
lines_shape = (3, 5, 5, 5, 8, 128)
internal_scratch = [lines_shape, (3, 5, 5, 8, 128), lines_shape, lines_shape, lines_shape, (2, 5, 5, 8, 128)]


def exchange(axis, first, second):
    count = lax.axis_size(axis)
    pairs = [(i, i + 1) for i in range(1, count - 1, 2)]
    first = lax.ppermute(first, axis, [(i, i ^ 1) for i in range(count)])
    return first, lax.ppermute(second, axis, pairs + [(j, i) for i, j in pairs])


def surface_tables():
    lane = np.arange(128)
    j, ey = lane // 8, lane % 8
    used = (j < 5) & (ey < 6)
    place = np.where(used, ey + 1, -9)
    source = lane[:, None]
    centre = source == place
    meet = centre | ((j == 0) & (source == place - 1)) | ((j == 4) & (source == place + 1))
    along = np.zeros((128, 128))
    for a in range(40):
        for b in range(40):
            if a % 8 == b % 8 and a % 8 < 6:
                along[a, b] = deriv[b // 8, a // 8]
    node = np.where(used, 4 * (ey - 1) + j, -9)
    fold = (lane[:, None] == node) & (lane[:, None] < 17)
    keep = fold & ((j < 4) & (ey < 5) | (j == 4) & (ey == 4))
    return np.stack([centre, meet, along, along.T, fold, keep]).astype(np.float32)


def full_dot(x, y, back=False):
    dims = (((1,), (1 if back else 0,)), ((), ()))
    return lax.dot_general(x, y, dims, precision=lax.Precision.HIGHEST, preferred_element_type=f32)


def deposit(faces, nodes_y, base_x, base_y, total):
    rows = faces.shape[1]
    sub = rows_of((8, 512)).astype(f32)
    total[...] = jnp.zeros_like(total)

    def one(step, carry):
        def wide(q):
            block = faces[q, pl.ds(4 * step, 4), :]
            return jnp.concatenate([block[n : n + 1] for n in range(4)], axis=1)

        ids = wide(3)
        node_x = jnp.floor((ids + 0.5) * (1.0 / nodes_y))
        rel_y = jnp.broadcast_to(ids - node_x * nodes_y - base_y, (8, 512))
        rel_x = jnp.broadcast_to(node_x - base_x, (8, 512))
        left = []
        hits = [(rel_x - i == 4.0 * sub) & (sub < 4.0) for i in range(5)]
        parts = [split_three(wide(c)) for c in range(3)]
        for part in range(3):
            for c in range(3):
                value = jnp.broadcast_to(parts[c][part].astype(f32), (8, 512))
                left += [jnp.where(hit, value, 0.0) for hit in hits]
        right = [jnp.where((rel_y - j == 4.0 * sub) & (sub < 6.0), 1.0, 0.0) for j in range(5)]
        right.append(jnp.zeros((88, 512), f32))
        left, right = jnp.concatenate(left, axis=0), jnp.concatenate(right, axis=0)
        total[...] += lax.dot_general(
            left.astype(jnp.bfloat16), right.astype(jnp.bfloat16), (((1,), (1,)), ((), ())), preferred_element_type=f32
        )
        return carry

    lax.fori_loop(0, rows // 4, one, 0)


def top_grid(rows, z):
    sub, lane = rows_of(), lanes_of()
    out = jnp.zeros((8, 128), f32)
    for x in range(3):
        for y in range(3):
            row = jnp.broadcast_to(rows[x][y], (8, 128))
            for ex in range(2):
                here = (sub == 2 * x + ex) & (lane >= 4 * y - 2) & (lane < 4 * y + 2) & (lane < 8)
                out = jnp.where(here, rolled(row, 4 * y - 2 - 8 * z - 4 * ex, 1), out)
    return out


def respond(total, grid, material, tables, out1, out2):
    sub, lane = rows_of(), lanes_of()
    top, below = top_grid(grid, 0), top_grid(grid, 1)
    centre, meet, along, along_t, fold, keep = [tables[n] for n in range(6)]
    sums0 = full_dot(lookup(material, 0, top), meet)
    sums1 = full_dot(lookup(material, 0, below), meet)
    lame = rolled(full_dot(lookup(material, 1, top), centre), -1)
    shear = rolled(full_dot(lookup(material, 2, top), centre), -1)
    weight_y = jnp.ones((8, 128), f32)
    for j in range(5):
        weight_y = jnp.where(lane // 8 == j, float(quad[j]), weight_y)

    def inverse(sums):
        mid = rolled(sums, -1)
        found = {0: mid + sums, 1: mid, 4: mid + rolled(sums, -2)}
        found = {i: jnp.where(s > 0.0, 1.0 / (s * weight_y), 0.0) for i, s in found.items()}
        found[2] = found[3] = found[1]
        return found

    light, heavy = inverse(sums0), inverse(sums0 + sums1)
    first = [[None] * 5 for _ in range(3)]
    moved = [[None] * 5 for _ in range(3)]
    for c in range(3):
        for i in range(5):
            at = (c * 5 + i) * 8
            force = total[at : at + 8] + total[at + 120 : at + 128] + total[at + 240 : at + 248]
            first[c][i] = force * light[i] * -accel_scale(i, 2, 0) * float(quad[2])
            moved[c][i] = first[c][i] * time_step**2
    gx = [line(deriv, moved[c]) for c in range(3)]
    gy = full_dot(jnp.concatenate([moved[c][i] for c in range(3) for i in range(5)], axis=0), along)
    gy = [[gy[(c * 5 + i) * 8 : (c * 5 + i) * 8 + 8] for i in range(5)] for c in range(3)]
    lame_w, shear_w = lame * weight_y * 2.0, shear * weight_y * 2.0
    d00 = float(deriv[0, 0])
    sx = [[], [], []]
    sy = [[], [], []]
    sz = [[], [], []]
    qs = [[], [], []]
    pressed = []
    for i in range(5):
        lw, mw = lame_w * float(quad[i]), shear_w * float(quad[i])
        d = [moved[c][i] for c in range(3)]
        gz = [d00 * x for x in d]
        dilated = lw * (gx[0][i] + gy[1][i] + gz[2])
        s01 = mw * (gx[1][i] + gy[0][i])
        s02 = mw * (gx[2][i] + gz[0])
        s12 = mw * (gy[2][i] + gz[1])
        for c, value in enumerate((dilated + 2.0 * mw * gx[0][i], s01, s02)):
            sx[c].append(value)
        for c, value in enumerate((s01, dilated + 2.0 * mw * gy[1][i], s12)):
            sy[c].append(value)
        for c, value in enumerate((s02, s12, dilated + 2.0 * mw * gz[2])):
            sz[c].append(value)
        for c, value in enumerate((mw * d[0], mw * d[1], (lw + 2.0 * mw) * d[2])):
            qs[c].append(value)
        pressed.append(lw * d[2])
    ydiv = full_dot(jnp.concatenate(sy[0] + sy[1] + sy[2] + pressed + qs[1], axis=0), along_t)
    ydiv = [[ydiv[(n * 5 + i) * 8 : (n * 5 + i) * 8 + 8] for i in range(5)] for n in range(5)]
    xdiv = [line(deriv_t, v) for v in sx + [pressed, qs[0]]]
    base = [xdiv[3], ydiv[3], [p + q for p, q in zip(xdiv[4], ydiv[4])]]
    second = {}
    for c in range(3):
        for i in range(5):
            for l in range(5):
                stiff = float(sum(deriv[k, l] * quad[k] * deriv[k, 0] for k in range(1, 5)))
                value = float(deriv[0, l] * quad[0]) * sz[c][i] + stiff * qs[c][i]
                if l:
                    value = value + float(deriv[l, 0] * quad[l]) * base[c][i]
                else:
                    value = value + float(quad[0]) * (xdiv[c][i] + ydiv[c][i])
                scale = (heavy if l == 4 else light)[i]
                second[c, i, l] = value * scale * (accel_scale(i, 2, l) * float(quad[2]))
    rows1, rows2 = [], []
    for c in range(3):
        for x in range(9):
            own = 1 if x < 4 else 2
            rows1.append(jnp.where(sub == 0, rolled(first[c][x - 4 * (own - 1)], -own), 0.0))
            block = jnp.zeros((8, 128), f32)
            for l in range(5):
                for ex in range(4):
                    i = x - 4 * (ex - 1)
                    if 0 <= i <= 4:
                        block = block + jnp.where(sub == l, rolled(second[c, i, l], l - ex), 0.0)
            rows2.append(block)
    blank = [jnp.zeros((40, 128), f32)]
    out1[...] = full_dot(keep[0:24], jnp.concatenate(rows1 + blank, axis=0), back=True)
    out2[...] = full_dot(fold[0:24], jnp.concatenate(rows2 + blank, axis=0), back=True)


def position(axis):
    return lax.axis_index(axis)


def along_y():
    return lax.axis_index("grp") * lax.axis_size("gy") + lax.axis_index("gy")


def primitives(state):
    inverse = 1.0 / state[0]
    v = [state[1 + c] * inverse for c in range(3)]
    p = (gamma_gas - 1.0) * (state[4] - 0.5 * (state[1] * v[0] + state[2] * v[1] + state[3] * v[2]))
    return v + [p, jnp.sqrt(gamma_gas * p * inverse), state[4] + p]


def flux(state, prim, d):
    out = [state[1 + d]] + [state[1 + c] * prim[d] for c in range(3)] + [prim[5] * prim[d]]
    out[1 + d] = out[1 + d] + prim[3]
    return out, jnp.abs(prim[d]) + prim[4]


def twice_face(low, high):
    fastest = jnp.maximum(low[2], high[2])
    return [fl + fh - fastest * (uh - ul) for ul, uh, fl, fh in zip(low[0], high[0], low[1], high[1])]


def turned_change(state, prim, d, axis, ends):
    size = state[0].shape[axis]
    fluxes, speed = flux(state, prim, d)
    up = lambda x: pltpu.roll(x, size - 1, axis)
    high = ([up(x) for x in state], [up(x) for x in fluxes], up(speed))
    upper = twice_face((state, fluxes, speed), high)
    if ends is None:
        return [g - pltpu.roll(g, 1, axis) for g in upper]
    upper = [jnp.where(ends[1], 2.0 * f, g) for f, g in zip(fluxes, upper)]
    return [g - jnp.where(ends[0], 2.0 * f, pltpu.roll(g, 1, axis)) for f, g in zip(fluxes, upper)]


def planes_kernel(density, momentum, energy, first, second, semaphores):
    odd = parity_x()
    pairs = []
    for out, down in ((first, odd), (second, 1 - odd)):
        for n, plane in enumerate((3 - 3 * down, 2 - down)):
            rows = pl.ds(32 * n, 32)
            pairs.append((density.at[plane], out.at[0, rows]))
            pairs.append((momentum.at[:, plane], out.at[pl.ds(1, 3), rows]))
            pairs.append((energy.at[plane], out.at[4, rows]))
    for copy in fetch(pairs, semaphores):
        copy.wait()


def deepest_block(nodes_y, cells, dest, slot, region_now, rows_low, rows_high):
    sub, lane = rows_of(), lanes_of()
    pick = jnp.where(lane == 125 + sub, 1.0, 0.0)
    pieces = []
    for f in range(5):
        columns = jnp.concatenate([cells[f, x, :, 128:256] for x in range(4)], axis=0)
        pieces.append(full_dot(pick, columns, back=True)[0:3])
        for t in range(2):
            lanes = slice(128 * t, 128 * t + 128)
            for out, pair in ((rows_low, (0, 1)), (rows_high, (31, 30))):
                out[f * 2 + t] = jnp.concatenate([cells[f, x, r : r + 1, lanes] for r in pair for x in range(4)], axis=0)
    count_gy, count_x = lax.axis_size("gy"), lax.axis_size("gx")
    target, node = dest[...].astype(f32), slot[...].astype(f32)
    grp = jnp.floor((target + 0.5) * (1.0 / (count_gy * count_x)))
    rest = target - grp * (count_gy * count_x)
    gx = jnp.floor((rest + 0.5) * (1.0 / count_gy))
    gy = rest - gx * count_gy
    i = jnp.floor((node + 0.5) * (1.0 / 17.0))
    j = node - 17.0 * i
    pieces.append((8.0 * gx + i) * nodes_y + 16.0 * (grp * count_gy + gy) + j)
    found = jnp.zeros((8, 128), f32)
    for z in range(2):
        found = jnp.where(lane == 8 * z + sub, jnp.broadcast_to(region_now[:, z : z + 1], (8, 128)), found)
    pieces.append(jnp.broadcast_to(jnp.sum(found, axis=0, keepdims=True), (8, 128)))
    return jnp.concatenate(pieces, axis=0)


def crater_kernel(density, momentum, energy, came1, came2, rows1, rows2, after, out, token,
                  wide, mid, prims, face, fluxes, semaphores):
    planes, inner = pl.ds(2, 4), pl.ds(0, 32)
    copies = fetch(
        [(density, wide.at[0, planes, inner]), (momentum, wide.at[pl.ds(1, 3), planes, inner]),
         (energy, wide.at[4, planes, inner])],
        semaphores,
    )
    place, last_y = along_y(), lax.axis_size("grp") * lax.axis_size("gy") - 1
    gx, last_x = position("gx"), lax.axis_size("gx") - 1
    odd, odd_y = parity_x(), parity_y()
    for f in range(5):
        low, high = sort_out(odd, came1[f], came2[f])
        for p, value in ((0, low[32:64]), (1, low[0:32]), (6, high[0:32]), (7, high[32:64])):
            wide[f, p, 0:32, :] = value
            wide[f, p, 32:40, :] = value[0:8]
    token[...] = after[...]
    for copy in copies:
        copy.wait()
    for f in range(5):
        for x in range(4):
            wide[f, 2 + x, 32:40, :] = wide[f, 2 + x, 24:32, :]
        for t in range(2):
            lanes = slice(128 * t, 128 * t + 128)
            at = 18 + f * 4 + t * 2
            below, above = sort_out(odd_y, rows1[at], rows2[at])
            sides_below, sides_above = sort_out(odd_y, rows1[at + 1], rows2[at + 1])

            def put(p, row, edge, value):
                clamped = jnp.where(edge == 0, place == 0, place == last_y)
                at_edge = wide[f, p, 31 * edge : 31 * edge + 1, lanes]
                wide[f, p, row : row + 1, lanes] = jnp.where(clamped, at_edge, value)

            for x in range(4):
                put(2 + x, 39, 0, below[x : x + 1])
                put(2 + x, 38, 0, below[4 + x : 5 + x])
                put(2 + x, 32, 1, above[x : x + 1])
                put(2 + x, 33, 1, above[4 + x : 5 + x])
            for p, n in ((1, 0), (6, 1)):
                put(p, 39, 0, sides_below[n : n + 1])
                put(p, 32, 1, sides_above[n : n + 1])

    @pl.when(gx == 0)
    def _():
        for f in range(5):
            wide[f, 0] = wide[f, 2]
            wide[f, 1] = wide[f, 2]

    @pl.when(gx == last_x)
    def _():
        for f in range(5):
            wide[f, 6] = wide[f, 5]
            wide[f, 7] = wide[f, 5]

    lane = lanes_of((40, 256))
    ends = (lane == 0, lane == 255)

    def step(source, low, high, put):
        def along_x(p):
            state = [source[f, p] for f in range(5)]
            prim = primitives(state)
            return state, prim, flux(state, prim, 0)

        state, prim, (fx, speed) = along_x(low - 1)
        next_state, next_prim, (next_fx, next_speed) = along_x(low)
        g = twice_face((state, fx, speed), (next_state, next_fx, next_speed))
        for f in range(5):
            face[f] = g[f]
            fluxes[f] = next_fx[f]
        for n in range(6):
            prims[n] = next_prim[n]
        fluxes[5] = next_speed

        def plane(p, carry):
            state = [source[f, p] for f in range(5)]
            prim = [prims[n] for n in range(6)]
            next_state, next_prim, (next_fx, next_speed) = along_x(p + 1)
            g = twice_face((state, [fluxes[f] for f in range(5)], fluxes[5]), (next_state, next_fx, next_speed))
            change = [g[f] - face[f] for f in range(5)]
            for f in range(5):
                face[f] = g[f]
                fluxes[f] = next_fx[f]
            for n in range(6):
                prims[n] = next_prim[n]
            fluxes[5] = next_speed
            change = [a + b for a, b in zip(change, turned_change(state, prim, 1, 0, None))]
            change = [a + b for a, b in zip(change, turned_change(state, prim, 2, 1, ends))]
            for f in range(5):
                put(f, p, state[f] - (0.5 * cell_ratio) * change[f])
            return carry

        lax.fori_loop(low, high, plane, 0)

    def put_mid(f, p, value):
        mid[f, p] = value

    def put_out(f, p, value):
        out[f, p - 2] = value[0:32]

    step(wide, 1, 7, put_mid)

    @pl.when(gx == 0)
    def _():
        for f in range(5):
            mid[f, 1] = mid[f, 2]

    @pl.when(gx == last_x)
    def _():
        for f in range(5):
            mid[f, 6] = mid[f, 5]

    for f in range(5):
        for p in range(2, 6):
            edge = mid[f, p, 39:40, :]
            mid[f, p, 39:40, :] = jnp.where(place == 0, mid[f, p, 0:1, :], edge)
            edge = mid[f, p, 32:33, :]
            mid[f, p, 32:33, :] = jnp.where(place == last_y, mid[f, p, 31:32, :], edge)
    step(mid, 2, 6, put_out)


def bottom_tractions(bottoms, count_x, faces):
    shape = (count_x, 128)
    sub, lane = rows_of(shape), lanes_of(shape)
    count_gy = lax.axis_size("gy")

    def columns(q):
        parts = []
        for y in range(4):
            start = (y // count_gy * count_x * count_gy + y % count_gy) * 24 + q
            parts.append(bottoms[pl.ds(start, count_x, stride=24 * count_gy), :])
        found = []
        for x in range(4):
            total = rolled(parts[0], -32 * x, 1)
            for y in range(1, 4):
                total = jnp.where(lane // 32 == y, rolled(parts[y], 32 * (y - x), 1), total)
            found.append(total)
        return found

    cells = [[columns(f * 3 + z) for f in range(5)] for z in range(3)]
    state = [[[cells[z][f][x] for f in range(5)] for x in range(4)] for z in range(3)]
    ends_y = (lane == 0, lane == 127)

    def across_x(states, prims):
        fluxes = [flux(s, p, 0) for s, p in zip(states, prims)]
        data = [(s, f, a) for s, (f, a) in zip(states, fluxes)]
        up = lambda x: rolled(x, -1)
        wrap = ([up(v) for v in data[0][0]], [up(v) for v in data[0][1]], up(data[0][2]))
        upper = [twice_face(data[x], data[x + 1] if x < 3 else wrap) for x in range(4)]
        upper[3] = [jnp.where(sub == count_x - 1, 2.0 * f, g) for f, g in zip(data[3][1], upper[3])]
        below = [jnp.where(sub == 0, 2.0 * f, rolled(g, 1)) for f, g in zip(data[0][1], upper[3])]
        lower = [below] + upper[:3]
        return [[a - b for a, b in zip(u, l)] for u, l in zip(upper, lower)]

    def advanced(above, here, under, prim_above, prim_here, prim_under):
        changes = across_x(here, prim_here)
        out = []
        for x in range(4):
            change = [a + b for a, b in zip(changes[x], turned_change(here[x], prim_here[x], 1, 1, ends_y))]
            fz, az = flux(here[x], prim_here[x], 2)
            fa, aa = flux(above[x], prim_above[x], 2)
            lower = twice_face((above[x], fa, aa), (here[x], fz, az))
            if under is None:
                upper = [2.0 * f for f in fz]
            else:
                fu, au = flux(under[x], prim_under[x], 2)
                upper = twice_face((here[x], fz, az), (under[x], fu, au))
            out.append([s - (0.5 * cell_ratio) * (c + u - l) for s, c, u, l in zip(here[x], change, upper, lower)])
        return out

    prims = [[primitives(state[z][x]) for x in range(4)] for z in range(3)]
    middle = advanced(state[0], state[1], state[2], prims[0], prims[1], prims[2])
    deepest = advanced(state[1], state[2], None, prims[1], prims[2], None)
    prim_mid, prim_deep = [primitives(s) for s in middle], [primitives(s) for s in deepest]
    final = advanced(middle, deepest, None, prim_mid, prim_deep, None)
    ids = columns(15)
    for x in range(4):
        s, prim = final[x], primitives(final[x])
        at = pl.ds(x * count_x, count_x)
        faces[0, at, :] = face_area * s[1] * prim[2]
        faces[1, at, :] = face_area * s[2] * prim[2]
        faces[2, at, :] = face_area * (s[3] * prim[2] + prim[3])
        faces[3, at, :] = ids[x]


def deposit_kernel(nodes_y, count_x, bottoms, after, total, faces):
    base_x = (8 * position("gx") - 4).astype(f32)
    base_y = (16 * along_y() - 4).astype(f32)
    bottom_tractions(bottoms, count_x, faces)
    deposit(faces, nodes_y, base_x, base_y, total)


def respond_kernel(count_x, total, bottoms, material, tables, after, out1, out2, token, held, rows, semaphores):
    gx, place, count_gy = position("gx"), along_y(), lax.axis_size("gy")
    last_y = lax.axis_size("grp") * count_gy - 1
    pairs = [(tables, held)]
    for x in range(3):
        for y in range(3):
            cx, cy = jnp.clip(gx + x - 1, 0, count_x - 1), jnp.clip(place + y - 1, 0, last_y)
            rank = (cy // count_gy) * (count_x * count_gy) + cx * count_gy + cy % count_gy
            pairs.append((bottoms.at[rank, pl.ds(16, 8), :], rows.at[3 * x + y]))
    copies = fetch(pairs, semaphores)
    for copy in copies:
        copy.wait()
    found = []
    for x in range(3):
        found.append([])
        for y in range(3):
            px, py = gx + x - 1, place + y - 1
            inside = (px >= 0) & (px < count_x) & (py >= 0) & (py <= last_y)
            found[x].append(jnp.where(inside, rows[3 * x + y, 0:1, :], 0.0))
    respond(total, found, material, held, out1, out2)
    token[...] = after[...]


def shards(density, momentum, energy, displacement, velocity_field, acceleration, material, element_region_index,
           face_dest, face_slot):
    along, rank = ("grp", "gy"), ("grp", "gx", "gy")
    nodes_y = 16 * lax.axis_size(along) + 1
    count_x, devices = lax.axis_size("gx"), lax.axis_size(rank)
    crater = (density, momentum, energy)
    u, v, a = [jnp.transpose(x, (1, 2, 0, 3)) for x in (displacement, velocity_field, acceleration)]
    register, held_shape = (8, 128), (4, 1224, 128)
    crater1, crater2 = call(
        planes_kernel, crater, [(5, 64, 256), (5, 64, 256)], [], away=(0, 1, 2), out_away=(0, 1), mib=56, copies=12
    )
    crater1, crater2 = exchange("gx", crater1, crater2)
    vectors = pltpu.VMEM((1, 128), jnp.int32)
    b, bottoms, f, x1, x2, y_low, y_high, rows_low, rows_high, region = call(
        functools.partial(first_kernel, float(nodes_y)),
        (u, v, a) + crater + (face_dest.reshape(1, -1), face_slot, element_region_index, material),
        [element_shape, (devices, 24, 128), element_shape, (31, 8, 128), (31, 8, 128), (16, 8, 128), (15, 8, 128),
         (10, 8, 128), (10, 8, 128), register],
        internal_scratch
        + [held_shape] * 3
        + [(3, 5, 5, 8, 256), (3, 5, 5, 8, 256), (600, 256), (600, 256), element_shape]
        + [(5, 4, 32, 256), (devices, 24, 128), vectors, vectors, pltpu.VMEM((2, 4, 128), jnp.int32)],
        smem=(9,),
        away=(0, 1, 2, 3, 4, 5, 6, 7, 8),
        out_away=(0, 1),
        mib=56,
        copies=20,
    )
    bottoms = lax.all_to_all(bottoms, rank, 0, 0, tiled=True)
    (total,) = call(
        functools.partial(deposit_kernel, float(nodes_y), count_x),
        (bottoms.reshape(devices * 24, 128), region),
        [(360, 128)],
        [(4, 4 * count_x, 128)],
    )
    x1, x2 = exchange("gx", x1, x2)
    y1, y2, token = call(
        first_edge_kernel,
        (y_low, y_high, x1, x2, rows_low, rows_high, crater1, crater2, total),
        [(38, 8, 128), (38, 8, 128), register],
        [(2, 5, 16, 256)],
        away=(6, 7),
        copies=4,
    )
    surf1, surf2, token = call(
        functools.partial(respond_kernel, count_x),
        (total, bottoms, material, jnp.asarray(surface_tables()), token),
        [(24, 256), (24, 256), register],
        [(6, 128, 128), (9, 8, 128)],
        smem=(2,),
        away=(1, 3),
        copies=10,
    )
    y1, y2 = exchange(along, y1, y2)
    a1, f2, p1, p2, y_low, y_high, scales, token = call(
        second_kernel,
        (b, f, x1, x2, y1, y2, region, material, token),
        [element_shape, element_shape, (30, 8, 128), (30, 8, 128), (15, 8, 128), (15, 8, 128), (3, 3, 2, 8, 128), register],
        internal_scratch,
        smem=(7,),
    )
    hydro_state, token = call(
        crater_kernel,
        crater + (crater1, crater2, y1, y2, token),
        [(5, 4, 32, 256), register],
        [(5, 8, 40, 256), (5, 8, 40, 256), (6, 40, 256), (5, 40, 256), (6, 40, 256)],
        away=(0, 1, 2),
        copies=3,
    )
    p1, p2 = exchange("gx", p1, p2)
    r1, r2, token = call(
        second_edge_kernel, (y_low, y_high, p1, p2, token), [(15, 8, 128), (15, 8, 128), register], []
    )
    u_out, v_part = call(
        place_kernel,
        (a1, surf1, u, v, a, token),
        [u.shape, held_shape],
        [held_shape] * 3 + [(2, 3, 5, 5, 8, 256), (27, 24, 128), held_shape],
        away=(2, 3, 4),
        out_away=(0,),
        mib=20,
        copies=16,
    )
    r1, r2 = exchange(along, r1, r2)
    v_out, a_out = call(
        last_kernel,
        (v_part, f2, p1, p2, r1, r2, scales, surf1, surf2),
        [u.shape] * 2,
        [held_shape] * 2 + [(2, 3, 5, 5, 8, 256), (2, 27, 24, 128), element_shape],
        out_away=(0, 1),
        mib=16,
        copies=8,
    )
    u_out, v_out, a_out = [jnp.transpose(x, (2, 0, 1, 3)) for x in (u_out, v_out, a_out)]
    return hydro_state, u_out, v_out, a_out


def solution(mesh):
    field = P(None, "gx", ("grp", "gy"), None)
    cells = P("gx", ("grp", "gy"), None)
    rank = ("grp", "gx", "gy")
    return jax.shard_map(
        shards,
        mesh=mesh,
        in_specs=(cells, field, cells, field, field, field, P(), cells, P(rank, None, None), P(rank, None)),
        out_specs=(field, field, field, field),
        check_vma=False,
    )
```

```python
import functools

import jax
import jax.numpy as jnp
import numpy as np
from jax import lax
from jax.experimental import pallas as pl
from jax.experimental.pallas import tpu as pltpu
from jax.sharding import PartitionSpec as P

gamma_gas = 1.4
cell_ratio = 0.05
half_size = 2.0
time_step = 0.1
face_area = 2.0


def gll_tables():
    root = np.sqrt(3.0 / 7.0)
    points = np.array([-1.0, -root, 0.0, root, 1.0])
    weights = np.array([0.1, 49.0 / 90.0, 32.0 / 45.0, 49.0 / 90.0, 0.1])
    products = [np.prod([points[r] - points[c] for c in range(5) if c != r]) for r in range(5)]
    derivative = np.zeros((5, 5))
    for r in range(5):
        for c in range(5):
            if r != c:
                derivative[r, c] = products[r] / products[c] / (points[r] - points[c])
        derivative[r, r] = sum(1.0 / (points[r] - points[c]) for c in range(5) if c != r)
    derivative[2, 2] = 0.0
    return derivative, weights


deriv, quad = gll_tables()
deriv_t = deriv.T
kind = [0, 1, 2, 1, 0]
f32 = jnp.float32


def line(matrix, v):
    even, odd = (matrix + matrix[:, ::-1]) / 2, (matrix - matrix[:, ::-1]) / 2
    e0, e1, o0, o1 = v[0] + v[4], v[1] + v[3], v[0] - v[4], v[1] - v[3]
    top = [float(even[i, 0]) * e0 + float(even[i, 1]) * e1 + float(matrix[i, 2]) * v[2] for i in range(2)]
    low = [float(odd[i, 0]) * o0 + float(odd[i, 1]) * o1 for i in range(2)]
    centre = float(matrix[2, 0]) * o0 + float(matrix[2, 1]) * o1
    return [top[0] + low[0], top[1] + low[1], centre, low[1] - top[1], low[0] - top[0]]


def rows_of(shape=(8, 128)):
    return lax.broadcasted_iota(jnp.int32, shape, 0)


def lanes_of(shape=(8, 128)):
    return lax.broadcasted_iota(jnp.int32, shape, 1)


def deeper(x):
    return jnp.where(lanes_of() == 127, 0.0, pltpu.roll(x, 127, 1))


def shallower(x):
    return jnp.where(lanes_of() == 0, 0.0, pltpu.roll(x, 1, 1))


def split_three(x):
    high = x.astype(jnp.bfloat16)
    rest = x - high.astype(f32)
    middle = rest.astype(jnp.bfloat16)
    return high, middle, (rest - middle.astype(f32)).astype(jnp.bfloat16)


def depth_table(back=False):
    a = lax.broadcasted_iota(jnp.int32, (256, 256), 1 if back else 0)
    b = lax.broadcasted_iota(jnp.int32, (256, 256), 0 if back else 1)
    table = jnp.where(a == 4 * (b & 63) + (b >> 6), 1.0, 0.0).astype(jnp.bfloat16)
    return jnp.concatenate([table] * 3, axis=0)


def moved_lanes(x, table):
    return jnp.dot(jnp.concatenate(split_three(x), axis=1), table, preferred_element_type=f32)


def interleave(x, y):
    front = lanes_of(x.shape) < 64
    return jnp.where(front, x, pltpu.roll(y, 64, 1)), jnp.where(front, pltpu.roll(x, 64, 1), y)


def node_at(i, j, r):
    start = ((4 * (r // 4) + i) * 17 + 4 * (r % 4) + j) * 8
    return pl.ds(start if isinstance(i, int) else pl.multiple_of(start, 8), 8)


def gather_rows(nodes):
    sub = rows_of()
    turned = [rolled(v, r) for r, v in enumerate(nodes)]
    out = []
    for c in range(3):
        total = turned[0]
        for r in range(1, 8):
            total = jnp.where(sub == (r + c) % 8, turned[r], total)
        out.append(rolled(total, -c))
    return out


def scatter_rows(parts, wanted):
    sub = rows_of()
    turned = [rolled(v, c) for c, v in enumerate(parts)]
    out = []
    for r in wanted:
        total = jnp.where(sub == r, turned[0], jnp.where(sub == (r + 1) % 8, turned[1], turned[2]))
        out.append((r, rolled(total, -r)))
    return out


def every_node(body):
    def column(i, carry):
        for j in range(5):
            body(i, j, range(8) if j < 4 else (3, 7))
        return carry

    lax.fori_loop(0, 4, column, 0)
    for j in range(5):
        body(4, j, range(4, 8) if j < 4 else (7,))


def tile_copies(field, held, semaphores, first, out=False):
    copies = []
    for t in range(4):
        outside = field.at[:, :, :, pl.ds(128 * t, 128)]
        inside = held.reshape(4, 9, 17, 8, 128).at[t, :, :, pl.ds(0, 3), :]
        ends = (inside, outside) if out else (outside, inside)
        copies.append(pltpu.make_async_copy(*ends, semaphores.at[first + t]))
    return copies


def to_elements(half, wide, table, kept, puts):
    moved = moved_lanes(wide[...].reshape(600, 256), table)
    if half == 0:
        kept[...] = moved
        return
    for pair in range(2):
        lanes = slice(128 * pair, 128 * pair + 128)
        for l, value in enumerate(interleave(kept[:, lanes], moved[:, lanes])):
            puts(2 * pair + l, value.reshape(3, 5, 5, 8, 128))


def to_nodes(get, table, tall):
    pairs = [interleave(get(2 * p).reshape(600, 128), get(2 * p + 1).reshape(600, 128)) for p in range(2)]
    for half in range(2):
        wide = jnp.concatenate([pairs[0][half], pairs[1][half]], axis=1)
        tall[half] = moved_lanes(wide, table).reshape(3, 5, 5, 8, 256)


def lookup(material, row, region):
    total = jnp.zeros_like(region)
    for m in range(material.shape[1]):
        total = jnp.where(region == float(m + 1), material[row, m], total)
    return total


def internal(u, out, lame, shear, gx, gz, cross, planes, side):
    def depth_lines(i, carry):
        for j in range(5):
            for c in range(3):
                v = [u[c, i, j, k] for k in range(4)]
                v.append(deeper(v[0]))
                u[c, i, j, 4] = v[4]
                for k, g in enumerate(line(deriv, v)):
                    gz[c, i, j, k] = g
        return carry

    lax.fori_loop(0, 5, depth_lines, 0)

    def plane(k, carry):
        weight = jnp.where((k == 0) | (k == 4), float(quad[0]), jnp.where(k == 2, float(quad[2]), float(quad[1])))
        lame_k, shear_k = lame * (2.0 * weight), shear * (2.0 * weight)
        pairs = {}
        for a in range(3):
            for b in range(a, 3):
                w = float(quad[a] * quad[b])
                pairs[a, b] = pairs[b, a] = (lame_k * w, shear_k * w, shear_k * (2.0 * w))
        for c in range(3):
            for j in range(5):
                for i, g in enumerate(line(deriv, [u[c, i, j, k] for i in range(5)])):
                    gx[c, i, j] = g
        for i in range(5):
            gy = [line(deriv, [u[c, i, j, k] for j in range(5)]) for c in range(3)]
            ys = [[], [], []]
            for j in range(5):
                lw, mw, mw2 = pairs[kind[i], kind[j]]
                g0, g1, g2 = [[gx[c, i, j], gy[c][j], gz[c, i, j, k]] for c in range(3)]
                dilated = lw * (g0[0] + g1[1] + g2[2])
                s01 = mw * (g0[1] + g1[0])
                s02 = mw * (g0[2] + g2[0])
                s12 = mw * (g1[2] + g2[1])
                side[0, i, j] = dilated + mw2 * g0[0]
                side[1, i, j] = s01
                cross[0, i, j, k] = s02
                cross[1, i, j, k] = s12
                cross[2, i, j, k] = dilated + mw2 * g2[2]
                ys[0].append(s01)
                ys[1].append(dilated + mw2 * g1[1])
                ys[2].append(s12)
            for c in range(3):
                for j, value in enumerate(line(deriv_t, ys[c])):
                    planes[c, i, j, k] = value
        for j in range(5):
            for c in range(3):
                v = [side[c, i, j] if c < 2 else cross[0, i, j, k] for i in range(5)]
                for i, value in enumerate(line(deriv_t, v)):
                    planes[c, i, j, k] += value
        return carry

    lax.fori_loop(0, 5, plane, 0)

    def depth_sums(i, carry):
        for j in range(5):
            for c in range(3):
                v = line(deriv_t, [cross[c, i, j, k] for k in range(5)])
                v = [v[k] + planes[c, i, j, k] for k in range(5)]
                out[c, i, j, 0] = v[0] + shallower(v[4])
                for k in range(1, 4):
                    out[c, i, j, k] = v[k]
        return carry

    lax.fori_loop(0, 5, depth_sums, 0)
    sub = rows_of()

    def fold(k, carry):
        for c in range(3):
            for i in range(5):
                low, high = out[c, i, 0, k], out[c, i, 4, k]
                out[c, i, 0, k] = low + jnp.where(sub % 4 == 0, 0.0, pltpu.roll(high, 1, 0))
                out[c, i, 4, k] = high + jnp.where(sub % 4 == 3, 0.0, pltpu.roll(low, 7, 0))
            for j in range(5):
                low, high = out[c, 0, j, k], out[c, 4, j, k]
                out[c, 0, j, k] = low + jnp.where(sub < 4, 0.0, pltpu.roll(high, 4, 0))
                out[c, 4, j, k] = high + jnp.where(sub < 4, pltpu.roll(low, 4, 0), 0.0)
        return carry

    lax.fori_loop(0, 4, fold, 0)


def rolled(x, amount, axis=0):
    amount = amount % x.shape[axis]
    return pltpu.roll(x, amount, axis) if amount else x


def parity_x():
    return position("gx") % 2


def parity_y():
    return along_y() % 2


def sort_out(odd, low, high):
    return jnp.where(odd == 1, low, high), jnp.where(odd == 1, high, low)


def pack_x(force, first, second):
    sub, odd = rows_of(), parity_x()
    for c in range(3):
        for j in range(5):
            for half in range(2):
                at = (c * 5 + j) * 2 + half
                a, b = force[c, 0, j, 2 * half], force[c, 0, j, 2 * half + 1]
                low = jnp.where(sub < 4, a, rolled(b, 4))
                a, b = force[c, 4, j, 2 * half], force[c, 4, j, 2 * half + 1]
                high = jnp.where(sub < 4, rolled(a, 4), b)
                first[at], second[at] = sort_out(odd, low, high)


def pack_y(force, low, high):
    sub = rows_of()
    for c in range(3):
        for i in range(5):
            a, b = force[c, i, 0, 0], rolled(force[c, i, 4, 0], -3)
            for k in range(1, 4):
                a = jnp.where(sub % 4 == k, rolled(force[c, i, 0, k], k), a)
                b = jnp.where(sub % 4 == k, rolled(force[c, i, 4, k], k - 3), b)
            low[c * 5 + i] = a
            high[c * 5 + i] = b


def add_x(force, first, second):
    sub, odd = rows_of(), parity_x()
    for c in range(3):
        for j in range(5):
            for half in range(2):
                at = (c * 5 + j) * 2 + half
                r, s = sort_out(odd, first[at], second[at])
                force[c, 0, j, 2 * half] += jnp.where(sub < 4, r, 0.0)
                force[c, 0, j, 2 * half + 1] += jnp.where(sub < 4, rolled(r, 4), 0.0)
                force[c, 4, j, 2 * half] += jnp.where(sub < 4, 0.0, rolled(s, 4))
                force[c, 4, j, 2 * half + 1] += jnp.where(sub < 4, 0.0, s)


def add_y(force, first, second):
    sub, odd = rows_of(), parity_y()
    for c in range(3):
        for i in range(5):
            r, s = sort_out(odd, first[c * 5 + i], second[c * 5 + i])
            for k in range(4):
                force[c, i, 0, k] += jnp.where(sub % 4 == 0, rolled(r, -k), 0.0)
                force[c, i, 4, k] += jnp.where(sub % 4 == 3, rolled(s, 3 - k), 0.0)


def edge_rows(low, high, came1, came2, first, second):
    sub, odd, odd_y = rows_of(), parity_x(), parity_y()
    for c in range(3):
        came = [[sort_out(odd, came1[at], came2[at]) for at in range((c * 5 + j) * 2, (c * 5 + j) * 2 + 2)] for j in (0, 4)]
        for i in range(5):
            rows = [low[c * 5 + i], high[c * 5 + i]]
            if i in (0, 4):
                start, side = i, i // 4
                for end, row in ((0, 0), (1, 3)):
                    for k in range(4):
                        r = rolled(came[end][k // 2][side], start + k - (4 * (k % 2) + row))
                        rows[end] = rows[end] + jnp.where(sub == start + k, r, 0.0)
            first[c * 5 + i], second[c * 5 + i] = sort_out(odd_y, *rows)


def first_edge_kernel(low, high, came1, came2, rows_low, rows_high, crater1, crater2, after, first, second, token, ends, semaphores):
    token[...] = after[0:8]
    copies = fetch(
        [(c.at[:, pl.ds(24 * h, 8), :], ends.at[n, :, pl.ds(8 * h, 8), :]) for n, c in enumerate((crater1, crater2)) for h in range(2)],
        semaphores,
    )
    edge_rows(low, high, came1, came2, first, second)
    odd, odd_y = parity_x(), parity_y()
    regions = sort_out(odd, came1[30], came2[30])
    for n, value in enumerate((low[15], regions[0], regions[1])):
        first[15 + n] = value
        second[15 + n] = value
    for copy in copies:
        copy.wait()
    for f in range(5):
        for t in range(2):
            lanes = slice(128 * t, 128 * t + 128)
            at = 18 + f * 4 + t * 2
            first[at], second[at] = sort_out(odd_y, rows_low[f * 2 + t], rows_high[f * 2 + t])
            found = []
            for row in (0, 15):
                sides = sort_out(odd, ends[0, f, row : row + 1, lanes], ends[1, f, row : row + 1, lanes])
                found.append(jnp.concatenate(list(sides) * 4, axis=0))
            first[at + 1], second[at + 1] = sort_out(odd_y, *found)


def second_edge_kernel(low, high, came1, came2, after, first, second, token):
    edge_rows(low, high, came1, came2, first, second)
    token[...] = after[...]


def region_grid(own, x1, x2, y1, y2):
    xl, xh = sort_out(parity_x(), x1[30], x2[30])
    yl, yh = [list(v) for v in zip(*[sort_out(parity_y(), y1[n], y2[n]) for n in (15, 16, 17)])]
    return [[yl[1], xl, yh[1]], [yl[0], own, yh[0]], [yl[2], xh, yh[2]]]


def shared_density(grid):
    sub = rows_of()
    across = []
    for y in range(3):
        low, mid, high = grid[0][y], grid[1][y], grid[2][y]
        turned = rolled(mid, 4)
        across.append([jnp.where(sub < 4, rolled(low, 4), turned), mid, jnp.where(sub < 4, turned, rolled(high, 4))])
    found = [[None] * 3 for _ in range(3)]
    for x in range(3):
        low, mid, high = across[0][x], across[1][x], across[2][x]
        found[x][0] = jnp.where(sub % 4 == 0, rolled(low, -3), rolled(mid, 1))
        found[x][1] = mid
        found[x][2] = jnp.where(sub % 4 == 3, rolled(high, 3), rolled(mid, -1))
    sums = []
    for x in ((1,), (0, 1), (1, 2)):
        row = []
        for y in ((1,), (0, 1), (1, 2)):
            total = sum(found[a][b] for a in x for b in y)
            row.append((total + shallower(total), total))
        sums.append(row)
    return sums


def mass_scales(sums):
    return [[[1.0 / s for s in pair] for pair in row] for row in sums]


def edge_kind(i):
    return 1 if i == 0 else 2 if i == 4 else 0


def accel_scale(i, j, k):
    return float(-1.0 / (half_size**3 * quad[i] * quad[j] * quad[k]))


def first_kernel(nodes_y, u, v, a, density, momentum, energy, dest, slot, region, material, after,
                 b_out, bottoms, f_out, x1, x2, y_low, y_high, rows_low, rows_high, region_out,
                 elem, gx, gz, cross, planes, side, u_in, v_in, a_in, wide_u, wide_b, kept_u, kept_b, b_held,
                 cells, copies_held, dest_in, slot_in, region_in, semaphores):
    early = fetch(
        [(region, region_in), (dest, dest_in), (slot, slot_in), (density, cells.at[0]),
         (momentum, cells.at[pl.ds(1, 3)]), (energy, cells.at[4])],
        semaphores.at[pl.ds(14, 6)],
    )
    copies = [tile_copies(f, h, semaphores, 4 * n) for n, (f, h) in enumerate(((u, u_in), (v, v_in), (a, a_in)))]
    for t in range(4):
        for copy in copies:
            copy[t].start()
    table = depth_table()
    for copy in early:
        copy.wait()
    region_now = jnp.concatenate([region_in[0], region_in[1]], axis=0).astype(f32) + 1.0
    region_out[...] = region_now
    block = deepest_block(nodes_y, cells, dest_in, slot_in, region_now, rows_low, rows_high)
    for n in range(bottoms.shape[0]):
        copies_held[n] = block
    save_bottoms = pltpu.make_async_copy(copies_held, bottoms, semaphores.at[13])
    save_bottoms.start()

    def put_u(l, value):
        elem[:, :, :, l] = value

    def put_b(l, value):
        b_held[:, :, :, l] = value

    for half in range(2):
        for t in (2 * half, 2 * half + 1):
            for copy in copies:
                copy[t].wait()

        def column(i, carry):
            for t in (2 * half, 2 * half + 1):
                lanes = slice(128 * (t % 2), 128 * (t % 2) + 128)
                for j in range(5):
                    now, later = [], []
                    for r in range(8):
                        at = (t, node_at(i, j, r), slice(None))
                        step = time_step * v_in[at] + (0.5 * time_step**2) * a_in[at]
                        now.append(u_in[at] + step)
                        later.append(now[-1] + step)
                    for c, value in enumerate(gather_rows(now)):
                        wide_u[c, i, j, :, lanes] = value
                    for c, value in enumerate(gather_rows(later)):
                        wide_b[c, i, j, :, lanes] = value
            return carry

        lax.fori_loop(0, 5, column, 0)
        to_elements(half, wide_u, table, kept_u, put_u)
        to_elements(half, wide_b, table, kept_b, put_b)
    save_b = pltpu.make_async_copy(b_held, b_out, semaphores.at[12])
    save_b.start()
    internal(elem, f_out, lookup(material, 1, region_now), lookup(material, 2, region_now), gx, gz, cross, planes, side)
    pack_x(f_out, x1, x2)
    pack_y(f_out, y_low, y_high)
    x1[30] = region_now
    x2[30] = region_now
    y_low[15] = region_now
    save_b.wait()
    save_bottoms.wait()


def second_kernel(b, f, came_x1, came_x2, came_y1, came_y2, region, material, after, a_out, f_out, x1, x2, y_low, y_high, scales, token,
                  elem, gx, gz, cross, planes, side):
    region_now = region[...]
    token[...] = after[...]
    a_out[...] = f[...]
    add_x(a_out, came_x1, came_x2)
    add_y(a_out, came_y1, came_y2)
    grid = region_grid(region_now, came_x1, came_x2, came_y1, came_y2)
    inverse = mass_scales(shared_density([[lookup(material, 0, r) for r in row] for row in grid]))
    for x in range(3):
        for y in range(3):
            for z in range(2):
                scales[x, y, z] = inverse[x][y][z]
    for i in range(5):
        for j in range(5):
            for k in range(4):
                scale = scales[edge_kind(i), edge_kind(j), min(k, 1)] * accel_scale(i, j, k)
                for c in range(3):
                    value = a_out[c, i, j, k] * scale
                    a_out[c, i, j, k] = value
                    elem[c, i, j, k] = b[c, i, j, k] + time_step**2 * value
    internal(elem, f_out, lookup(material, 1, region_now), lookup(material, 2, region_now), gx, gz, cross, planes, side)
    pack_x(f_out, x1, x2)
    pack_y(f_out, y_low, y_high)


def spread_surface(source, held, count):
    lane = lanes_of((24, 128))
    for n in range(27):
        at = 8 * n
        tile, shift = at // 128, (128 - at % 128) % 128
        moved = rolled(source[:, 128 * tile : 128 * tile + 128], shift, 1)
        held[n] = jnp.where(lane < count, moved, 0.0)


def add_surface(held, tall):
    for c in range(3):
        for i in range(5):
            for j in range(5):
                for ex in range(2):
                    value = held[c * 9 + 4 * ex + i, pl.ds(j, 4, stride=4), :]
                    tall[0, c, i, j, 4 * ex : 4 * ex + 4, 0:128] += value


def place_kernel(a1, surf1, u, v, a, after, u_out, v_part, u_in, v_in, a_in, tall, surface, u_held, semaphores):
    copies = [tile_copies(f, h, semaphores, 4 * n) for n, (f, h) in enumerate(((u, u_in), (v, v_in), (a, a_in)))]
    for t in range(4):
        for copy in copies:
            copy[t].start()
    spread_surface(surf1, surface, 1)
    to_nodes(lambda l: a1[:, :, :, l], depth_table(back=True), tall)
    add_surface(surface, tall)
    saves = tile_copies(u_out, u_held, semaphores, 12, out=True)
    for t in range(4):
        for copy in copies:
            copy[t].wait()
        lanes = slice(128 * (t % 2), 128 * (t % 2) + 128)

        def body(i, j, wanted):
            for r, accel in scatter_rows([tall[t // 2, c, i, j, :, lanes] for c in range(3)], wanted):
                at = (t, node_at(i, j, r), slice(None))
                vv, aa = v_in[at], a_in[at]
                u_held[at] = u_in[at] + 2.0 * time_step * vv + time_step**2 * (aa + accel)
                v_part[at] = vv + (0.5 * time_step) * (aa + 2.0 * accel)

        every_node(body)
        saves[t].start()
    for save in saves:
        save.wait()


def last_kernel(v_part, f, x1, x2, y1, y2, scales, surf1, surf2, v_out, a_out, v_held, a_held, tall, surface, force, semaphores):
    force[...] = f[...]
    add_x(force, x1, x2)
    add_y(force, y1, y2)
    for i in range(5):
        for j in range(5):
            for k in range(4):
                scale = scales[edge_kind(i), edge_kind(j), min(k, 1)] * accel_scale(i, j, k)
                for c in range(3):
                    force[c, i, j, k] = force[c, i, j, k] * scale
    spread_surface(surf1, surface.at[0], 1)
    spread_surface(surf2, surface.at[1], 5)
    surface[0] = surface[0] + surface[1]
    to_nodes(lambda l: force[:, :, :, l], depth_table(back=True), tall)
    add_surface(surface.at[0], tall)
    saves = tile_copies(v_out, v_held, semaphores, 0, out=True) + tile_copies(a_out, a_held, semaphores, 4, out=True)
    for t in range(4):
        lanes = slice(128 * (t % 2), 128 * (t % 2) + 128)

        def body(i, j, wanted):
            for r, accel in scatter_rows([tall[t // 2, c, i, j, :, lanes] for c in range(3)], wanted):
                at = (t, node_at(i, j, r), slice(None))
                a_held[at] = accel
                v_held[at] = v_part[at] + (0.5 * time_step) * accel

        every_node(body)
        saves[t].start()
        saves[4 + t].start()
    for save in saves:
        save.wait()


def whole():
    return pl.BlockSpec(memory_space=pltpu.VMEM)


def scalars():
    return pl.BlockSpec(memory_space=pltpu.SMEM)


def call(kernel, ins, outs, scratch, smem=(), away=(), out_away=(), mib=10, copies=0):
    def spec(n):
        return scalars() if n in smem else pl.BlockSpec(memory_space=pltpu.HBM) if n in away else whole()

    scratch = [pltpu.VMEM(s, f32) if isinstance(s, tuple) else s for s in scratch]
    return pl.pallas_call(
        kernel,
        out_shape=[jax.ShapeDtypeStruct(s, f32) for s in outs],
        in_specs=[spec(n) for n in range(len(ins))],
        out_specs=[pl.BlockSpec(memory_space=pltpu.HBM) if n in out_away else whole() for n in range(len(outs))],
        scratch_shapes=scratch + ([pltpu.SemaphoreType.DMA((copies,))] if copies else []),
        compiler_params=pltpu.CompilerParams(vmem_limit_bytes=mib * 1024 * 1024),
    )(*ins)


def fetch(pairs, semaphores):
    copies = [pltpu.make_async_copy(source, target, semaphores.at[n]) for n, (source, target) in enumerate(pairs)]
    for copy in copies:
        copy.start()
    return copies


element_shape = (3, 5, 5, 4, 8, 128)
lines_shape = (3, 5, 5, 5, 8, 128)
internal_scratch = [lines_shape, (3, 5, 5, 8, 128), lines_shape, lines_shape, lines_shape, (2, 5, 5, 8, 128)]


def exchange(axis, first, second):
    count = lax.axis_size(axis)
    pairs = [(i, i + 1) for i in range(1, count - 1, 2)]
    first = lax.ppermute(first, axis, [(i, i ^ 1) for i in range(count)])
    return first, lax.ppermute(second, axis, pairs + [(j, i) for i, j in pairs])


def surface_tables():
    lane = np.arange(128)
    j, ey = lane // 8, lane % 8
    used = (j < 5) & (ey < 6)
    place = np.where(used, ey + 1, -9)
    source = lane[:, None]
    centre = source == place
    meet = centre | ((j == 0) & (source == place - 1)) | ((j == 4) & (source == place + 1))
    along = np.zeros((128, 128))
    for a in range(40):
        for b in range(40):
            if a % 8 == b % 8 and a % 8 < 6:
                along[a, b] = deriv[b // 8, a // 8]
    node = np.where(used, 4 * (ey - 1) + j, -9)
    fold = (lane[:, None] == node) & (lane[:, None] < 17)
    keep = fold & ((j < 4) & (ey < 5) | (j == 4) & (ey == 4))
    return np.stack([centre, meet, along, along.T, fold, keep]).astype(np.float32)


def full_dot(x, y, back=False):
    dims = (((1,), (1 if back else 0,)), ((), ()))
    return lax.dot_general(x, y, dims, precision=lax.Precision.HIGHEST, preferred_element_type=f32)


def deposit(faces, nodes_y, base_x, base_y, total):
    rows = faces.shape[1]
    sub = rows_of((8, 512)).astype(f32)
    total[...] = jnp.zeros_like(total)

    def one(step, carry):
        def wide(q):
            block = faces[q, pl.ds(4 * step, 4), :]
            return jnp.concatenate([block[n : n + 1] for n in range(4)], axis=1)

        ids = wide(3)
        node_x = jnp.floor((ids + 0.5) * (1.0 / nodes_y))
        rel_y = jnp.broadcast_to(ids - node_x * nodes_y - base_y, (8, 512))
        rel_x = jnp.broadcast_to(node_x - base_x, (8, 512))
        left = []
        hits = [(rel_x - i == 4.0 * sub) & (sub < 4.0) for i in range(5)]
        parts = [split_three(wide(c)) for c in range(3)]
        for part in range(3):
            for c in range(3):
                value = jnp.broadcast_to(parts[c][part].astype(f32), (8, 512))
                left += [jnp.where(hit, value, 0.0) for hit in hits]
        right = [jnp.where((rel_y - j == 4.0 * sub) & (sub < 6.0), 1.0, 0.0) for j in range(5)]
        right.append(jnp.zeros((88, 512), f32))
        left, right = jnp.concatenate(left, axis=0), jnp.concatenate(right, axis=0)
        total[...] += lax.dot_general(
            left.astype(jnp.bfloat16), right.astype(jnp.bfloat16), (((1,), (1,)), ((), ())), preferred_element_type=f32
        )
        return carry

    lax.fori_loop(0, rows // 4, one, 0)


def top_grid(rows, z):
    sub, lane = rows_of(), lanes_of()
    out = jnp.zeros((8, 128), f32)
    for x in range(3):
        for y in range(3):
            row = jnp.broadcast_to(rows[x][y], (8, 128))
            for ex in range(2):
                here = (sub == 2 * x + ex) & (lane >= 4 * y - 2) & (lane < 4 * y + 2) & (lane < 8)
                out = jnp.where(here, rolled(row, 4 * y - 2 - 8 * z - 4 * ex, 1), out)
    return out


def respond(total, grid, material, tables, out1, out2):
    sub, lane = rows_of(), lanes_of()
    top, below = top_grid(grid, 0), top_grid(grid, 1)
    centre, meet, along, along_t, fold, keep = [tables[n] for n in range(6)]
    sums0 = full_dot(lookup(material, 0, top), meet)
    sums1 = full_dot(lookup(material, 0, below), meet)
    lame = rolled(full_dot(lookup(material, 1, top), centre), -1)
    shear = rolled(full_dot(lookup(material, 2, top), centre), -1)
    weight_y = jnp.ones((8, 128), f32)
    for j in range(5):
        weight_y = jnp.where(lane // 8 == j, float(quad[j]), weight_y)

    def inverse(sums):
        mid = rolled(sums, -1)
        found = {0: mid + sums, 1: mid, 4: mid + rolled(sums, -2)}
        found = {i: jnp.where(s > 0.0, 1.0 / (s * weight_y), 0.0) for i, s in found.items()}
        found[2] = found[3] = found[1]
        return found

    light, heavy = inverse(sums0), inverse(sums0 + sums1)
    first = [[None] * 5 for _ in range(3)]
    moved = [[None] * 5 for _ in range(3)]
    for c in range(3):
        for i in range(5):
            at = (c * 5 + i) * 8
            force = total[at : at + 8] + total[at + 120 : at + 128] + total[at + 240 : at + 248]
            first[c][i] = force * light[i] * -accel_scale(i, 2, 0) * float(quad[2])
            moved[c][i] = first[c][i] * time_step**2
    gx = [line(deriv, moved[c]) for c in range(3)]
    gy = full_dot(jnp.concatenate([moved[c][i] for c in range(3) for i in range(5)], axis=0), along)
    gy = [[gy[(c * 5 + i) * 8 : (c * 5 + i) * 8 + 8] for i in range(5)] for c in range(3)]
    lame_w, shear_w = lame * weight_y * 2.0, shear * weight_y * 2.0
    d00 = float(deriv[0, 0])
    sx = [[], [], []]
    sy = [[], [], []]
    sz = [[], [], []]
    qs = [[], [], []]
    pressed = []
    for i in range(5):
        lw, mw = lame_w * float(quad[i]), shear_w * float(quad[i])
        d = [moved[c][i] for c in range(3)]
        gz = [d00 * x for x in d]
        dilated = lw * (gx[0][i] + gy[1][i] + gz[2])
        s01 = mw * (gx[1][i] + gy[0][i])
        s02 = mw * (gx[2][i] + gz[0])
        s12 = mw * (gy[2][i] + gz[1])
        for c, value in enumerate((dilated + 2.0 * mw * gx[0][i], s01, s02)):
            sx[c].append(value)
        for c, value in enumerate((s01, dilated + 2.0 * mw * gy[1][i], s12)):
            sy[c].append(value)
        for c, value in enumerate((s02, s12, dilated + 2.0 * mw * gz[2])):
            sz[c].append(value)
        for c, value in enumerate((mw * d[0], mw * d[1], (lw + 2.0 * mw) * d[2])):
            qs[c].append(value)
        pressed.append(lw * d[2])
    ydiv = full_dot(jnp.concatenate(sy[0] + sy[1] + sy[2] + pressed + qs[1], axis=0), along_t)
    ydiv = [[ydiv[(n * 5 + i) * 8 : (n * 5 + i) * 8 + 8] for i in range(5)] for n in range(5)]
    xdiv = [line(deriv_t, v) for v in sx + [pressed, qs[0]]]
    base = [xdiv[3], ydiv[3], [p + q for p, q in zip(xdiv[4], ydiv[4])]]
    second = {}
    for c in range(3):
        for i in range(5):
            for l in range(5):
                stiff = float(sum(deriv[k, l] * quad[k] * deriv[k, 0] for k in range(1, 5)))
                value = float(deriv[0, l] * quad[0]) * sz[c][i] + stiff * qs[c][i]
                if l:
                    value = value + float(deriv[l, 0] * quad[l]) * base[c][i]
                else:
                    value = value + float(quad[0]) * (xdiv[c][i] + ydiv[c][i])
                scale = (heavy if l == 4 else light)[i]
                second[c, i, l] = value * scale * (accel_scale(i, 2, l) * float(quad[2]))
    rows1, rows2 = [], []
    for c in range(3):
        for x in range(9):
            own = 1 if x < 4 else 2
            rows1.append(jnp.where(sub == 0, rolled(first[c][x - 4 * (own - 1)], -own), 0.0))
            block = jnp.zeros((8, 128), f32)
            for l in range(5):
                for ex in range(4):
                    i = x - 4 * (ex - 1)
                    if 0 <= i <= 4:
                        block = block + jnp.where(sub == l, rolled(second[c, i, l], l - ex), 0.0)
            rows2.append(block)
    blank = [jnp.zeros((40, 128), f32)]
    out1[...] = full_dot(keep[0:24], jnp.concatenate(rows1 + blank, axis=0), back=True)
    out2[...] = full_dot(fold[0:24], jnp.concatenate(rows2 + blank, axis=0), back=True)


def position(axis):
    return lax.axis_index(axis)


def along_y():
    return lax.axis_index("grp") * lax.axis_size("gy") + lax.axis_index("gy")


def primitives(state):
    inverse = 1.0 / state[0]
    v = [state[1 + c] * inverse for c in range(3)]
    p = (gamma_gas - 1.0) * (state[4] - 0.5 * (state[1] * v[0] + state[2] * v[1] + state[3] * v[2]))
    return v + [p, jnp.sqrt(gamma_gas * p * inverse), state[4] + p]


def flux(state, prim, d):
    out = [state[1 + d]] + [state[1 + c] * prim[d] for c in range(3)] + [prim[5] * prim[d]]
    out[1 + d] = out[1 + d] + prim[3]
    return out, jnp.abs(prim[d]) + prim[4]


def twice_face(low, high):
    fastest = jnp.maximum(low[2], high[2])
    return [fl + fh - fastest * (uh - ul) for ul, uh, fl, fh in zip(low[0], high[0], low[1], high[1])]


def turned_change(state, prim, d, axis, ends):
    size = state[0].shape[axis]
    fluxes, speed = flux(state, prim, d)
    up = lambda x: pltpu.roll(x, size - 1, axis)
    high = ([up(x) for x in state], [up(x) for x in fluxes], up(speed))
    upper = twice_face((state, fluxes, speed), high)
    if ends is None:
        return [g - pltpu.roll(g, 1, axis) for g in upper]
    upper = [jnp.where(ends[1], 2.0 * f, g) for f, g in zip(fluxes, upper)]
    return [g - jnp.where(ends[0], 2.0 * f, pltpu.roll(g, 1, axis)) for f, g in zip(fluxes, upper)]


def planes_kernel(density, momentum, energy, first, second, token, semaphores):
    odd = parity_x()
    pairs = []
    for out, down in ((first, odd), (second, 1 - odd)):
        for n, plane in enumerate((3 - 3 * down, 2 - down)):
            rows = pl.ds(32 * n, 32)
            pairs.append((density.at[plane], out.at[0, rows]))
            pairs.append((momentum.at[:, plane], out.at[pl.ds(1, 3), rows]))
            pairs.append((energy.at[plane], out.at[4, rows]))
    token[...] = jnp.zeros((8, 128), f32)
    for copy in fetch(pairs, semaphores):
        copy.wait()


def deepest_block(nodes_y, cells, dest, slot, region_now, rows_low, rows_high):
    sub, lane = rows_of(), lanes_of()
    pick = jnp.where(lane == 125 + sub, 1.0, 0.0)
    pieces = []
    for f in range(5):
        columns = jnp.concatenate([cells[f, x, :, 128:256] for x in range(4)], axis=0)
        pieces.append(full_dot(pick, columns, back=True)[0:3])
        for t in range(2):
            lanes = slice(128 * t, 128 * t + 128)
            for out, pair in ((rows_low, (0, 1)), (rows_high, (31, 30))):
                out[f * 2 + t] = jnp.concatenate([cells[f, x, r : r + 1, lanes] for r in pair for x in range(4)], axis=0)
    count_gy, count_x = lax.axis_size("gy"), lax.axis_size("gx")
    target, node = dest[...].astype(f32), slot[...].astype(f32)
    grp = jnp.floor((target + 0.5) * (1.0 / (count_gy * count_x)))
    rest = target - grp * (count_gy * count_x)
    gx = jnp.floor((rest + 0.5) * (1.0 / count_gy))
    gy = rest - gx * count_gy
    i = jnp.floor((node + 0.5) * (1.0 / 17.0))
    j = node - 17.0 * i
    pieces.append((8.0 * gx + i) * nodes_y + 16.0 * (grp * count_gy + gy) + j)
    found = jnp.zeros((8, 128), f32)
    for z in range(2):
        found = jnp.where(lane == 8 * z + sub, jnp.broadcast_to(region_now[:, z : z + 1], (8, 128)), found)
    pieces.append(jnp.broadcast_to(jnp.sum(found, axis=0, keepdims=True), (8, 128)))
    return jnp.concatenate(pieces, axis=0)


def crater_kernel(density, momentum, energy, came1, came2, rows1, rows2, after, out, token,
                  wide, mid, prims, face, fluxes, semaphores):
    planes, inner = pl.ds(2, 4), pl.ds(0, 32)
    copies = fetch(
        [(density, wide.at[0, planes, inner]), (momentum, wide.at[pl.ds(1, 3), planes, inner]),
         (energy, wide.at[4, planes, inner])],
        semaphores,
    )
    place, last_y = along_y(), lax.axis_size("grp") * lax.axis_size("gy") - 1
    gx, last_x = position("gx"), lax.axis_size("gx") - 1
    odd, odd_y = parity_x(), parity_y()
    for f in range(5):
        low, high = sort_out(odd, came1[f], came2[f])
        for p, value in ((0, low[32:64]), (1, low[0:32]), (6, high[0:32]), (7, high[32:64])):
            wide[f, p, 0:32, :] = value
            wide[f, p, 32:40, :] = value[0:8]
    token[...] = after[...]
    for copy in copies:
        copy.wait()
    for f in range(5):
        for x in range(4):
            wide[f, 2 + x, 32:40, :] = wide[f, 2 + x, 24:32, :]
        for t in range(2):
            lanes = slice(128 * t, 128 * t + 128)
            at = 18 + f * 4 + t * 2
            below, above = sort_out(odd_y, rows1[at], rows2[at])
            sides_below, sides_above = sort_out(odd_y, rows1[at + 1], rows2[at + 1])

            def put(p, row, edge, value):
                clamped = jnp.where(edge == 0, place == 0, place == last_y)
                at_edge = wide[f, p, 31 * edge : 31 * edge + 1, lanes]
                wide[f, p, row : row + 1, lanes] = jnp.where(clamped, at_edge, value)

            for x in range(4):
                put(2 + x, 39, 0, below[x : x + 1])
                put(2 + x, 38, 0, below[4 + x : 5 + x])
                put(2 + x, 32, 1, above[x : x + 1])
                put(2 + x, 33, 1, above[4 + x : 5 + x])
            for p, n in ((1, 0), (6, 1)):
                put(p, 39, 0, sides_below[n : n + 1])
                put(p, 32, 1, sides_above[n : n + 1])

    @pl.when(gx == 0)
    def _():
        for f in range(5):
            wide[f, 0] = wide[f, 2]
            wide[f, 1] = wide[f, 2]

    @pl.when(gx == last_x)
    def _():
        for f in range(5):
            wide[f, 6] = wide[f, 5]
            wide[f, 7] = wide[f, 5]

    lane = lanes_of((40, 256))
    ends = (lane == 0, lane == 255)

    def step(source, low, high, put):
        def along_x(p):
            state = [source[f, p] for f in range(5)]
            prim = primitives(state)
            return state, prim, flux(state, prim, 0)

        state, prim, (fx, speed) = along_x(low - 1)
        next_state, next_prim, (next_fx, next_speed) = along_x(low)
        g = twice_face((state, fx, speed), (next_state, next_fx, next_speed))
        for f in range(5):
            face[f] = g[f]
            fluxes[f] = next_fx[f]
        for n in range(6):
            prims[n] = next_prim[n]
        fluxes[5] = next_speed

        def plane(p, carry):
            state = [source[f, p] for f in range(5)]
            prim = [prims[n] for n in range(6)]
            next_state, next_prim, (next_fx, next_speed) = along_x(p + 1)
            g = twice_face((state, [fluxes[f] for f in range(5)], fluxes[5]), (next_state, next_fx, next_speed))
            change = [g[f] - face[f] for f in range(5)]
            for f in range(5):
                face[f] = g[f]
                fluxes[f] = next_fx[f]
            for n in range(6):
                prims[n] = next_prim[n]
            fluxes[5] = next_speed
            change = [a + b for a, b in zip(change, turned_change(state, prim, 1, 0, None))]
            change = [a + b for a, b in zip(change, turned_change(state, prim, 2, 1, ends))]
            for f in range(5):
                put(f, p, state[f] - (0.5 * cell_ratio) * change[f])
            return carry

        lax.fori_loop(low, high, plane, 0)

    def put_mid(f, p, value):
        mid[f, p] = value

    def put_out(f, p, value):
        out[f, p - 2] = value[0:32]

    step(wide, 1, 7, put_mid)

    @pl.when(gx == 0)
    def _():
        for f in range(5):
            mid[f, 1] = mid[f, 2]

    @pl.when(gx == last_x)
    def _():
        for f in range(5):
            mid[f, 6] = mid[f, 5]

    for f in range(5):
        for p in range(2, 6):
            edge = mid[f, p, 39:40, :]
            mid[f, p, 39:40, :] = jnp.where(place == 0, mid[f, p, 0:1, :], edge)
            edge = mid[f, p, 32:33, :]
            mid[f, p, 32:33, :] = jnp.where(place == last_y, mid[f, p, 31:32, :], edge)
    step(mid, 2, 6, put_out)


def bottom_tractions(bottoms, count_x, faces):
    shape = (count_x, 128)
    sub, lane = rows_of(shape), lanes_of(shape)
    count_gy = lax.axis_size("gy")

    def columns(q):
        parts = []
        for y in range(4):
            start = (y // count_gy * count_x * count_gy + y % count_gy) * 24 + q
            parts.append(bottoms[pl.ds(start, count_x, stride=24 * count_gy), :])
        found = []
        for x in range(4):
            total = rolled(parts[0], -32 * x, 1)
            for y in range(1, 4):
                total = jnp.where(lane // 32 == y, rolled(parts[y], 32 * (y - x), 1), total)
            found.append(total)
        return found

    cells = [[columns(f * 3 + z) for f in range(5)] for z in range(3)]
    state = [[[cells[z][f][x] for f in range(5)] for x in range(4)] for z in range(3)]
    ends_y = (lane == 0, lane == 127)

    def across_x(states, prims):
        fluxes = [flux(s, p, 0) for s, p in zip(states, prims)]
        data = [(s, f, a) for s, (f, a) in zip(states, fluxes)]
        up = lambda x: rolled(x, -1)
        wrap = ([up(v) for v in data[0][0]], [up(v) for v in data[0][1]], up(data[0][2]))
        upper = [twice_face(data[x], data[x + 1] if x < 3 else wrap) for x in range(4)]
        upper[3] = [jnp.where(sub == count_x - 1, 2.0 * f, g) for f, g in zip(data[3][1], upper[3])]
        below = [jnp.where(sub == 0, 2.0 * f, rolled(g, 1)) for f, g in zip(data[0][1], upper[3])]
        lower = [below] + upper[:3]
        return [[a - b for a, b in zip(u, l)] for u, l in zip(upper, lower)]

    def advanced(above, here, under, prim_above, prim_here, prim_under):
        changes = across_x(here, prim_here)
        out = []
        for x in range(4):
            change = [a + b for a, b in zip(changes[x], turned_change(here[x], prim_here[x], 1, 1, ends_y))]
            fz, az = flux(here[x], prim_here[x], 2)
            fa, aa = flux(above[x], prim_above[x], 2)
            lower = twice_face((above[x], fa, aa), (here[x], fz, az))
            if under is None:
                upper = [2.0 * f for f in fz]
            else:
                fu, au = flux(under[x], prim_under[x], 2)
                upper = twice_face((here[x], fz, az), (under[x], fu, au))
            out.append([s - (0.5 * cell_ratio) * (c + u - l) for s, c, u, l in zip(here[x], change, upper, lower)])
        return out

    prims = [[primitives(state[z][x]) for x in range(4)] for z in range(3)]
    middle = advanced(state[0], state[1], state[2], prims[0], prims[1], prims[2])
    deepest = advanced(state[1], state[2], None, prims[1], prims[2], None)
    prim_mid, prim_deep = [primitives(s) for s in middle], [primitives(s) for s in deepest]
    final = advanced(middle, deepest, None, prim_mid, prim_deep, None)
    ids = columns(15)
    for x in range(4):
        s, prim = final[x], primitives(final[x])
        at = pl.ds(x * count_x, count_x)
        faces[0, at, :] = face_area * s[1] * prim[2]
        faces[1, at, :] = face_area * s[2] * prim[2]
        faces[2, at, :] = face_area * (s[3] * prim[2] + prim[3])
        faces[3, at, :] = ids[x]


def deposit_kernel(nodes_y, count_x, bottoms, after, total, faces):
    base_x = (8 * position("gx") - 4).astype(f32)
    base_y = (16 * along_y() - 4).astype(f32)
    bottom_tractions(bottoms, count_x, faces)
    deposit(faces, nodes_y, base_x, base_y, total)


def respond_kernel(count_x, total, bottoms, material, tables, after, out1, out2, token, held, rows, semaphores):
    gx, place, count_gy = position("gx"), along_y(), lax.axis_size("gy")
    last_y = lax.axis_size("grp") * count_gy - 1
    pairs = [(tables, held)]
    for x in range(3):
        for y in range(3):
            cx, cy = jnp.clip(gx + x - 1, 0, count_x - 1), jnp.clip(place + y - 1, 0, last_y)
            rank = (cy // count_gy) * (count_x * count_gy) + cx * count_gy + cy % count_gy
            pairs.append((bottoms.at[rank, pl.ds(16, 8), :], rows.at[3 * x + y]))
    copies = fetch(pairs, semaphores)
    for copy in copies:
        copy.wait()
    found = []
    for x in range(3):
        found.append([])
        for y in range(3):
            px, py = gx + x - 1, place + y - 1
            inside = (px >= 0) & (px < count_x) & (py >= 0) & (py <= last_y)
            found[x].append(jnp.where(inside, rows[3 * x + y, 0:1, :], 0.0))
    respond(total, found, material, held, out1, out2)
    token[...] = after[...]


def shards(density, momentum, energy, displacement, velocity_field, acceleration, material, element_region_index,
           face_dest, face_slot):
    along, rank = ("grp", "gy"), ("grp", "gx", "gy")
    nodes_y = 16 * lax.axis_size(along) + 1
    count_x, devices = lax.axis_size("gx"), lax.axis_size(rank)
    crater = (density, momentum, energy)
    u, v, a = [jnp.transpose(x, (1, 2, 0, 3)) for x in (displacement, velocity_field, acceleration)]
    register, held_shape = (8, 128), (4, 1224, 128)
    crater1, crater2, token = call(
        planes_kernel, crater, [(5, 64, 256), (5, 64, 256), register], [], away=(0, 1, 2), mib=56, copies=12
    )
    crater1, crater2 = exchange("gx", crater1, crater2)
    vectors = pltpu.VMEM((1, 128), jnp.int32)
    b, bottoms, f, x1, x2, y_low, y_high, rows_low, rows_high, region = call(
        functools.partial(first_kernel, float(nodes_y)),
        (u, v, a) + crater + (face_dest.reshape(1, -1), face_slot, element_region_index, material, token),
        [element_shape, (devices, 24, 128), element_shape, (31, 8, 128), (31, 8, 128), (16, 8, 128), (15, 8, 128),
         (10, 8, 128), (10, 8, 128), register],
        internal_scratch
        + [held_shape] * 3
        + [(3, 5, 5, 8, 256), (3, 5, 5, 8, 256), (600, 256), (600, 256), element_shape]
        + [(5, 4, 32, 256), (devices, 24, 128), vectors, vectors, pltpu.VMEM((2, 4, 128), jnp.int32)],
        smem=(9,),
        away=(0, 1, 2, 3, 4, 5, 6, 7, 8),
        out_away=(0, 1),
        mib=56,
        copies=20,
    )
    bottoms = lax.all_to_all(bottoms, rank, 0, 0, tiled=True)
    (total,) = call(
        functools.partial(deposit_kernel, float(nodes_y), count_x),
        (bottoms.reshape(devices * 24, 128), region),
        [(360, 128)],
        [(4, 4 * count_x, 128)],
    )
    x1, x2 = exchange("gx", x1, x2)
    y1, y2, token = call(
        first_edge_kernel,
        (y_low, y_high, x1, x2, rows_low, rows_high, crater1, crater2, total),
        [(38, 8, 128), (38, 8, 128), register],
        [(2, 5, 16, 256)],
        away=(6, 7),
        copies=4,
    )
    surf1, surf2, token = call(
        functools.partial(respond_kernel, count_x),
        (total, bottoms, material, jnp.asarray(surface_tables()), token),
        [(24, 256), (24, 256), register],
        [(6, 128, 128), (9, 8, 128)],
        smem=(2,),
        away=(1, 3),
        copies=10,
    )
    y1, y2 = exchange(along, y1, y2)
    a1, f2, p1, p2, y_low, y_high, scales, token = call(
        second_kernel,
        (b, f, x1, x2, y1, y2, region, material, token),
        [element_shape, element_shape, (30, 8, 128), (30, 8, 128), (15, 8, 128), (15, 8, 128), (3, 3, 2, 8, 128), register],
        internal_scratch,
        smem=(7,),
    )
    hydro_state, token = call(
        crater_kernel,
        crater + (crater1, crater2, y1, y2, token),
        [(5, 4, 32, 256), register],
        [(5, 8, 40, 256), (5, 8, 40, 256), (6, 40, 256), (5, 40, 256), (6, 40, 256)],
        away=(0, 1, 2),
        copies=3,
    )
    p1, p2 = exchange("gx", p1, p2)
    r1, r2, token = call(
        second_edge_kernel, (y_low, y_high, p1, p2, token), [(15, 8, 128), (15, 8, 128), register], []
    )
    u_out, v_part = call(
        place_kernel,
        (a1, surf1, u, v, a, token),
        [u.shape, held_shape],
        [held_shape] * 3 + [(2, 3, 5, 5, 8, 256), (27, 24, 128), held_shape],
        away=(2, 3, 4),
        out_away=(0,),
        mib=20,
        copies=16,
    )
    r1, r2 = exchange(along, r1, r2)
    v_out, a_out = call(
        last_kernel,
        (v_part, f2, p1, p2, r1, r2, scales, surf1, surf2),
        [u.shape] * 2,
        [held_shape] * 2 + [(2, 3, 5, 5, 8, 256), (2, 27, 24, 128), element_shape],
        out_away=(0, 1),
        mib=16,
        copies=8,
    )
    u_out, v_out, a_out = [jnp.transpose(x, (2, 0, 1, 3)) for x in (u_out, v_out, a_out)]
    return hydro_state, u_out, v_out, a_out


def solution(mesh):
    field = P(None, "gx", ("grp", "gy"), None)
    cells = P("gx", ("grp", "gy"), None)
    rank = ("grp", "gx", "gy")
    return jax.shard_map(
        shards,
        mesh=mesh,
        in_specs=(cells, field, cells, field, field, field, P(), cells, P(rank, None, None), P(rank, None)),
        out_specs=(field, field, field, field),
        check_vma=False,
    )
```

```python
import functools

import jax
import jax.numpy as jnp
import numpy as np
from jax import lax
from jax.experimental import pallas as pl
from jax.experimental.pallas import tpu as pltpu
from jax.sharding import PartitionSpec as P

gamma_gas = 1.4
cell_ratio = 0.05
half_size = 2.0
time_step = 0.1
face_area = 2.0


def gll_tables():
    root = np.sqrt(3.0 / 7.0)
    points = np.array([-1.0, -root, 0.0, root, 1.0])
    weights = np.array([0.1, 49.0 / 90.0, 32.0 / 45.0, 49.0 / 90.0, 0.1])
    products = [np.prod([points[r] - points[c] for c in range(5) if c != r]) for r in range(5)]
    derivative = np.zeros((5, 5))
    for r in range(5):
        for c in range(5):
            if r != c:
                derivative[r, c] = products[r] / products[c] / (points[r] - points[c])
        derivative[r, r] = sum(1.0 / (points[r] - points[c]) for c in range(5) if c != r)
    derivative[2, 2] = 0.0
    return derivative, weights


deriv, quad = gll_tables()
deriv_t = deriv.T
kind = [0, 1, 2, 1, 0]
f32 = jnp.float32


def line(matrix, v):
    even, odd = (matrix + matrix[:, ::-1]) / 2, (matrix - matrix[:, ::-1]) / 2
    e0, e1, o0, o1 = v[0] + v[4], v[1] + v[3], v[0] - v[4], v[1] - v[3]
    top = [float(even[i, 0]) * e0 + float(even[i, 1]) * e1 + float(matrix[i, 2]) * v[2] for i in range(2)]
    low = [float(odd[i, 0]) * o0 + float(odd[i, 1]) * o1 for i in range(2)]
    centre = float(matrix[2, 0]) * o0 + float(matrix[2, 1]) * o1
    return [top[0] + low[0], top[1] + low[1], centre, low[1] - top[1], low[0] - top[0]]


def rows_of(shape=(8, 128)):
    return lax.broadcasted_iota(jnp.int32, shape, 0)


def lanes_of(shape=(8, 128)):
    return lax.broadcasted_iota(jnp.int32, shape, 1)


def deeper(x):
    return jnp.where(lanes_of() == 127, 0.0, pltpu.roll(x, 127, 1))


def shallower(x):
    return jnp.where(lanes_of() == 0, 0.0, pltpu.roll(x, 1, 1))


def split_three(x):
    high = x.astype(jnp.bfloat16)
    rest = x - high.astype(f32)
    middle = rest.astype(jnp.bfloat16)
    return high, middle, (rest - middle.astype(f32)).astype(jnp.bfloat16)


def depth_table(back=False):
    a = lax.broadcasted_iota(jnp.int32, (256, 256), 1 if back else 0)
    b = lax.broadcasted_iota(jnp.int32, (256, 256), 0 if back else 1)
    table = jnp.where(a == 4 * (b & 63) + (b >> 6), 1.0, 0.0).astype(jnp.bfloat16)
    return jnp.concatenate([table] * 3, axis=0)


def moved_lanes(x, table):
    return jnp.dot(jnp.concatenate(split_three(x), axis=1), table, preferred_element_type=f32)


def interleave(x, y):
    front = lanes_of(x.shape) < 64
    return jnp.where(front, x, pltpu.roll(y, 64, 1)), jnp.where(front, pltpu.roll(x, 64, 1), y)


def node_at(i, j, r):
    start = ((4 * (r // 4) + i) * 17 + 4 * (r % 4) + j) * 8
    return pl.ds(start if isinstance(i, int) else pl.multiple_of(start, 8), 8)


def gather_rows(nodes):
    sub = rows_of()
    turned = [rolled(v, r) for r, v in enumerate(nodes)]
    out = []
    for c in range(3):
        total = turned[0]
        for r in range(1, 8):
            total = jnp.where(sub == (r + c) % 8, turned[r], total)
        out.append(rolled(total, -c))
    return out


def scatter_rows(parts, wanted):
    sub = rows_of()
    turned = [rolled(v, c) for c, v in enumerate(parts)]
    out = []
    for r in wanted:
        total = jnp.where(sub == r, turned[0], jnp.where(sub == (r + 1) % 8, turned[1], turned[2]))
        out.append((r, rolled(total, -r)))
    return out


def every_node(body):
    def column(i, carry):
        for j in range(5):
            body(i, j, range(8) if j < 4 else (3, 7))
        return carry

    lax.fori_loop(0, 4, column, 0)
    for j in range(5):
        body(4, j, range(4, 8) if j < 4 else (7,))


def tile_copies(field, held, semaphores, first, out=False):
    copies = []
    for t in range(4):
        outside = field.at[:, :, :, pl.ds(128 * t, 128)]
        inside = held.reshape(4, 9, 17, 8, 128).at[t, :, :, pl.ds(0, 3), :]
        ends = (inside, outside) if out else (outside, inside)
        copies.append(pltpu.make_async_copy(*ends, semaphores.at[first + t]))
    return copies


def to_elements(half, wide, table, kept, puts):
    moved = moved_lanes(wide[...].reshape(600, 256), table)
    if half == 0:
        kept[...] = moved
        return
    for pair in range(2):
        lanes = slice(128 * pair, 128 * pair + 128)
        for l, value in enumerate(interleave(kept[:, lanes], moved[:, lanes])):
            puts(2 * pair + l, value.reshape(3, 5, 5, 8, 128))


def to_nodes(get, table, tall):
    pairs = [interleave(get(2 * p).reshape(600, 128), get(2 * p + 1).reshape(600, 128)) for p in range(2)]
    for half in range(2):
        wide = jnp.concatenate([pairs[0][half], pairs[1][half]], axis=1)
        tall[half] = moved_lanes(wide, table).reshape(3, 5, 5, 8, 256)


def lookup(material, row, region):
    total = jnp.zeros_like(region)
    for m in range(material.shape[1]):
        total = jnp.where(region == float(m + 1), material[row, m], total)
    return total


def internal(u, out, lame, shear, gx, gz, cross, planes, side):
    def depth_lines(i, carry):
        for j in range(5):
            for c in range(3):
                v = [u[c, i, j, k] for k in range(4)]
                v.append(deeper(v[0]))
                u[c, i, j, 4] = v[4]
                for k, g in enumerate(line(deriv, v)):
                    gz[c, i, j, k] = g
        return carry

    lax.fori_loop(0, 5, depth_lines, 0)

    def plane(k, carry):
        weight = jnp.where((k == 0) | (k == 4), float(quad[0]), jnp.where(k == 2, float(quad[2]), float(quad[1])))
        lame_k, shear_k = lame * (2.0 * weight), shear * (2.0 * weight)
        pairs = {}
        for a in range(3):
            for b in range(a, 3):
                w = float(quad[a] * quad[b])
                pairs[a, b] = pairs[b, a] = (lame_k * w, shear_k * w, shear_k * (2.0 * w))
        for c in range(3):
            for j in range(5):
                for i, g in enumerate(line(deriv, [u[c, i, j, k] for i in range(5)])):
                    gx[c, i, j] = g
        for i in range(5):
            gy = [line(deriv, [u[c, i, j, k] for j in range(5)]) for c in range(3)]
            ys = [[], [], []]
            for j in range(5):
                lw, mw, mw2 = pairs[kind[i], kind[j]]
                g0, g1, g2 = [[gx[c, i, j], gy[c][j], gz[c, i, j, k]] for c in range(3)]
                dilated = lw * (g0[0] + g1[1] + g2[2])
                s01 = mw * (g0[1] + g1[0])
                s02 = mw * (g0[2] + g2[0])
                s12 = mw * (g1[2] + g2[1])
                side[0, i, j] = dilated + mw2 * g0[0]
                side[1, i, j] = s01
                cross[0, i, j, k] = s02
                cross[1, i, j, k] = s12
                cross[2, i, j, k] = dilated + mw2 * g2[2]
                ys[0].append(s01)
                ys[1].append(dilated + mw2 * g1[1])
                ys[2].append(s12)
            for c in range(3):
                for j, value in enumerate(line(deriv_t, ys[c])):
                    planes[c, i, j, k] = value
        for j in range(5):
            for c in range(3):
                v = [side[c, i, j] if c < 2 else cross[0, i, j, k] for i in range(5)]
                for i, value in enumerate(line(deriv_t, v)):
                    planes[c, i, j, k] += value
        return carry

    lax.fori_loop(0, 5, plane, 0)

    def depth_sums(i, carry):
        for j in range(5):
            for c in range(3):
                v = line(deriv_t, [cross[c, i, j, k] for k in range(5)])
                v = [v[k] + planes[c, i, j, k] for k in range(5)]
                out[c, i, j, 0] = v[0] + shallower(v[4])
                for k in range(1, 4):
                    out[c, i, j, k] = v[k]
        return carry

    lax.fori_loop(0, 5, depth_sums, 0)
    sub = rows_of()

    def fold(k, carry):
        for c in range(3):
            for i in range(5):
                low, high = out[c, i, 0, k], out[c, i, 4, k]
                out[c, i, 0, k] = low + jnp.where(sub % 4 == 0, 0.0, pltpu.roll(high, 1, 0))
                out[c, i, 4, k] = high + jnp.where(sub % 4 == 3, 0.0, pltpu.roll(low, 7, 0))
            for j in range(5):
                low, high = out[c, 0, j, k], out[c, 4, j, k]
                out[c, 0, j, k] = low + jnp.where(sub < 4, 0.0, pltpu.roll(high, 4, 0))
                out[c, 4, j, k] = high + jnp.where(sub < 4, pltpu.roll(low, 4, 0), 0.0)
        return carry

    lax.fori_loop(0, 4, fold, 0)


def rolled(x, amount, axis=0):
    amount = amount % x.shape[axis]
    return pltpu.roll(x, amount, axis) if amount else x


def parity_x():
    return position("gx") % 2


def parity_y():
    return along_y() % 2


def sort_out(odd, low, high):
    return jnp.where(odd == 1, low, high), jnp.where(odd == 1, high, low)


def pack_x(force, first, second):
    sub, odd = rows_of(), parity_x()
    for c in range(3):
        for j in range(5):
            for half in range(2):
                at = (c * 5 + j) * 2 + half
                a, b = force[c, 0, j, 2 * half], force[c, 0, j, 2 * half + 1]
                low = jnp.where(sub < 4, a, rolled(b, 4))
                a, b = force[c, 4, j, 2 * half], force[c, 4, j, 2 * half + 1]
                high = jnp.where(sub < 4, rolled(a, 4), b)
                first[at], second[at] = sort_out(odd, low, high)


def pack_y(force, low, high):
    sub = rows_of()
    for c in range(3):
        for i in range(5):
            a, b = force[c, i, 0, 0], rolled(force[c, i, 4, 0], -3)
            for k in range(1, 4):
                a = jnp.where(sub % 4 == k, rolled(force[c, i, 0, k], k), a)
                b = jnp.where(sub % 4 == k, rolled(force[c, i, 4, k], k - 3), b)
            low[c * 5 + i] = a
            high[c * 5 + i] = b


def add_x(force, first, second):
    sub, odd = rows_of(), parity_x()
    for c in range(3):
        for j in range(5):
            for half in range(2):
                at = (c * 5 + j) * 2 + half
                r, s = sort_out(odd, first[at], second[at])
                force[c, 0, j, 2 * half] += jnp.where(sub < 4, r, 0.0)
                force[c, 0, j, 2 * half + 1] += jnp.where(sub < 4, rolled(r, 4), 0.0)
                force[c, 4, j, 2 * half] += jnp.where(sub < 4, 0.0, rolled(s, 4))
                force[c, 4, j, 2 * half + 1] += jnp.where(sub < 4, 0.0, s)


def add_y(force, first, second):
    sub, odd = rows_of(), parity_y()
    for c in range(3):
        for i in range(5):
            r, s = sort_out(odd, first[c * 5 + i], second[c * 5 + i])
            for k in range(4):
                force[c, i, 0, k] += jnp.where(sub % 4 == 0, rolled(r, -k), 0.0)
                force[c, i, 4, k] += jnp.where(sub % 4 == 3, rolled(s, 3 - k), 0.0)


def edge_rows(low, high, came1, came2, first, second):
    sub, odd, odd_y = rows_of(), parity_x(), parity_y()
    for c in range(3):
        came = [[sort_out(odd, came1[at], came2[at]) for at in range((c * 5 + j) * 2, (c * 5 + j) * 2 + 2)] for j in (0, 4)]
        for i in range(5):
            rows = [low[c * 5 + i], high[c * 5 + i]]
            if i in (0, 4):
                start, side = i, i // 4
                for end, row in ((0, 0), (1, 3)):
                    for k in range(4):
                        r = rolled(came[end][k // 2][side], start + k - (4 * (k % 2) + row))
                        rows[end] = rows[end] + jnp.where(sub == start + k, r, 0.0)
            first[c * 5 + i], second[c * 5 + i] = sort_out(odd_y, *rows)


def first_edge_kernel(low, high, came1, came2, rows_low, rows_high, crater1, crater2, after, first, second, token, ends, semaphores):
    token[...] = after[0:8]
    copies = fetch(
        [(c.at[:, pl.ds(24 * h, 8), :], ends.at[n, :, pl.ds(8 * h, 8), :]) for n, c in enumerate((crater1, crater2)) for h in range(2)],
        semaphores,
    )
    edge_rows(low, high, came1, came2, first, second)
    odd, odd_y = parity_x(), parity_y()
    regions = sort_out(odd, came1[30], came2[30])
    for n, value in enumerate((low[15], regions[0], regions[1])):
        first[15 + n] = value
        second[15 + n] = value
    for copy in copies:
        copy.wait()
    for f in range(5):
        for t in range(2):
            lanes = slice(128 * t, 128 * t + 128)
            at = 18 + f * 4 + t * 2
            first[at], second[at] = sort_out(odd_y, rows_low[f * 2 + t], rows_high[f * 2 + t])
            found = []
            for row in (0, 15):
                sides = sort_out(odd, ends[0, f, row : row + 1, lanes], ends[1, f, row : row + 1, lanes])
                found.append(jnp.concatenate(list(sides) * 4, axis=0))
            first[at + 1], second[at + 1] = sort_out(odd_y, *found)


def second_edge_kernel(low, high, came1, came2, after, first, second, token):
    edge_rows(low, high, came1, came2, first, second)
    token[...] = after[...]


def region_grid(own, x1, x2, y1, y2):
    xl, xh = sort_out(parity_x(), x1[30], x2[30])
    yl, yh = [list(v) for v in zip(*[sort_out(parity_y(), y1[n], y2[n]) for n in (15, 16, 17)])]
    return [[yl[1], xl, yh[1]], [yl[0], own, yh[0]], [yl[2], xh, yh[2]]]


def shared_density(grid):
    sub = rows_of()
    across = []
    for y in range(3):
        low, mid, high = grid[0][y], grid[1][y], grid[2][y]
        turned = rolled(mid, 4)
        across.append([jnp.where(sub < 4, rolled(low, 4), turned), mid, jnp.where(sub < 4, turned, rolled(high, 4))])
    found = [[None] * 3 for _ in range(3)]
    for x in range(3):
        low, mid, high = across[0][x], across[1][x], across[2][x]
        found[x][0] = jnp.where(sub % 4 == 0, rolled(low, -3), rolled(mid, 1))
        found[x][1] = mid
        found[x][2] = jnp.where(sub % 4 == 3, rolled(high, 3), rolled(mid, -1))
    sums = []
    for x in ((1,), (0, 1), (1, 2)):
        row = []
        for y in ((1,), (0, 1), (1, 2)):
            total = sum(found[a][b] for a in x for b in y)
            row.append((total + shallower(total), total))
        sums.append(row)
    return sums


def mass_scales(sums):
    return [[[1.0 / s for s in pair] for pair in row] for row in sums]


def edge_kind(i):
    return 1 if i == 0 else 2 if i == 4 else 0


def accel_scale(i, j, k):
    return float(-1.0 / (half_size**3 * quad[i] * quad[j] * quad[k]))


def first_kernel(nodes_y, u, v, a, density, momentum, energy, dest, slot, region, material, after,
                 b_out, bottoms, f_out, x1, x2, y_low, y_high, rows_low, rows_high, region_out,
                 elem, gx, gz, cross, planes, side, u_in, v_in, a_in, wide_u, wide_b, kept_u, kept_b, b_held,
                 cells, copies_held, dest_in, slot_in, region_in, semaphores):
    early = fetch(
        [(region, region_in), (dest, dest_in), (slot, slot_in), (density, cells.at[0]),
         (momentum, cells.at[pl.ds(1, 3)]), (energy, cells.at[4])],
        semaphores.at[pl.ds(14, 6)],
    )
    copies = [tile_copies(f, h, semaphores, 4 * n) for n, (f, h) in enumerate(((u, u_in), (v, v_in), (a, a_in)))]
    for t in range(4):
        for copy in copies:
            copy[t].start()
    table = depth_table()
    for copy in early:
        copy.wait()
    region_now = jnp.concatenate([region_in[0], region_in[1]], axis=0).astype(f32) + 1.0
    region_out[...] = region_now
    block = deepest_block(nodes_y, cells, dest_in, slot_in, region_now, rows_low, rows_high)
    for n in range(bottoms.shape[0]):
        copies_held[n] = block
    save_bottoms = pltpu.make_async_copy(copies_held, bottoms, semaphores.at[13])
    save_bottoms.start()

    def put_u(l, value):
        elem[:, :, :, l] = value

    def put_b(l, value):
        b_held[:, :, :, l] = value

    for half in range(2):
        for t in (2 * half, 2 * half + 1):
            for copy in copies:
                copy[t].wait()

        def column(i, carry):
            for t in (2 * half, 2 * half + 1):
                lanes = slice(128 * (t % 2), 128 * (t % 2) + 128)
                for j in range(5):
                    now, later = [], []
                    for r in range(8):
                        at = (t, node_at(i, j, r), slice(None))
                        step = time_step * v_in[at] + (0.5 * time_step**2) * a_in[at]
                        now.append(u_in[at] + step)
                        later.append(now[-1] + step)
                    for c, value in enumerate(gather_rows(now)):
                        wide_u[c, i, j, :, lanes] = value
                    for c, value in enumerate(gather_rows(later)):
                        wide_b[c, i, j, :, lanes] = value
            return carry

        lax.fori_loop(0, 5, column, 0)
        to_elements(half, wide_u, table, kept_u, put_u)
        to_elements(half, wide_b, table, kept_b, put_b)
    save_b = pltpu.make_async_copy(b_held, b_out, semaphores.at[12])
    save_b.start()
    internal(elem, f_out, lookup(material, 1, region_now), lookup(material, 2, region_now), gx, gz, cross, planes, side)
    pack_x(f_out, x1, x2)
    pack_y(f_out, y_low, y_high)
    x1[30] = region_now
    x2[30] = region_now
    y_low[15] = region_now
    save_b.wait()
    save_bottoms.wait()


def second_kernel(b, f, came_x1, came_x2, came_y1, came_y2, region, material, after, a_out, f_out, x1, x2, y_low, y_high, scales, token,
                  elem, gx, gz, cross, planes, side):
    region_now = region[...]
    token[...] = after[...]
    a_out[...] = f[...]
    add_x(a_out, came_x1, came_x2)
    add_y(a_out, came_y1, came_y2)
    grid = region_grid(region_now, came_x1, came_x2, came_y1, came_y2)
    inverse = mass_scales(shared_density([[lookup(material, 0, r) for r in row] for row in grid]))
    for x in range(3):
        for y in range(3):
            for z in range(2):
                scales[x, y, z] = inverse[x][y][z]
    for i in range(5):
        for j in range(5):
            for k in range(4):
                scale = scales[edge_kind(i), edge_kind(j), min(k, 1)] * accel_scale(i, j, k)
                for c in range(3):
                    value = a_out[c, i, j, k] * scale
                    a_out[c, i, j, k] = value
                    elem[c, i, j, k] = b[c, i, j, k] + time_step**2 * value
    internal(elem, f_out, lookup(material, 1, region_now), lookup(material, 2, region_now), gx, gz, cross, planes, side)
    pack_x(f_out, x1, x2)
    pack_y(f_out, y_low, y_high)


def spread_surface(source, held, count):
    lane = lanes_of((24, 128))
    for n in range(27):
        at = 8 * n
        tile, shift = at // 128, (128 - at % 128) % 128
        moved = rolled(source[:, 128 * tile : 128 * tile + 128], shift, 1)
        held[n] = jnp.where(lane < count, moved, 0.0)


def add_surface(held, tall):
    for c in range(3):
        for i in range(5):
            for j in range(5):
                for ex in range(2):
                    value = held[c * 9 + 4 * ex + i, pl.ds(j, 4, stride=4), :]
                    tall[0, c, i, j, 4 * ex : 4 * ex + 4, 0:128] += value


def place_kernel(a1, surf1, u, v, a, after, u_out, v_part, u_in, v_in, a_in, tall, surface, u_held, semaphores):
    copies = [tile_copies(f, h, semaphores, 4 * n) for n, (f, h) in enumerate(((u, u_in), (v, v_in), (a, a_in)))]
    for t in range(4):
        for copy in copies:
            copy[t].start()
    spread_surface(surf1, surface, 1)
    to_nodes(lambda l: a1[:, :, :, l], depth_table(back=True), tall)
    add_surface(surface, tall)
    saves = tile_copies(u_out, u_held, semaphores, 12, out=True)
    for t in range(4):
        for copy in copies:
            copy[t].wait()
        lanes = slice(128 * (t % 2), 128 * (t % 2) + 128)

        def body(i, j, wanted):
            for r, accel in scatter_rows([tall[t // 2, c, i, j, :, lanes] for c in range(3)], wanted):
                at = (t, node_at(i, j, r), slice(None))
                vv, aa = v_in[at], a_in[at]
                u_held[at] = u_in[at] + 2.0 * time_step * vv + time_step**2 * (aa + accel)
                v_part[at] = vv + (0.5 * time_step) * (aa + 2.0 * accel)

        every_node(body)
        saves[t].start()
    for save in saves:
        save.wait()


def last_kernel(v_part, f, x1, x2, y1, y2, scales, surf1, surf2, v_out, a_out, v_held, a_held, tall, surface, force, semaphores):
    force[...] = f[...]
    add_x(force, x1, x2)
    add_y(force, y1, y2)
    for i in range(5):
        for j in range(5):
            for k in range(4):
                scale = scales[edge_kind(i), edge_kind(j), min(k, 1)] * accel_scale(i, j, k)
                for c in range(3):
                    force[c, i, j, k] = force[c, i, j, k] * scale
    spread_surface(surf1, surface.at[0], 1)
    spread_surface(surf2, surface.at[1], 5)
    surface[0] = surface[0] + surface[1]
    to_nodes(lambda l: force[:, :, :, l], depth_table(back=True), tall)
    add_surface(surface.at[0], tall)
    saves = tile_copies(v_out, v_held, semaphores, 0, out=True) + tile_copies(a_out, a_held, semaphores, 4, out=True)
    for t in range(4):
        lanes = slice(128 * (t % 2), 128 * (t % 2) + 128)

        def body(i, j, wanted):
            for r, accel in scatter_rows([tall[t // 2, c, i, j, :, lanes] for c in range(3)], wanted):
                at = (t, node_at(i, j, r), slice(None))
                a_held[at] = accel
                v_held[at] = v_part[at] + (0.5 * time_step) * accel

        every_node(body)
        saves[t].start()
        saves[4 + t].start()
    for save in saves:
        save.wait()


def whole():
    return pl.BlockSpec(memory_space=pltpu.VMEM)


def scalars():
    return pl.BlockSpec(memory_space=pltpu.SMEM)


def call(kernel, ins, outs, scratch, smem=(), away=(), out_away=(), mib=10, copies=0):
    def spec(n):
        return scalars() if n in smem else pl.BlockSpec(memory_space=pltpu.HBM) if n in away else whole()

    scratch = [pltpu.VMEM(s, f32) if isinstance(s, tuple) else s for s in scratch]
    return pl.pallas_call(
        kernel,
        out_shape=[jax.ShapeDtypeStruct(s, f32) for s in outs],
        in_specs=[spec(n) for n in range(len(ins))],
        out_specs=[pl.BlockSpec(memory_space=pltpu.HBM) if n in out_away else whole() for n in range(len(outs))],
        scratch_shapes=scratch + ([pltpu.SemaphoreType.DMA((copies,))] if copies else []),
        compiler_params=pltpu.CompilerParams(vmem_limit_bytes=mib * 1024 * 1024),
        cost_estimate=pl.CostEstimate(flops=0, bytes_accessed=0, transcendentals=0),
    )(*ins)


def fetch(pairs, semaphores):
    copies = [pltpu.make_async_copy(source, target, semaphores.at[n]) for n, (source, target) in enumerate(pairs)]
    for copy in copies:
        copy.start()
    return copies


element_shape = (3, 5, 5, 4, 8, 128)
lines_shape = (3, 5, 5, 5, 8, 128)
internal_scratch = [lines_shape, (3, 5, 5, 8, 128), lines_shape, lines_shape, lines_shape, (2, 5, 5, 8, 128)]


def exchange(axis, first, second):
    count = lax.axis_size(axis)
    pairs = [(i, i + 1) for i in range(1, count - 1, 2)]
    first = lax.ppermute(first, axis, [(i, i ^ 1) for i in range(count)])
    return first, lax.ppermute(second, axis, pairs + [(j, i) for i, j in pairs])


def surface_tables():
    lane = np.arange(128)
    j, ey = lane // 8, lane % 8
    used = (j < 5) & (ey < 6)
    place = np.where(used, ey + 1, -9)
    source = lane[:, None]
    centre = source == place
    meet = centre | ((j == 0) & (source == place - 1)) | ((j == 4) & (source == place + 1))
    along = np.zeros((128, 128))
    for a in range(40):
        for b in range(40):
            if a % 8 == b % 8 and a % 8 < 6:
                along[a, b] = deriv[b // 8, a // 8]
    node = np.where(used, 4 * (ey - 1) + j, -9)
    fold = (lane[:, None] == node) & (lane[:, None] < 17)
    keep = fold & ((j < 4) & (ey < 5) | (j == 4) & (ey == 4))
    return np.stack([centre, meet, along, along.T, fold, keep]).astype(np.float32)


def full_dot(x, y, back=False):
    dims = (((1,), (1 if back else 0,)), ((), ()))
    return lax.dot_general(x, y, dims, precision=lax.Precision.HIGHEST, preferred_element_type=f32)


def deposit(faces, nodes_y, base_x, base_y, total):
    rows = faces.shape[1]
    sub = rows_of((8, 512)).astype(f32)
    total[...] = jnp.zeros_like(total)

    def one(step, carry):
        def wide(q):
            block = faces[q, pl.ds(4 * step, 4), :]
            return jnp.concatenate([block[n : n + 1] for n in range(4)], axis=1)

        ids = wide(3)
        node_x = jnp.floor((ids + 0.5) * (1.0 / nodes_y))
        rel_y = jnp.broadcast_to(ids - node_x * nodes_y - base_y, (8, 512))
        rel_x = jnp.broadcast_to(node_x - base_x, (8, 512))
        left = []
        hits = [(rel_x - i == 4.0 * sub) & (sub < 4.0) for i in range(5)]
        parts = [split_three(wide(c)) for c in range(3)]
        for part in range(3):
            for c in range(3):
                value = jnp.broadcast_to(parts[c][part].astype(f32), (8, 512))
                left += [jnp.where(hit, value, 0.0) for hit in hits]
        right = [jnp.where((rel_y - j == 4.0 * sub) & (sub < 6.0), 1.0, 0.0) for j in range(5)]
        right.append(jnp.zeros((88, 512), f32))
        left, right = jnp.concatenate(left, axis=0), jnp.concatenate(right, axis=0)
        total[...] += lax.dot_general(
            left.astype(jnp.bfloat16), right.astype(jnp.bfloat16), (((1,), (1,)), ((), ())), preferred_element_type=f32
        )
        return carry

    lax.fori_loop(0, rows // 4, one, 0)


def top_grid(rows, z):
    sub, lane = rows_of(), lanes_of()
    out = jnp.zeros((8, 128), f32)
    for x in range(3):
        for y in range(3):
            row = jnp.broadcast_to(rows[x][y], (8, 128))
            for ex in range(2):
                here = (sub == 2 * x + ex) & (lane >= 4 * y - 2) & (lane < 4 * y + 2) & (lane < 8)
                out = jnp.where(here, rolled(row, 4 * y - 2 - 8 * z - 4 * ex, 1), out)
    return out


def respond(total, grid, material, tables, out1, out2):
    sub, lane = rows_of(), lanes_of()
    top, below = top_grid(grid, 0), top_grid(grid, 1)
    centre, meet, along, along_t, fold, keep = [tables[n] for n in range(6)]
    sums0 = full_dot(lookup(material, 0, top), meet)
    sums1 = full_dot(lookup(material, 0, below), meet)
    lame = rolled(full_dot(lookup(material, 1, top), centre), -1)
    shear = rolled(full_dot(lookup(material, 2, top), centre), -1)
    weight_y = jnp.ones((8, 128), f32)
    for j in range(5):
        weight_y = jnp.where(lane // 8 == j, float(quad[j]), weight_y)

    def inverse(sums):
        mid = rolled(sums, -1)
        found = {0: mid + sums, 1: mid, 4: mid + rolled(sums, -2)}
        found = {i: jnp.where(s > 0.0, 1.0 / (s * weight_y), 0.0) for i, s in found.items()}
        found[2] = found[3] = found[1]
        return found

    light, heavy = inverse(sums0), inverse(sums0 + sums1)
    first = [[None] * 5 for _ in range(3)]
    moved = [[None] * 5 for _ in range(3)]
    for c in range(3):
        for i in range(5):
            at = (c * 5 + i) * 8
            force = total[at : at + 8] + total[at + 120 : at + 128] + total[at + 240 : at + 248]
            first[c][i] = force * light[i] * -accel_scale(i, 2, 0) * float(quad[2])
            moved[c][i] = first[c][i] * time_step**2
    gx = [line(deriv, moved[c]) for c in range(3)]
    gy = full_dot(jnp.concatenate([moved[c][i] for c in range(3) for i in range(5)], axis=0), along)
    gy = [[gy[(c * 5 + i) * 8 : (c * 5 + i) * 8 + 8] for i in range(5)] for c in range(3)]
    lame_w, shear_w = lame * weight_y * 2.0, shear * weight_y * 2.0
    d00 = float(deriv[0, 0])
    sx = [[], [], []]
    sy = [[], [], []]
    sz = [[], [], []]
    qs = [[], [], []]
    pressed = []
    for i in range(5):
        lw, mw = lame_w * float(quad[i]), shear_w * float(quad[i])
        d = [moved[c][i] for c in range(3)]
        gz = [d00 * x for x in d]
        dilated = lw * (gx[0][i] + gy[1][i] + gz[2])
        s01 = mw * (gx[1][i] + gy[0][i])
        s02 = mw * (gx[2][i] + gz[0])
        s12 = mw * (gy[2][i] + gz[1])
        for c, value in enumerate((dilated + 2.0 * mw * gx[0][i], s01, s02)):
            sx[c].append(value)
        for c, value in enumerate((s01, dilated + 2.0 * mw * gy[1][i], s12)):
            sy[c].append(value)
        for c, value in enumerate((s02, s12, dilated + 2.0 * mw * gz[2])):
            sz[c].append(value)
        for c, value in enumerate((mw * d[0], mw * d[1], (lw + 2.0 * mw) * d[2])):
            qs[c].append(value)
        pressed.append(lw * d[2])
    ydiv = full_dot(jnp.concatenate(sy[0] + sy[1] + sy[2] + pressed + qs[1], axis=0), along_t)
    ydiv = [[ydiv[(n * 5 + i) * 8 : (n * 5 + i) * 8 + 8] for i in range(5)] for n in range(5)]
    xdiv = [line(deriv_t, v) for v in sx + [pressed, qs[0]]]
    base = [xdiv[3], ydiv[3], [p + q for p, q in zip(xdiv[4], ydiv[4])]]
    second = {}
    for c in range(3):
        for i in range(5):
            for l in range(5):
                stiff = float(sum(deriv[k, l] * quad[k] * deriv[k, 0] for k in range(1, 5)))
                value = float(deriv[0, l] * quad[0]) * sz[c][i] + stiff * qs[c][i]
                if l:
                    value = value + float(deriv[l, 0] * quad[l]) * base[c][i]
                else:
                    value = value + float(quad[0]) * (xdiv[c][i] + ydiv[c][i])
                scale = (heavy if l == 4 else light)[i]
                second[c, i, l] = value * scale * (accel_scale(i, 2, l) * float(quad[2]))
    rows1, rows2 = [], []
    for c in range(3):
        for x in range(9):
            own = 1 if x < 4 else 2
            rows1.append(jnp.where(sub == 0, rolled(first[c][x - 4 * (own - 1)], -own), 0.0))
            block = jnp.zeros((8, 128), f32)
            for l in range(5):
                for ex in range(4):
                    i = x - 4 * (ex - 1)
                    if 0 <= i <= 4:
                        block = block + jnp.where(sub == l, rolled(second[c, i, l], l - ex), 0.0)
            rows2.append(block)
    blank = [jnp.zeros((40, 128), f32)]
    out1[...] = full_dot(keep[0:24], jnp.concatenate(rows1 + blank, axis=0), back=True)
    out2[...] = full_dot(fold[0:24], jnp.concatenate(rows2 + blank, axis=0), back=True)


def position(axis):
    return lax.axis_index(axis)


def along_y():
    return lax.axis_index("grp") * lax.axis_size("gy") + lax.axis_index("gy")


def primitives(state):
    inverse = 1.0 / state[0]
    v = [state[1 + c] * inverse for c in range(3)]
    p = (gamma_gas - 1.0) * (state[4] - 0.5 * (state[1] * v[0] + state[2] * v[1] + state[3] * v[2]))
    return v + [p, jnp.sqrt(gamma_gas * p * inverse), state[4] + p]


def flux(state, prim, d):
    out = [state[1 + d]] + [state[1 + c] * prim[d] for c in range(3)] + [prim[5] * prim[d]]
    out[1 + d] = out[1 + d] + prim[3]
    return out, jnp.abs(prim[d]) + prim[4]


def twice_face(low, high):
    fastest = jnp.maximum(low[2], high[2])
    return [fl + fh - fastest * (uh - ul) for ul, uh, fl, fh in zip(low[0], high[0], low[1], high[1])]


def turned_change(state, prim, d, axis, ends):
    size = state[0].shape[axis]
    fluxes, speed = flux(state, prim, d)
    up = lambda x: pltpu.roll(x, size - 1, axis)
    high = ([up(x) for x in state], [up(x) for x in fluxes], up(speed))
    upper = twice_face((state, fluxes, speed), high)
    if ends is None:
        return [g - pltpu.roll(g, 1, axis) for g in upper]
    upper = [jnp.where(ends[1], 2.0 * f, g) for f, g in zip(fluxes, upper)]
    return [g - jnp.where(ends[0], 2.0 * f, pltpu.roll(g, 1, axis)) for f, g in zip(fluxes, upper)]


def planes_kernel(density, momentum, energy, first, second, token, semaphores):
    odd = parity_x()
    pairs = []
    for out, down in ((first, odd), (second, 1 - odd)):
        for n, plane in enumerate((3 - 3 * down, 2 - down)):
            rows = pl.ds(32 * n, 32)
            pairs.append((density.at[plane], out.at[0, rows]))
            pairs.append((momentum.at[:, plane], out.at[pl.ds(1, 3), rows]))
            pairs.append((energy.at[plane], out.at[4, rows]))
    token[...] = jnp.zeros((8, 128), f32)
    for copy in fetch(pairs, semaphores):
        copy.wait()


def deepest_block(nodes_y, cells, dest, slot, region_now, rows_low, rows_high):
    sub, lane = rows_of(), lanes_of()
    pick = jnp.where(lane == 125 + sub, 1.0, 0.0)
    pieces = []
    for f in range(5):
        columns = jnp.concatenate([cells[f, x, :, 128:256] for x in range(4)], axis=0)
        pieces.append(full_dot(pick, columns, back=True)[0:3])
        for t in range(2):
            lanes = slice(128 * t, 128 * t + 128)
            for out, pair in ((rows_low, (0, 1)), (rows_high, (31, 30))):
                out[f * 2 + t] = jnp.concatenate([cells[f, x, r : r + 1, lanes] for r in pair for x in range(4)], axis=0)
    count_gy, count_x = lax.axis_size("gy"), lax.axis_size("gx")
    target, node = dest[...].astype(f32), slot[...].astype(f32)
    grp = jnp.floor((target + 0.5) * (1.0 / (count_gy * count_x)))
    rest = target - grp * (count_gy * count_x)
    gx = jnp.floor((rest + 0.5) * (1.0 / count_gy))
    gy = rest - gx * count_gy
    i = jnp.floor((node + 0.5) * (1.0 / 17.0))
    j = node - 17.0 * i
    pieces.append((8.0 * gx + i) * nodes_y + 16.0 * (grp * count_gy + gy) + j)
    found = jnp.zeros((8, 128), f32)
    for z in range(2):
        found = jnp.where(lane == 8 * z + sub, jnp.broadcast_to(region_now[:, z : z + 1], (8, 128)), found)
    pieces.append(jnp.broadcast_to(jnp.sum(found, axis=0, keepdims=True), (8, 128)))
    return jnp.concatenate(pieces, axis=0)


def crater_kernel(density, momentum, energy, came1, came2, rows1, rows2, after, out, token,
                  wide, mid, prims, face, fluxes, semaphores):
    planes, inner = pl.ds(2, 4), pl.ds(0, 32)
    copies = fetch(
        [(density, wide.at[0, planes, inner]), (momentum, wide.at[pl.ds(1, 3), planes, inner]),
         (energy, wide.at[4, planes, inner])],
        semaphores,
    )
    place, last_y = along_y(), lax.axis_size("grp") * lax.axis_size("gy") - 1
    gx, last_x = position("gx"), lax.axis_size("gx") - 1
    odd, odd_y = parity_x(), parity_y()
    for f in range(5):
        low, high = sort_out(odd, came1[f], came2[f])
        for p, value in ((0, low[32:64]), (1, low[0:32]), (6, high[0:32]), (7, high[32:64])):
            wide[f, p, 0:32, :] = value
            wide[f, p, 32:40, :] = value[0:8]
    token[...] = after[...]
    for copy in copies:
        copy.wait()
    for f in range(5):
        for x in range(4):
            wide[f, 2 + x, 32:40, :] = wide[f, 2 + x, 24:32, :]
        for t in range(2):
            lanes = slice(128 * t, 128 * t + 128)
            at = 18 + f * 4 + t * 2
            below, above = sort_out(odd_y, rows1[at], rows2[at])
            sides_below, sides_above = sort_out(odd_y, rows1[at + 1], rows2[at + 1])

            def put(p, row, edge, value):
                clamped = jnp.where(edge == 0, place == 0, place == last_y)
                at_edge = wide[f, p, 31 * edge : 31 * edge + 1, lanes]
                wide[f, p, row : row + 1, lanes] = jnp.where(clamped, at_edge, value)

            for x in range(4):
                put(2 + x, 39, 0, below[x : x + 1])
                put(2 + x, 38, 0, below[4 + x : 5 + x])
                put(2 + x, 32, 1, above[x : x + 1])
                put(2 + x, 33, 1, above[4 + x : 5 + x])
            for p, n in ((1, 0), (6, 1)):
                put(p, 39, 0, sides_below[n : n + 1])
                put(p, 32, 1, sides_above[n : n + 1])

    @pl.when(gx == 0)
    def _():
        for f in range(5):
            wide[f, 0] = wide[f, 2]
            wide[f, 1] = wide[f, 2]

    @pl.when(gx == last_x)
    def _():
        for f in range(5):
            wide[f, 6] = wide[f, 5]
            wide[f, 7] = wide[f, 5]

    lane = lanes_of((40, 256))
    ends = (lane == 0, lane == 255)

    def step(source, low, high, put):
        def along_x(p):
            state = [source[f, p] for f in range(5)]
            prim = primitives(state)
            return state, prim, flux(state, prim, 0)

        state, prim, (fx, speed) = along_x(low - 1)
        next_state, next_prim, (next_fx, next_speed) = along_x(low)
        g = twice_face((state, fx, speed), (next_state, next_fx, next_speed))
        for f in range(5):
            face[f] = g[f]
            fluxes[f] = next_fx[f]
        for n in range(6):
            prims[n] = next_prim[n]
        fluxes[5] = next_speed

        def plane(p, carry):
            state = [source[f, p] for f in range(5)]
            prim = [prims[n] for n in range(6)]
            next_state, next_prim, (next_fx, next_speed) = along_x(p + 1)
            g = twice_face((state, [fluxes[f] for f in range(5)], fluxes[5]), (next_state, next_fx, next_speed))
            change = [g[f] - face[f] for f in range(5)]
            for f in range(5):
                face[f] = g[f]
                fluxes[f] = next_fx[f]
            for n in range(6):
                prims[n] = next_prim[n]
            fluxes[5] = next_speed
            change = [a + b for a, b in zip(change, turned_change(state, prim, 1, 0, None))]
            change = [a + b for a, b in zip(change, turned_change(state, prim, 2, 1, ends))]
            for f in range(5):
                put(f, p, state[f] - (0.5 * cell_ratio) * change[f])
            return carry

        lax.fori_loop(low, high, plane, 0)

    def put_mid(f, p, value):
        mid[f, p] = value

    def put_out(f, p, value):
        out[f, p - 2] = value[0:32]

    step(wide, 1, 7, put_mid)

    @pl.when(gx == 0)
    def _():
        for f in range(5):
            mid[f, 1] = mid[f, 2]

    @pl.when(gx == last_x)
    def _():
        for f in range(5):
            mid[f, 6] = mid[f, 5]

    for f in range(5):
        for p in range(2, 6):
            edge = mid[f, p, 39:40, :]
            mid[f, p, 39:40, :] = jnp.where(place == 0, mid[f, p, 0:1, :], edge)
            edge = mid[f, p, 32:33, :]
            mid[f, p, 32:33, :] = jnp.where(place == last_y, mid[f, p, 31:32, :], edge)
    step(mid, 2, 6, put_out)


def bottom_tractions(bottoms, count_x, faces):
    shape = (count_x, 128)
    sub, lane = rows_of(shape), lanes_of(shape)
    count_gy = lax.axis_size("gy")

    def columns(q):
        parts = []
        for y in range(4):
            start = (y // count_gy * count_x * count_gy + y % count_gy) * 24 + q
            parts.append(bottoms[pl.ds(start, count_x, stride=24 * count_gy), :])
        found = []
        for x in range(4):
            total = rolled(parts[0], -32 * x, 1)
            for y in range(1, 4):
                total = jnp.where(lane // 32 == y, rolled(parts[y], 32 * (y - x), 1), total)
            found.append(total)
        return found

    cells = [[columns(f * 3 + z) for f in range(5)] for z in range(3)]
    state = [[[cells[z][f][x] for f in range(5)] for x in range(4)] for z in range(3)]
    ends_y = (lane == 0, lane == 127)

    def across_x(states, prims):
        fluxes = [flux(s, p, 0) for s, p in zip(states, prims)]
        data = [(s, f, a) for s, (f, a) in zip(states, fluxes)]
        up = lambda x: rolled(x, -1)
        wrap = ([up(v) for v in data[0][0]], [up(v) for v in data[0][1]], up(data[0][2]))
        upper = [twice_face(data[x], data[x + 1] if x < 3 else wrap) for x in range(4)]
        upper[3] = [jnp.where(sub == count_x - 1, 2.0 * f, g) for f, g in zip(data[3][1], upper[3])]
        below = [jnp.where(sub == 0, 2.0 * f, rolled(g, 1)) for f, g in zip(data[0][1], upper[3])]
        lower = [below] + upper[:3]
        return [[a - b for a, b in zip(u, l)] for u, l in zip(upper, lower)]

    def advanced(above, here, under, prim_above, prim_here, prim_under):
        changes = across_x(here, prim_here)
        out = []
        for x in range(4):
            change = [a + b for a, b in zip(changes[x], turned_change(here[x], prim_here[x], 1, 1, ends_y))]
            fz, az = flux(here[x], prim_here[x], 2)
            fa, aa = flux(above[x], prim_above[x], 2)
            lower = twice_face((above[x], fa, aa), (here[x], fz, az))
            if under is None:
                upper = [2.0 * f for f in fz]
            else:
                fu, au = flux(under[x], prim_under[x], 2)
                upper = twice_face((here[x], fz, az), (under[x], fu, au))
            out.append([s - (0.5 * cell_ratio) * (c + u - l) for s, c, u, l in zip(here[x], change, upper, lower)])
        return out

    prims = [[primitives(state[z][x]) for x in range(4)] for z in range(3)]
    middle = advanced(state[0], state[1], state[2], prims[0], prims[1], prims[2])
    deepest = advanced(state[1], state[2], None, prims[1], prims[2], None)
    prim_mid, prim_deep = [primitives(s) for s in middle], [primitives(s) for s in deepest]
    final = advanced(middle, deepest, None, prim_mid, prim_deep, None)
    ids = columns(15)
    for x in range(4):
        s, prim = final[x], primitives(final[x])
        at = pl.ds(x * count_x, count_x)
        faces[0, at, :] = face_area * s[1] * prim[2]
        faces[1, at, :] = face_area * s[2] * prim[2]
        faces[2, at, :] = face_area * (s[3] * prim[2] + prim[3])
        faces[3, at, :] = ids[x]


def deposit_kernel(nodes_y, count_x, bottoms, after, total, faces):
    base_x = (8 * position("gx") - 4).astype(f32)
    base_y = (16 * along_y() - 4).astype(f32)
    bottom_tractions(bottoms, count_x, faces)
    deposit(faces, nodes_y, base_x, base_y, total)


def respond_kernel(count_x, total, bottoms, material, tables, after, out1, out2, token, held, rows, semaphores):
    gx, place, count_gy = position("gx"), along_y(), lax.axis_size("gy")
    last_y = lax.axis_size("grp") * count_gy - 1
    pairs = [(tables, held)]
    for x in range(3):
        for y in range(3):
            cx, cy = jnp.clip(gx + x - 1, 0, count_x - 1), jnp.clip(place + y - 1, 0, last_y)
            rank = (cy // count_gy) * (count_x * count_gy) + cx * count_gy + cy % count_gy
            pairs.append((bottoms.at[rank, pl.ds(16, 8), :], rows.at[3 * x + y]))
    copies = fetch(pairs, semaphores)
    for copy in copies:
        copy.wait()
    found = []
    for x in range(3):
        found.append([])
        for y in range(3):
            px, py = gx + x - 1, place + y - 1
            inside = (px >= 0) & (px < count_x) & (py >= 0) & (py <= last_y)
            found[x].append(jnp.where(inside, rows[3 * x + y, 0:1, :], 0.0))
    respond(total, found, material, held, out1, out2)
    token[...] = after[...]


def shards(density, momentum, energy, displacement, velocity_field, acceleration, material, element_region_index,
           face_dest, face_slot):
    along, rank = ("grp", "gy"), ("grp", "gx", "gy")
    nodes_y = 16 * lax.axis_size(along) + 1
    count_x, devices = lax.axis_size("gx"), lax.axis_size(rank)
    crater = (density, momentum, energy)
    u, v, a = [jnp.transpose(x, (1, 2, 0, 3)) for x in (displacement, velocity_field, acceleration)]
    register, held_shape = (8, 128), (4, 1224, 128)
    crater1, crater2, token = call(
        planes_kernel, crater, [(5, 64, 256), (5, 64, 256), register], [], away=(0, 1, 2), mib=56, copies=12
    )
    crater1, crater2 = exchange("gx", crater1, crater2)
    vectors = pltpu.VMEM((1, 128), jnp.int32)
    b, bottoms, f, x1, x2, y_low, y_high, rows_low, rows_high, region = call(
        functools.partial(first_kernel, float(nodes_y)),
        (u, v, a) + crater + (face_dest.reshape(1, -1), face_slot, element_region_index, material, token),
        [element_shape, (devices, 24, 128), element_shape, (31, 8, 128), (31, 8, 128), (16, 8, 128), (15, 8, 128),
         (10, 8, 128), (10, 8, 128), register],
        internal_scratch
        + [held_shape] * 3
        + [(3, 5, 5, 8, 256), (3, 5, 5, 8, 256), (600, 256), (600, 256), element_shape]
        + [(5, 4, 32, 256), (devices, 24, 128), vectors, vectors, pltpu.VMEM((2, 4, 128), jnp.int32)],
        smem=(9,),
        away=(0, 1, 2, 3, 4, 5, 6, 7, 8),
        out_away=(0, 1),
        mib=56,
        copies=20,
    )
    bottoms = lax.all_to_all(bottoms, rank, 0, 0, tiled=True)
    (total,) = call(
        functools.partial(deposit_kernel, float(nodes_y), count_x),
        (bottoms.reshape(devices * 24, 128), region),
        [(360, 128)],
        [(4, 4 * count_x, 128)],
    )
    x1, x2 = exchange("gx", x1, x2)
    y1, y2, token = call(
        first_edge_kernel,
        (y_low, y_high, x1, x2, rows_low, rows_high, crater1, crater2, total),
        [(38, 8, 128), (38, 8, 128), register],
        [(2, 5, 16, 256)],
        away=(6, 7),
        copies=4,
    )
    surf1, surf2, token = call(
        functools.partial(respond_kernel, count_x),
        (total, bottoms, material, jnp.asarray(surface_tables()), token),
        [(24, 256), (24, 256), register],
        [(6, 128, 128), (9, 8, 128)],
        smem=(2,),
        away=(1, 3),
        copies=10,
    )
    y1, y2 = exchange(along, y1, y2)
    a1, f2, p1, p2, y_low, y_high, scales, token = call(
        second_kernel,
        (b, f, x1, x2, y1, y2, region, material, token),
        [element_shape, element_shape, (30, 8, 128), (30, 8, 128), (15, 8, 128), (15, 8, 128), (3, 3, 2, 8, 128), register],
        internal_scratch,
        smem=(7,),
    )
    hydro_state, token = call(
        crater_kernel,
        crater + (crater1, crater2, y1, y2, token),
        [(5, 4, 32, 256), register],
        [(5, 8, 40, 256), (5, 8, 40, 256), (6, 40, 256), (5, 40, 256), (6, 40, 256)],
        away=(0, 1, 2),
        copies=3,
    )
    p1, p2 = exchange("gx", p1, p2)
    r1, r2, token = call(
        second_edge_kernel, (y_low, y_high, p1, p2, token), [(15, 8, 128), (15, 8, 128), register], []
    )
    u_out, v_part = call(
        place_kernel,
        (a1, surf1, u, v, a, token),
        [u.shape, held_shape],
        [held_shape] * 3 + [(2, 3, 5, 5, 8, 256), (27, 24, 128), held_shape],
        away=(2, 3, 4),
        out_away=(0,),
        mib=20,
        copies=16,
    )
    r1, r2 = exchange(along, r1, r2)
    v_out, a_out = call(
        last_kernel,
        (v_part, f2, p1, p2, r1, r2, scales, surf1, surf2),
        [u.shape] * 2,
        [held_shape] * 2 + [(2, 3, 5, 5, 8, 256), (2, 27, 24, 128), element_shape],
        out_away=(0, 1),
        mib=16,
        copies=8,
    )
    u_out, v_out, a_out = [jnp.transpose(x, (2, 0, 1, 3)) for x in (u_out, v_out, a_out)]
    return hydro_state, u_out, v_out, a_out


def solution(mesh):
    field = P(None, "gx", ("grp", "gy"), None)
    cells = P("gx", ("grp", "gy"), None)
    rank = ("grp", "gx", "gy")
    return jax.shard_map(
        shards,
        mesh=mesh,
        in_specs=(cells, field, cells, field, field, field, P(), cells, P(rank, None, None), P(rank, None)),
        out_specs=(field, field, field, field),
        check_vma=False,
    )
```

```python
import functools

import jax
import jax.numpy as jnp
import numpy as np
from jax import lax
from jax.experimental import pallas as pl
from jax.experimental.pallas import tpu as pltpu
from jax.sharding import PartitionSpec as P

gamma_gas = 1.4
cell_ratio = 0.05
half_size = 2.0
time_step = 0.1
face_area = 2.0


def gll_tables():
    root = np.sqrt(3.0 / 7.0)
    points = np.array([-1.0, -root, 0.0, root, 1.0])
    weights = np.array([0.1, 49.0 / 90.0, 32.0 / 45.0, 49.0 / 90.0, 0.1])
    products = [np.prod([points[r] - points[c] for c in range(5) if c != r]) for r in range(5)]
    derivative = np.zeros((5, 5))
    for r in range(5):
        for c in range(5):
            if r != c:
                derivative[r, c] = products[r] / products[c] / (points[r] - points[c])
        derivative[r, r] = sum(1.0 / (points[r] - points[c]) for c in range(5) if c != r)
    derivative[2, 2] = 0.0
    return derivative, weights


deriv, quad = gll_tables()
deriv_t = deriv.T
kind = [0, 1, 2, 1, 0]
f32 = jnp.float32


def line(matrix, v):
    even, odd = (matrix + matrix[:, ::-1]) / 2, (matrix - matrix[:, ::-1]) / 2
    e0, e1, o0, o1 = v[0] + v[4], v[1] + v[3], v[0] - v[4], v[1] - v[3]
    top = [float(even[i, 0]) * e0 + float(even[i, 1]) * e1 + float(matrix[i, 2]) * v[2] for i in range(2)]
    low = [float(odd[i, 0]) * o0 + float(odd[i, 1]) * o1 for i in range(2)]
    centre = float(matrix[2, 0]) * o0 + float(matrix[2, 1]) * o1
    return [top[0] + low[0], top[1] + low[1], centre, low[1] - top[1], low[0] - top[0]]


def rows_of(shape=(8, 128)):
    return lax.broadcasted_iota(jnp.int32, shape, 0)


def lanes_of(shape=(8, 128)):
    return lax.broadcasted_iota(jnp.int32, shape, 1)


def deeper(x):
    return jnp.where(lanes_of() == 127, 0.0, pltpu.roll(x, 127, 1))


def shallower(x):
    return jnp.where(lanes_of() == 0, 0.0, pltpu.roll(x, 1, 1))


def split_three(x):
    high = x.astype(jnp.bfloat16)
    rest = x - high.astype(f32)
    middle = rest.astype(jnp.bfloat16)
    return high, middle, (rest - middle.astype(f32)).astype(jnp.bfloat16)


def depth_table(back=False):
    a = lax.broadcasted_iota(jnp.int32, (256, 256), 1 if back else 0)
    b = lax.broadcasted_iota(jnp.int32, (256, 256), 0 if back else 1)
    table = jnp.where(a == 4 * (b & 63) + (b >> 6), 1.0, 0.0).astype(jnp.bfloat16)
    return jnp.concatenate([table] * 3, axis=0)


def moved_lanes(x, table):
    return jnp.dot(jnp.concatenate(split_three(x), axis=1), table, preferred_element_type=f32)


def interleave(x, y):
    front = lanes_of(x.shape) < 64
    return jnp.where(front, x, pltpu.roll(y, 64, 1)), jnp.where(front, pltpu.roll(x, 64, 1), y)


def node_at(i, j, r):
    start = ((4 * (r // 4) + i) * 17 + 4 * (r % 4) + j) * 8
    return pl.ds(start if isinstance(i, int) else pl.multiple_of(start, 8), 8)


def gather_rows(nodes):
    sub = rows_of()
    turned = [rolled(v, r) for r, v in enumerate(nodes)]
    out = []
    for c in range(3):
        total = turned[0]
        for r in range(1, 8):
            total = jnp.where(sub == (r + c) % 8, turned[r], total)
        out.append(rolled(total, -c))
    return out


def scatter_rows(parts, wanted):
    sub = rows_of()
    turned = [rolled(v, c) for c, v in enumerate(parts)]
    out = []
    for r in wanted:
        total = jnp.where(sub == r, turned[0], jnp.where(sub == (r + 1) % 8, turned[1], turned[2]))
        out.append((r, rolled(total, -r)))
    return out


def every_node(body):
    def column(i, carry):
        for j in range(5):
            body(i, j, range(8) if j < 4 else (3, 7))
        return carry

    lax.fori_loop(0, 4, column, 0)
    for j in range(5):
        body(4, j, range(4, 8) if j < 4 else (7,))


def tile_copies(field, held, semaphores, first, out=False):
    copies = []
    for t in range(4):
        outside = field.at[:, :, :, pl.ds(128 * t, 128)]
        inside = held.reshape(4, 9, 17, 8, 128).at[t, :, :, pl.ds(0, 3), :]
        ends = (inside, outside) if out else (outside, inside)
        copies.append(pltpu.make_async_copy(*ends, semaphores.at[first + t]))
    return copies


def to_elements(half, wide, table, kept, puts):
    moved = moved_lanes(wide[...].reshape(600, 256), table)
    if half == 0:
        kept[...] = moved
        return
    for pair in range(2):
        lanes = slice(128 * pair, 128 * pair + 128)
        for l, value in enumerate(interleave(kept[:, lanes], moved[:, lanes])):
            puts(2 * pair + l, value.reshape(3, 5, 5, 8, 128))


def to_nodes(get, table, tall):
    pairs = [interleave(get(2 * p).reshape(600, 128), get(2 * p + 1).reshape(600, 128)) for p in range(2)]
    for half in range(2):
        wide = jnp.concatenate([pairs[0][half], pairs[1][half]], axis=1)
        tall[half] = moved_lanes(wide, table).reshape(3, 5, 5, 8, 256)


def lookup(material, row, region):
    total = jnp.zeros_like(region)
    for m in range(material.shape[1]):
        total = jnp.where(region == float(m + 1), material[row, m], total)
    return total


def internal(u, out, lame, shear, gx, gz, cross, planes, side):
    def depth_lines(i, carry):
        for j in range(5):
            for c in range(3):
                v = [u[c, i, j, k] for k in range(4)]
                v.append(deeper(v[0]))
                u[c, i, j, 4] = v[4]
                for k, g in enumerate(line(deriv, v)):
                    gz[c, i, j, k] = g
        return carry

    lax.fori_loop(0, 5, depth_lines, 0)

    def plane(k, carry):
        weight = jnp.where((k == 0) | (k == 4), float(quad[0]), jnp.where(k == 2, float(quad[2]), float(quad[1])))
        lame_k, shear_k = lame * (2.0 * weight), shear * (2.0 * weight)
        pairs = {}
        for a in range(3):
            for b in range(a, 3):
                w = float(quad[a] * quad[b])
                pairs[a, b] = pairs[b, a] = (lame_k * w, shear_k * w, shear_k * (2.0 * w))
        for c in range(3):
            for j in range(5):
                for i, g in enumerate(line(deriv, [u[c, i, j, k] for i in range(5)])):
                    gx[c, i, j] = g
        for i in range(5):
            gy = [line(deriv, [u[c, i, j, k] for j in range(5)]) for c in range(3)]
            ys = [[], [], []]
            for j in range(5):
                lw, mw, mw2 = pairs[kind[i], kind[j]]
                g0, g1, g2 = [[gx[c, i, j], gy[c][j], gz[c, i, j, k]] for c in range(3)]
                dilated = lw * (g0[0] + g1[1] + g2[2])
                s01 = mw * (g0[1] + g1[0])
                s02 = mw * (g0[2] + g2[0])
                s12 = mw * (g1[2] + g2[1])
                side[0, i, j] = dilated + mw2 * g0[0]
                side[1, i, j] = s01
                cross[0, i, j, k] = s02
                cross[1, i, j, k] = s12
                cross[2, i, j, k] = dilated + mw2 * g2[2]
                ys[0].append(s01)
                ys[1].append(dilated + mw2 * g1[1])
                ys[2].append(s12)
            for c in range(3):
                for j, value in enumerate(line(deriv_t, ys[c])):
                    planes[c, i, j, k] = value
        for j in range(5):
            for c in range(3):
                v = [side[c, i, j] if c < 2 else cross[0, i, j, k] for i in range(5)]
                for i, value in enumerate(line(deriv_t, v)):
                    planes[c, i, j, k] += value
        return carry

    lax.fori_loop(0, 5, plane, 0)

    def depth_sums(i, carry):
        for j in range(5):
            for c in range(3):
                v = line(deriv_t, [cross[c, i, j, k] for k in range(5)])
                v = [v[k] + planes[c, i, j, k] for k in range(5)]
                out[c, i, j, 0] = v[0] + shallower(v[4])
                for k in range(1, 4):
                    out[c, i, j, k] = v[k]
        return carry

    lax.fori_loop(0, 5, depth_sums, 0)
    sub = rows_of()

    def fold(k, carry):
        for c in range(3):
            for i in range(5):
                low, high = out[c, i, 0, k], out[c, i, 4, k]
                out[c, i, 0, k] = low + jnp.where(sub % 4 == 0, 0.0, pltpu.roll(high, 1, 0))
                out[c, i, 4, k] = high + jnp.where(sub % 4 == 3, 0.0, pltpu.roll(low, 7, 0))
            for j in range(5):
                low, high = out[c, 0, j, k], out[c, 4, j, k]
                out[c, 0, j, k] = low + jnp.where(sub < 4, 0.0, pltpu.roll(high, 4, 0))
                out[c, 4, j, k] = high + jnp.where(sub < 4, pltpu.roll(low, 4, 0), 0.0)
        return carry

    lax.fori_loop(0, 4, fold, 0)


def rolled(x, amount, axis=0):
    amount = amount % x.shape[axis]
    return pltpu.roll(x, amount, axis) if amount else x


def parity_x():
    return position("gx") % 2


def parity_y():
    return along_y() % 2


def sort_out(odd, low, high):
    return jnp.where(odd == 1, low, high), jnp.where(odd == 1, high, low)


def pack_x(force, first, second):
    sub, odd = rows_of(), parity_x()
    for c in range(3):
        for j in range(5):
            for half in range(2):
                at = (c * 5 + j) * 2 + half
                a, b = force[c, 0, j, 2 * half], force[c, 0, j, 2 * half + 1]
                low = jnp.where(sub < 4, a, rolled(b, 4))
                a, b = force[c, 4, j, 2 * half], force[c, 4, j, 2 * half + 1]
                high = jnp.where(sub < 4, rolled(a, 4), b)
                first[at], second[at] = sort_out(odd, low, high)


def pack_y(force, low, high):
    sub = rows_of()
    for c in range(3):
        for i in range(5):
            a, b = force[c, i, 0, 0], rolled(force[c, i, 4, 0], -3)
            for k in range(1, 4):
                a = jnp.where(sub % 4 == k, rolled(force[c, i, 0, k], k), a)
                b = jnp.where(sub % 4 == k, rolled(force[c, i, 4, k], k - 3), b)
            low[c * 5 + i] = a
            high[c * 5 + i] = b


def add_x(force, first, second):
    sub, odd = rows_of(), parity_x()
    for c in range(3):
        for j in range(5):
            for half in range(2):
                at = (c * 5 + j) * 2 + half
                r, s = sort_out(odd, first[at], second[at])
                force[c, 0, j, 2 * half] += jnp.where(sub < 4, r, 0.0)
                force[c, 0, j, 2 * half + 1] += jnp.where(sub < 4, rolled(r, 4), 0.0)
                force[c, 4, j, 2 * half] += jnp.where(sub < 4, 0.0, rolled(s, 4))
                force[c, 4, j, 2 * half + 1] += jnp.where(sub < 4, 0.0, s)


def add_y(force, first, second):
    sub, odd = rows_of(), parity_y()
    for c in range(3):
        for i in range(5):
            r, s = sort_out(odd, first[c * 5 + i], second[c * 5 + i])
            for k in range(4):
                force[c, i, 0, k] += jnp.where(sub % 4 == 0, rolled(r, -k), 0.0)
                force[c, i, 4, k] += jnp.where(sub % 4 == 3, rolled(s, 3 - k), 0.0)


def edge_rows(low, high, came1, came2, first, second):
    sub, odd, odd_y = rows_of(), parity_x(), parity_y()
    for c in range(3):
        came = [[sort_out(odd, came1[at], came2[at]) for at in range((c * 5 + j) * 2, (c * 5 + j) * 2 + 2)] for j in (0, 4)]
        for i in range(5):
            rows = [low[c * 5 + i], high[c * 5 + i]]
            if i in (0, 4):
                start, side = i, i // 4
                for end, row in ((0, 0), (1, 3)):
                    for k in range(4):
                        r = rolled(came[end][k // 2][side], start + k - (4 * (k % 2) + row))
                        rows[end] = rows[end] + jnp.where(sub == start + k, r, 0.0)
            first[c * 5 + i], second[c * 5 + i] = sort_out(odd_y, *rows)


def first_edge_kernel(low, high, came1, came2, rows_low, rows_high, crater1, crater2, after, first, second, token, ends, semaphores):
    token[...] = after[0:8]
    copies = fetch(
        [(c.at[:, pl.ds(24 * h, 8), :], ends.at[n, :, pl.ds(8 * h, 8), :]) for n, c in enumerate((crater1, crater2)) for h in range(2)],
        semaphores,
    )
    edge_rows(low, high, came1, came2, first, second)
    odd, odd_y = parity_x(), parity_y()
    regions = sort_out(odd, came1[30], came2[30])
    for n, value in enumerate((low[15], regions[0], regions[1])):
        first[15 + n] = value
        second[15 + n] = value
    for copy in copies:
        copy.wait()
    for f in range(5):
        for t in range(2):
            lanes = slice(128 * t, 128 * t + 128)
            at = 18 + f * 4 + t * 2
            first[at], second[at] = sort_out(odd_y, rows_low[f * 2 + t], rows_high[f * 2 + t])
            found = []
            for row in (0, 15):
                sides = sort_out(odd, ends[0, f, row : row + 1, lanes], ends[1, f, row : row + 1, lanes])
                found.append(jnp.concatenate(list(sides) * 4, axis=0))
            first[at + 1], second[at + 1] = sort_out(odd_y, *found)


def second_edge_kernel(low, high, came1, came2, after, first, second, token):
    edge_rows(low, high, came1, came2, first, second)
    token[...] = after[...]


def region_grid(own, x1, x2, y1, y2):
    xl, xh = sort_out(parity_x(), x1[30], x2[30])
    yl, yh = [list(v) for v in zip(*[sort_out(parity_y(), y1[n], y2[n]) for n in (15, 16, 17)])]
    return [[yl[1], xl, yh[1]], [yl[0], own, yh[0]], [yl[2], xh, yh[2]]]


def shared_density(grid):
    sub = rows_of()
    across = []
    for y in range(3):
        low, mid, high = grid[0][y], grid[1][y], grid[2][y]
        turned = rolled(mid, 4)
        across.append([jnp.where(sub < 4, rolled(low, 4), turned), mid, jnp.where(sub < 4, turned, rolled(high, 4))])
    found = [[None] * 3 for _ in range(3)]
    for x in range(3):
        low, mid, high = across[0][x], across[1][x], across[2][x]
        found[x][0] = jnp.where(sub % 4 == 0, rolled(low, -3), rolled(mid, 1))
        found[x][1] = mid
        found[x][2] = jnp.where(sub % 4 == 3, rolled(high, 3), rolled(mid, -1))
    sums = []
    for x in ((1,), (0, 1), (1, 2)):
        row = []
        for y in ((1,), (0, 1), (1, 2)):
            total = sum(found[a][b] for a in x for b in y)
            row.append((total + shallower(total), total))
        sums.append(row)
    return sums


def mass_scales(sums):
    return [[[1.0 / s for s in pair] for pair in row] for row in sums]


def edge_kind(i):
    return 1 if i == 0 else 2 if i == 4 else 0


def accel_scale(i, j, k):
    return float(-1.0 / (half_size**3 * quad[i] * quad[j] * quad[k]))


def first_kernel(u, v, a, region, material, b_out, f_out, x1, x2, y_low, y_high, token,
                 elem, gx, gz, cross, planes, side, u_in, v_in, a_in, wide_u, wide_b, kept_u, kept_b, b_held, semaphores):
    copies = [tile_copies(f, h, semaphores, 4 * n) for n, (f, h) in enumerate(((u, u_in), (v, v_in), (a, a_in)))]
    for t in range(4):
        for copy in copies:
            copy[t].start()
    table = depth_table()
    region_now = region[...]

    def put_u(l, value):
        elem[:, :, :, l] = value

    def put_b(l, value):
        b_held[:, :, :, l] = value

    for half in range(2):
        for t in (2 * half, 2 * half + 1):
            for copy in copies:
                copy[t].wait()

        def column(i, carry):
            for t in (2 * half, 2 * half + 1):
                lanes = slice(128 * (t % 2), 128 * (t % 2) + 128)
                for j in range(5):
                    now, later = [], []
                    for r in range(8):
                        at = (t, node_at(i, j, r), slice(None))
                        step = time_step * v_in[at] + (0.5 * time_step**2) * a_in[at]
                        now.append(u_in[at] + step)
                        later.append(now[-1] + step)
                    for c, value in enumerate(gather_rows(now)):
                        wide_u[c, i, j, :, lanes] = value
                    for c, value in enumerate(gather_rows(later)):
                        wide_b[c, i, j, :, lanes] = value
            return carry

        lax.fori_loop(0, 5, column, 0)
        to_elements(half, wide_u, table, kept_u, put_u)
        to_elements(half, wide_b, table, kept_b, put_b)
    save_b = pltpu.make_async_copy(b_held, b_out, semaphores.at[12])
    save_b.start()
    internal(elem, f_out, lookup(material, 1, region_now), lookup(material, 2, region_now), gx, gz, cross, planes, side)
    pack_x(f_out, x1, x2)
    pack_y(f_out, y_low, y_high)
    x1[30] = region_now
    x2[30] = region_now
    y_low[15] = region_now
    token[...] = region_now
    save_b.wait()


def second_kernel(b, f, came_x1, came_x2, came_y1, came_y2, region, material, after, a_out, f_out, x1, x2, y_low, y_high, scales, token,
                  elem, gx, gz, cross, planes, side):
    region_now = region[...]
    token[...] = after[...]
    a_out[...] = f[...]
    add_x(a_out, came_x1, came_x2)
    add_y(a_out, came_y1, came_y2)
    grid = region_grid(region_now, came_x1, came_x2, came_y1, came_y2)
    inverse = mass_scales(shared_density([[lookup(material, 0, r) for r in row] for row in grid]))
    for x in range(3):
        for y in range(3):
            for z in range(2):
                scales[x, y, z] = inverse[x][y][z]
    for i in range(5):
        for j in range(5):
            for k in range(4):
                scale = scales[edge_kind(i), edge_kind(j), min(k, 1)] * accel_scale(i, j, k)
                for c in range(3):
                    value = a_out[c, i, j, k] * scale
                    a_out[c, i, j, k] = value
                    elem[c, i, j, k] = b[c, i, j, k] + time_step**2 * value
    internal(elem, f_out, lookup(material, 1, region_now), lookup(material, 2, region_now), gx, gz, cross, planes, side)
    pack_x(f_out, x1, x2)
    pack_y(f_out, y_low, y_high)


def spread_surface(source, held, count):
    lane = lanes_of((24, 128))
    for n in range(27):
        at = 8 * n
        tile, shift = at // 128, (128 - at % 128) % 128
        moved = rolled(source[:, 128 * tile : 128 * tile + 128], shift, 1)
        held[n] = jnp.where(lane < count, moved, 0.0)


def add_surface(held, tall):
    for c in range(3):
        for i in range(5):
            for j in range(5):
                for ex in range(2):
                    value = held[c * 9 + 4 * ex + i, pl.ds(j, 4, stride=4), :]
                    tall[0, c, i, j, 4 * ex : 4 * ex + 4, 0:128] += value


def place_kernel(a1, surf1, u, v, a, after, u_out, v_part, u_in, v_in, a_in, tall, surface, u_held, semaphores):
    copies = [tile_copies(f, h, semaphores, 4 * n) for n, (f, h) in enumerate(((u, u_in), (v, v_in), (a, a_in)))]
    for t in range(4):
        for copy in copies:
            copy[t].start()
    spread_surface(surf1, surface, 1)
    to_nodes(lambda l: a1[:, :, :, l], depth_table(back=True), tall)
    add_surface(surface, tall)
    saves = tile_copies(u_out, u_held, semaphores, 12, out=True)
    for t in range(4):
        for copy in copies:
            copy[t].wait()
        lanes = slice(128 * (t % 2), 128 * (t % 2) + 128)

        def body(i, j, wanted):
            for r, accel in scatter_rows([tall[t // 2, c, i, j, :, lanes] for c in range(3)], wanted):
                at = (t, node_at(i, j, r), slice(None))
                vv, aa = v_in[at], a_in[at]
                u_held[at] = u_in[at] + 2.0 * time_step * vv + time_step**2 * (aa + accel)
                v_part[at] = vv + (0.5 * time_step) * (aa + 2.0 * accel)

        every_node(body)
        saves[t].start()
    for save in saves:
        save.wait()


def last_kernel(v_part, f, x1, x2, y1, y2, scales, surf1, surf2, v_out, a_out, v_held, a_held, tall, surface, force, semaphores):
    force[...] = f[...]
    add_x(force, x1, x2)
    add_y(force, y1, y2)
    for i in range(5):
        for j in range(5):
            for k in range(4):
                scale = scales[edge_kind(i), edge_kind(j), min(k, 1)] * accel_scale(i, j, k)
                for c in range(3):
                    force[c, i, j, k] = force[c, i, j, k] * scale
    spread_surface(surf1, surface.at[0], 1)
    spread_surface(surf2, surface.at[1], 5)
    surface[0] = surface[0] + surface[1]
    to_nodes(lambda l: force[:, :, :, l], depth_table(back=True), tall)
    add_surface(surface.at[0], tall)
    saves = tile_copies(v_out, v_held, semaphores, 0, out=True) + tile_copies(a_out, a_held, semaphores, 4, out=True)
    for t in range(4):
        lanes = slice(128 * (t % 2), 128 * (t % 2) + 128)

        def body(i, j, wanted):
            for r, accel in scatter_rows([tall[t // 2, c, i, j, :, lanes] for c in range(3)], wanted):
                at = (t, node_at(i, j, r), slice(None))
                a_held[at] = accel
                v_held[at] = v_part[at] + (0.5 * time_step) * accel

        every_node(body)
        saves[t].start()
        saves[4 + t].start()
    for save in saves:
        save.wait()


def whole():
    return pl.BlockSpec(memory_space=pltpu.VMEM)


def scalars():
    return pl.BlockSpec(memory_space=pltpu.SMEM)


def call(kernel, ins, outs, scratch, smem=(), away=(), out_away=(), mib=10, copies=0):
    def spec(n):
        return scalars() if n in smem else pl.BlockSpec(memory_space=pltpu.HBM) if n in away else whole()

    scratch = [pltpu.VMEM(s, f32) if isinstance(s, tuple) else s for s in scratch]
    return pl.pallas_call(
        kernel,
        out_shape=[jax.ShapeDtypeStruct(s, f32) for s in outs],
        in_specs=[spec(n) for n in range(len(ins))],
        out_specs=[pl.BlockSpec(memory_space=pltpu.HBM) if n in out_away else whole() for n in range(len(outs))],
        scratch_shapes=scratch + ([pltpu.SemaphoreType.DMA((copies,))] if copies else []),
        compiler_params=pltpu.CompilerParams(vmem_limit_bytes=mib * 1024 * 1024),
    )(*ins)


def fetch(pairs, semaphores):
    copies = [pltpu.make_async_copy(source, target, semaphores.at[n]) for n, (source, target) in enumerate(pairs)]
    for copy in copies:
        copy.start()
    return copies


element_shape = (3, 5, 5, 4, 8, 128)
lines_shape = (3, 5, 5, 5, 8, 128)
internal_scratch = [lines_shape, (3, 5, 5, 8, 128), lines_shape, lines_shape, lines_shape, (2, 5, 5, 8, 128)]


def exchange(axis, first, second):
    count = lax.axis_size(axis)
    pairs = [(i, i + 1) for i in range(1, count - 1, 2)]
    first = lax.ppermute(first, axis, [(i, i ^ 1) for i in range(count)])
    return first, lax.ppermute(second, axis, pairs + [(j, i) for i, j in pairs])


def surface_tables():
    lane = np.arange(128)
    j, ey = lane // 8, lane % 8
    used = (j < 5) & (ey < 6)
    place = np.where(used, ey + 1, -9)
    source = lane[:, None]
    centre = source == place
    meet = centre | ((j == 0) & (source == place - 1)) | ((j == 4) & (source == place + 1))
    along = np.zeros((128, 128))
    for a in range(40):
        for b in range(40):
            if a % 8 == b % 8 and a % 8 < 6:
                along[a, b] = deriv[b // 8, a // 8]
    node = np.where(used, 4 * (ey - 1) + j, -9)
    fold = (lane[:, None] == node) & (lane[:, None] < 17)
    keep = fold & ((j < 4) & (ey < 5) | (j == 4) & (ey == 4))
    return np.stack([centre, meet, along, along.T, fold, keep]).astype(np.float32)


def full_dot(x, y, back=False):
    dims = (((1,), (1 if back else 0,)), ((), ()))
    return lax.dot_general(x, y, dims, precision=lax.Precision.HIGHEST, preferred_element_type=f32)


def deposit(faces, nodes_y, base_x, base_y, total):
    rows = faces.shape[1]
    sub = rows_of((8, 512)).astype(f32)
    total[...] = jnp.zeros_like(total)

    def one(step, carry):
        def wide(q):
            block = faces[q, pl.ds(4 * step, 4), :]
            return jnp.concatenate([block[n : n + 1] for n in range(4)], axis=1)

        ids = wide(3)
        node_x = jnp.floor((ids + 0.5) * (1.0 / nodes_y))
        rel_y = jnp.broadcast_to(ids - node_x * nodes_y - base_y, (8, 512))
        rel_x = jnp.broadcast_to(node_x - base_x, (8, 512))
        left = []
        hits = [(rel_x - i == 4.0 * sub) & (sub < 4.0) for i in range(5)]
        parts = [split_three(wide(c)) for c in range(3)]
        for part in range(3):
            for c in range(3):
                value = jnp.broadcast_to(parts[c][part].astype(f32), (8, 512))
                left += [jnp.where(hit, value, 0.0) for hit in hits]
        right = [jnp.where((rel_y - j == 4.0 * sub) & (sub < 6.0), 1.0, 0.0) for j in range(5)]
        right.append(jnp.zeros((88, 512), f32))
        left, right = jnp.concatenate(left, axis=0), jnp.concatenate(right, axis=0)
        total[...] += lax.dot_general(
            left.astype(jnp.bfloat16), right.astype(jnp.bfloat16), (((1,), (1,)), ((), ())), preferred_element_type=f32
        )
        return carry

    lax.fori_loop(0, rows // 4, one, 0)


def top_grid(rows, z):
    sub, lane = rows_of(), lanes_of()
    out = jnp.zeros((8, 128), f32)
    for x in range(3):
        for y in range(3):
            row = jnp.broadcast_to(rows[x][y], (8, 128))
            for ex in range(2):
                here = (sub == 2 * x + ex) & (lane >= 4 * y - 2) & (lane < 4 * y + 2) & (lane < 8)
                out = jnp.where(here, rolled(row, 4 * y - 2 - 8 * z - 4 * ex, 1), out)
    return out


def respond(total, grid, material, tables, out1, out2):
    sub, lane = rows_of(), lanes_of()
    top, below = top_grid(grid, 0), top_grid(grid, 1)
    centre, meet, along, along_t, fold, keep = [tables[n] for n in range(6)]
    sums0 = full_dot(lookup(material, 0, top), meet)
    sums1 = full_dot(lookup(material, 0, below), meet)
    lame = rolled(full_dot(lookup(material, 1, top), centre), -1)
    shear = rolled(full_dot(lookup(material, 2, top), centre), -1)
    weight_y = jnp.ones((8, 128), f32)
    for j in range(5):
        weight_y = jnp.where(lane // 8 == j, float(quad[j]), weight_y)

    def inverse(sums):
        mid = rolled(sums, -1)
        found = {0: mid + sums, 1: mid, 4: mid + rolled(sums, -2)}
        found = {i: jnp.where(s > 0.0, 1.0 / (s * weight_y), 0.0) for i, s in found.items()}
        found[2] = found[3] = found[1]
        return found

    light, heavy = inverse(sums0), inverse(sums0 + sums1)
    first = [[None] * 5 for _ in range(3)]
    moved = [[None] * 5 for _ in range(3)]
    for c in range(3):
        for i in range(5):
            at = (c * 5 + i) * 8
            force = total[at : at + 8] + total[at + 120 : at + 128] + total[at + 240 : at + 248]
            first[c][i] = force * light[i] * -accel_scale(i, 2, 0) * float(quad[2])
            moved[c][i] = first[c][i] * time_step**2
    gx = [line(deriv, moved[c]) for c in range(3)]
    gy = full_dot(jnp.concatenate([moved[c][i] for c in range(3) for i in range(5)], axis=0), along)
    gy = [[gy[(c * 5 + i) * 8 : (c * 5 + i) * 8 + 8] for i in range(5)] for c in range(3)]
    lame_w, shear_w = lame * weight_y * 2.0, shear * weight_y * 2.0
    d00 = float(deriv[0, 0])
    sx = [[], [], []]
    sy = [[], [], []]
    sz = [[], [], []]
    qs = [[], [], []]
    pressed = []
    for i in range(5):
        lw, mw = lame_w * float(quad[i]), shear_w * float(quad[i])
        d = [moved[c][i] for c in range(3)]
        gz = [d00 * x for x in d]
        dilated = lw * (gx[0][i] + gy[1][i] + gz[2])
        s01 = mw * (gx[1][i] + gy[0][i])
        s02 = mw * (gx[2][i] + gz[0])
        s12 = mw * (gy[2][i] + gz[1])
        for c, value in enumerate((dilated + 2.0 * mw * gx[0][i], s01, s02)):
            sx[c].append(value)
        for c, value in enumerate((s01, dilated + 2.0 * mw * gy[1][i], s12)):
            sy[c].append(value)
        for c, value in enumerate((s02, s12, dilated + 2.0 * mw * gz[2])):
            sz[c].append(value)
        for c, value in enumerate((mw * d[0], mw * d[1], (lw + 2.0 * mw) * d[2])):
            qs[c].append(value)
        pressed.append(lw * d[2])
    ydiv = full_dot(jnp.concatenate(sy[0] + sy[1] + sy[2] + pressed + qs[1], axis=0), along_t)
    ydiv = [[ydiv[(n * 5 + i) * 8 : (n * 5 + i) * 8 + 8] for i in range(5)] for n in range(5)]
    xdiv = [line(deriv_t, v) for v in sx + [pressed, qs[0]]]
    base = [xdiv[3], ydiv[3], [p + q for p, q in zip(xdiv[4], ydiv[4])]]
    second = {}
    for c in range(3):
        for i in range(5):
            for l in range(5):
                stiff = float(sum(deriv[k, l] * quad[k] * deriv[k, 0] for k in range(1, 5)))
                value = float(deriv[0, l] * quad[0]) * sz[c][i] + stiff * qs[c][i]
                if l:
                    value = value + float(deriv[l, 0] * quad[l]) * base[c][i]
                else:
                    value = value + float(quad[0]) * (xdiv[c][i] + ydiv[c][i])
                scale = (heavy if l == 4 else light)[i]
                second[c, i, l] = value * scale * (accel_scale(i, 2, l) * float(quad[2]))
    rows1, rows2 = [], []
    for c in range(3):
        for x in range(9):
            own = 1 if x < 4 else 2
            rows1.append(jnp.where(sub == 0, rolled(first[c][x - 4 * (own - 1)], -own), 0.0))
            block = jnp.zeros((8, 128), f32)
            for l in range(5):
                for ex in range(4):
                    i = x - 4 * (ex - 1)
                    if 0 <= i <= 4:
                        block = block + jnp.where(sub == l, rolled(second[c, i, l], l - ex), 0.0)
            rows2.append(block)
    blank = [jnp.zeros((40, 128), f32)]
    out1[...] = full_dot(keep[0:24], jnp.concatenate(rows1 + blank, axis=0), back=True)
    out2[...] = full_dot(fold[0:24], jnp.concatenate(rows2 + blank, axis=0), back=True)


def position(axis):
    return lax.axis_index(axis)


def along_y():
    return lax.axis_index("grp") * lax.axis_size("gy") + lax.axis_index("gy")


def primitives(state):
    inverse = 1.0 / state[0]
    v = [state[1 + c] * inverse for c in range(3)]
    p = (gamma_gas - 1.0) * (state[4] - 0.5 * (state[1] * v[0] + state[2] * v[1] + state[3] * v[2]))
    return v + [p, jnp.sqrt(gamma_gas * p * inverse), state[4] + p]


def flux(state, prim, d):
    out = [state[1 + d]] + [state[1 + c] * prim[d] for c in range(3)] + [prim[5] * prim[d]]
    out[1 + d] = out[1 + d] + prim[3]
    return out, jnp.abs(prim[d]) + prim[4]


def twice_face(low, high):
    fastest = jnp.maximum(low[2], high[2])
    return [fl + fh - fastest * (uh - ul) for ul, uh, fl, fh in zip(low[0], high[0], low[1], high[1])]


def turned_change(state, prim, d, axis, ends):
    size = state[0].shape[axis]
    fluxes, speed = flux(state, prim, d)
    up = lambda x: pltpu.roll(x, size - 1, axis)
    high = ([up(x) for x in state], [up(x) for x in fluxes], up(speed))
    upper = twice_face((state, fluxes, speed), high)
    if ends is None:
        return [g - pltpu.roll(g, 1, axis) for g in upper]
    upper = [jnp.where(ends[1], 2.0 * f, g) for f, g in zip(fluxes, upper)]
    return [g - jnp.where(ends[0], 2.0 * f, pltpu.roll(g, 1, axis)) for f, g in zip(fluxes, upper)]


def start_kernel(nodes_y, density, momentum, energy, dest, slot, region, bottoms, first, second, rows_low, rows_high,
                 region_out, cells, dest_in, slot_in, region_in, semaphores):
    copies = fetch(
        [(dest, dest_in), (slot, slot_in), (region, region_in), (density, cells.at[0]),
         (momentum, cells.at[pl.ds(1, 3)]), (energy, cells.at[4])],
        semaphores,
    )
    for copy in copies:
        copy.wait()
    sub, lane = rows_of(), lanes_of()
    pick = jnp.where(lane == 125 + sub, 1.0, 0.0)
    pieces = []
    odd = parity_x()
    for f in range(5):
        columns = jnp.concatenate([cells[f, x, :, 128:256] for x in range(4)], axis=0)
        pieces.append(full_dot(pick, columns, back=True)[0:3])
        for out, down in ((first, odd), (second, 1 - odd)):
            out[f, 0:32, :] = cells[f, 3 - 3 * down]
            out[f, 32:64, :] = cells[f, 2 - down]
        for t in range(2):
            lanes = slice(128 * t, 128 * t + 128)
            for out, pair in ((rows_low, (0, 1)), (rows_high, (31, 30))):
                out[f * 2 + t] = jnp.concatenate([cells[f, x, r : r + 1, lanes] for r in pair for x in range(4)], axis=0)
    count_gy, count_x = lax.axis_size("gy"), lax.axis_size("gx")
    target, node = dest_in[...].astype(f32), slot_in[...].astype(f32)
    grp = jnp.floor((target + 0.5) * (1.0 / (count_gy * count_x)))
    rest = target - grp * (count_gy * count_x)
    gx = jnp.floor((rest + 0.5) * (1.0 / count_gy))
    gy = rest - gx * count_gy
    i = jnp.floor((node + 0.5) * (1.0 / 17.0))
    j = node - 17.0 * i
    pieces.append((8.0 * gx + i) * nodes_y + 16.0 * (grp * count_gy + gy) + j)
    region_now = jnp.concatenate([region_in[0], region_in[1]], axis=0).astype(f32) + 1.0
    region_out[...] = region_now
    found = jnp.zeros((8, 128), f32)
    for z in range(2):
        found = jnp.where(lane == 8 * z + sub, jnp.broadcast_to(region_now[:, z : z + 1], (8, 128)), found)
    pieces.append(jnp.broadcast_to(jnp.sum(found, axis=0, keepdims=True), (8, 128)))
    block = jnp.concatenate(pieces, axis=0)
    for n in range(bottoms.shape[0]):
        bottoms[n] = block


def crater_kernel(density, momentum, energy, came1, came2, rows1, rows2, after, out, token,
                  wide, mid, prims, face, fluxes, semaphores):
    planes, inner = pl.ds(2, 4), pl.ds(0, 32)
    copies = fetch(
        [(density, wide.at[0, planes, inner]), (momentum, wide.at[pl.ds(1, 3), planes, inner]),
         (energy, wide.at[4, planes, inner])],
        semaphores,
    )
    place, last_y = along_y(), lax.axis_size("grp") * lax.axis_size("gy") - 1
    gx, last_x = position("gx"), lax.axis_size("gx") - 1
    odd, odd_y = parity_x(), parity_y()
    for f in range(5):
        low, high = sort_out(odd, came1[f], came2[f])
        for p, value in ((0, low[32:64]), (1, low[0:32]), (6, high[0:32]), (7, high[32:64])):
            wide[f, p, 0:32, :] = value
            wide[f, p, 32:40, :] = value[0:8]
    token[...] = after[...]
    for copy in copies:
        copy.wait()
    for f in range(5):
        for x in range(4):
            wide[f, 2 + x, 32:40, :] = wide[f, 2 + x, 24:32, :]
        for t in range(2):
            lanes = slice(128 * t, 128 * t + 128)
            at = 18 + f * 4 + t * 2
            below, above = sort_out(odd_y, rows1[at], rows2[at])
            sides_below, sides_above = sort_out(odd_y, rows1[at + 1], rows2[at + 1])

            def put(p, row, edge, value):
                clamped = jnp.where(edge == 0, place == 0, place == last_y)
                at_edge = wide[f, p, 31 * edge : 31 * edge + 1, lanes]
                wide[f, p, row : row + 1, lanes] = jnp.where(clamped, at_edge, value)

            for x in range(4):
                put(2 + x, 39, 0, below[x : x + 1])
                put(2 + x, 38, 0, below[4 + x : 5 + x])
                put(2 + x, 32, 1, above[x : x + 1])
                put(2 + x, 33, 1, above[4 + x : 5 + x])
            for p, n in ((1, 0), (6, 1)):
                put(p, 39, 0, sides_below[n : n + 1])
                put(p, 32, 1, sides_above[n : n + 1])

    @pl.when(gx == 0)
    def _():
        for f in range(5):
            wide[f, 0] = wide[f, 2]
            wide[f, 1] = wide[f, 2]

    @pl.when(gx == last_x)
    def _():
        for f in range(5):
            wide[f, 6] = wide[f, 5]
            wide[f, 7] = wide[f, 5]

    lane = lanes_of((40, 256))
    ends = (lane == 0, lane == 255)

    def step(source, low, high, put):
        def along_x(p):
            state = [source[f, p] for f in range(5)]
            prim = primitives(state)
            return state, prim, flux(state, prim, 0)

        state, prim, (fx, speed) = along_x(low - 1)
        next_state, next_prim, (next_fx, next_speed) = along_x(low)
        g = twice_face((state, fx, speed), (next_state, next_fx, next_speed))
        for f in range(5):
            face[f] = g[f]
            fluxes[f] = next_fx[f]
        for n in range(6):
            prims[n] = next_prim[n]
        fluxes[5] = next_speed

        def plane(p, carry):
            state = [source[f, p] for f in range(5)]
            prim = [prims[n] for n in range(6)]
            next_state, next_prim, (next_fx, next_speed) = along_x(p + 1)
            g = twice_face((state, [fluxes[f] for f in range(5)], fluxes[5]), (next_state, next_fx, next_speed))
            change = [g[f] - face[f] for f in range(5)]
            for f in range(5):
                face[f] = g[f]
                fluxes[f] = next_fx[f]
            for n in range(6):
                prims[n] = next_prim[n]
            fluxes[5] = next_speed
            change = [a + b for a, b in zip(change, turned_change(state, prim, 1, 0, None))]
            change = [a + b for a, b in zip(change, turned_change(state, prim, 2, 1, ends))]
            for f in range(5):
                put(f, p, state[f] - (0.5 * cell_ratio) * change[f])
            return carry

        lax.fori_loop(low, high, plane, 0)

    def put_mid(f, p, value):
        mid[f, p] = value

    def put_out(f, p, value):
        out[f, p - 2] = value[0:32]

    step(wide, 1, 7, put_mid)

    @pl.when(gx == 0)
    def _():
        for f in range(5):
            mid[f, 1] = mid[f, 2]

    @pl.when(gx == last_x)
    def _():
        for f in range(5):
            mid[f, 6] = mid[f, 5]

    for f in range(5):
        for p in range(2, 6):
            edge = mid[f, p, 39:40, :]
            mid[f, p, 39:40, :] = jnp.where(place == 0, mid[f, p, 0:1, :], edge)
            edge = mid[f, p, 32:33, :]
            mid[f, p, 32:33, :] = jnp.where(place == last_y, mid[f, p, 31:32, :], edge)
    step(mid, 2, 6, put_out)


def bottom_tractions(bottoms, count_x, faces):
    shape = (count_x, 128)
    sub, lane = rows_of(shape), lanes_of(shape)
    count_gy = lax.axis_size("gy")

    def columns(q):
        parts = []
        for y in range(4):
            start = (y // count_gy * count_x * count_gy + y % count_gy) * 24 + q
            parts.append(bottoms[pl.ds(start, count_x, stride=24 * count_gy), :])
        found = []
        for x in range(4):
            total = rolled(parts[0], -32 * x, 1)
            for y in range(1, 4):
                total = jnp.where(lane // 32 == y, rolled(parts[y], 32 * (y - x), 1), total)
            found.append(total)
        return found

    cells = [[columns(f * 3 + z) for f in range(5)] for z in range(3)]
    state = [[[cells[z][f][x] for f in range(5)] for x in range(4)] for z in range(3)]
    ends_y = (lane == 0, lane == 127)

    def across_x(states, prims):
        fluxes = [flux(s, p, 0) for s, p in zip(states, prims)]
        data = [(s, f, a) for s, (f, a) in zip(states, fluxes)]
        up = lambda x: rolled(x, -1)
        wrap = ([up(v) for v in data[0][0]], [up(v) for v in data[0][1]], up(data[0][2]))
        upper = [twice_face(data[x], data[x + 1] if x < 3 else wrap) for x in range(4)]
        upper[3] = [jnp.where(sub == count_x - 1, 2.0 * f, g) for f, g in zip(data[3][1], upper[3])]
        below = [jnp.where(sub == 0, 2.0 * f, rolled(g, 1)) for f, g in zip(data[0][1], upper[3])]
        lower = [below] + upper[:3]
        return [[a - b for a, b in zip(u, l)] for u, l in zip(upper, lower)]

    def advanced(above, here, under, prim_above, prim_here, prim_under):
        changes = across_x(here, prim_here)
        out = []
        for x in range(4):
            change = [a + b for a, b in zip(changes[x], turned_change(here[x], prim_here[x], 1, 1, ends_y))]
            fz, az = flux(here[x], prim_here[x], 2)
            fa, aa = flux(above[x], prim_above[x], 2)
            lower = twice_face((above[x], fa, aa), (here[x], fz, az))
            if under is None:
                upper = [2.0 * f for f in fz]
            else:
                fu, au = flux(under[x], prim_under[x], 2)
                upper = twice_face((here[x], fz, az), (under[x], fu, au))
            out.append([s - (0.5 * cell_ratio) * (c + u - l) for s, c, u, l in zip(here[x], change, upper, lower)])
        return out

    prims = [[primitives(state[z][x]) for x in range(4)] for z in range(3)]
    middle = advanced(state[0], state[1], state[2], prims[0], prims[1], prims[2])
    deepest = advanced(state[1], state[2], None, prims[1], prims[2], None)
    prim_mid, prim_deep = [primitives(s) for s in middle], [primitives(s) for s in deepest]
    final = advanced(middle, deepest, None, prim_mid, prim_deep, None)
    ids = columns(15)
    for x in range(4):
        s, prim = final[x], primitives(final[x])
        at = pl.ds(x * count_x, count_x)
        faces[0, at, :] = face_area * s[1] * prim[2]
        faces[1, at, :] = face_area * s[2] * prim[2]
        faces[2, at, :] = face_area * (s[3] * prim[2] + prim[3])
        faces[3, at, :] = ids[x]


def deposit_kernel(nodes_y, count_x, bottoms, after, total, faces):
    base_x = (8 * position("gx") - 4).astype(f32)
    base_y = (16 * along_y() - 4).astype(f32)
    bottom_tractions(bottoms, count_x, faces)
    deposit(faces, nodes_y, base_x, base_y, total)


def respond_kernel(count_x, total, bottoms, material, tables, after, out1, out2, token, held, rows, semaphores):
    gx, place, count_gy = position("gx"), along_y(), lax.axis_size("gy")
    last_y = lax.axis_size("grp") * count_gy - 1
    pairs = [(tables, held)]
    for x in range(3):
        for y in range(3):
            cx, cy = jnp.clip(gx + x - 1, 0, count_x - 1), jnp.clip(place + y - 1, 0, last_y)
            rank = (cy // count_gy) * (count_x * count_gy) + cx * count_gy + cy % count_gy
            pairs.append((bottoms.at[rank, pl.ds(16, 8), :], rows.at[3 * x + y]))
    copies = fetch(pairs, semaphores)
    for copy in copies:
        copy.wait()
    found = []
    for x in range(3):
        found.append([])
        for y in range(3):
            px, py = gx + x - 1, place + y - 1
            inside = (px >= 0) & (px < count_x) & (py >= 0) & (py <= last_y)
            found[x].append(jnp.where(inside, rows[3 * x + y, 0:1, :], 0.0))
    respond(total, found, material, held, out1, out2)
    token[...] = after[...]


def shards(density, momentum, energy, displacement, velocity_field, acceleration, material, element_region_index,
           face_dest, face_slot):
    along, rank = ("grp", "gy"), ("grp", "gx", "gy")
    nodes_y = 16 * lax.axis_size(along) + 1
    count_x, devices = lax.axis_size("gx"), lax.axis_size(rank)
    crater = (density, momentum, energy)
    u, v, a = [jnp.transpose(x, (1, 2, 0, 3)) for x in (displacement, velocity_field, acceleration)]
    register, held_shape = (8, 128), (4, 1224, 128)
    bottoms, crater1, crater2, rows_low, rows_high, region = call(
        functools.partial(start_kernel, float(nodes_y)),
        crater + (face_dest.reshape(1, -1), face_slot, element_region_index),
        [(devices, 24, 128), (5, 64, 256), (5, 64, 256), (10, 8, 128), (10, 8, 128), register],
        [(5, 4, 32, 256), pltpu.VMEM((1, 128), jnp.int32), pltpu.VMEM((1, 128), jnp.int32),
         pltpu.VMEM((2, 4, 128), jnp.int32)],
        away=(0, 1, 2, 3, 4, 5),
        mib=56,
        copies=6,
    )
    bottoms = lax.all_to_all(bottoms, rank, 0, 0, tiled=True)
    crater1, crater2 = exchange("gx", crater1, crater2)
    b, f, x1, x2, y_low, y_high, token = call(
        first_kernel,
        (u, v, a, region, material),
        [element_shape, element_shape, (31, 8, 128), (31, 8, 128), (16, 8, 128), (15, 8, 128), register],
        internal_scratch
        + [held_shape] * 3
        + [(3, 5, 5, 8, 256), (3, 5, 5, 8, 256), (600, 256), (600, 256), element_shape],
        smem=(4,),
        away=(0, 1, 2),
        out_away=(0,),
        mib=28,
        copies=13,
    )
    (total,) = call(
        functools.partial(deposit_kernel, float(nodes_y), count_x),
        (bottoms.reshape(devices * 24, 128), token),
        [(360, 128)],
        [(4, 4 * count_x, 128)],
    )
    x1, x2 = exchange("gx", x1, x2)
    y1, y2, token = call(
        first_edge_kernel,
        (y_low, y_high, x1, x2, rows_low, rows_high, crater1, crater2, total),
        [(38, 8, 128), (38, 8, 128), register],
        [(2, 5, 16, 256)],
        away=(6, 7),
        copies=4,
    )
    surf1, surf2, token = call(
        functools.partial(respond_kernel, count_x),
        (total, bottoms, material, jnp.asarray(surface_tables()), token),
        [(24, 256), (24, 256), register],
        [(6, 128, 128), (9, 8, 128)],
        smem=(2,),
        away=(1, 3),
        copies=10,
    )
    y1, y2 = exchange(along, y1, y2)
    a1, f2, p1, p2, y_low, y_high, scales, token = call(
        second_kernel,
        (b, f, x1, x2, y1, y2, region, material, token),
        [element_shape, element_shape, (30, 8, 128), (30, 8, 128), (15, 8, 128), (15, 8, 128), (3, 3, 2, 8, 128), register],
        internal_scratch,
        smem=(7,),
    )
    hydro_state, token = call(
        crater_kernel,
        crater + (crater1, crater2, y1, y2, token),
        [(5, 4, 32, 256), register],
        [(5, 8, 40, 256), (5, 8, 40, 256), (6, 40, 256), (5, 40, 256), (6, 40, 256)],
        away=(0, 1, 2),
        copies=3,
    )
    p1, p2 = exchange("gx", p1, p2)
    r1, r2, token = call(
        second_edge_kernel, (y_low, y_high, p1, p2, token), [(15, 8, 128), (15, 8, 128), register], []
    )
    u_out, v_part = call(
        place_kernel,
        (a1, surf1, u, v, a, token),
        [u.shape, held_shape],
        [held_shape] * 3 + [(2, 3, 5, 5, 8, 256), (27, 24, 128), held_shape],
        away=(2, 3, 4),
        out_away=(0,),
        mib=20,
        copies=16,
    )
    r1, r2 = exchange(along, r1, r2)
    v_out, a_out = call(
        last_kernel,
        (v_part, f2, p1, p2, r1, r2, scales, surf1, surf2),
        [u.shape] * 2,
        [held_shape] * 2 + [(2, 3, 5, 5, 8, 256), (2, 27, 24, 128), element_shape],
        out_away=(0, 1),
        mib=16,
        copies=8,
    )
    u_out, v_out, a_out = [jnp.transpose(x, (2, 0, 1, 3)) for x in (u_out, v_out, a_out)]
    return hydro_state, u_out, v_out, a_out


def solution(mesh):
    field = P(None, "gx", ("grp", "gy"), None)
    cells = P("gx", ("grp", "gy"), None)
    rank = ("grp", "gx", "gy")
    return jax.shard_map(
        shards,
        mesh=mesh,
        in_specs=(cells, field, cells, field, field, field, P(), cells, P(rank, None, None), P(rank, None)),
        out_specs=(field, field, field, field),
        check_vma=False,
    )
```

```python
import functools

import jax
import jax.numpy as jnp
import numpy as np
from jax import lax
from jax.experimental import pallas as pl
from jax.experimental.pallas import tpu as pltpu
from jax.sharding import PartitionSpec as P

gamma_gas = 1.4
cell_ratio = 0.05
half_size = 2.0
time_step = 0.1
face_area = 2.0


def gll_tables():
    root = np.sqrt(3.0 / 7.0)
    points = np.array([-1.0, -root, 0.0, root, 1.0])
    weights = np.array([0.1, 49.0 / 90.0, 32.0 / 45.0, 49.0 / 90.0, 0.1])
    products = [np.prod([points[r] - points[c] for c in range(5) if c != r]) for r in range(5)]
    derivative = np.zeros((5, 5))
    for r in range(5):
        for c in range(5):
            if r != c:
                derivative[r, c] = products[r] / products[c] / (points[r] - points[c])
        derivative[r, r] = sum(1.0 / (points[r] - points[c]) for c in range(5) if c != r)
    derivative[2, 2] = 0.0
    return derivative, weights


deriv, quad = gll_tables()
deriv_t = deriv.T
kind = [0, 1, 2, 1, 0]
f32 = jnp.float32


def line(matrix, v):
    even, odd = (matrix + matrix[:, ::-1]) / 2, (matrix - matrix[:, ::-1]) / 2
    e0, e1, o0, o1 = v[0] + v[4], v[1] + v[3], v[0] - v[4], v[1] - v[3]
    top = [float(even[i, 0]) * e0 + float(even[i, 1]) * e1 + float(matrix[i, 2]) * v[2] for i in range(2)]
    low = [float(odd[i, 0]) * o0 + float(odd[i, 1]) * o1 for i in range(2)]
    centre = float(matrix[2, 0]) * o0 + float(matrix[2, 1]) * o1
    return [top[0] + low[0], top[1] + low[1], centre, low[1] - top[1], low[0] - top[0]]


def rows_of(shape=(8, 128)):
    return lax.broadcasted_iota(jnp.int32, shape, 0)


def lanes_of(shape=(8, 128)):
    return lax.broadcasted_iota(jnp.int32, shape, 1)


def deeper(x):
    return jnp.where(lanes_of() == 127, 0.0, pltpu.roll(x, 127, 1))


def shallower(x):
    return jnp.where(lanes_of() == 0, 0.0, pltpu.roll(x, 1, 1))


def split_three(x):
    high = x.astype(jnp.bfloat16)
    rest = x - high.astype(f32)
    middle = rest.astype(jnp.bfloat16)
    return high, middle, (rest - middle.astype(f32)).astype(jnp.bfloat16)


def depth_table(back=False):
    a = lax.broadcasted_iota(jnp.int32, (256, 256), 1 if back else 0)
    b = lax.broadcasted_iota(jnp.int32, (256, 256), 0 if back else 1)
    table = jnp.where(a == 4 * (b & 63) + (b >> 6), 1.0, 0.0).astype(jnp.bfloat16)
    return jnp.concatenate([table] * 3, axis=0)


def moved_lanes(x, table):
    return jnp.dot(jnp.concatenate(split_three(x), axis=1), table, preferred_element_type=f32)


def interleave(x, y):
    front = lanes_of(x.shape) < 64
    return jnp.where(front, x, pltpu.roll(y, 64, 1)), jnp.where(front, pltpu.roll(x, 64, 1), y)


def node_at(i, j, r):
    start = ((4 * (r // 4) + i) * 17 + 4 * (r % 4) + j) * 8
    return pl.ds(start if isinstance(i, int) else pl.multiple_of(start, 8), 8)


def gather_rows(nodes):
    sub = rows_of()
    turned = [rolled(v, r) for r, v in enumerate(nodes)]
    out = []
    for c in range(3):
        total = turned[0]
        for r in range(1, 8):
            total = jnp.where(sub == (r + c) % 8, turned[r], total)
        out.append(rolled(total, -c))
    return out


def scatter_rows(parts, wanted):
    sub = rows_of()
    turned = [rolled(v, c) for c, v in enumerate(parts)]
    out = []
    for r in wanted:
        total = jnp.where(sub == r, turned[0], jnp.where(sub == (r + 1) % 8, turned[1], turned[2]))
        out.append((r, rolled(total, -r)))
    return out


def every_node(body):
    def column(i, carry):
        for j in range(5):
            body(i, j, range(8) if j < 4 else (3, 7))
        return carry

    lax.fori_loop(0, 4, column, 0)
    for j in range(5):
        body(4, j, range(4, 8) if j < 4 else (7,))


def tile_copies(field, held, semaphores, first, out=False):
    copies = []
    for t in range(4):
        outside = field.at[:, :, :, pl.ds(128 * t, 128)]
        inside = held.reshape(4, 9, 17, 8, 128).at[t, :, :, pl.ds(0, 3), :]
        ends = (inside, outside) if out else (outside, inside)
        copies.append(pltpu.make_async_copy(*ends, semaphores.at[first + t]))
    return copies


def to_elements(half, wide, table, kept, puts):
    moved = moved_lanes(wide[...].reshape(600, 256), table)
    if half == 0:
        kept[...] = moved
        return
    for pair in range(2):
        lanes = slice(128 * pair, 128 * pair + 128)
        for l, value in enumerate(interleave(kept[:, lanes], moved[:, lanes])):
            puts(2 * pair + l, value.reshape(3, 5, 5, 8, 128))


def to_nodes(get, table, tall):
    pairs = [interleave(get(2 * p).reshape(600, 128), get(2 * p + 1).reshape(600, 128)) for p in range(2)]
    for half in range(2):
        wide = jnp.concatenate([pairs[0][half], pairs[1][half]], axis=1)
        tall[half] = moved_lanes(wide, table).reshape(3, 5, 5, 8, 256)


def lookup(material, row, region):
    total = jnp.zeros_like(region)
    for m in range(material.shape[1]):
        total = jnp.where(region == float(m + 1), material[row, m], total)
    return total


def internal(u, out, lame, shear, gx, gz, cross, planes, side):
    def depth_lines(i, carry):
        for j in range(5):
            for c in range(3):
                v = [u[c, i, j, k] for k in range(4)]
                v.append(deeper(v[0]))
                u[c, i, j, 4] = v[4]
                for k, g in enumerate(line(deriv, v)):
                    gz[c, i, j, k] = g
        return carry

    lax.fori_loop(0, 5, depth_lines, 0)

    def plane(k, carry):
        weight = jnp.where((k == 0) | (k == 4), float(quad[0]), jnp.where(k == 2, float(quad[2]), float(quad[1])))
        lame_k, shear_k = lame * (2.0 * weight), shear * (2.0 * weight)
        pairs = {}
        for a in range(3):
            for b in range(a, 3):
                w = float(quad[a] * quad[b])
                pairs[a, b] = pairs[b, a] = (lame_k * w, shear_k * w, shear_k * (2.0 * w))
        for c in range(3):
            for j in range(5):
                for i, g in enumerate(line(deriv, [u[c, i, j, k] for i in range(5)])):
                    gx[c, i, j] = g
        for i in range(5):
            gy = [line(deriv, [u[c, i, j, k] for j in range(5)]) for c in range(3)]
            ys = [[], [], []]
            for j in range(5):
                lw, mw, mw2 = pairs[kind[i], kind[j]]
                g0, g1, g2 = [[gx[c, i, j], gy[c][j], gz[c, i, j, k]] for c in range(3)]
                dilated = lw * (g0[0] + g1[1] + g2[2])
                s01 = mw * (g0[1] + g1[0])
                s02 = mw * (g0[2] + g2[0])
                s12 = mw * (g1[2] + g2[1])
                side[0, i, j] = dilated + mw2 * g0[0]
                side[1, i, j] = s01
                cross[0, i, j, k] = s02
                cross[1, i, j, k] = s12
                cross[2, i, j, k] = dilated + mw2 * g2[2]
                ys[0].append(s01)
                ys[1].append(dilated + mw2 * g1[1])
                ys[2].append(s12)
            for c in range(3):
                for j, value in enumerate(line(deriv_t, ys[c])):
                    planes[c, i, j, k] = value
        for j in range(5):
            for c in range(3):
                v = [side[c, i, j] if c < 2 else cross[0, i, j, k] for i in range(5)]
                for i, value in enumerate(line(deriv_t, v)):
                    planes[c, i, j, k] += value
        return carry

    lax.fori_loop(0, 5, plane, 0)

    def depth_sums(i, carry):
        for j in range(5):
            for c in range(3):
                v = line(deriv_t, [cross[c, i, j, k] for k in range(5)])
                v = [v[k] + planes[c, i, j, k] for k in range(5)]
                out[c, i, j, 0] = v[0] + shallower(v[4])
                for k in range(1, 4):
                    out[c, i, j, k] = v[k]
        return carry

    lax.fori_loop(0, 5, depth_sums, 0)
    sub = rows_of()

    def fold(k, carry):
        for c in range(3):
            for i in range(5):
                low, high = out[c, i, 0, k], out[c, i, 4, k]
                out[c, i, 0, k] = low + jnp.where(sub % 4 == 0, 0.0, pltpu.roll(high, 1, 0))
                out[c, i, 4, k] = high + jnp.where(sub % 4 == 3, 0.0, pltpu.roll(low, 7, 0))
            for j in range(5):
                low, high = out[c, 0, j, k], out[c, 4, j, k]
                out[c, 0, j, k] = low + jnp.where(sub < 4, 0.0, pltpu.roll(high, 4, 0))
                out[c, 4, j, k] = high + jnp.where(sub < 4, pltpu.roll(low, 4, 0), 0.0)
        return carry

    lax.fori_loop(0, 4, fold, 0)


def rolled(x, amount, axis=0):
    amount = amount % x.shape[axis]
    return pltpu.roll(x, amount, axis) if amount else x


def parity_x():
    return position("gx") % 2


def parity_y():
    return along_y() % 2


def sort_out(odd, low, high):
    return jnp.where(odd == 1, low, high), jnp.where(odd == 1, high, low)


def pack_x(force, first, second):
    sub, odd = rows_of(), parity_x()
    for c in range(3):
        for j in range(5):
            for half in range(2):
                at = (c * 5 + j) * 2 + half
                a, b = force[c, 0, j, 2 * half], force[c, 0, j, 2 * half + 1]
                low = jnp.where(sub < 4, a, rolled(b, 4))
                a, b = force[c, 4, j, 2 * half], force[c, 4, j, 2 * half + 1]
                high = jnp.where(sub < 4, rolled(a, 4), b)
                first[at], second[at] = sort_out(odd, low, high)


def pack_y(force, low, high):
    sub = rows_of()
    for c in range(3):
        for i in range(5):
            a, b = force[c, i, 0, 0], rolled(force[c, i, 4, 0], -3)
            for k in range(1, 4):
                a = jnp.where(sub % 4 == k, rolled(force[c, i, 0, k], k), a)
                b = jnp.where(sub % 4 == k, rolled(force[c, i, 4, k], k - 3), b)
            low[c * 5 + i] = a
            high[c * 5 + i] = b


def add_x(force, first, second):
    sub, odd = rows_of(), parity_x()
    for c in range(3):
        for j in range(5):
            for half in range(2):
                at = (c * 5 + j) * 2 + half
                r, s = sort_out(odd, first[at], second[at])
                force[c, 0, j, 2 * half] += jnp.where(sub < 4, r, 0.0)
                force[c, 0, j, 2 * half + 1] += jnp.where(sub < 4, rolled(r, 4), 0.0)
                force[c, 4, j, 2 * half] += jnp.where(sub < 4, 0.0, rolled(s, 4))
                force[c, 4, j, 2 * half + 1] += jnp.where(sub < 4, 0.0, s)


def add_y(force, first, second):
    sub, odd = rows_of(), parity_y()
    for c in range(3):
        for i in range(5):
            r, s = sort_out(odd, first[c * 5 + i], second[c * 5 + i])
            for k in range(4):
                force[c, i, 0, k] += jnp.where(sub % 4 == 0, rolled(r, -k), 0.0)
                force[c, i, 4, k] += jnp.where(sub % 4 == 3, rolled(s, 3 - k), 0.0)


def edge_rows(low, high, came1, came2, first, second):
    sub, odd, odd_y = rows_of(), parity_x(), parity_y()
    for c in range(3):
        came = [[sort_out(odd, came1[at], came2[at]) for at in range((c * 5 + j) * 2, (c * 5 + j) * 2 + 2)] for j in (0, 4)]
        for i in range(5):
            rows = [low[c * 5 + i], high[c * 5 + i]]
            if i in (0, 4):
                start, side = i, i // 4
                for end, row in ((0, 0), (1, 3)):
                    for k in range(4):
                        r = rolled(came[end][k // 2][side], start + k - (4 * (k % 2) + row))
                        rows[end] = rows[end] + jnp.where(sub == start + k, r, 0.0)
            first[c * 5 + i], second[c * 5 + i] = sort_out(odd_y, *rows)


def first_edge_kernel(y_rows, came1, came2, rows_low, rows_high, crater1, crater2, after, first, second, token, ends, semaphores):
    token[...] = after[0:8]
    copies = fetch(
        [(c.at[:, pl.ds(24 * h, 8), :], ends.at[n, :, pl.ds(8 * h, 8), :]) for n, c in enumerate((crater1, crater2)) for h in range(2)],
        semaphores,
    )
    edge_rows(y_rows.at[pl.ds(0, 15)], y_rows.at[pl.ds(16, 15)], came1, came2, first, second)
    odd, odd_y = parity_x(), parity_y()
    regions = sort_out(odd, came1[30], came2[30])
    for n, value in enumerate((y_rows[15], regions[0], regions[1])):
        first[15 + n] = value
        second[15 + n] = value
    for copy in copies:
        copy.wait()
    for f in range(5):
        for t in range(2):
            at = 18 + f * 2 + t
            first[at], second[at] = sort_out(odd_y, rows_low[f * 2 + t], rows_high[f * 2 + t])
        found = []
        for row in (0, 15):
            sides = []
            for t in range(2):
                lanes = slice(128 * t, 128 * t + 128)
                sides += sort_out(odd, ends[0, f, row : row + 1, lanes], ends[1, f, row : row + 1, lanes])
            found.append(jnp.concatenate(sides * 2, axis=0))
        first[28 + f], second[28 + f] = sort_out(odd_y, *found)


def second_edge_kernel(low, high, came1, came2, after, first, second, token):
    edge_rows(low, high, came1, came2, first, second)
    token[...] = after[...]


def region_grid(own, x1, x2, y1, y2):
    xl, xh = sort_out(parity_x(), x1[30], x2[30])
    yl, yh = [list(v) for v in zip(*[sort_out(parity_y(), y1[n], y2[n]) for n in (15, 16, 17)])]
    return [[yl[1], xl, yh[1]], [yl[0], own, yh[0]], [yl[2], xh, yh[2]]]


def shared_density(grid):
    sub = rows_of()
    across = []
    for y in range(3):
        low, mid, high = grid[0][y], grid[1][y], grid[2][y]
        turned = rolled(mid, 4)
        across.append([jnp.where(sub < 4, rolled(low, 4), turned), mid, jnp.where(sub < 4, turned, rolled(high, 4))])
    found = [[None] * 3 for _ in range(3)]
    for x in range(3):
        low, mid, high = across[0][x], across[1][x], across[2][x]
        found[x][0] = jnp.where(sub % 4 == 0, rolled(low, -3), rolled(mid, 1))
        found[x][1] = mid
        found[x][2] = jnp.where(sub % 4 == 3, rolled(high, 3), rolled(mid, -1))
    sums = []
    for x in ((1,), (0, 1), (1, 2)):
        row = []
        for y in ((1,), (0, 1), (1, 2)):
            total = sum(found[a][b] for a in x for b in y)
            row.append((total + shallower(total), total))
        sums.append(row)
    return sums


def mass_scales(sums):
    return [[[1.0 / s for s in pair] for pair in row] for row in sums]


def edge_kind(i):
    return 1 if i == 0 else 2 if i == 4 else 0


def accel_scale(i, j, k):
    return float(-1.0 / (half_size**3 * quad[i] * quad[j] * quad[k]))


def first_kernel(u, v, a, region, material, b_out, f_out, x1, x2, y_rows,
                 elem, gx, gz, cross, planes, side, u_in, v_in, a_in, wide_u, wide_b, kept_u, kept_b, b_held, semaphores):
    copies = [tile_copies(f, h, semaphores, 4 * n) for n, (f, h) in enumerate(((u, u_in), (v, v_in), (a, a_in)))]
    for t in range(4):
        for copy in copies:
            copy[t].start()
    table = depth_table()
    region_now = region[...]

    def put_u(l, value):
        elem[:, :, :, l] = value

    def put_b(l, value):
        b_held[:, :, :, l] = value

    for half in range(2):
        for t in (2 * half, 2 * half + 1):
            for copy in copies:
                copy[t].wait()

        def column(i, carry):
            for t in (2 * half, 2 * half + 1):
                lanes = slice(128 * (t % 2), 128 * (t % 2) + 128)
                for j in range(5):
                    now, later = [], []
                    for r in range(8):
                        at = (t, node_at(i, j, r), slice(None))
                        step = time_step * v_in[at] + (0.5 * time_step**2) * a_in[at]
                        now.append(u_in[at] + step)
                        later.append(now[-1] + step)
                    for c, value in enumerate(gather_rows(now)):
                        wide_u[c, i, j, :, lanes] = value
                    for c, value in enumerate(gather_rows(later)):
                        wide_b[c, i, j, :, lanes] = value
            return carry

        lax.fori_loop(0, 5, column, 0)
        to_elements(half, wide_u, table, kept_u, put_u)
        to_elements(half, wide_b, table, kept_b, put_b)
    save_b = pltpu.make_async_copy(b_held, b_out, semaphores.at[12])
    save_b.start()
    internal(elem, f_out, lookup(material, 1, region_now), lookup(material, 2, region_now), gx, gz, cross, planes, side)
    pack_x(f_out, x1, x2)
    pack_y(f_out, y_rows.at[pl.ds(0, 15)], y_rows.at[pl.ds(16, 15)])
    x1[30] = region_now
    x2[30] = region_now
    y_rows[15] = region_now
    save_b.wait()


def second_kernel(b, f, came_x1, came_x2, came_y1, came_y2, region, material, after, a_out, f_out, x1, x2, y_low, y_high, scales, token,
                  elem, gx, gz, cross, planes, side):
    region_now = region[...]
    token[...] = after[...]
    a_out[...] = f[...]
    add_x(a_out, came_x1, came_x2)
    add_y(a_out, came_y1, came_y2)
    grid = region_grid(region_now, came_x1, came_x2, came_y1, came_y2)
    inverse = mass_scales(shared_density([[lookup(material, 0, r) for r in row] for row in grid]))
    for x in range(3):
        for y in range(3):
            for z in range(2):
                scales[x, y, z] = inverse[x][y][z]
    for i in range(5):
        for j in range(5):
            for k in range(4):
                scale = scales[edge_kind(i), edge_kind(j), min(k, 1)] * accel_scale(i, j, k)
                for c in range(3):
                    value = a_out[c, i, j, k] * scale
                    a_out[c, i, j, k] = value
                    elem[c, i, j, k] = b[c, i, j, k] + time_step**2 * value
    internal(elem, f_out, lookup(material, 1, region_now), lookup(material, 2, region_now), gx, gz, cross, planes, side)
    pack_x(f_out, x1, x2)
    pack_y(f_out, y_low, y_high)


def spread_surface(source, held, count):
    lane = lanes_of((24, 128))
    for n in range(27):
        at = 8 * n
        tile, shift = at // 128, (128 - at % 128) % 128
        moved = rolled(source[:, 128 * tile : 128 * tile + 128], shift, 1)
        held[n] = jnp.where(lane < count, moved, 0.0)


def add_surface(held, tall):
    for c in range(3):
        for i in range(5):
            for j in range(5):
                for ex in range(2):
                    value = held[c * 9 + 4 * ex + i, pl.ds(j, 4, stride=4), :]
                    tall[0, c, i, j, 4 * ex : 4 * ex + 4, 0:128] += value


def place_kernel(a1, surf1, u, v, a, after, u_out, v_part, u_in, v_in, a_in, tall, surface, u_held, semaphores):
    copies = [tile_copies(f, h, semaphores, 4 * n) for n, (f, h) in enumerate(((u, u_in), (v, v_in), (a, a_in)))]
    for t in range(4):
        for copy in copies:
            copy[t].start()
    spread_surface(surf1, surface, 1)
    to_nodes(lambda l: a1[:, :, :, l], depth_table(back=True), tall)
    add_surface(surface, tall)
    saves = tile_copies(u_out, u_held, semaphores, 12, out=True)
    for t in range(4):
        for copy in copies:
            copy[t].wait()
        lanes = slice(128 * (t % 2), 128 * (t % 2) + 128)

        def body(i, j, wanted):
            for r, accel in scatter_rows([tall[t // 2, c, i, j, :, lanes] for c in range(3)], wanted):
                at = (t, node_at(i, j, r), slice(None))
                vv, aa = v_in[at], a_in[at]
                u_held[at] = u_in[at] + 2.0 * time_step * vv + time_step**2 * (aa + accel)
                v_part[at] = vv + (0.5 * time_step) * (aa + 2.0 * accel)

        every_node(body)
        saves[t].start()
    for save in saves:
        save.wait()


def last_kernel(v_part, f, x1, x2, y1, y2, scales, surf1, surf2, v_out, a_out, v_held, a_held, tall, surface, force, semaphores):
    force[...] = f[...]
    add_x(force, x1, x2)
    add_y(force, y1, y2)
    for i in range(5):
        for j in range(5):
            for k in range(4):
                scale = scales[edge_kind(i), edge_kind(j), min(k, 1)] * accel_scale(i, j, k)
                for c in range(3):
                    force[c, i, j, k] = force[c, i, j, k] * scale
    spread_surface(surf1, surface.at[0], 1)
    spread_surface(surf2, surface.at[1], 5)
    surface[0] = surface[0] + surface[1]
    to_nodes(lambda l: force[:, :, :, l], depth_table(back=True), tall)
    add_surface(surface.at[0], tall)
    saves = tile_copies(v_out, v_held, semaphores, 0, out=True) + tile_copies(a_out, a_held, semaphores, 4, out=True)
    for t in range(4):
        lanes = slice(128 * (t % 2), 128 * (t % 2) + 128)

        def body(i, j, wanted):
            for r, accel in scatter_rows([tall[t // 2, c, i, j, :, lanes] for c in range(3)], wanted):
                at = (t, node_at(i, j, r), slice(None))
                a_held[at] = accel
                v_held[at] = v_part[at] + (0.5 * time_step) * accel

        every_node(body)
        saves[t].start()
        saves[4 + t].start()
    for save in saves:
        save.wait()


def whole():
    return pl.BlockSpec(memory_space=pltpu.VMEM)


def scalars():
    return pl.BlockSpec(memory_space=pltpu.SMEM)


def call(kernel, ins, outs, scratch, smem=(), away=(), out_away=(), mib=10, copies=0):
    def spec(n):
        return scalars() if n in smem else pl.BlockSpec(memory_space=pltpu.HBM) if n in away else whole()

    scratch = [pltpu.VMEM(s, f32) if isinstance(s, tuple) else s for s in scratch]
    return pl.pallas_call(
        kernel,
        out_shape=[jax.ShapeDtypeStruct(s, f32) for s in outs],
        in_specs=[spec(n) for n in range(len(ins))],
        out_specs=[pl.BlockSpec(memory_space=pltpu.HBM) if n in out_away else whole() for n in range(len(outs))],
        scratch_shapes=scratch + ([pltpu.SemaphoreType.DMA((copies,))] if copies else []),
        compiler_params=pltpu.CompilerParams(vmem_limit_bytes=mib * 1024 * 1024),
    )(*ins)


def fetch(pairs, semaphores):
    copies = [pltpu.make_async_copy(source, target, semaphores.at[n]) for n, (source, target) in enumerate(pairs)]
    for copy in copies:
        copy.start()
    return copies


element_shape = (3, 5, 5, 4, 8, 128)
lines_shape = (3, 5, 5, 5, 8, 128)
internal_scratch = [lines_shape, (3, 5, 5, 8, 128), lines_shape, lines_shape, lines_shape, (2, 5, 5, 8, 128)]


def exchange(axis, first, second):
    count = lax.axis_size(axis)
    pairs = [(i, i + 1) for i in range(1, count - 1, 2)]
    first = lax.ppermute(first, axis, [(i, i ^ 1) for i in range(count)])
    return first, lax.ppermute(second, axis, pairs + [(j, i) for i, j in pairs])


def surface_tables():
    lane = np.arange(128)
    j, ey = lane // 8, lane % 8
    used = (j < 5) & (ey < 6)
    place = np.where(used, ey + 1, -9)
    source = lane[:, None]
    centre = source == place
    meet = centre | ((j == 0) & (source == place - 1)) | ((j == 4) & (source == place + 1))
    along = np.zeros((128, 128))
    for a in range(40):
        for b in range(40):
            if a % 8 == b % 8 and a % 8 < 6:
                along[a, b] = deriv[b // 8, a // 8]
    node = np.where(used, 4 * (ey - 1) + j, -9)
    fold = (lane[:, None] == node) & (lane[:, None] < 17)
    keep = fold & ((j < 4) & (ey < 5) | (j == 4) & (ey == 4))
    return np.stack([centre, meet, along, along.T, fold, keep]).astype(np.float32)


def full_dot(x, y, back=False):
    dims = (((1,), (1 if back else 0,)), ((), ()))
    return lax.dot_general(x, y, dims, precision=lax.Precision.HIGHEST, preferred_element_type=f32)


def deposit(faces, nodes_y, base_x, base_y, total):
    rows = faces.shape[1]
    sub = rows_of((8, 512)).astype(f32)
    total[...] = jnp.zeros_like(total)

    def one(step, carry):
        def wide(q):
            block = faces[q, pl.ds(4 * step, 4), :]
            return jnp.concatenate([block[n : n + 1] for n in range(4)], axis=1)

        ids = wide(3)
        node_x = jnp.floor((ids + 0.5) * (1.0 / nodes_y))
        rel_y = jnp.broadcast_to(ids - node_x * nodes_y - base_y, (8, 512))
        rel_x = jnp.broadcast_to(node_x - base_x, (8, 512))
        left = []
        hits = [(rel_x - i == 4.0 * sub) & (sub < 4.0) for i in range(5)]
        parts = [split_three(wide(c)) for c in range(3)]
        for part in range(3):
            for c in range(3):
                value = jnp.broadcast_to(parts[c][part].astype(f32), (8, 512))
                left += [jnp.where(hit, value, 0.0) for hit in hits]
        right = [jnp.where((rel_y - j == 4.0 * sub) & (sub < 6.0), 1.0, 0.0) for j in range(5)]
        right.append(jnp.zeros((88, 512), f32))
        left, right = jnp.concatenate(left, axis=0), jnp.concatenate(right, axis=0)
        total[...] += lax.dot_general(
            left.astype(jnp.bfloat16), right.astype(jnp.bfloat16), (((1,), (1,)), ((), ())), preferred_element_type=f32
        )
        return carry

    lax.fori_loop(0, rows // 4, one, 0)


def top_grid(rows, z):
    sub, lane = rows_of(), lanes_of()
    out = jnp.zeros((8, 128), f32)
    for x in range(3):
        for y in range(3):
            row = jnp.broadcast_to(rows[x][y], (8, 128))
            for ex in range(2):
                here = (sub == 2 * x + ex) & (lane >= 4 * y - 2) & (lane < 4 * y + 2) & (lane < 8)
                out = jnp.where(here, rolled(row, 4 * y - 2 - 8 * z - 4 * ex, 1), out)
    return out


def respond(total, grid, material, tables, out1, out2):
    sub, lane = rows_of(), lanes_of()
    top, below = top_grid(grid, 0), top_grid(grid, 1)
    centre, meet, along, along_t, fold, keep = [tables[n] for n in range(6)]
    sums0 = full_dot(lookup(material, 0, top), meet)
    sums1 = full_dot(lookup(material, 0, below), meet)
    lame = rolled(full_dot(lookup(material, 1, top), centre), -1)
    shear = rolled(full_dot(lookup(material, 2, top), centre), -1)
    weight_y = jnp.ones((8, 128), f32)
    for j in range(5):
        weight_y = jnp.where(lane // 8 == j, float(quad[j]), weight_y)

    def inverse(sums):
        mid = rolled(sums, -1)
        found = {0: mid + sums, 1: mid, 4: mid + rolled(sums, -2)}
        found = {i: jnp.where(s > 0.0, 1.0 / (s * weight_y), 0.0) for i, s in found.items()}
        found[2] = found[3] = found[1]
        return found

    light, heavy = inverse(sums0), inverse(sums0 + sums1)
    first = [[None] * 5 for _ in range(3)]
    moved = [[None] * 5 for _ in range(3)]
    for c in range(3):
        for i in range(5):
            at = (c * 5 + i) * 8
            force = total[at : at + 8] + total[at + 120 : at + 128] + total[at + 240 : at + 248]
            first[c][i] = force * light[i] * -accel_scale(i, 2, 0) * float(quad[2])
            moved[c][i] = first[c][i] * time_step**2
    gx = [line(deriv, moved[c]) for c in range(3)]
    gy = full_dot(jnp.concatenate([moved[c][i] for c in range(3) for i in range(5)], axis=0), along)
    gy = [[gy[(c * 5 + i) * 8 : (c * 5 + i) * 8 + 8] for i in range(5)] for c in range(3)]
    lame_w, shear_w = lame * weight_y * 2.0, shear * weight_y * 2.0
    d00 = float(deriv[0, 0])
    sx = [[], [], []]
    sy = [[], [], []]
    sz = [[], [], []]
    qs = [[], [], []]
    pressed = []
    for i in range(5):
        lw, mw = lame_w * float(quad[i]), shear_w * float(quad[i])
        d = [moved[c][i] for c in range(3)]
        gz = [d00 * x for x in d]
        dilated = lw * (gx[0][i] + gy[1][i] + gz[2])
        s01 = mw * (gx[1][i] + gy[0][i])
        s02 = mw * (gx[2][i] + gz[0])
        s12 = mw * (gy[2][i] + gz[1])
        for c, value in enumerate((dilated + 2.0 * mw * gx[0][i], s01, s02)):
            sx[c].append(value)
        for c, value in enumerate((s01, dilated + 2.0 * mw * gy[1][i], s12)):
            sy[c].append(value)
        for c, value in enumerate((s02, s12, dilated + 2.0 * mw * gz[2])):
            sz[c].append(value)
        for c, value in enumerate((mw * d[0], mw * d[1], (lw + 2.0 * mw) * d[2])):
            qs[c].append(value)
        pressed.append(lw * d[2])
    ydiv = full_dot(jnp.concatenate(sy[0] + sy[1] + sy[2] + pressed + qs[1], axis=0), along_t)
    ydiv = [[ydiv[(n * 5 + i) * 8 : (n * 5 + i) * 8 + 8] for i in range(5)] for n in range(5)]
    xdiv = [line(deriv_t, v) for v in sx + [pressed, qs[0]]]
    base = [xdiv[3], ydiv[3], [p + q for p, q in zip(xdiv[4], ydiv[4])]]
    second = {}
    for c in range(3):
        for i in range(5):
            for l in range(5):
                stiff = float(sum(deriv[k, l] * quad[k] * deriv[k, 0] for k in range(1, 5)))
                value = float(deriv[0, l] * quad[0]) * sz[c][i] + stiff * qs[c][i]
                if l:
                    value = value + float(deriv[l, 0] * quad[l]) * base[c][i]
                else:
                    value = value + float(quad[0]) * (xdiv[c][i] + ydiv[c][i])
                scale = (heavy if l == 4 else light)[i]
                second[c, i, l] = value * scale * (accel_scale(i, 2, l) * float(quad[2]))
    rows1, rows2 = [], []
    for c in range(3):
        for x in range(9):
            own = 1 if x < 4 else 2
            rows1.append(jnp.where(sub == 0, rolled(first[c][x - 4 * (own - 1)], -own), 0.0))
            block = jnp.zeros((8, 128), f32)
            for l in range(5):
                for ex in range(4):
                    i = x - 4 * (ex - 1)
                    if 0 <= i <= 4:
                        block = block + jnp.where(sub == l, rolled(second[c, i, l], l - ex), 0.0)
            rows2.append(block)
    blank = [jnp.zeros((40, 128), f32)]
    out1[...] = full_dot(keep[0:24], jnp.concatenate(rows1 + blank, axis=0), back=True)
    out2[...] = full_dot(fold[0:24], jnp.concatenate(rows2 + blank, axis=0), back=True)


def position(axis):
    return lax.axis_index(axis)


def along_y():
    return lax.axis_index("grp") * lax.axis_size("gy") + lax.axis_index("gy")


def primitives(state):
    inverse = 1.0 / state[0]
    v = [state[1 + c] * inverse for c in range(3)]
    p = (gamma_gas - 1.0) * (state[4] - 0.5 * (state[1] * v[0] + state[2] * v[1] + state[3] * v[2]))
    return v + [p, jnp.sqrt(gamma_gas * p * inverse), state[4] + p]


def flux(state, prim, d):
    out = [state[1 + d]] + [state[1 + c] * prim[d] for c in range(3)] + [prim[5] * prim[d]]
    out[1 + d] = out[1 + d] + prim[3]
    return out, jnp.abs(prim[d]) + prim[4]


def twice_face(low, high):
    fastest = jnp.maximum(low[2], high[2])
    return [fl + fh - fastest * (uh - ul) for ul, uh, fl, fh in zip(low[0], high[0], low[1], high[1])]


def turned_change(state, prim, d, axis, ends):
    size = state[0].shape[axis]
    fluxes, speed = flux(state, prim, d)
    up = lambda x: pltpu.roll(x, size - 1, axis)
    high = ([up(x) for x in state], [up(x) for x in fluxes], up(speed))
    upper = twice_face((state, fluxes, speed), high)
    if ends is None:
        return [g - pltpu.roll(g, 1, axis) for g in upper]
    upper = [jnp.where(ends[1], 2.0 * f, g) for f, g in zip(fluxes, upper)]
    return [g - jnp.where(ends[0], 2.0 * f, pltpu.roll(g, 1, axis)) for f, g in zip(fluxes, upper)]


def start_kernel(nodes_y, density, momentum, energy, dest, slot, region, bottoms, first, second, rows_low, rows_high,
                 region_out, cells, dest_in, slot_in, region_in, semaphores):
    copies = fetch(
        [(dest, dest_in), (slot, slot_in), (region, region_in), (density, cells.at[0]),
         (momentum, cells.at[pl.ds(1, 3)]), (energy, cells.at[4])],
        semaphores,
    )
    for copy in copies:
        copy.wait()
    sub, lane = rows_of(), lanes_of()
    pick = jnp.where(lane == 125 + sub, 1.0, 0.0)
    pieces = []
    odd = parity_x()
    for f in range(5):
        columns = jnp.concatenate([cells[f, x, :, 128:256] for x in range(4)], axis=0)
        pieces.append(full_dot(pick, columns, back=True)[0:3])
        for out, down in ((first, odd), (second, 1 - odd)):
            out[f, 0:32, :] = cells[f, 3 - 3 * down]
            out[f, 32:64, :] = cells[f, 2 - down]
        for t in range(2):
            lanes = slice(128 * t, 128 * t + 128)
            for out, pair in ((rows_low, (0, 1)), (rows_high, (31, 30))):
                out[f * 2 + t] = jnp.concatenate([cells[f, x, r : r + 1, lanes] for r in pair for x in range(4)], axis=0)
    count_gy, count_x = lax.axis_size("gy"), lax.axis_size("gx")
    target, node = dest_in[...].astype(f32), slot_in[...].astype(f32)
    grp = jnp.floor((target + 0.5) * (1.0 / (count_gy * count_x)))
    rest = target - grp * (count_gy * count_x)
    gx = jnp.floor((rest + 0.5) * (1.0 / count_gy))
    gy = rest - gx * count_gy
    i = jnp.floor((node + 0.5) * (1.0 / 17.0))
    j = node - 17.0 * i
    pieces.append((8.0 * gx + i) * nodes_y + 16.0 * (grp * count_gy + gy) + j)
    region_now = jnp.concatenate([region_in[0], region_in[1]], axis=0).astype(f32) + 1.0
    region_out[...] = region_now
    found = jnp.zeros((8, 128), f32)
    for z in range(2):
        found = jnp.where(lane == 8 * z + sub, jnp.broadcast_to(region_now[:, z : z + 1], (8, 128)), found)
    pieces.append(jnp.broadcast_to(jnp.sum(found, axis=0, keepdims=True), (8, 128)))
    block = jnp.concatenate(pieces, axis=0)
    for n in range(bottoms.shape[0]):
        bottoms[n] = block


def crater_kernel(density, momentum, energy, came1, came2, rows1, rows2, after, out, token,
                  wide, mid, prims, face, fluxes, semaphores):
    planes, inner = pl.ds(2, 4), pl.ds(0, 32)
    copies = fetch(
        [(density, wide.at[0, planes, inner]), (momentum, wide.at[pl.ds(1, 3), planes, inner]),
         (energy, wide.at[4, planes, inner])],
        semaphores,
    )
    place, last_y = along_y(), lax.axis_size("grp") * lax.axis_size("gy") - 1
    gx, last_x = position("gx"), lax.axis_size("gx") - 1
    odd, odd_y = parity_x(), parity_y()
    for f in range(5):
        low, high = sort_out(odd, came1[f], came2[f])
        for p, value in ((0, low[32:64]), (1, low[0:32]), (6, high[0:32]), (7, high[32:64])):
            wide[f, p, 0:32, :] = value
            wide[f, p, 32:40, :] = value[0:8]
    token[...] = after[...]
    for copy in copies:
        copy.wait()
    for f in range(5):
        for x in range(4):
            wide[f, 2 + x, 32:40, :] = wide[f, 2 + x, 24:32, :]
        for t in range(2):
            lanes = slice(128 * t, 128 * t + 128)
            at = 18 + f * 2 + t
            below, above = sort_out(odd_y, rows1[at], rows2[at])
            sides_below, sides_above = sort_out(odd_y, rows1[28 + f], rows2[28 + f])

            def put(p, row, edge, value):
                clamped = jnp.where(edge == 0, place == 0, place == last_y)
                at_edge = wide[f, p, 31 * edge : 31 * edge + 1, lanes]
                wide[f, p, row : row + 1, lanes] = jnp.where(clamped, at_edge, value)

            for x in range(4):
                put(2 + x, 39, 0, below[x : x + 1])
                put(2 + x, 38, 0, below[4 + x : 5 + x])
                put(2 + x, 32, 1, above[x : x + 1])
                put(2 + x, 33, 1, above[4 + x : 5 + x])
            for p, n in ((1, 2 * t), (6, 2 * t + 1)):
                put(p, 39, 0, sides_below[n : n + 1])
                put(p, 32, 1, sides_above[n : n + 1])

    @pl.when(gx == 0)
    def _():
        for f in range(5):
            wide[f, 0] = wide[f, 2]
            wide[f, 1] = wide[f, 2]

    @pl.when(gx == last_x)
    def _():
        for f in range(5):
            wide[f, 6] = wide[f, 5]
            wide[f, 7] = wide[f, 5]

    lane = lanes_of((40, 256))
    ends = (lane == 0, lane == 255)

    def step(source, low, high, put):
        def along_x(p):
            state = [source[f, p] for f in range(5)]
            prim = primitives(state)
            return state, prim, flux(state, prim, 0)

        state, prim, (fx, speed) = along_x(low - 1)
        next_state, next_prim, (next_fx, next_speed) = along_x(low)
        g = twice_face((state, fx, speed), (next_state, next_fx, next_speed))
        for f in range(5):
            face[f] = g[f]
            fluxes[f] = next_fx[f]
        for n in range(6):
            prims[n] = next_prim[n]
        fluxes[5] = next_speed

        def plane(p, carry):
            state = [source[f, p] for f in range(5)]
            prim = [prims[n] for n in range(6)]
            next_state, next_prim, (next_fx, next_speed) = along_x(p + 1)
            g = twice_face((state, [fluxes[f] for f in range(5)], fluxes[5]), (next_state, next_fx, next_speed))
            change = [g[f] - face[f] for f in range(5)]
            for f in range(5):
                face[f] = g[f]
                fluxes[f] = next_fx[f]
            for n in range(6):
                prims[n] = next_prim[n]
            fluxes[5] = next_speed
            change = [a + b for a, b in zip(change, turned_change(state, prim, 1, 0, None))]
            change = [a + b for a, b in zip(change, turned_change(state, prim, 2, 1, ends))]
            for f in range(5):
                put(f, p, state[f] - (0.5 * cell_ratio) * change[f])
            return carry

        lax.fori_loop(low, high, plane, 0)

    def put_mid(f, p, value):
        mid[f, p] = value

    def put_out(f, p, value):
        out[f, p - 2] = value[0:32]

    step(wide, 1, 7, put_mid)

    @pl.when(gx == 0)
    def _():
        for f in range(5):
            mid[f, 1] = mid[f, 2]

    @pl.when(gx == last_x)
    def _():
        for f in range(5):
            mid[f, 6] = mid[f, 5]

    for f in range(5):
        for p in range(2, 6):
            edge = mid[f, p, 39:40, :]
            mid[f, p, 39:40, :] = jnp.where(place == 0, mid[f, p, 0:1, :], edge)
            edge = mid[f, p, 32:33, :]
            mid[f, p, 32:33, :] = jnp.where(place == last_y, mid[f, p, 31:32, :], edge)
    step(mid, 2, 6, put_out)


def bottom_tractions(bottoms, count_x, faces):
    shape = (count_x, 128)
    sub, lane = rows_of(shape), lanes_of(shape)
    count_gy = lax.axis_size("gy")

    def columns(q):
        parts = []
        for y in range(4):
            start = (y // count_gy * count_x * count_gy + y % count_gy) * 24 + q
            parts.append(bottoms[pl.ds(start, count_x, stride=24 * count_gy), :])
        found = []
        for x in range(4):
            total = rolled(parts[0], -32 * x, 1)
            for y in range(1, 4):
                total = jnp.where(lane // 32 == y, rolled(parts[y], 32 * (y - x), 1), total)
            found.append(total)
        return found

    cells = [[columns(f * 3 + z) for f in range(5)] for z in range(3)]
    state = [[[cells[z][f][x] for f in range(5)] for x in range(4)] for z in range(3)]
    ends_y = (lane == 0, lane == 127)

    def across_x(states, prims):
        fluxes = [flux(s, p, 0) for s, p in zip(states, prims)]
        data = [(s, f, a) for s, (f, a) in zip(states, fluxes)]
        up = lambda x: rolled(x, -1)
        wrap = ([up(v) for v in data[0][0]], [up(v) for v in data[0][1]], up(data[0][2]))
        upper = [twice_face(data[x], data[x + 1] if x < 3 else wrap) for x in range(4)]
        upper[3] = [jnp.where(sub == count_x - 1, 2.0 * f, g) for f, g in zip(data[3][1], upper[3])]
        below = [jnp.where(sub == 0, 2.0 * f, rolled(g, 1)) for f, g in zip(data[0][1], upper[3])]
        lower = [below] + upper[:3]
        return [[a - b for a, b in zip(u, l)] for u, l in zip(upper, lower)]

    def advanced(above, here, under, prim_above, prim_here, prim_under):
        changes = across_x(here, prim_here)
        out = []
        for x in range(4):
            change = [a + b for a, b in zip(changes[x], turned_change(here[x], prim_here[x], 1, 1, ends_y))]
            fz, az = flux(here[x], prim_here[x], 2)
            fa, aa = flux(above[x], prim_above[x], 2)
            lower = twice_face((above[x], fa, aa), (here[x], fz, az))
            if under is None:
                upper = [2.0 * f for f in fz]
            else:
                fu, au = flux(under[x], prim_under[x], 2)
                upper = twice_face((here[x], fz, az), (under[x], fu, au))
            out.append([s - (0.5 * cell_ratio) * (c + u - l) for s, c, u, l in zip(here[x], change, upper, lower)])
        return out

    prims = [[primitives(state[z][x]) for x in range(4)] for z in range(3)]
    middle = advanced(state[0], state[1], state[2], prims[0], prims[1], prims[2])
    deepest = advanced(state[1], state[2], None, prims[1], prims[2], None)
    prim_mid, prim_deep = [primitives(s) for s in middle], [primitives(s) for s in deepest]
    final = advanced(middle, deepest, None, prim_mid, prim_deep, None)
    ids = columns(15)
    for x in range(4):
        s, prim = final[x], primitives(final[x])
        at = pl.ds(x * count_x, count_x)
        faces[0, at, :] = face_area * s[1] * prim[2]
        faces[1, at, :] = face_area * s[2] * prim[2]
        faces[2, at, :] = face_area * (s[3] * prim[2] + prim[3])
        faces[3, at, :] = ids[x]


def deposit_kernel(nodes_y, count_x, bottoms, after, total, faces):
    base_x = (8 * position("gx") - 4).astype(f32)
    base_y = (16 * along_y() - 4).astype(f32)
    bottom_tractions(bottoms, count_x, faces)
    deposit(faces, nodes_y, base_x, base_y, total)


def respond_kernel(count_x, total, bottoms, material, tables, after, out1, out2, token, held, rows, semaphores):
    gx, place, count_gy = position("gx"), along_y(), lax.axis_size("gy")
    last_y = lax.axis_size("grp") * count_gy - 1
    pairs = [(tables, held)]
    for x in range(3):
        for y in range(3):
            cx, cy = jnp.clip(gx + x - 1, 0, count_x - 1), jnp.clip(place + y - 1, 0, last_y)
            rank = (cy // count_gy) * (count_x * count_gy) + cx * count_gy + cy % count_gy
            pairs.append((bottoms.at[rank, pl.ds(16, 8), :], rows.at[3 * x + y]))
    copies = fetch(pairs, semaphores)
    for copy in copies:
        copy.wait()
    found = []
    for x in range(3):
        found.append([])
        for y in range(3):
            px, py = gx + x - 1, place + y - 1
            inside = (px >= 0) & (px < count_x) & (py >= 0) & (py <= last_y)
            found[x].append(jnp.where(inside, rows[3 * x + y, 0:1, :], 0.0))
    respond(total, found, material, held, out1, out2)
    token[...] = after[...]


def shards(density, momentum, energy, displacement, velocity_field, acceleration, material, element_region_index,
           face_dest, face_slot):
    along, rank = ("grp", "gy"), ("grp", "gx", "gy")
    nodes_y = 16 * lax.axis_size(along) + 1
    count_x, devices = lax.axis_size("gx"), lax.axis_size(rank)
    crater = (density, momentum, energy)
    u, v, a = [jnp.transpose(x, (1, 2, 0, 3)) for x in (displacement, velocity_field, acceleration)]
    register, held_shape = (8, 128), (4, 1224, 128)
    bottoms, crater1, crater2, rows_low, rows_high, region = call(
        functools.partial(start_kernel, float(nodes_y)),
        crater + (face_dest.reshape(1, -1), face_slot, element_region_index),
        [(devices, 24, 128), (5, 64, 256), (5, 64, 256), (10, 8, 128), (10, 8, 128), register],
        [(5, 4, 32, 256), pltpu.VMEM((1, 128), jnp.int32), pltpu.VMEM((1, 128), jnp.int32),
         pltpu.VMEM((2, 4, 128), jnp.int32)],
        away=(0, 1, 2, 3, 4, 5),
        mib=56,
        copies=6,
    )
    bottoms = lax.all_to_all(bottoms, rank, 0, 0, tiled=True)
    crater1, crater2 = exchange("gx", crater1, crater2)
    b, f, x1, x2, y_rows = call(
        first_kernel,
        (u, v, a, region, material),
        [element_shape, element_shape, (31, 8, 128), (31, 8, 128), (31, 8, 128)],
        internal_scratch
        + [held_shape] * 3
        + [(3, 5, 5, 8, 256), (3, 5, 5, 8, 256), (600, 256), (600, 256), element_shape],
        smem=(4,),
        away=(0, 1, 2),
        out_away=(0,),
        mib=56,
        copies=13,
    )
    (total,) = call(
        functools.partial(deposit_kernel, float(nodes_y), count_x),
        (bottoms.reshape(devices * 24, 128), y_rows),
        [(360, 128)],
        [(4, 4 * count_x, 128)],
    )
    x1, x2 = exchange("gx", x1, x2)
    y1, y2, token = call(
        first_edge_kernel,
        (y_rows, x1, x2, rows_low, rows_high, crater1, crater2, total),
        [(33, 8, 128), (33, 8, 128), register],
        [(2, 5, 16, 256)],
        away=(5, 6),
        copies=4,
    )
    surf1, surf2, token = call(
        functools.partial(respond_kernel, count_x),
        (total, bottoms, material, jnp.asarray(surface_tables()), token),
        [(24, 256), (24, 256), register],
        [(6, 128, 128), (9, 8, 128)],
        smem=(2,),
        away=(1, 3),
        copies=10,
    )
    y1, y2 = exchange(along, y1, y2)
    a1, f2, p1, p2, y_low, y_high, scales, token = call(
        second_kernel,
        (b, f, x1, x2, y1, y2, region, material, token),
        [element_shape, element_shape, (30, 8, 128), (30, 8, 128), (15, 8, 128), (15, 8, 128), (3, 3, 2, 8, 128), register],
        internal_scratch,
        smem=(7,),
    )
    hydro_state, token = call(
        crater_kernel,
        crater + (crater1, crater2, y1, y2, token),
        [(5, 4, 32, 256), register],
        [(5, 8, 40, 256), (5, 8, 40, 256), (6, 40, 256), (5, 40, 256), (6, 40, 256)],
        away=(0, 1, 2),
        copies=3,
    )
    p1, p2 = exchange("gx", p1, p2)
    r1, r2, token = call(
        second_edge_kernel, (y_low, y_high, p1, p2, token), [(15, 8, 128), (15, 8, 128), register], []
    )
    u_out, v_part = call(
        place_kernel,
        (a1, surf1, u, v, a, token),
        [u.shape, held_shape],
        [held_shape] * 3 + [(2, 3, 5, 5, 8, 256), (27, 24, 128), held_shape],
        away=(2, 3, 4),
        out_away=(0,),
        mib=20,
        copies=16,
    )
    r1, r2 = exchange(along, r1, r2)
    v_out, a_out = call(
        last_kernel,
        (v_part, f2, p1, p2, r1, r2, scales, surf1, surf2),
        [u.shape] * 2,
        [held_shape] * 2 + [(2, 3, 5, 5, 8, 256), (2, 27, 24, 128), element_shape],
        out_away=(0, 1),
        mib=16,
        copies=8,
    )
    u_out, v_out, a_out = [jnp.transpose(x, (2, 0, 1, 3)) for x in (u_out, v_out, a_out)]
    return hydro_state, u_out, v_out, a_out


def solution(mesh):
    field = P(None, "gx", ("grp", "gy"), None)
    cells = P("gx", ("grp", "gy"), None)
    rank = ("grp", "gx", "gy")
    return jax.shard_map(
        shards,
        mesh=mesh,
        in_specs=(cells, field, cells, field, field, field, P(), cells, P(rank, None, None), P(rank, None)),
        out_specs=(field, field, field, field),
        check_vma=False,
    )
```
